32 devices in a mesh: fsdp: 8 (over y, x, core), tensor: 4 (over z).
Axes of the slice: x: 2, y: 2, z: 4, core: 2. Of those that a mesh axis runs over, the one named last changes fastest.
Arguments:
- image_rows: bfloat16 [16, 1024, 1024], P('fsdp', 'tensor'), may hold values from -6 to 6
- text_rows: bfloat16 [16, 128, 1024], P('fsdp', 'tensor'), may hold values from -6 to 6
- segment_ids: int32 [16, 128], P('fsdp'), may hold values from 0 to 3, as said below
- cotangent: bfloat16 [16, 1024, 1024], P('fsdp', 'tensor'), may hold values from -6 to 6
- query_weight: bfloat16 [1024, 1024], P('fsdp', 'tensor'), may hold values from -0.1875 to 0.1875
- key_weight: bfloat16 [1024, 1024], P('fsdp', 'tensor'), may hold values from -0.1875 to 0.1875
- value_weight: bfloat16 [1024, 1024], P('fsdp', 'tensor'), may hold values from -0.1875 to 0.1875
- attn_output: bfloat16 [1024, 1024], P('fsdp', 'tensor'), may hold values from -1.5 to 1.5
- cross_query: bfloat16 [1024, 1024], P('fsdp', 'tensor'), may hold values from -0.1875 to 0.1875
- cross_key: bfloat16 [1024, 1024], P('fsdp', 'tensor'), may hold values from -0.1875 to 0.1875
- cross_value: bfloat16 [1024, 1024], P('fsdp', 'tensor'), may hold values from -0.1875 to 0.1875
- cross_output: bfloat16 [1024, 1024], P('fsdp', 'tensor'), may hold values from -0.75 to 0.75
- hidden_in: bfloat16 [1024, 4096], P('fsdp', 'tensor'), may hold values from -0.1875 to 0.1875
- hidden_out: bfloat16 [1024, 4096], P('fsdp', 'tensor'), may hold values from -0.09375 to 0.09375
- gain_attn: float32 [1024], P('fsdp'), may hold values from 0.25 to 1.75
- bias_attn: float32 [1024], P('fsdp'), may hold values from -4 to 4
- gain_cross: float32 [1024], P('fsdp'), may hold values from 0.25 to 1.75
- bias_cross: float32 [1024], P('fsdp'), may hold values from -4 to 4
- gain_mlp: float32 [1024], P('fsdp'), may hold values from 0.25 to 1.75
- bias_mlp: float32 [1024], P('fsdp'), may hold values from -4 to 4
Outputs:
- result: bfloat16 [16, 1024, 1024], P('fsdp', 'tensor')
- input_grad: float32 [16, 1024, 1024], P('fsdp', 'tensor')
- text_grad: float32 [16, 128, 1024], P('fsdp', 'tensor')
- grad_query_weight: float32 [1024, 1024], P('fsdp', 'tensor')
- grad_key_weight: float32 [1024, 1024], P('fsdp', 'tensor')
- grad_value_weight: float32 [1024, 1024], P('fsdp', 'tensor')
- grad_attn_output: float32 [1024, 1024], P('fsdp', 'tensor')
- grad_cross_query: float32 [1024, 1024], P('fsdp', 'tensor')
- grad_cross_key: float32 [1024, 1024], P('fsdp', 'tensor')
- grad_cross_value: float32 [1024, 1024], P('fsdp', 'tensor')
- grad_cross_output: float32 [1024, 1024], P('fsdp', 'tensor')
- grad_hidden_in: float32 [1024, 4096], P('fsdp', 'tensor')
- grad_hidden_out: float32 [1024, 4096], P('fsdp', 'tensor')
- grad_gain_attn: float32 [1024], P('fsdp')
- grad_bias_attn: float32 [1024], P('fsdp')
- grad_gain_cross: float32 [1024], P('fsdp')
- grad_bias_cross: float32 [1024], P('fsdp')
- grad_gain_mlp: float32 [1024], P('fsdp')
- grad_bias_mlp: float32 [1024], P('fsdp')
The draws below stay inside these ranges and needn't reach their ends.
Inputs may be any that keep to these rules, and one draw needn't show every extreme that they name: `segment_ids`: along each row the ids never fall, and each of the 4 ids appears.
All inputs are finite; a program needn't handle non-finite values.
Results may differ from the reference program's by a relative error of at most 0.035.
Values may be sent and summed in bfloat16 or wider, within the bound.
No kernel may reach another device: no remote copies, remote signals or barrier semaphores. Data moves between devices by JAX's collectives and lax.ppermute only.
A program may use at most 192 MiB of HBM per device.

```python
import math
import jax
import jax.numpy as jnp
from jax import lax

D = 1024
H = 16
HD = 64
FF = 4096
SEQ = 1024
TXT = 128
SEGS = 4
IMAGES = 16


def draw_segment_ids(key, part):
    key = jax.random.fold_in(key, 7)
    long_key, short_key = jax.random.split(key)
    short_most = max(TXT // 32, 1)
    longest = jax.random.randint(long_key, (IMAGES, 1), 0, SEGS)
    lengths = jax.random.randint(short_key, (IMAGES, SEGS), 1, short_most + 1)
    slot_ids = lax.iota(jnp.int32, SEGS)[None, :]
    is_long = slot_ids == longest
    others = jnp.sum(jnp.where(is_long, 0, lengths), 1, keepdims=True)
    lengths = jnp.where(is_long, TXT - others, lengths)
    segment_end = jnp.cumsum(lengths, 1)
    positions = lax.iota(jnp.int32, TXT)[None, :, None]
    return jnp.sum((positions >= segment_end[:, None, :]).astype(jnp.int32), -1).astype(jnp.int32)


def with_spikes(values, key, source, target, blocks, factor):
    def block_of(position):
        return (jnp.arange(values.shape[position]) // (values.shape[position] // blocks)).reshape((-1,) + (1,) * (values.ndim - 1 - position))

    one_side = jax.random.permutation(key, blocks)[block_of(target)]
    other_side = (block_of(target) + blocks // 2) % blocks
    return jnp.where((block_of(source) == one_side) | (block_of(source) == other_side), factor * values, values)


def shard_levels(key, dims, pieces, smallest, largest):
    def one(axis_at, shards_of):
        heights = jax.random.uniform(jax.random.fold_in(jax.random.fold_in(key, 6), axis_at), (shards_of,), jnp.float32, smallest / len(pieces), largest / len(pieces))
        return jnp.repeat(jnp.exp(heights), dims[axis_at] // shards_of).reshape((-1,) + (1,) * (len(dims) - axis_at - 1))

    level = one(*pieces[0])
    for cut in pieces[1:]:
        level = level * one(*cut)
    return level


def scatter_about(key, shape, scale, most, pieces=(), dtype=jnp.bfloat16):
    array = scale * jax.random.normal(key, shape, jnp.float32)
    if pieces:
        array = array * shard_levels(key, shape, pieces, -0.22, 0.18)
    return jnp.clip(array, -most, most).astype(dtype)


def heavy_noise(stream_key, dims, scale, most, pieces, heavy, dtype=jnp.bfloat16):
    values = scale * jax.random.normal(stream_key, dims, jnp.float32)
    if pieces:
        values = values * shard_levels(stream_key, dims, pieces, -0.22, 0.18)
    return jnp.clip(with_spikes(values, jax.random.fold_in(stream_key, 3), *heavy), -most, most).astype(dtype)


def setup_inputs(seed: int = 0) -> dict:
    splits = jax.random.split(jax.random.key(seed), 21)
    return {
        "image_rows": heavy_noise(splits[0], (IMAGES, SEQ, D), 1.0, 6.0, ((0, 8), (1, 4)), (0, 2, 8, 2.0)),
        "text_rows": scatter_about(splits[1], (IMAGES, TXT, D), 1.0, 6.0, ((0, 8), (1, 4))),
        "segment_ids": draw_segment_ids(jax.random.fold_in(splits[20], 71), 0),
        "cotangent": heavy_noise(splits[3], (IMAGES, SEQ, D), 1.0, 6.0, ((0, 8), (1, 4)), (0, 2, 8, 2.0)),
        "query_weight": scatter_about(splits[4], (D, H * HD), D ** -0.5, 0.1875, ((0, 8), (1, 4))),
        "key_weight": scatter_about(splits[5], (D, H * HD), D ** -0.5, 0.1875, ((0, 8), (1, 4))),
        "value_weight": scatter_about(splits[6], (D, H * HD), D ** -0.5, 0.1875, ((0, 8), (1, 4))),
        "attn_output": scatter_about(splits[7], (D, H * HD), (D // 64) ** -0.5, 1.5, ((0, 8), (1, 4))),
        "cross_query": scatter_about(splits[8], (D, H * HD), D ** -0.5, 0.1875, ((0, 8), (1, 4))),
        "cross_key": scatter_about(splits[9], (D, H * HD), D ** -0.5, 0.1875, ((0, 8), (1, 4))),
        "cross_value": scatter_about(splits[10], (D, H * HD), D ** -0.5, 0.1875, ((0, 8), (1, 4))),
        "cross_output": scatter_about(splits[11], (D, H * HD), (D // 16) ** -0.5, 0.75, ((0, 8), (1, 4))),
        "hidden_in": scatter_about(splits[12], (D, FF), D ** -0.5, 0.1875, ((0, 8), (1, 4))),
        "hidden_out": scatter_about(splits[13], (D, FF), FF ** -0.5, 0.09375, ((0, 8), (1, 4))),
        "gain_attn": jnp.clip(1.0 + 0.15 * jax.random.normal(splits[14], (D,), jnp.float32), 0.25, 1.75),
        "bias_attn": scatter_about(splits[15], (D,), 0.3, 4.0, ((0, 8),), jnp.float32),
        "gain_cross": jnp.clip(1.0 + 0.15 * jax.random.normal(splits[16], (D,), jnp.float32), 0.25, 1.75),
        "bias_cross": scatter_about(splits[17], (D,), 0.3, 4.0, ((0, 8),), jnp.float32),
        "gain_mlp": jnp.clip(1.0 + 0.15 * jax.random.normal(splits[18], (D,), jnp.float32), 0.25, 1.75),
        "bias_mlp": scatter_about(splits[19], (D,), 0.3, 4.0, ((0, 8),), jnp.float32),
    }


EPS = 1e-05
NEG = -1e+30
HIGH = lax.Precision.HIGHEST

@jax.custom_vjp
def low(v):
    return lax.optimization_barrier(v.astype(jnp.bfloat16)).astype(jnp.float32)

@jax.custom_vjp
def low_back(v):
    return v

def low_keep(v):
    return (low(v), None)

def low_pass(kept, grad):
    return (grad,)

def back_keep(v):
    return (v, None)

def back_low(kept, grad):
    return (low(grad),)
low.defvjp(low_keep, low_pass)
low_back.defvjp(back_keep, back_low)

def layer_norm(values, gain, offset):
    center = values - lax.optimization_barrier(jnp.mean(values, -1, keepdims=True))
    spread = lax.optimization_barrier(jnp.mean(center * center, -1, keepdims=True))
    return center * lax.rsqrt(spread + EPS) * gain + offset

def gelu_tanh(values):
    return 0.5 * values * (1.0 + jnp.tanh(math.sqrt(2.0 / math.pi) * (values + 0.044715 * values * values * values)))

def matmul_high(left, right):
    return jnp.dot(left, right, precision=HIGH)

def attention(queries, key_rows, value_rows, visible):
    query_heads = queries.reshape(queries.shape[0], -1, HD)
    key_heads = key_rows.reshape(key_rows.shape[0], -1, HD)
    value_heads = value_rows.reshape(value_rows.shape[0], -1, HD)
    scores = low_back(jnp.einsum('qhd,khd->hqk', query_heads, key_heads, precision=HIGH) * HD ** (-0.5))
    scores = jnp.where(visible[None], scores, NEG)
    peak_score = lax.optimization_barrier(jnp.max(scores, -1, keepdims=True))
    exponent = jnp.exp(scores - peak_score)
    attn_prob = low(exponent / lax.optimization_barrier(jnp.sum(exponent, -1, keepdims=True)))
    mixed_rows = jnp.einsum('hqk,khd->qhd', attn_prob, value_heads, precision=HIGH)
    return low(low_back(mixed_rows.reshape(queries.shape[0], -1)))

def image_layer(rows, text, segs_row, params):
    query_weight, key_weight, value_weight, attn_output, cross_query, cross_key, cross_value, cross_output, hidden_in, hidden_out, gain_attn, bias_attn, gain_cross, bias_cross, gain_mlp, bias_mlp = params
    positions = lax.iota(jnp.int32, SEQ)
    causal = positions[None, :] <= positions[:, None]
    normed_one = low(layer_norm(rows, gain_attn, bias_attn))
    self_q = low(low_back(matmul_high(normed_one, query_weight)))
    self_k = low(low_back(matmul_high(normed_one, key_weight)))
    self_v = low(low_back(matmul_high(normed_one, value_weight)))
    attn_branch = low_back(matmul_high(attention(self_q, self_k, self_v, causal), attn_output.T))
    after_attn = rows + attn_branch
    normed_two = low(layer_norm(after_attn, gain_cross, bias_cross))
    text_low = low(text)
    cross_q = low(low_back(matmul_high(normed_two, cross_query)))
    cross_k = low(low_back(matmul_high(text_low, cross_key)))
    cross_v = low(low_back(matmul_high(text_low, cross_value)))
    text_place = (positions * TXT // SEQ).astype(jnp.int32)
    bands = segs_row[text_place]
    visible = segs_row[None, :] == bands[:, None]
    cross_branch = low_back(matmul_high(attention(cross_q, cross_k, cross_v, visible), cross_output.T))
    after_cross = after_attn + cross_branch
    normed_three = low(layer_norm(after_cross, gain_mlp, bias_mlp))
    hidden_pre = low_back(matmul_high(normed_three, hidden_in))
    hidden_act = low(gelu_tanh(hidden_pre))
    return after_cross + low_back(matmul_high(hidden_act, hidden_out.T))

def reference(image_rows, text_rows, segment_ids, cotangent, query_weight, key_weight, value_weight, attn_output, cross_query, cross_key, cross_value, cross_output, hidden_in, hidden_out, gain_attn, bias_attn, gain_cross, bias_cross, gain_mlp, bias_mlp):
    params = tuple((weight_in.astype(jnp.float32) for weight_in in (query_weight, key_weight, value_weight, attn_output, cross_query, cross_key, cross_value, cross_output, hidden_in, hidden_out, gain_attn, bias_attn, gain_cross, bias_cross, gain_mlp, bias_mlp)))
    checked = jax.checkpoint(image_layer)

    def forward(rows, text, params_in):
        return lax.map(lambda packed_in: checked(packed_in[0], packed_in[1], packed_in[2], params_in), (rows, text, segment_ids))
    result, pullback = jax.vjp(forward, image_rows.astype(jnp.float32), text_rows.astype(jnp.float32), params)
    input_grad, text_grad, grads = pullback(cotangent.astype(jnp.float32))
    return (result.astype(jnp.bfloat16), input_grad, text_grad, grads[0], grads[1], grads[2], grads[3], grads[4], grads[5], grads[6], grads[7], grads[8], grads[9], grads[10], grads[11], grads[12], grads[13], grads[14], grads[15])
```

```python
import functools
import math

import jax
import jax.numpy as jnp
from jax import lax
from jax.experimental import pallas as pl
from jax.experimental.pallas import tpu as pltpu
from jax.sharding import Mesh
from jax.sharding import PartitionSpec as P

HD = 64
EPS = 1e-05
NEG = -1e30
LOG2E = math.log2(math.e)
BF = jnp.bfloat16
F32 = jnp.float32
NT = (((1,), (1,)), ((), ()))
TN = (((0,), (0,)), ((), ()))
NN = (((1,), (0,)), ((), ()))


def dot(left, right, dims=NN):
    return lax.dot_general(left, right, dims, preferred_element_type=F32)


def lane_head(shape, axis, head):
    return lax.broadcasted_iota(jnp.int32, shape, axis) // HD == head


def self_forward_kernel(q_ref, k_ref, v_ref, mix_ref, lse_ref, *, block):
    length = q_ref.shape[0]
    scale = LOG2E * HD**-0.5
    causal = lax.broadcasted_iota(jnp.int32, (block, block), 0) <= lax.broadcasted_iota(
        jnp.int32, (block, block), 1
    )
    for at in range(length // block):
        lo, hi = at * block, (at + 1) * block
        query = q_ref[lo:hi, :]
        mixes = []
        for head in range(2):
            one = jnp.where(lane_head((1, 2 * HD), 1, head), query, jnp.zeros_like(query))
            diag = jnp.where(causal, dot(k_ref[lo:hi, :], one, NT), NEG)
            peak = jnp.max(diag, 0, keepdims=True)
            if at:
                past = dot(k_ref[:lo, :], one, NT)
                peak = jnp.maximum(peak, jnp.max(past, 0, keepdims=True))
            weights = jnp.exp2((diag - peak) * scale)
            total = jnp.sum(weights, 0, keepdims=True)
            mixed = dot(v_ref[lo:hi, :], weights.astype(BF), TN)
            if at:
                weights = jnp.exp2((past - peak) * scale)
                total = total + jnp.sum(weights, 0, keepdims=True)
                mixed = mixed + dot(v_ref[:lo, :], weights.astype(BF), TN)
            mixes.append(mixed / total)
            lse_ref[0, head : head + 1, lo:hi] = peak * scale + jnp.log2(total)
        both = jnp.where(lane_head((2 * HD, 1), 0, 0), mixes[0], mixes[1])
        mix_ref[lo:hi, :] = both.T.astype(BF)


def self_backward_kernel(
    q_ref, k_ref, v_ref, mix_ref, grad_ref, lse_ref, dq_ref, dk_ref, dv_ref, dk_sum, dv_sum, *, block
):
    length = q_ref.shape[0]
    scale = LOG2E * HD**-0.5
    causal = lax.broadcasted_iota(jnp.int32, (block, block), 0) <= lax.broadcasted_iota(
        jnp.int32, (block, block), 1
    )
    dk_sum[...] = jnp.zeros_like(dk_sum)
    dv_sum[...] = jnp.zeros_like(dv_sum)
    for at in range(length // block):
        lo, hi = at * block, (at + 1) * block
        query = q_ref[lo:hi, :]
        grad = grad_ref[lo:hi, :]
        product = (grad.astype(F32) * mix_ref[lo:hi, :].astype(F32)).T
        grads = []
        for head in range(2):
            picked = lane_head((1, 2 * HD), 1, head)
            one = jnp.where(picked, query, jnp.zeros_like(query))
            one_grad = jnp.where(picked, grad, jnp.zeros_like(grad))
            delta = jnp.sum(product[head * HD : (head + 1) * HD], 0, keepdims=True)
            lse = lse_ref[0, head : head + 1, lo:hi]
            total = jnp.zeros((2 * HD, block), F32)
            for start, stop in ((0, lo), (lo, hi)):
                if start == stop:
                    continue
                keys = k_ref[start:stop, :]
                weights = jnp.exp2(dot(keys, one, NT) * scale - lse)
                if start == lo:
                    weights = jnp.where(causal, weights, 0.0)
                slope = dot(v_ref[start:stop, :], one_grad, NT)
                score_grad = (weights * (slope - delta)).astype(BF)
                dv_sum[start:stop, :] += dot(weights.astype(BF), one_grad)
                dk_sum[start:stop, :] += dot(score_grad, one)
                total = total + dot(keys, score_grad, TN)
            grads.append(total)
        both = jnp.where(lane_head((2 * HD, 1), 0, 0), grads[0], grads[1])
        dq_ref[lo:hi, :] = (both.T * HD**-0.5).astype(BF)
    dk_ref[...] = (dk_sum[...] * HD**-0.5).astype(BF)
    dv_ref[...] = dv_sum[...].astype(BF)


def cross_forward_kernel(q_ref, k_ref, v_ref, ids_ref, caption_ref, mix_ref, lse_ref, *, block):
    length = q_ref.shape[0]
    scale = LOG2E * HD**-0.5
    for at in range(length // block):
        lo, hi = at * block, (at + 1) * block
        query = q_ref[lo:hi, :]
        seen = ids_ref[...] == caption_ref[:, lo:hi]
        mixes = []
        for head in range(2):
            one = jnp.where(lane_head((1, 2 * HD), 1, head), query, jnp.zeros_like(query))
            scores = jnp.where(seen, dot(k_ref[...], one, NT), NEG)
            peak = jnp.max(scores, 0, keepdims=True)
            weights = jnp.exp2((scores - peak) * scale)
            total = jnp.sum(weights, 0, keepdims=True)
            mixes.append(dot(v_ref[...], weights.astype(BF), TN) / total)
            lse_ref[0, head : head + 1, lo:hi] = peak * scale + jnp.log2(total)
        both = jnp.where(lane_head((2 * HD, 1), 0, 0), mixes[0], mixes[1])
        mix_ref[lo:hi, :] = both.T.astype(BF)


def cross_backward_kernel(
    q_ref, k_ref, v_ref, mix_ref, grad_ref, lse_ref, ids_ref, caption_ref, dq_ref, dk_ref, dv_ref, *, block
):
    length = q_ref.shape[0]
    scale = LOG2E * HD**-0.5
    keys, values = k_ref[...], v_ref[...]
    dk_sum = jnp.zeros(keys.shape, F32)
    dv_sum = jnp.zeros(keys.shape, F32)
    for at in range(length // block):
        lo, hi = at * block, (at + 1) * block
        query = q_ref[lo:hi, :]
        grad = grad_ref[lo:hi, :]
        product = (grad.astype(F32) * mix_ref[lo:hi, :].astype(F32)).T
        seen = ids_ref[...] == caption_ref[:, lo:hi]
        grads = []
        for head in range(2):
            picked = lane_head((1, 2 * HD), 1, head)
            one = jnp.where(picked, query, jnp.zeros_like(query))
            one_grad = jnp.where(picked, grad, jnp.zeros_like(grad))
            delta = jnp.sum(product[head * HD : (head + 1) * HD], 0, keepdims=True)
            lse = lse_ref[0, head : head + 1, lo:hi]
            weights = jnp.where(seen, jnp.exp2(dot(keys, one, NT) * scale - lse), 0.0)
            slope = dot(values, one_grad, NT)
            score_grad = (weights * (slope - delta)).astype(BF)
            dv_sum = dv_sum + dot(weights.astype(BF), one_grad)
            dk_sum = dk_sum + dot(score_grad, one)
            grads.append(dot(keys, score_grad, TN))
        both = jnp.where(lane_head((2 * HD, 1), 0, 0), grads[0], grads[1])
        dq_ref[lo:hi, :] = (both.T * HD**-0.5).astype(BF)
    dk_ref[...] = (dk_sum * HD**-0.5).astype(BF)
    dv_ref[...] = dv_sum.astype(BF)


def feed_kernel(
    rows_ref, cot_ref, win_ref, wout_ref, out_in, back_in, gin_ref, gout_ref, out_ref, back_ref, rows_t, cot_t, *, first
):
    step = pl.program_id(0)

    @pl.when(step == 0)
    def _():
        rows_t[...] = rows_ref[...].T
        cot_t[...] = cot_ref[...].T
        if first:
            out_ref[...] = jnp.zeros_like(out_ref)
            back_ref[...] = jnp.zeros_like(back_ref)
        else:
            out_ref[...] = out_in[...]
            back_ref[...] = back_in[...]

    pre = dot(rows_ref[...], win_ref[...])
    square = pre * pre
    slope = math.sqrt(2.0 / math.pi)
    bent = jnp.tanh(pre * (slope + slope * 0.044715 * square))
    half = 0.5 * (1.0 + bent)
    act = (pre * half).astype(BF)
    out_ref[...] += dot(act, wout_ref[...], NT)
    gout_ref[...] = dot(cot_t[...], act).astype(BF)
    bend = half + pre * (0.5 * (1.0 - bent * bent)) * (slope + 3.0 * slope * 0.044715 * square)
    pre_grad = (dot(cot_ref[...], wout_ref[...]) * bend).astype(BF)
    gin_ref[...] = dot(rows_t[...], pre_grad).astype(BF)
    back_ref[...] += dot(pre_grad, win_ref[...], NT)


VMEM_LIMIT = 60 * 1024 * 1024


def params():
    return pltpu.CompilerParams(vmem_limit_bytes=VMEM_LIMIT)


def column(rows, offset):
    return pl.BlockSpec((rows, 2 * HD), lambda i: (0, offset + i))


def self_forward(packed):
    length, width = packed.shape
    pairs = width // (6 * HD)
    return pl.pallas_call(
        functools.partial(self_forward_kernel, block=256),
        grid=(pairs,),
        in_specs=[column(length, 0), column(length, pairs), column(length, 2 * pairs)],
        out_specs=[column(length, 0), pl.BlockSpec((1, 2, length), lambda i: (i, 0, 0))],
        out_shape=[
            jax.ShapeDtypeStruct((length, pairs * 2 * HD), BF),
            jax.ShapeDtypeStruct((pairs, 2, length), F32),
        ],
        compiler_params=params(),
        cost_estimate=pl.CostEstimate(
            flops=8 * pairs * length * length * 2 * HD * 2,
            bytes_accessed=8 * pairs * length * 2 * HD,
            transcendentals=2 * pairs * length * length,
        ),
    )(packed, packed, packed)


def self_backward(packed, mix, grad, lse):
    length, width = packed.shape
    pairs = width // (6 * HD)
    part = jax.ShapeDtypeStruct((length, pairs * 2 * HD), BF)
    return pl.pallas_call(
        functools.partial(self_backward_kernel, block=256),
        grid=(pairs,),
        in_specs=[
            column(length, 0),
            column(length, pairs),
            column(length, 2 * pairs),
            column(length, 0),
            column(length, 0),
            pl.BlockSpec((1, 2, length), lambda i: (i, 0, 0)),
        ],
        out_specs=[column(length, 0)] * 3,
        out_shape=[part] * 3,
        scratch_shapes=[pltpu.VMEM((length, 2 * HD), F32)] * 2,
        compiler_params=params(),
        cost_estimate=pl.CostEstimate(
            flops=20 * pairs * length * length * 2 * HD * 2,
            bytes_accessed=16 * pairs * length * 2 * HD,
            transcendentals=2 * pairs * length * length,
        ),
    )(packed, packed, packed, mix, grad, lse)


def cross_forward(queries, keys, ids, captions):
    length, width = queries.shape
    texts = keys.shape[0]
    pairs = width // (2 * HD)
    return pl.pallas_call(
        functools.partial(cross_forward_kernel, block=min(512, length)),
        grid=(pairs,),
        in_specs=[
            column(length, 0),
            column(texts, 0),
            column(texts, pairs),
            pl.BlockSpec((texts, 1), lambda i: (0, 0)),
            pl.BlockSpec((1, length), lambda i: (0, 0)),
        ],
        out_specs=[column(length, 0), pl.BlockSpec((1, 2, length), lambda i: (i, 0, 0))],
        out_shape=[
            jax.ShapeDtypeStruct((length, width), BF),
            jax.ShapeDtypeStruct((pairs, 2, length), F32),
        ],
        compiler_params=params(),
    )(queries, keys, keys, ids, captions)


def cross_backward(queries, keys, mix, grad, lse, ids, captions):
    length, width = queries.shape
    texts = keys.shape[0]
    pairs = width // (2 * HD)
    return pl.pallas_call(
        functools.partial(cross_backward_kernel, block=min(512, length)),
        grid=(pairs,),
        in_specs=[
            column(length, 0),
            column(texts, 0),
            column(texts, pairs),
            column(length, 0),
            column(length, 0),
            pl.BlockSpec((1, 2, length), lambda i: (i, 0, 0)),
            pl.BlockSpec((texts, 1), lambda i: (0, 0)),
            pl.BlockSpec((1, length), lambda i: (0, 0)),
        ],
        out_specs=[column(length, 0), column(texts, 0), column(texts, 0)],
        out_shape=[
            jax.ShapeDtypeStruct((length, width), BF),
            jax.ShapeDtypeStruct((texts, width), BF),
            jax.ShapeDtypeStruct((texts, width), BF),
        ],
        compiler_params=params(),
    )(queries, keys, keys, mix, grad, lse, ids, captions)


def feed(rows, cot, w_in, w_out, sums):
    length, width = rows.shape
    units = w_in.shape[1]
    block = min(256, units)
    whole = pl.BlockSpec((length, width), lambda i: (0, 0))
    cut = pl.BlockSpec((width, block), lambda i: (0, i))
    first = sums is None
    kernel = functools.partial(feed_kernel, first=first)
    operands = [rows, cot, w_in, w_out]
    specs = [whole, whole, cut, cut]
    if first:
        body = lambda a, b, c, d, *rest: kernel(a, b, c, d, None, None, *rest)
    else:
        body = kernel
        operands += list(sums)
        specs += [whole, whole]
    total = jax.ShapeDtypeStruct((length, width), F32)
    part = jax.ShapeDtypeStruct((width, units), BF)
    return pl.pallas_call(
        body,
        grid=(units // block,),
        in_specs=specs,
        out_specs=[cut, cut, whole, whole],
        out_shape=[part, part, total, total],
        scratch_shapes=[pltpu.VMEM((width, length), BF)] * 2,
        compiler_params=params(),
        cost_estimate=pl.CostEstimate(
            flops=12 * length * width * units,
            bytes_accessed=8 * width * units + 8 * length * width,
            transcendentals=length * units,
        ),
    )(*operands)


def norm_parts(values):
    center = values - jnp.mean(values, -1, keepdims=True)
    inverse = lax.rsqrt(jnp.mean(center * center, -1, keepdims=True) + EPS)
    return center * inverse, inverse


def layer_norm(values, gain, offset):
    return (norm_parts(values)[0] * gain + offset).astype(BF)


def norm_back(values, gain, grad):
    hat, inverse = norm_parts(values)
    scaled = grad * gain
    back = inverse * (
        scaled
        - jnp.mean(scaled, -1, keepdims=True)
        - hat * jnp.mean(scaled * hat, -1, keepdims=True)
    )
    lead = tuple(range(values.ndim - 1))
    return back, jnp.sum(grad * hat, lead), jnp.sum(grad, lead)


def layer(shape, args):
    chips, tops, lows = shape["chip"], shape["hi"], shape["lo"]
    (
        image_rows,
        text_rows,
        segment_ids,
        cotangent,
        query_weight,
        key_weight,
        value_weight,
        attn_output,
        cross_query,
        cross_key,
        cross_value,
        cross_output,
        hidden_in,
        hidden_out,
        *norms,
    ) = args
    images, rows, width = image_rows.shape
    texts = text_rows.shape[1]
    half_rows = rows // 2
    length = rows * lows * tops
    shard = query_weight.shape[0]
    chip, core = lax.axis_index("chip"), lax.axis_index("core")
    top = lax.axis_index("hi")
    own_slot = core * images + top % images

    def swap(value):
        return lax.ppermute(value, "core", [(0, 1), (1, 0)])

    def across(value, bit):
        return lax.ppermute(value, "chip", [(i, i ^ bit) for i in range(chips)])

    def shift(value, step):
        return lax.ppermute(value, "hi", [((i + step) % tops, i) for i in range(tops)])

    def matching(number, back):
        pairs = []
        for source_core in range(2):
            for source_top in range(tops):
                slot = source_top ^ number
                target = (slot // images) * tops + source_core * images + slot % images
                source = source_core * tops + source_top
                pairs.append((target, source) if back else (source, target))
        return pairs

    def to_image(piece_of):
        got = [
            lax.ppermute(piece_of(top ^ number), ("core", "hi"), matching(number, False))
            for number in range(tops)
        ]
        whole = jnp.stack(got)
        return jnp.stack(
            [lax.dynamic_index_in_dim(whole, own_slot ^ place, 0, False) for place in range(tops)]
        )

    def from_image(pieces):
        return [
            lax.ppermute(
                lax.dynamic_index_in_dim(pieces, own_slot ^ number, 0, False),
                ("core", "hi"),
                matching(number, True),
            )
            for number in range(tops)
        ]

    def image_piece(value):
        def piece(slot):
            return lax.dynamic_slice(
                value,
                (slot % images, (slot // images) * half_rows, 0),
                (1, half_rows, width),
            )[0]

        return piece

    def to_rows(pieces):
        got = jnp.stack(from_image(pieces))
        ordered = jnp.stack(
            [lax.dynamic_index_in_dim(got, top ^ slot, 0, False) for slot in range(tops)]
        )
        ordered = ordered.reshape(2, images, half_rows, width)
        return jnp.swapaxes(ordered, 0, 1).reshape(images, rows, width)

    def tp_gather(mine):
        if lows == 1:
            other = swap(mine)
            first = jnp.where(core == 0, mine, other)
            second = jnp.where(core == 0, other, mine)
            return jnp.stack([first, second], 1).reshape(length, width)
        every = lax.all_gather(mine, ("lo", "core"))
        every = every.reshape(lows * 2, tops, half_rows, width)
        return jnp.swapaxes(every, 0, 1).reshape(length, width)

    def tp_reduce(partial):
        if lows == 1:
            cut = partial.reshape(tops, 2, half_rows, width)
            sent = lax.dynamic_index_in_dim(cut, 1 - core, 1, False).astype(BF)
            kept = lax.dynamic_index_in_dim(cut, core, 1, False)
            return kept + swap(sent).astype(F32)
        cut = jnp.swapaxes(partial.astype(BF).reshape(tops, lows * 2, half_rows, width), 0, 1)
        cut = lax.psum_scatter(cut, ("lo", "core"), scatter_dimension=0, tiled=False)
        return cut.astype(F32)

    def core_half(weight, which):
        columns = weight.shape[1] // 2
        return lax.dynamic_slice_in_dim(weight, which * columns, columns, 1)

    def pack(which):
        feeds = [core_half(weight, which) for weight in (hidden_in, hidden_out)]
        cuts = feeds[0].shape[1] // 2
        groups = [
            [core_half(w, which) for w in (query_weight, key_weight, value_weight, attn_output)],
            [core_half(w, which) for w in (cross_query, cross_key, cross_value, cross_output)],
            [w[:, :cuts] for w in feeds],
            [w[:, cuts:] for w in feeds],
        ]
        return jnp.concatenate([w for group in groups for w in group], 1)

    kept = pack(core)
    taken = swap(pack(1 - core))
    own = jnp.concatenate(
        [jnp.where(core == 0, kept, taken), jnp.where(core == 0, taken, kept)], 0
    )
    block_rows = 2 * shard
    group_width = own.shape[1] // 4

    def plane_gather(piece):
        if chips != 4:
            return lax.all_gather(piece, "chip", axis=0, tiled=True)
        side = across(piece, 1)
        over = across(piece, 2)
        corner_low = across(side[:shard], 2)
        corner_high = across(over[shard:], 1)
        corner = jnp.concatenate([corner_low, corner_high], 0)
        pieces = jnp.stack([piece, side, over, corner])
        ordered = [lax.dynamic_index_in_dim(pieces, chip ^ place, 0, False) for place in range(4)]
        return jnp.concatenate(ordered, 0)

    def plane_scatter(grads):
        if chips != 4:
            return lax.psum_scatter(grads, "chip", scatter_dimension=0, tiled=True).astype(F32)

        def rows_of(place, low, count):
            return lax.dynamic_slice_in_dim(grads, (chip ^ place) * block_rows + low, count, 0)

        by_side = across(rows_of(3, 0, shard), 1)
        by_over = across(rows_of(3, shard, shard), 2)
        to_over = jnp.concatenate(
            [rows_of(2, 0, shard).astype(F32) + by_side.astype(F32), rows_of(2, shard, shard).astype(F32)], 0
        ).astype(BF)
        to_side = jnp.concatenate(
            [rows_of(1, 0, shard).astype(F32), rows_of(1, shard, shard).astype(F32) + by_over.astype(F32)], 0
        ).astype(BF)
        over, side = across(to_over, 2), across(to_side, 1)
        return rows_of(0, 0, block_rows).astype(F32) + over.astype(F32) + side.astype(F32)

    def top_scatter(pieces):
        total = pieces[0].astype(F32)
        for step in range(1, tops):
            total = total + shift(pieces[step].astype(BF), tops - step).astype(F32)
        return total

    def core_split(total):
        cut = total.reshape(2, shard, total.shape[1])
        mine = lax.dynamic_index_in_dim(cut, core, 0, False)
        other = swap(lax.dynamic_index_in_dim(cut, 1 - core, 0, False).astype(BF)).astype(F32)
        return jnp.where(core == 0, mine, other), jnp.where(core == 0, other, mine)

    own_wide = plane_gather(own)

    def fetch(group, count):
        part = own[:, group * group_width : (group + 1) * group_width]
        columns = group_width // count
        got = [shift(part, step).reshape(block_rows, count, 1, columns) for step in range(1, tops)]
        rest = jnp.concatenate(got, 2).reshape(block_rows, (tops - 1) * group_width)
        rest = plane_gather(rest).reshape(width, count, (tops - 1) * columns)
        near = own_wide[:, group * group_width : (group + 1) * group_width]
        near = near.reshape(width, count, columns)
        return [
            jnp.concatenate([near[:, one], rest[:, one]], 1) for one in range(count)
        ]

    def give(grads):
        count = len(grads)
        columns = grads[0].shape[1] // tops
        summed = plane_scatter(jnp.concatenate(grads, 1)).reshape(block_rows, count, tops, columns)
        pieces = [summed[:, :, step].reshape(block_rows, count * columns) for step in range(tops)]
        low, high = core_split(top_scatter(pieces))
        low, high = low.reshape(shard, count, columns), high.reshape(shard, count, columns)
        return [(low[:, one], high[:, one]) for one in range(count)]

    packed_norms = lax.all_gather(jnp.stack(norms), ("chip", "core"), axis=1, tiled=True)
    gain_one, bias_one, gain_two, bias_two, gain_three, bias_three = packed_norms

    w_query, w_key, w_value, w_out = fetch(0, 4)
    inputs = to_image(image_piece(image_rows)).astype(F32)
    c_query, c_key, c_value, c_out = fetch(1, 4)
    in_low, out_low = fetch(2, 2)
    in_high, out_high = fetch(3, 2)

    text = to_image(lambda slot: text_rows[slot % images])
    if lows > 1:
        text = lax.all_gather(text, "lo", axis=1)
    text = text.reshape(tops * lows * texts, width)
    other_ids = swap(segment_ids)
    ids = jnp.where(core == top // images, segment_ids, other_ids)
    ids = lax.dynamic_index_in_dim(ids, top % images, 0, False)
    captions = jnp.repeat(ids, length // ids.shape[0])[None, :]
    ids = ids[:, None]
    cot = to_image(image_piece(cotangent))

    full_one = tp_gather(layer_norm(inputs, gain_one, bias_one))
    packed = dot(full_one, jnp.concatenate([w_query, w_key, w_value], 1)).astype(BF)
    self_mix, self_lse = self_forward(packed)
    after_attn = inputs + tp_reduce(dot(self_mix, w_out, NT))
    full_two = tp_gather(layer_norm(after_attn, gain_two, bias_two))
    queries = dot(full_two, c_query).astype(BF)
    w_text = jnp.concatenate([c_key, c_value], 1)
    keys = dot(text, w_text).astype(BF)
    cross_mix, cross_lse = cross_forward(queries, keys, ids, captions)
    after_cross = after_attn + tp_reduce(dot(cross_mix, c_out, NT))
    full_three = tp_gather(layer_norm(after_cross, gain_three, bias_three))
    full_cot = tp_gather(cot)
    gin_low, gout_low, *sums = feed(full_three, full_cot, in_low, out_low, None)
    gin_high, gout_high, out_sum, back_sum = feed(full_three, full_cot, in_high, out_high, sums)
    low_grads = give([gin_low, gout_low])
    high_grads = give([gin_high, gout_high])
    result = to_rows((after_cross + tp_reduce(out_sum)).astype(BF))

    back_three, dgain_three, dbias_three = norm_back(after_cross, gain_three, tp_reduce(back_sum))
    grad_cross = cot.astype(F32) + back_three
    full_grad = tp_gather(grad_cross.astype(BF))
    mix_grad = dot(full_grad, c_out).astype(BF)
    dq, dk, dv = cross_backward(queries, keys, cross_mix, mix_grad, cross_lse, ids, captions)
    back_sum = dot(dq, c_query, NT)
    dkv = jnp.concatenate([dk, dv], 1)
    cross_grads = give(
        [
            dot(full_two, dq, TN).astype(BF),
            dot(text, dk, TN).astype(BF),
            dot(text, dv, TN).astype(BF),
            dot(full_grad, cross_mix, TN).astype(BF),
        ]
    )
    text_part = dot(dkv, w_text, NT).astype(BF).reshape(tops, lows, texts, width)
    if lows > 1:
        text_part = lax.psum_scatter(text_part, "lo", scatter_dimension=1, tiled=True)
    got = [part.astype(F32) for part in from_image(text_part[:, 0])]
    got = jnp.stack(got)
    got = [lax.dynamic_index_in_dim(got, top ^ slot, 0, False) for slot in range(tops)]
    text_grad = jnp.stack([got[i] + got[images + i] for i in range(images)])

    back_two, dgain_two, dbias_two = norm_back(after_attn, gain_two, tp_reduce(back_sum))
    grad_attn = grad_cross + back_two
    full_grad = tp_gather(grad_attn.astype(BF))
    mix_grad = dot(full_grad, w_out).astype(BF)
    dq, dk, dv = self_backward(packed, self_mix, mix_grad, self_lse)
    dqkv = jnp.concatenate([dq, dk, dv], 1)
    dwqkv = dot(full_one, dqkv, TN).astype(BF)
    span = dq.shape[1]
    self_grads = give(
        [
            dwqkv[:, :span],
            dwqkv[:, span : 2 * span],
            dwqkv[:, 2 * span :],
            dot(full_grad, self_mix, TN).astype(BF),
        ]
    )
    back_sum = dot(dqkv, jnp.concatenate([w_query, w_key, w_value], 1), NT)
    back_one, dgain_one, dbias_one = norm_back(inputs, gain_one, tp_reduce(back_sum))
    input_grad = to_rows((grad_attn + back_one).astype(BF)).astype(F32)

    norm_sums = lax.psum(
        jnp.stack([dgain_one, dbias_one, dgain_two, dbias_two, dgain_three, dbias_three]),
        ("chip", "core", "hi", "lo"),
    )
    norm_sums = lax.dynamic_slice_in_dim(norm_sums, (chip * 2 + core) * shard, shard, 1)

    feeds = [
        jnp.concatenate([low_grads[i][0], high_grads[i][0], low_grads[i][1], high_grads[i][1]], 1)
        for i in range(2)
    ]
    joined = [jnp.concatenate(pair, 1) for pair in (*self_grads, *cross_grads)]
    return (result, input_grad, text_grad, *joined, *feeds, *[norm_sums[i] for i in range(6)])


def solution(mesh):
    fsdp, tensor = mesh.shape["fsdp"], mesh.shape["tensor"]

    def run(*args):
        images = args[0].shape[0] // fsdp
        tops = 2 * images
        shape = {"chip": fsdp // 2, "core": 2, "hi": tops, "lo": tensor // tops}
        fine = Mesh(mesh.devices.reshape(tuple(shape.values())), tuple(shape))
        first, second = ("chip", "core"), ("hi", "lo")
        wide, weight, norm = P(first, second, None), P(first, second), P(first)
        outs = (wide,) * 3 + (weight,) * 10 + (norm,) * 6
        return jax.shard_map(
            lambda *local: layer(shape, local),
            mesh=fine,
            in_specs=(wide, wide, P(first, None), wide) + (weight,) * 10 + (norm,) * 6,
            out_specs=outs,
            check_vma=False,
        )(*args)

    return run
```

```python
import functools
import math

import jax
import jax.numpy as jnp
from jax import lax
from jax.experimental import pallas as pl
from jax.experimental.pallas import tpu as pltpu
from jax.sharding import Mesh
from jax.sharding import PartitionSpec as P

HD = 64
EPS = 1e-05
NEG = -1e30
LOG2E = math.log2(math.e)
BF = jnp.bfloat16
F32 = jnp.float32
NT = (((1,), (1,)), ((), ()))
TN = (((0,), (0,)), ((), ()))
NN = (((1,), (0,)), ((), ()))


def dot(left, right, dims=NN):
    return lax.dot_general(left, right, dims, preferred_element_type=F32)


def lane_head(shape, axis, head):
    return lax.broadcasted_iota(jnp.int32, shape, axis) // HD == head


def self_forward_kernel(q_ref, k_ref, v_ref, mix_ref, lse_ref, *, block):
    length = q_ref.shape[0]
    scale = LOG2E * HD**-0.5
    causal = lax.broadcasted_iota(jnp.int32, (block, block), 0) <= lax.broadcasted_iota(
        jnp.int32, (block, block), 1
    )
    for at in range(length // block):
        lo, hi = at * block, (at + 1) * block
        query = q_ref[lo:hi, :]
        mixes = []
        for head in range(2):
            one = jnp.where(lane_head((1, 2 * HD), 1, head), query, jnp.zeros_like(query))
            diag = jnp.where(causal, dot(k_ref[lo:hi, :], one, NT), NEG)
            peak = jnp.max(diag, 0, keepdims=True)
            if at:
                past = dot(k_ref[:lo, :], one, NT)
                peak = jnp.maximum(peak, jnp.max(past, 0, keepdims=True))
            weights = jnp.exp2((diag - peak) * scale)
            total = jnp.sum(weights, 0, keepdims=True)
            mixed = dot(v_ref[lo:hi, :], weights.astype(BF), TN)
            if at:
                weights = jnp.exp2((past - peak) * scale)
                total = total + jnp.sum(weights, 0, keepdims=True)
                mixed = mixed + dot(v_ref[:lo, :], weights.astype(BF), TN)
            mixes.append(mixed / total)
            lse_ref[0, head : head + 1, lo:hi] = peak * scale + jnp.log2(total)
        both = jnp.where(lane_head((2 * HD, 1), 0, 0), mixes[0], mixes[1])
        mix_ref[lo:hi, :] = both.T.astype(BF)


def self_backward_kernel(
    q_ref, k_ref, v_ref, mix_ref, grad_ref, lse_ref, dq_ref, dk_ref, dv_ref, dk_sum, dv_sum, *, block
):
    length = q_ref.shape[0]
    scale = LOG2E * HD**-0.5
    causal = lax.broadcasted_iota(jnp.int32, (block, block), 0) <= lax.broadcasted_iota(
        jnp.int32, (block, block), 1
    )
    dk_sum[...] = jnp.zeros_like(dk_sum)
    dv_sum[...] = jnp.zeros_like(dv_sum)
    for at in range(length // block):
        lo, hi = at * block, (at + 1) * block
        query = q_ref[lo:hi, :]
        grad = grad_ref[lo:hi, :]
        product = (grad.astype(F32) * mix_ref[lo:hi, :].astype(F32)).T
        grads = []
        for head in range(2):
            picked = lane_head((1, 2 * HD), 1, head)
            one = jnp.where(picked, query, jnp.zeros_like(query))
            one_grad = jnp.where(picked, grad, jnp.zeros_like(grad))
            delta = jnp.sum(product[head * HD : (head + 1) * HD], 0, keepdims=True)
            lse = lse_ref[0, head : head + 1, lo:hi]
            total = jnp.zeros((2 * HD, block), F32)
            for start, stop in ((0, lo), (lo, hi)):
                if start == stop:
                    continue
                keys = k_ref[start:stop, :]
                weights = jnp.exp2(dot(keys, one, NT) * scale - lse)
                if start == lo:
                    weights = jnp.where(causal, weights, 0.0)
                slope = dot(v_ref[start:stop, :], one_grad, NT)
                score_grad = (weights * (slope - delta)).astype(BF)
                dv_sum[start:stop, :] += dot(weights.astype(BF), one_grad)
                dk_sum[start:stop, :] += dot(score_grad, one)
                total = total + dot(keys, score_grad, TN)
            grads.append(total)
        both = jnp.where(lane_head((2 * HD, 1), 0, 0), grads[0], grads[1])
        dq_ref[lo:hi, :] = (both.T * HD**-0.5).astype(BF)
    dk_ref[...] = (dk_sum[...] * HD**-0.5).astype(BF)
    dv_ref[...] = dv_sum[...].astype(BF)


def cross_forward_kernel(q_ref, k_ref, v_ref, ids_ref, caption_ref, mix_ref, lse_ref, *, block):
    length = q_ref.shape[0]
    scale = LOG2E * HD**-0.5
    for at in range(length // block):
        lo, hi = at * block, (at + 1) * block
        query = q_ref[lo:hi, :]
        seen = ids_ref[...] == caption_ref[:, lo:hi]
        mixes = []
        for head in range(2):
            one = jnp.where(lane_head((1, 2 * HD), 1, head), query, jnp.zeros_like(query))
            scores = jnp.where(seen, dot(k_ref[...], one, NT), NEG)
            peak = jnp.max(scores, 0, keepdims=True)
            weights = jnp.exp2((scores - peak) * scale)
            total = jnp.sum(weights, 0, keepdims=True)
            mixes.append(dot(v_ref[...], weights.astype(BF), TN) / total)
            lse_ref[0, head : head + 1, lo:hi] = peak * scale + jnp.log2(total)
        both = jnp.where(lane_head((2 * HD, 1), 0, 0), mixes[0], mixes[1])
        mix_ref[lo:hi, :] = both.T.astype(BF)


def cross_backward_kernel(
    q_ref, k_ref, v_ref, mix_ref, grad_ref, lse_ref, ids_ref, caption_ref, dq_ref, dk_ref, dv_ref, *, block
):
    length = q_ref.shape[0]
    scale = LOG2E * HD**-0.5
    keys, values = k_ref[...], v_ref[...]
    dk_sum = jnp.zeros(keys.shape, F32)
    dv_sum = jnp.zeros(keys.shape, F32)
    for at in range(length // block):
        lo, hi = at * block, (at + 1) * block
        query = q_ref[lo:hi, :]
        grad = grad_ref[lo:hi, :]
        product = (grad.astype(F32) * mix_ref[lo:hi, :].astype(F32)).T
        seen = ids_ref[...] == caption_ref[:, lo:hi]
        grads = []
        for head in range(2):
            picked = lane_head((1, 2 * HD), 1, head)
            one = jnp.where(picked, query, jnp.zeros_like(query))
            one_grad = jnp.where(picked, grad, jnp.zeros_like(grad))
            delta = jnp.sum(product[head * HD : (head + 1) * HD], 0, keepdims=True)
            lse = lse_ref[0, head : head + 1, lo:hi]
            weights = jnp.where(seen, jnp.exp2(dot(keys, one, NT) * scale - lse), 0.0)
            slope = dot(values, one_grad, NT)
            score_grad = (weights * (slope - delta)).astype(BF)
            dv_sum = dv_sum + dot(weights.astype(BF), one_grad)
            dk_sum = dk_sum + dot(score_grad, one)
            grads.append(dot(keys, score_grad, TN))
        both = jnp.where(lane_head((2 * HD, 1), 0, 0), grads[0], grads[1])
        dq_ref[lo:hi, :] = (both.T * HD**-0.5).astype(BF)
    dk_ref[...] = (dk_sum * HD**-0.5).astype(BF)
    dv_ref[...] = dv_sum.astype(BF)


def feed_kernel(
    rows_ref, cot_ref, win_ref, wout_ref, out_in, back_in, gin_ref, gout_ref, out_ref, back_ref, rows_t, cot_t, *, first
):
    step = pl.program_id(0)

    @pl.when(step == 0)
    def _():
        rows_t[...] = rows_ref[...].T
        cot_t[...] = cot_ref[...].T
        if first:
            out_ref[...] = jnp.zeros_like(out_ref)
            back_ref[...] = jnp.zeros_like(back_ref)
        else:
            out_ref[...] = out_in[...]
            back_ref[...] = back_in[...]

    pre = dot(rows_ref[...], win_ref[...])
    square = pre * pre
    slope = math.sqrt(2.0 / math.pi)
    bent = jnp.tanh(pre * (slope + slope * 0.044715 * square))
    half = 0.5 * (1.0 + bent)
    act = (pre * half).astype(BF)
    out_ref[...] += dot(act, wout_ref[...], NT)
    gout_ref[...] = dot(cot_t[...], act).astype(BF)
    bend = half + pre * (0.5 * (1.0 - bent * bent)) * (slope + 3.0 * slope * 0.044715 * square)
    pre_grad = (dot(cot_ref[...], wout_ref[...]) * bend).astype(BF)
    gin_ref[...] = dot(rows_t[...], pre_grad).astype(BF)
    back_ref[...] += dot(pre_grad, win_ref[...], NT)


VMEM_LIMIT = 60 * 1024 * 1024


def params():
    return pltpu.CompilerParams(vmem_limit_bytes=VMEM_LIMIT)


def column(rows, offset):
    return pl.BlockSpec((rows, 2 * HD), lambda i: (0, offset + i))


def self_forward(packed):
    length, width = packed.shape
    pairs = width // (6 * HD)
    return pl.pallas_call(
        functools.partial(self_forward_kernel, block=256),
        grid=(pairs,),
        in_specs=[column(length, 0), column(length, pairs), column(length, 2 * pairs)],
        out_specs=[column(length, 0), pl.BlockSpec((1, 2, length), lambda i: (i, 0, 0))],
        out_shape=[
            jax.ShapeDtypeStruct((length, pairs * 2 * HD), BF),
            jax.ShapeDtypeStruct((pairs, 2, length), F32),
        ],
        compiler_params=params(),
        cost_estimate=pl.CostEstimate(
            flops=8 * pairs * length * length * 2 * HD * 2,
            bytes_accessed=8 * pairs * length * 2 * HD,
            transcendentals=2 * pairs * length * length,
        ),
    )(packed, packed, packed)


def self_backward(packed, mix, grad, lse):
    length, width = packed.shape
    pairs = width // (6 * HD)
    part = jax.ShapeDtypeStruct((length, pairs * 2 * HD), BF)
    return pl.pallas_call(
        functools.partial(self_backward_kernel, block=256),
        grid=(pairs,),
        in_specs=[
            column(length, 0),
            column(length, pairs),
            column(length, 2 * pairs),
            column(length, 0),
            column(length, 0),
            pl.BlockSpec((1, 2, length), lambda i: (i, 0, 0)),
        ],
        out_specs=[column(length, 0)] * 3,
        out_shape=[part] * 3,
        scratch_shapes=[pltpu.VMEM((length, 2 * HD), F32)] * 2,
        compiler_params=params(),
        cost_estimate=pl.CostEstimate(
            flops=20 * pairs * length * length * 2 * HD * 2,
            bytes_accessed=16 * pairs * length * 2 * HD,
            transcendentals=2 * pairs * length * length,
        ),
    )(packed, packed, packed, mix, grad, lse)


def cross_forward(queries, keys, ids, captions):
    length, width = queries.shape
    texts = keys.shape[0]
    pairs = width // (2 * HD)
    return pl.pallas_call(
        functools.partial(cross_forward_kernel, block=min(512, length)),
        grid=(pairs,),
        in_specs=[
            column(length, 0),
            column(texts, 0),
            column(texts, pairs),
            pl.BlockSpec((texts, 1), lambda i: (0, 0)),
            pl.BlockSpec((1, length), lambda i: (0, 0)),
        ],
        out_specs=[column(length, 0), pl.BlockSpec((1, 2, length), lambda i: (i, 0, 0))],
        out_shape=[
            jax.ShapeDtypeStruct((length, width), BF),
            jax.ShapeDtypeStruct((pairs, 2, length), F32),
        ],
        compiler_params=params(),
    )(queries, keys, keys, ids, captions)


def cross_backward(queries, keys, mix, grad, lse, ids, captions):
    length, width = queries.shape
    texts = keys.shape[0]
    pairs = width // (2 * HD)
    return pl.pallas_call(
        functools.partial(cross_backward_kernel, block=min(512, length)),
        grid=(pairs,),
        in_specs=[
            column(length, 0),
            column(texts, 0),
            column(texts, pairs),
            column(length, 0),
            column(length, 0),
            pl.BlockSpec((1, 2, length), lambda i: (i, 0, 0)),
            pl.BlockSpec((texts, 1), lambda i: (0, 0)),
            pl.BlockSpec((1, length), lambda i: (0, 0)),
        ],
        out_specs=[column(length, 0), column(texts, 0), column(texts, 0)],
        out_shape=[
            jax.ShapeDtypeStruct((length, width), BF),
            jax.ShapeDtypeStruct((texts, width), BF),
            jax.ShapeDtypeStruct((texts, width), BF),
        ],
        compiler_params=params(),
    )(queries, keys, keys, mix, grad, lse, ids, captions)


def feed(rows, cot, w_in, w_out, sums):
    length, width = rows.shape
    units = w_in.shape[1]
    block = min(256, units)
    whole = pl.BlockSpec((length, width), lambda i: (0, 0))
    cut = pl.BlockSpec((width, block), lambda i: (0, i))
    first = sums is None
    kernel = functools.partial(feed_kernel, first=first)
    operands = [rows, cot, w_in, w_out]
    specs = [whole, whole, cut, cut]
    if first:
        body = lambda a, b, c, d, *rest: kernel(a, b, c, d, None, None, *rest)
    else:
        body = kernel
        operands += list(sums)
        specs += [whole, whole]
    total = jax.ShapeDtypeStruct((length, width), F32)
    part = jax.ShapeDtypeStruct((width, units), BF)
    return pl.pallas_call(
        body,
        grid=(units // block,),
        in_specs=specs,
        out_specs=[cut, cut, whole, whole],
        out_shape=[part, part, total, total],
        scratch_shapes=[pltpu.VMEM((width, length), BF)] * 2,
        compiler_params=params(),
        cost_estimate=pl.CostEstimate(
            flops=12 * length * width * units,
            bytes_accessed=8 * width * units + 8 * length * width,
            transcendentals=length * units,
        ),
    )(*operands)


def norm_parts(values):
    center = values - jnp.mean(values, -1, keepdims=True)
    inverse = lax.rsqrt(jnp.mean(center * center, -1, keepdims=True) + EPS)
    return center * inverse, inverse


def layer_norm(values, gain, offset):
    return (norm_parts(values)[0] * gain + offset).astype(BF)


def norm_back(values, gain, grad):
    hat, inverse = norm_parts(values)
    scaled = grad * gain
    back = inverse * (
        scaled
        - jnp.mean(scaled, -1, keepdims=True)
        - hat * jnp.mean(scaled * hat, -1, keepdims=True)
    )
    lead = tuple(range(values.ndim - 1))
    return back, jnp.sum(grad * hat, lead), jnp.sum(grad, lead)


def layer(shape, args):
    chips, tops, lows = shape["chip"], shape["hi"], shape["lo"]
    (
        image_rows,
        text_rows,
        segment_ids,
        cotangent,
        query_weight,
        key_weight,
        value_weight,
        attn_output,
        cross_query,
        cross_key,
        cross_value,
        cross_output,
        hidden_in,
        hidden_out,
        *norms,
    ) = args
    images, rows, width = image_rows.shape
    texts = text_rows.shape[1]
    half_rows = rows // 2
    length = rows * lows * tops
    shard = query_weight.shape[0]
    chip, core = lax.axis_index("chip"), lax.axis_index("core")
    top = lax.axis_index("hi")
    own_slot = core * images + top % images

    def swap(value):
        return lax.ppermute(value, "core", [(0, 1), (1, 0)])

    def across(value, bit):
        return lax.ppermute(value, "chip", [(i, i ^ bit) for i in range(chips)])

    def shift(value, step):
        return lax.ppermute(value, "hi", [((i + step) % tops, i) for i in range(tops)])

    def matching(number, back):
        pairs = []
        for source_core in range(2):
            for source_top in range(tops):
                slot = source_top ^ number
                target = (slot // images) * tops + source_core * images + slot % images
                source = source_core * tops + source_top
                pairs.append((target, source) if back else (source, target))
        return pairs

    def to_image(piece_of):
        got = [
            lax.ppermute(piece_of(top ^ number), ("core", "hi"), matching(number, False))
            for number in range(tops)
        ]
        whole = jnp.stack(got)
        return jnp.stack(
            [lax.dynamic_index_in_dim(whole, own_slot ^ place, 0, False) for place in range(tops)]
        )

    def from_image(pieces):
        return [
            lax.ppermute(
                lax.dynamic_index_in_dim(pieces, own_slot ^ number, 0, False),
                ("core", "hi"),
                matching(number, True),
            )
            for number in range(tops)
        ]

    def image_piece(value):
        def piece(slot):
            return lax.dynamic_slice(
                value,
                (slot % images, (slot // images) * half_rows, 0),
                (1, half_rows, width),
            )[0]

        return piece

    def to_rows(pieces):
        got = jnp.stack(from_image(pieces))
        ordered = jnp.stack(
            [lax.dynamic_index_in_dim(got, top ^ slot, 0, False) for slot in range(tops)]
        )
        ordered = ordered.reshape(2, images, half_rows, width)
        return jnp.swapaxes(ordered, 0, 1).reshape(images, rows, width)

    def tp_gather(mine):
        if lows == 1:
            other = swap(mine)
            first = jnp.where(core == 0, mine, other)
            second = jnp.where(core == 0, other, mine)
            return jnp.stack([first, second], 1).reshape(length, width)
        every = lax.all_gather(mine, ("lo", "core"))
        every = every.reshape(lows * 2, tops, half_rows, width)
        return jnp.swapaxes(every, 0, 1).reshape(length, width)

    def tp_reduce(partial):
        if lows == 1:
            cut = partial.reshape(tops, 2, half_rows, width)
            sent = lax.dynamic_index_in_dim(cut, 1 - core, 1, False).astype(BF)
            kept = lax.dynamic_index_in_dim(cut, core, 1, False)
            return kept + swap(sent).astype(F32)
        cut = jnp.swapaxes(partial.astype(BF).reshape(tops, lows * 2, half_rows, width), 0, 1)
        cut = lax.psum_scatter(cut, ("lo", "core"), scatter_dimension=0, tiled=False)
        return cut.astype(F32)

    def core_half(weight, which):
        columns = weight.shape[1] // 2
        return lax.dynamic_slice_in_dim(weight, which * columns, columns, 1)

    def pack(which):
        feeds = [core_half(weight, which) for weight in (hidden_in, hidden_out)]
        cuts = feeds[0].shape[1] // 2
        groups = [
            [core_half(w, which) for w in (query_weight, key_weight, value_weight, attn_output)],
            [core_half(w, which) for w in (cross_query, cross_key, cross_value, cross_output)],
            [w[:, :cuts] for w in feeds],
            [w[:, cuts:] for w in feeds],
        ]
        return jnp.concatenate([w for group in groups for w in group], 1)

    kept = pack(core)
    taken = swap(pack(1 - core))
    own = jnp.concatenate(
        [jnp.where(core == 0, kept, taken), jnp.where(core == 0, taken, kept)], 0
    )
    block_rows = 2 * shard
    group_width = own.shape[1] // 4

    def plane_gather(piece):
        if chips != 4:
            return lax.all_gather(piece, "chip", axis=0, tiled=True)
        side = across(piece, 1)
        over = across(piece, 2)
        corner_low = across(side[:shard], 2)
        corner_high = across(over[shard:], 1)
        corner = jnp.concatenate([corner_low, corner_high], 0)
        pieces = jnp.stack([piece, side, over, corner])
        ordered = [lax.dynamic_index_in_dim(pieces, chip ^ place, 0, False) for place in range(4)]
        return jnp.concatenate(ordered, 0)

    def plane_scatter(grads):
        if chips != 4:
            return lax.psum_scatter(grads, "chip", scatter_dimension=0, tiled=True).astype(F32)

        def rows_of(place, low, count):
            return lax.dynamic_slice_in_dim(grads, (chip ^ place) * block_rows + low, count, 0)

        by_side = across(rows_of(3, 0, shard), 1)
        by_over = across(rows_of(3, shard, shard), 2)
        to_over = jnp.concatenate(
            [rows_of(2, 0, shard).astype(F32) + by_side.astype(F32), rows_of(2, shard, shard).astype(F32)], 0
        ).astype(BF)
        to_side = jnp.concatenate(
            [rows_of(1, 0, shard).astype(F32), rows_of(1, shard, shard).astype(F32) + by_over.astype(F32)], 0
        ).astype(BF)
        over, side = across(to_over, 2), across(to_side, 1)
        return rows_of(0, 0, block_rows).astype(F32) + over.astype(F32) + side.astype(F32)

    def top_scatter(pieces):
        total = pieces[0].astype(F32)
        for step in range(1, tops):
            total = total + shift(pieces[step].astype(BF), tops - step).astype(F32)
        return total

    def core_split(total):
        cut = total.reshape(2, shard, total.shape[1])
        mine = lax.dynamic_index_in_dim(cut, core, 0, False)
        other = swap(lax.dynamic_index_in_dim(cut, 1 - core, 0, False).astype(BF)).astype(F32)
        return jnp.where(core == 0, mine, other), jnp.where(core == 0, other, mine)

    own_wide = plane_gather(own)

    def fetch(group, count):
        part = own[:, group * group_width : (group + 1) * group_width]
        columns = group_width // count
        got = [shift(part, step).reshape(block_rows, count, 1, columns) for step in range(1, tops)]
        rest = jnp.concatenate(got, 2).reshape(block_rows, (tops - 1) * group_width)
        rest = plane_gather(rest).reshape(width, count, (tops - 1) * columns)
        near = own_wide[:, group * group_width : (group + 1) * group_width]
        near = near.reshape(width, count, columns)
        return [
            jnp.concatenate([near[:, one], rest[:, one]], 1) for one in range(count)
        ]

    def give(grads):
        count = len(grads)
        columns = grads[0].shape[1] // tops
        summed = plane_scatter(jnp.concatenate(grads, 1)).reshape(block_rows, count, tops, columns)
        pieces = [summed[:, :, step].reshape(block_rows, count * columns) for step in range(tops)]
        low, high = core_split(top_scatter(pieces))
        low, high = low.reshape(shard, count, columns), high.reshape(shard, count, columns)
        return [(low[:, one], high[:, one]) for one in range(count)]

    packed_norms = lax.all_gather(jnp.stack(norms), ("chip", "core"), axis=1, tiled=True)
    gain_one, bias_one, gain_two, bias_two, gain_three, bias_three = packed_norms

    w_query, w_key, w_value, w_out = fetch(0, 4)
    inputs = to_image(image_piece(image_rows)).astype(F32)
    c_query, c_key, c_value, c_out = fetch(1, 4)
    in_low, out_low = fetch(2, 2)
    in_high, out_high = fetch(3, 2)

    text = to_image(lambda slot: text_rows[slot % images])
    if lows > 1:
        text = lax.all_gather(text, "lo", axis=1)
    text = text.reshape(tops * lows * texts, width)
    other_ids = swap(segment_ids)
    ids = jnp.where(core == top // images, segment_ids, other_ids)
    ids = lax.dynamic_index_in_dim(ids, top % images, 0, False)
    captions = jnp.repeat(ids, length // ids.shape[0])[None, :]
    ids = ids[:, None]
    cot = to_image(image_piece(cotangent))

    full_one = tp_gather(layer_norm(inputs, gain_one, bias_one))
    packed = dot(full_one, jnp.concatenate([w_query, w_key, w_value], 1)).astype(BF)
    self_mix, self_lse = self_forward(packed)
    after_attn = inputs + tp_reduce(dot(self_mix, w_out, NT))
    full_two = tp_gather(layer_norm(after_attn, gain_two, bias_two))
    queries = dot(full_two, c_query).astype(BF)
    w_text = jnp.concatenate([c_key, c_value], 1)
    keys = dot(text, w_text).astype(BF)
    cross_mix, cross_lse = cross_forward(queries, keys, ids, captions)
    after_cross = after_attn + tp_reduce(dot(cross_mix, c_out, NT))
    full_three = tp_gather(layer_norm(after_cross, gain_three, bias_three))
    full_cot = tp_gather(cot)
    gin_low, gout_low, *sums = feed(full_three, full_cot, in_low, out_low, None)
    gin_high, gout_high, out_sum, back_sum = feed(full_three, full_cot, in_high, out_high, sums)
    low_grads = give([gin_low, gout_low])
    high_grads = give([gin_high, gout_high])
    result = to_rows((after_cross + tp_reduce(out_sum)).astype(BF))

    back_three, dgain_three, dbias_three = norm_back(after_cross, gain_three, tp_reduce(back_sum))
    grad_cross = cot.astype(F32) + back_three
    full_grad = tp_gather(grad_cross.astype(BF))
    mix_grad = dot(full_grad, c_out).astype(BF)
    dq, dk, dv = cross_backward(queries, keys, cross_mix, mix_grad, cross_lse, ids, captions)
    back_sum = dot(dq, c_query, NT)
    dkv = jnp.concatenate([dk, dv], 1)
    cross_grads = give(
        [
            dot(full_two, dq, TN).astype(BF),
            dot(text, dk, TN).astype(BF),
            dot(text, dv, TN).astype(BF),
            dot(full_grad, cross_mix, TN).astype(BF),
        ]
    )
    text_part = dot(dkv, w_text, NT).astype(BF).reshape(tops, lows, texts, width)
    if lows > 1:
        text_part = lax.psum_scatter(text_part, "lo", scatter_dimension=1, tiled=True)
    got = [part.astype(F32) for part in from_image(text_part[:, 0])]
    got = jnp.stack(got)
    got = [lax.dynamic_index_in_dim(got, top ^ slot, 0, False) for slot in range(tops)]
    text_grad = jnp.stack([got[i] + got[images + i] for i in range(images)])

    back_two, dgain_two, dbias_two = norm_back(after_attn, gain_two, tp_reduce(back_sum))
    grad_attn = grad_cross + back_two
    full_grad = tp_gather(grad_attn.astype(BF))
    mix_grad = dot(full_grad, w_out).astype(BF)
    dq, dk, dv = self_backward(packed, self_mix, mix_grad, self_lse)
    dqkv = jnp.concatenate([dq, dk, dv], 1)
    dwqkv = dot(full_one, dqkv, TN).astype(BF)
    span = dq.shape[1]
    self_grads = give(
        [
            dwqkv[:, :span],
            dwqkv[:, span : 2 * span],
            dwqkv[:, 2 * span :],
            dot(full_grad, self_mix, TN).astype(BF),
        ]
    )
    back_sum = dot(dqkv, jnp.concatenate([w_query, w_key, w_value], 1), NT)
    back_one, dgain_one, dbias_one = norm_back(inputs, gain_one, tp_reduce(back_sum))
    input_grad = to_rows((grad_attn + back_one).astype(BF)).astype(F32)

    norm_sums = lax.psum(
        jnp.stack([dgain_one, dbias_one, dgain_two, dbias_two, dgain_three, dbias_three]),
        ("chip", "core", "hi", "lo"),
    )
    norm_sums = lax.dynamic_slice_in_dim(norm_sums, (chip * 2 + core) * shard, shard, 1)

    feeds = [
        jnp.concatenate([low_grads[i][0], high_grads[i][0], low_grads[i][1], high_grads[i][1]], 1)
        for i in range(2)
    ]
    joined = [jnp.concatenate(pair, 1) for pair in (*self_grads, *cross_grads)]
    return (result, input_grad, text_grad, *joined, *feeds, *[norm_sums[i] for i in range(6)])


BLOCK = 256
ANY = pl.BlockSpec(memory_space=pl.ANY)
SMEM = pl.BlockSpec(memory_space=pltpu.SMEM)
VMEM = pl.BlockSpec(memory_space=pltpu.VMEM)
MIB = 1024 * 1024


def like(*shape, dtype=BF):
    return jax.ShapeDtypeStruct(shape, dtype)


def call(body, outs, ins, operands, scratch=(), limit=56, grid=None, flops=0, moved=0):
    single = not isinstance(outs, (list, tuple))
    extra = {} if grid is None else {"grid": grid}
    cost = pl.CostEstimate(flops=flops, bytes_accessed=moved, transcendentals=0) if flops or moved else None
    out_specs, out_shape = ([outs[0]], [outs[1]]) if single else ([o[0] for o in outs], [o[1] for o in outs])
    return pl.pallas_call(
        body,
        in_specs=ins,
        out_specs=out_specs,
        out_shape=out_shape,
        scratch_shapes=list(scratch),
        compiler_params=pltpu.CompilerParams(vmem_limit_bytes=limit * MIB),
        cost_estimate=cost,
        **extra,
    )(*operands)


def run_copies(copies, sems):
    started = [pltpu.make_async_copy(source, target, sems.at[i]) for i, (source, target) in enumerate(copies)]
    for copy in started:
        copy.start()
    for copy in started:
        copy.wait()


def at(offset, count, unit=128):
    return pl.ds(pl.multiple_of(offset, unit), count)


def prepare_kernel(place, image, text, ids, cot, wq, wk, wv, wo, cq, ck, cv, co, win, wout, *rest):
    messages, cots, keep, sent, sems = rest[:4], rest[4:8], rest[8], rest[9], rest[10]
    core, top = place[1], place[2]
    copies = []
    for target, which in ((sent, 1 - core), (keep, core)):
        for group, weights in enumerate(((wq, wk, wv, wo), (cq, ck, cv, co))):
            for one, weight in enumerate(weights):
                copies.append((weight.at[:, at(which * 128, 128)], target.at[group, :, one * 128 : (one + 1) * 128]))
        for part in range(2):
            for one, weight in enumerate((win, wout)):
                copies.append(
                    (
                        weight.at[:, at(which * 512 + part * 256, 256)],
                        target.at[2 + part, :, one * 256 : (one + 1) * 256],
                    )
                )
    for number in range(4):
        slot = top ^ number
        one, half = slot % 2, slot // 2
        copies.append((image.at[one, at(half * 128, 128), :], messages[number].at[0:128, :]))
        copies.append((text.at[one], messages[number].at[128:160, :]))
        copies.append((ids.at[one], messages[number].at[160:176, :]))
    for number in range(4):
        slot = top ^ number
        one, half = slot % 2, slot // 2
        copies.append((cot.at[one, at(half * 128, 128), :], cots[number]))
    run_copies(copies, sems)


def prepare(place, image, text, ids, cot, weights):
    return call(
        prepare_kernel,
        [(ANY, like(176, 1024))] * 4 + [(ANY, like(128, 1024))] * 4 + [(ANY, like(4, 128, 512))] * 2,
        [SMEM] + [ANY] * 14,
        (place, image, text, ids, cot, *weights),
        [pltpu.SemaphoreType.DMA((40,))],
        limit=4,
    )


def join_kernel(*refs):
    keep, taken, singles, doubles, sems = refs[0], refs[1], refs[2:6], refs[6:8], refs[8]
    copies = []
    for group in range(4):
        for half, source in enumerate((keep, taken)):
            copies.append((source.at[group], singles[group].at[half * 128 : (half + 1) * 128, :]))
            low = (group % 2) * 256 + half * 128
            copies.append((source.at[group], doubles[group // 2].at[low : low + 128, :]))
    run_copies(copies, sems)


def join(keep, taken):
    return call(
        join_kernel,
        [(ANY, like(256, 512))] * 4 + [(ANY, like(512, 512))] * 2,
        [ANY] * 2,
        (keep, taken),
        [pltpu.SemaphoreType.DMA((16,))],
        limit=4,
    )


def stack_kernel(*refs):
    *parts, whole, sems = refs
    copies, low = [], 0
    for part in parts:
        copies.append((part, whole.at[low : low + part.shape[0]]))
        low += part.shape[0]
    run_copies(copies, sems)


def stack(parts):
    rows = sum(part.shape[0] for part in parts)
    return call(
        stack_kernel,
        [(ANY, like(rows, *parts[0].shape[1:]))],
        [ANY] * len(parts),
        parts,
        [pltpu.SemaphoreType.DMA((len(parts),))],
        limit=4,
    )[0]


def arrange_kernel(place, *refs):
    messages, rows, text, sems = refs[:4], refs[4], refs[5], refs[6]
    copies = []
    for number, message in enumerate(messages):
        copies.append((message.at[0:128, :], rows.at[number]))
        copies.append((message.at[128:160, :], text.at[at((place[3] ^ number) * 32, 32, 32), :]))
    run_copies(copies, sems)


def arrange(place, messages):
    return call(
        arrange_kernel,
        [(ANY, like(4, 128, 1024)), (ANY, like(128, 1024))],
        [SMEM] + [ANY] * 4,
        (place, *messages),
        [pltpu.SemaphoreType.DMA((8,))],
        limit=4,
    )


def assemble_kernel(place, *refs, low):
    own, side, over, corner, rest, rside, rover, rlow, rhigh, whole, sems = refs
    chip, core = place[0], place[1]
    copies = []
    for source in range(4):
        for half in range(2):
            row = (chip ^ source) * 256 + (core ^ half) * 128
            near = (own, side, over, corner)[source]
            first = half * 128 + (0 if source == 3 else low)
            copies.append((near.at[first : first + 128, :], whole.at[at(row, 128), 0:512]))
            for step in range(3):
                first = step * 256 + half * 128
                far = (rest, rside, rover, rlow if first < 384 else rhigh)[source]
                if source == 3:
                    first %= 384
                columns = slice((step + 1) * 512, (step + 2) * 512)
                copies.append((far.at[first : first + 128, :], whole.at[at(row, 128), columns]))
    run_copies(copies, sems)


def assemble(place, near, far, low):
    return call(
        functools.partial(assemble_kernel, low=low),
        [(ANY, like(1024, 2048))],
        [SMEM] + [ANY] * 9,
        (place, *near, *far),
        [pltpu.SemaphoreType.DMA((32,))],
        limit=4,
    )[0]


def normalized(values, gain, bias):
    center = values - jnp.mean(values, -1, keepdims=True)
    inverse = lax.rsqrt(jnp.mean(center * center, -1, keepdims=True) + EPS)
    return (center * inverse * gain + bias).astype(BF)


def columns_of(weights, one, count=128):
    return jnp.concatenate([weights[:, s * 512 + one * count : s * 512 + (one + 1) * count] for s in range(4)], 1)


def image_blocks(place, own, other):
    core, slot = place[1], place[3]
    for number in range(4):
        yield (slot ^ number) * 256 + core * 128, own, number
        yield (slot ^ 2 ^ number) * 256 + (1 - core) * 128, other, number


def one_head(values, head):
    return jnp.where(lane_head((1, 2 * HD), 1, head), values, jnp.zeros_like(values))


def softmax_mix(scores, values):
    scale = LOG2E * HD**-0.5
    peak = jnp.max(scores[0], 0, keepdims=True)
    for part in scores[1:]:
        peak = jnp.maximum(peak, jnp.max(part, 0, keepdims=True))
    total, mixed = 0.0, 0.0
    for part, rows in zip(scores, values):
        weights = jnp.exp2((part - peak) * scale)
        total = total + jnp.sum(weights, 0, keepdims=True)
        mixed = mixed + dot(rows, weights.astype(BF), TN)
    return mixed / total, peak * scale + jnp.log2(total)


def causal_mask():
    return lax.broadcasted_iota(jnp.int32, (BLOCK, BLOCK), 0) <= lax.broadcasted_iota(
        jnp.int32, (BLOCK, BLOCK), 1
    )


def self_fwd_kernel(place, own, other, gain, bias, weights, normed, qkv, mix, lse, part):
    for row, half, number in image_blocks(place, own, other):
        normed[at(row, 128), :] = normalized(half[number].astype(F32), gain[...], bias[...])
    w_in = jnp.concatenate([columns_of(weights, one) for one in range(3)], 1)
    for low in range(0, 1024, BLOCK):
        qkv[low : low + BLOCK, :] = dot(normed[low : low + BLOCK, :], w_in).astype(BF)
    causal = causal_mask()

    def pair_step(pair, carry):
        lanes = at(pair * 128, 128)
        k_lanes, v_lanes = at(512 + pair * 128, 128), at(1024 + pair * 128, 128)
        for low in range(0, 1024, BLOCK):
            high = low + BLOCK
            query = qkv[low:high, lanes]
            mixes = []
            for head in range(2):
                one = one_head(query, head)
                scores = [jnp.where(causal, dot(qkv[low:high, k_lanes], one, NT), NEG)]
                values = [qkv[low:high, v_lanes]]
                if low:
                    scores.append(dot(qkv[:low, k_lanes], one, NT))
                    values.append(qkv[:low, v_lanes])
                mixed, logsum = softmax_mix(scores, values)
                mixes.append(mixed)
                lse[pair, head : head + 1, low:high] = logsum
            both = jnp.where(lane_head((128, 1), 0, 0), mixes[0], mixes[1])
            mix[low:high, lanes] = both.T.astype(BF)
        return carry

    lax.fori_loop(0, 4, pair_step, 0)
    w_out = columns_of(weights, 3)
    for low in range(0, 1024, BLOCK):
        part[low : low + BLOCK, :] = dot(mix[low : low + BLOCK, :], w_out, NT).astype(BF)


def fused_self_forward(place, own, other, gain, bias, weights):
    return call(
        self_fwd_kernel,
        [
            (VMEM, like(1024, 1024)),
            (VMEM, like(1024, 1536)),
            (VMEM, like(1024, 512)),
            (VMEM, like(4, 2, 1024, dtype=F32)),
            (VMEM, like(1024, 1024)),
        ],
        [SMEM] + [VMEM] * 5,
        (place, own, other, gain, bias, weights),
        limit=40,
        flops=10 * 2**30,
        moved=14 * MIB,
    )


def cross_fwd_kernel(
    place, own, other, mine, theirs, gain, bias, text, ids, caption, weights, after, normed, queries, keys, mix, lse, part
):
    for row, half, number in image_blocks(place, own, other):
        rows = at(row, 128)
        values = half[number].astype(F32) + (mine[rows, :].astype(F32) + theirs[rows, :].astype(F32))
        after[rows, :] = values
        normed[rows, :] = normalized(values, gain[...], bias[...])
    w_query = columns_of(weights, 0)
    for low in range(0, 1024, BLOCK):
        queries[low : low + BLOCK, :] = dot(normed[low : low + BLOCK, :], w_query).astype(BF)
    w_text = jnp.concatenate([columns_of(weights, 1), columns_of(weights, 2)], 1)
    keys[...] = dot(text[...], w_text).astype(BF)

    def pair_step(pair, carry):
        lanes, v_lanes = at(pair * 128, 128), at(512 + pair * 128, 128)
        for low in range(0, 1024, 512):
            high = low + 512
            query = queries[low:high, lanes]
            seen = ids[...] == caption[:, low:high]
            mixes = []
            for head in range(2):
                scores = jnp.where(seen, dot(keys[:, lanes], one_head(query, head), NT), NEG)
                mixed, logsum = softmax_mix([scores], [keys[:, v_lanes]])
                mixes.append(mixed)
                lse[pair, head : head + 1, low:high] = logsum
            both = jnp.where(lane_head((128, 1), 0, 0), mixes[0], mixes[1])
            mix[low:high, lanes] = both.T.astype(BF)
        return carry

    lax.fori_loop(0, 4, pair_step, 0)
    w_out = columns_of(weights, 3)
    for low in range(0, 1024, BLOCK):
        part[low : low + BLOCK, :] = dot(mix[low : low + BLOCK, :], w_out, NT).astype(BF)


def fused_cross_forward(place, own, other, mine, theirs, gain, bias, text, ids, caption, weights):
    return call(
        cross_fwd_kernel,
        [
            (VMEM, like(1024, 1024, dtype=F32)),
            (VMEM, like(1024, 1024)),
            (VMEM, like(1024, 512)),
            (VMEM, like(128, 1024)),
            (VMEM, like(1024, 512)),
            (VMEM, like(4, 2, 1024, dtype=F32)),
            (VMEM, like(1024, 1024)),
        ],
        [SMEM] + [VMEM] * 10,
        (place, own, other, mine, theirs, gain, bias, text, ids, caption, weights),
        limit=44,
        flops=5 * 2**30,
        moved=20 * MIB,
    )


def cut_grads(place, grads, columns, own, side, over, low, high):
    chip = place[0]
    own[:, columns] = grads[at(chip * 256, 256), :].astype(BF)
    side[:, columns] = grads[at((chip ^ 1) * 256, 256), :].astype(BF)
    over[:, columns] = grads[at((chip ^ 2) * 256, 256), :].astype(BF)
    low[:, columns] = grads[at((chip ^ 3) * 256, 128), :].astype(BF)
    high[:, columns] = grads[at((chip ^ 3) * 256 + 128, 128), :].astype(BF)


GRAD_SHAPES = [(256, 2048)] * 3 + [(128, 2048)] * 2


def feed_step(rows, cot, rows_t, cot_t, weights, out_sum, back_sum, grads):
    w_in, w_out = weights[:, :256], weights[:, 256:]
    slope = math.sqrt(2.0 / math.pi)
    acts, pre_grads = [], []
    for low in range(0, 1024, BLOCK):
        part = slice(low, low + BLOCK)
        pre = dot(rows[part, :], w_in)
        square = pre * pre
        bent = jnp.tanh(pre * (slope + slope * 0.044715 * square))
        half = 0.5 * (1.0 + bent)
        act = (pre * half).astype(BF)
        bend = half + pre * (0.5 * (1.0 - bent * bent)) * (slope + 3.0 * slope * 0.044715 * square)
        pre_grad = (dot(cot[part, :], w_out) * bend).astype(BF)
        out_sum[part, :] += dot(act, w_out, NT)
        back_sum[part, :] += dot(pre_grad, w_in, NT)
        acts.append(act)
        pre_grads.append(pre_grad)
    grads[:, :256] = dot(rows_t[...], jnp.concatenate(pre_grads, 0))
    grads[:, 256:] = dot(cot_t[...], jnp.concatenate(acts, 0))


def feed_first_kernel(
    place, after, mine, theirs, gain, bias, cot_own, cot_other, weights,
    g_own, g_side, g_over, g_low, g_high, after_cross, normed, cot, out_sum, back_sum, rows_t, cot_t, grads,
):
    @pl.when(pl.program_id(0) == 0)
    def _():
        for low in range(0, 1024, 128):
            rows = slice(low, low + 128)
            values = after[rows, :] + (mine[rows, :].astype(F32) + theirs[rows, :].astype(F32))
            after_cross[rows, :] = values
            normed[rows, :] = normalized(values, gain[...], bias[...])
        for row, half, number in image_blocks(place, cot_own, cot_other):
            cot[at(row, 128), :] = half[number]
        rows_t[...] = normed[...].T
        cot_t[...] = cot[...].T
        out_sum[...] = jnp.zeros_like(out_sum)
        back_sum[...] = jnp.zeros_like(back_sum)

    feed_step(normed, cot, rows_t, cot_t, weights, out_sum, back_sum, grads)
    cut_grads(place, grads, slice(None), g_own, g_side, g_over, g_low, g_high)


def feed_second_kernel(
    place, normed, cot, out_in, back_in, weights,
    g_own, g_side, g_over, g_low, g_high, out_keep, out_sent, back, out_sum, back_sum, rows_t, cot_t, grads,
):
    step, core = pl.program_id(0), place[1]

    @pl.when(step == 0)
    def _():
        rows_t[...] = normed[...].T
        cot_t[...] = cot[...].T
        out_sum[...] = out_in[...]
        back_sum[...] = back_in[...]

    feed_step(normed, cot, rows_t, cot_t, weights, out_sum, back_sum, grads)
    cut_grads(place, grads, slice(None), g_own, g_side, g_over, g_low, g_high)

    @pl.when(step == 3)
    def _():
        back[...] = back_sum[...].astype(BF)
        for block in range(4):
            out_keep[block] = out_sum[at(block * 256 + core * 128, 128), :]
            out_sent[block] = out_sum[at(block * 256 + (1 - core) * 128, 128), :].astype(BF)


def once(*shape):
    zeros = (0,) * len(shape)
    return pl.BlockSpec(shape, lambda i: zeros, pipeline_mode=pl.Buffered(1))


def grad_outs():
    return [(pl.BlockSpec((rows, 512), lambda i: (0, i)), like(rows, n)) for rows, n in GRAD_SHAPES]


FEED_FLOPS = 13 * 2**30


def feed_first(place, after, mine, theirs, gain, bias, cot_own, cot_other, weights):
    square = once(1024, 1024)
    return call(
        feed_first_kernel,
        grad_outs()
        + [
            (square, like(1024, 1024, dtype=F32)),
            (square, like(1024, 1024)),
            (square, like(1024, 1024)),
            (square, like(1024, 1024, dtype=F32)),
            (square, like(1024, 1024, dtype=F32)),
        ],
        [SMEM, square, square, square, once(1, 1024), once(1, 1024), once(4, 128, 1024), once(4, 128, 1024)]
        + [pl.BlockSpec((1024, 512), lambda i: (0, i))],
        (place, after, mine, theirs, gain, bias, cot_own, cot_other, weights),
        [pltpu.VMEM((1024, 1024), BF)] * 2 + [pltpu.VMEM((1024, 512), F32)],
        limit=60,
        grid=(4,),
        flops=FEED_FLOPS,
        moved=30 * MIB,
    )


def feed_second(place, normed, cot, out_in, back_in, weights):
    square = once(1024, 1024)
    return call(
        feed_second_kernel,
        grad_outs()
        + [
            (once(4, 128, 1024), like(4, 128, 1024, dtype=F32)),
            (once(4, 128, 1024), like(4, 128, 1024)),
            (square, like(1024, 1024)),
        ],
        [SMEM, square, square, square, square, pl.BlockSpec((1024, 512), lambda i: (0, i))],
        (place, normed, cot, out_in, back_in, weights),
        [pltpu.VMEM((1024, 1024), F32)] * 2
        + [pltpu.VMEM((1024, 1024), BF)] * 2
        + [pltpu.VMEM((1024, 512), F32)],
        limit=60,
        grid=(4,),
        flops=FEED_FLOPS,
        moved=26 * MIB,
    )


def norm_backward(values, gain, grad):
    center = values - jnp.mean(values, -1, keepdims=True)
    inverse = lax.rsqrt(jnp.mean(center * center, -1, keepdims=True) + EPS)
    hat = center * inverse
    scaled = grad * gain
    back = inverse * (
        scaled - jnp.mean(scaled, -1, keepdims=True) - hat * jnp.mean(scaled * hat, -1, keepdims=True)
    )
    return back, grad * hat


def norm_block(values_of, mine, theirs, base_of, gain, norms, keep):
    gain_sum, bias_sum = jnp.zeros((8, 1024), F32), jnp.zeros((8, 1024), F32)
    for low in range(0, 1024, 128):
        rows = slice(low, low + 128)
        grad = mine[rows, :].astype(F32) + theirs[rows, :].astype(F32)
        back, term = norm_backward(values_of(rows), gain[...], grad)
        keep(rows, base_of(rows) + back)
        gain_sum = gain_sum + jnp.sum(term.reshape(16, 8, 1024), 0)
        bias_sum = bias_sum + jnp.sum(grad.reshape(16, 8, 1024), 0)
    norms[0:1, :] = jnp.sum(gain_sum, 0, keepdims=True)
    norms[1:2, :] = jnp.sum(bias_sum, 0, keepdims=True)


def head_grads(keys, values, one, one_grad, lse, delta, mask):
    weights = jnp.exp2(dot(keys, one, NT) * (LOG2E * HD**-0.5) - lse)
    if mask is not None:
        weights = jnp.where(mask, weights, 0.0)
    slope = dot(values, one_grad, NT)
    return weights.astype(BF), (weights * (slope - delta)).astype(BF)


def cross_bwd_kernel(
    place, after, mine, theirs, cot, gain, weights, normed, text, queries, keys, mix, lse, ids, caption,
    grad_cross, part, norms, text_part, g_own, g_side, g_over, g_low, g_high, low_grad, mix_grad, dq, dkv, grads,
):
    def keep(rows, value):
        grad_cross[rows, :] = value
        low_grad[rows, :] = value.astype(BF)

    norm_block(lambda rows: after[rows, :], mine, theirs, lambda rows: cot[rows, :].astype(F32), gain, norms, keep)
    w_out = columns_of(weights, 3)
    for low in range(0, 1024, BLOCK):
        mix_grad[low : low + BLOCK, :] = dot(low_grad[low : low + BLOCK, :], w_out).astype(BF)

    def pair_step(pair, carry):
        lanes, v_lanes = at(pair * 128, 128), at(512 + pair * 128, 128)
        dk_sum, dv_sum = jnp.zeros((128, 128), F32), jnp.zeros((128, 128), F32)
        for low in range(0, 1024, 512):
            high = low + 512
            query, grad = queries[low:high, lanes], mix_grad[low:high, lanes]
            product = (grad.astype(F32) * mix[low:high, lanes].astype(F32)).T
            seen = ids[...] == caption[:, low:high]
            back = []
            for head in range(2):
                one, one_grad = one_head(query, head), one_head(grad, head)
                delta = jnp.sum(product[head * HD : (head + 1) * HD], 0, keepdims=True)
                prob, score_grad = head_grads(
                    keys[:, lanes], keys[:, v_lanes], one, one_grad, lse[pair, head : head + 1, low:high], delta, seen
                )
                dv_sum = dv_sum + dot(prob, one_grad)
                dk_sum = dk_sum + dot(score_grad, one)
                back.append(dot(keys[:, lanes], score_grad, TN))
            both = jnp.where(lane_head((128, 1), 0, 0), back[0], back[1])
            dq[low:high, lanes] = (both.T * HD**-0.5).astype(BF)
        dkv[:, lanes] = (dk_sum * HD**-0.5).astype(BF)
        dkv[:, v_lanes] = dv_sum.astype(BF)
        return carry

    lax.fori_loop(0, 4, pair_step, 0)
    w_query = columns_of(weights, 0)
    for low in range(0, 1024, BLOCK):
        part[low : low + BLOCK, :] = dot(dq[low : low + BLOCK, :], w_query, NT).astype(BF)
    w_text = jnp.concatenate([columns_of(weights, 1), columns_of(weights, 2)], 1)
    text_part[...] = dot(dkv[...], w_text, NT).astype(BF)
    for one, (left, right) in enumerate(
        ((normed, dq[...]), (text, dkv[:, :512]), (text, dkv[:, 512:]), (low_grad, mix[...]))
    ):
        grads[...] = dot(left[...], right, TN)
        for s in range(4):
            columns = slice(s * 512 + one * 128, s * 512 + (one + 1) * 128)
            cut_grads(
                place, grads.at[:, s * 128 : (s + 1) * 128], columns, g_own, g_side, g_over, g_low, g_high
            )


def fused_cross_backward(place, after, mine, theirs, cot, gain, weights, normed, text, queries, keys, mix, lse, ids, caption):
    return call(
        cross_bwd_kernel,
        [
            (VMEM, like(1024, 1024, dtype=F32)),
            (VMEM, like(1024, 1024)),
            (VMEM, like(8, 1024, dtype=F32)),
            (VMEM, like(128, 1024)),
        ]
        + [(VMEM, like(*shape)) for shape in GRAD_SHAPES],
        [SMEM] + [VMEM] * 14,
        (place, after, mine, theirs, cot, gain, weights, normed, text, queries, keys, mix, lse, ids, caption),
        [
            pltpu.VMEM((1024, 1024), BF),
            pltpu.VMEM((1024, 512), BF),
            pltpu.VMEM((1024, 512), BF),
            pltpu.VMEM((128, 1024), BF),
            pltpu.VMEM((1024, 512), F32),
        ],
        limit=60,
        flops=9 * 2**30,
        moved=32 * MIB,
    )


def self_bwd_kernel(
    place, after, mine, theirs, base, gain, weights, qkv, mix, lse,
    grad_own, low_grad, norms, dqkv, mix_grad, dk_sum, dv_sum,
):
    core = place[1]

    def keep(rows, value):
        low_grad[rows, :] = value.astype(BF)

        @pl.when(core == (rows.start // 128) % 2)
        def _():
            grad_own[rows.start // 256] = value

    norm_block(lambda rows: after[rows, :], mine, theirs, lambda rows: base[rows, :], gain, norms, keep)
    w_out = columns_of(weights, 3)
    for low in range(0, 1024, BLOCK):
        mix_grad[low : low + BLOCK, :] = dot(low_grad[low : low + BLOCK, :], w_out).astype(BF)
    causal = causal_mask()

    def pair_step(pair, carry):
        lanes = at(pair * 128, 128)
        k_lanes, v_lanes = at(512 + pair * 128, 128), at(1024 + pair * 128, 128)
        dk_sum[...] = jnp.zeros_like(dk_sum)
        dv_sum[...] = jnp.zeros_like(dv_sum)
        for low in range(0, 1024, BLOCK):
            high = low + BLOCK
            query, grad = qkv[low:high, lanes], mix_grad[low:high, lanes]
            product = (grad.astype(F32) * mix[low:high, lanes].astype(F32)).T
            back = []
            for head in range(2):
                one, one_grad = one_head(query, head), one_head(grad, head)
                delta = jnp.sum(product[head * HD : (head + 1) * HD], 0, keepdims=True)
                total = jnp.zeros((128, BLOCK), F32)
                for start, stop in ((0, low), (low, high)):
                    if start == stop:
                        continue
                    prob, score_grad = head_grads(
                        qkv[start:stop, k_lanes],
                        qkv[start:stop, v_lanes],
                        one,
                        one_grad,
                        lse[pair, head : head + 1, low:high],
                        delta,
                        causal if start == low else None,
                    )
                    dv_sum[start:stop, :] += dot(prob, one_grad)
                    dk_sum[start:stop, :] += dot(score_grad, one)
                    total = total + dot(qkv[start:stop, k_lanes], score_grad, TN)
                back.append(total)
            both = jnp.where(lane_head((128, 1), 0, 0), back[0], back[1])
            dqkv[low:high, lanes] = (both.T * HD**-0.5).astype(BF)
        dqkv[:, k_lanes] = (dk_sum[...] * HD**-0.5).astype(BF)
        dqkv[:, v_lanes] = dv_sum[...].astype(BF)
        return carry

    lax.fori_loop(0, 4, pair_step, 0)


def fused_self_backward(place, after, mine, theirs, base, gain, weights, qkv, mix, lse):
    return call(
        self_bwd_kernel,
        [
            (VMEM, like(4, 128, 1024, dtype=F32)),
            (VMEM, like(1024, 1024)),
            (VMEM, like(8, 1024, dtype=F32)),
            (VMEM, like(1024, 1536)),
        ],
        [SMEM] + [VMEM] * 9,
        (place, after, mine, theirs, base, gain, weights, qkv, mix, lse),
        [pltpu.VMEM((1024, 512), BF), pltpu.VMEM((1024, 128), F32), pltpu.VMEM((1024, 128), F32)],
        limit=56,
        flops=9 * 2**30,
        moved=32 * MIB,
    )


def self_grads_kernel(place, normed, low_grad, dq, dk, dv, mix, g_own, g_side, g_over, g_low, g_high, rows_t, grad_t, grads):
    @pl.when(pl.program_id(0) == 0)
    def _():
        rows_t[...] = normed[...].T
        grad_t[...] = low_grad[...].T

    grads[:, :384] = dot(rows_t[...], jnp.concatenate([dq[...], dk[...], dv[...]], 1))
    grads[:, 384:] = dot(grad_t[...], mix[...])
    cut_grads(place, grads, slice(None), g_own, g_side, g_over, g_low, g_high)


def self_grads(place, normed, low_grad, dqkv, mix):
    square = once(1024, 1024)

    def cut(offset):
        return pl.BlockSpec((1024, 128), lambda i: (0, offset + i))

    return call(
        self_grads_kernel,
        grad_outs(),
        [SMEM, square, square, cut(0), cut(4), cut(8), cut(0)],
        (place, normed, low_grad, dqkv, dqkv, dqkv, mix),
        [pltpu.VMEM((1024, 1024), BF)] * 2 + [pltpu.VMEM((1024, 512), F32)],
        limit=32,
        grid=(4,),
        flops=4 * 2**30,
        moved=12 * MIB,
    )


def self_back_kernel(place, dqkv, weights, kept, sent):
    core = place[1]
    w_in = jnp.concatenate([columns_of(weights, one) for one in range(3)], 1)
    for block in range(4):
        for target, half in ((sent, 1 - core), (kept, core)):
            value = dot(dqkv[at(block * 256 + half * 128, 128), :], w_in, NT)
            target[block] = value.astype(target.dtype)


def self_back(place, dqkv, weights):
    return call(
        self_back_kernel,
        [(VMEM, like(4, 128, 1024, dtype=F32)), (VMEM, like(4, 128, 1024))],
        [SMEM, VMEM, VMEM],
        (place, dqkv, weights),
        limit=32,
        flops=3 * 2**30,
        moved=10 * MIB,
    )


def last_norm_kernel(place, rows, grad_own, mine, theirs, gain, *outs):
    pieces, norms = outs[:4], outs[4]
    gain_sum, bias_sum = jnp.zeros((8, 1024), F32), jnp.zeros((8, 1024), F32)
    for number in range(4):
        block = place[3] ^ number
        grad = mine[block] + theirs[block].astype(F32)
        back, term = norm_backward(rows[number].astype(F32), gain[...], grad)
        pieces[number][...] = (grad_own[block] + back).astype(BF)
        gain_sum = gain_sum + jnp.sum(term.reshape(16, 8, 1024), 0)
        bias_sum = bias_sum + jnp.sum(grad.reshape(16, 8, 1024), 0)
    norms[0:1, :] = jnp.sum(gain_sum, 0, keepdims=True)
    norms[1:2, :] = jnp.sum(bias_sum, 0, keepdims=True)


def last_norm(place, rows, grad_own, mine, theirs, gain):
    return call(
        last_norm_kernel,
        [(VMEM, like(128, 1024))] * 4 + [(VMEM, like(8, 1024, dtype=F32))],
        [SMEM] + [VMEM] * 5,
        (place, rows, grad_own, mine, theirs, gain),
        limit=24,
        moved=8 * MIB,
    )


def finish_kernel(place, after, out_keep, theirs, text_part, *rest):
    messages, rows, sems = rest[:4], rest[4], rest[5]
    core, slot = place[1], place[3]
    run_copies(
        [(after.at[at((slot ^ n) * 256 + core * 128, 128), :], rows.at[n]) for n in range(4)], sems
    )
    for number in range(4):
        block = slot ^ number
        value = rows[number] + (out_keep[block] + theirs[block].astype(F32))
        messages[number][0:128, :] = value.astype(BF)
        messages[number][128:160, :] = text_part[at(block * 32, 32, 32), :]


def finish(place, after, out_keep, theirs, text_part):
    return call(
        finish_kernel,
        [(VMEM, like(160, 1024))] * 4,
        [SMEM, ANY] + [VMEM] * 3,
        (place, after, out_keep, theirs, text_part),
        [pltpu.VMEM((4, 128, 1024), F32), pltpu.SemaphoreType.DMA((4,))],
        limit=24,
        moved=8 * MIB,
    )


def land_kernel(place, *refs):
    messages, result, text = refs[:4], refs[4], refs[5]
    top = place[2]
    text[...] = jnp.zeros_like(text)
    for number in range(4):
        slot = top ^ number
        result[slot % 2, at((slot // 2) * 128, 128), :] = messages[number][0:128, :]
        text[slot % 2] += messages[number][128:160, :].astype(F32)


def land(place, messages):
    return call(
        land_kernel,
        [(VMEM, like(2, 256, 1024)), (VMEM, like(2, 32, 1024, dtype=F32))],
        [SMEM] + [VMEM] * 4,
        (place, *messages),
        limit=16,
        moved=3 * MIB,
    )


def land_wide_kernel(place, *refs):
    pieces, rows = refs[:4], refs[4]
    for number in range(4):
        slot = place[2] ^ number
        rows[slot % 2, at((slot // 2) * 128, 128), :] = pieces[number][...].astype(F32)


def land_wide(place, pieces):
    return call(
        land_wide_kernel,
        [(VMEM, like(2, 256, 1024, dtype=F32))],
        [SMEM] + [VMEM] * 4,
        (place, *pieces),
        limit=16,
        moved=3 * MIB,
    )[0]


def relay_kernel(over, side, from_side, from_over, to_over, to_side):
    to_over[0:128, :] = (over[0:128, :].astype(F32) + from_side[...].astype(F32)).astype(BF)
    to_over[128:256, :] = over[128:256, :]
    to_side[0:128, :] = side[0:128, :]
    to_side[128:256, :] = (side[128:256, :].astype(F32) + from_over[...].astype(F32)).astype(BF)


def relay(over, side, from_side, from_over):
    return call(
        relay_kernel,
        [(VMEM, like(256, 2048))] * 2,
        [VMEM] * 4,
        (over, side, from_side, from_over),
        limit=16,
        moved=5 * MIB,
    )


def plane_sum_kernel(own, over, side, keep, *sent):
    for s in range(4):
        columns = slice(s * 512, (s + 1) * 512)
        total = own[:, columns].astype(F32) + over[:, columns].astype(F32) + side[:, columns].astype(F32)
        if s:
            sent[s - 1][...] = total.astype(BF)
        else:
            keep[...] = total


def plane_sum(own, over, side):
    return call(
        plane_sum_kernel,
        [(VMEM, like(256, 512, dtype=F32))] + [(VMEM, like(256, 512))] * 3,
        [VMEM] * 3,
        (own, over, side),
        limit=16,
        moved=5 * MIB,
    )


def line_sum_kernel(place, keep, one, two, three, mine, other):
    core = place[1]
    for target, half in ((other, 1 - core), (mine, core)):
        rows = at(half * 128, 128)
        total = keep[rows, :]
        for part in (one, two, three):
            total = total + part[rows, :].astype(F32)
        target[...] = total.astype(target.dtype)


def line_sum(place, keep, parts):
    return call(
        line_sum_kernel,
        [(VMEM, like(128, 512, dtype=F32)), (VMEM, like(128, 512))],
        [SMEM] + [VMEM] * 4,
        (place, keep, *parts),
        limit=8,
        moved=2 * MIB,
    )


def spread_kernel(place, mine, other, *outs):
    core, columns = place[1], mine.shape[1] // len(outs)
    for one, out in enumerate(outs):
        cut = slice(one * columns, (one + 1) * columns)
        out[:, at(core * columns, columns)] = mine[:, cut]
        out[:, at((1 - core) * columns, columns)] = other[:, cut].astype(F32)


def spread(place, mine, other):
    return call(
        spread_kernel,
        [(VMEM, like(128, 256, dtype=F32))] * 4,
        [SMEM] + [VMEM] * 2,
        (place, mine, other),
        limit=8,
        moved=MIB,
    )


def spread_feed_kernel(place, mine_one, other_one, mine_two, other_two, *outs):
    core = place[1]
    for part, (mine, other) in enumerate(((mine_one, other_one), (mine_two, other_two))):
        for one, out in enumerate(outs):
            cut = slice(one * 256, (one + 1) * 256)
            out[:, at(core * 512 + part * 256, 256)] = mine[:, cut]
            out[:, at((1 - core) * 512 + part * 256, 256)] = other[:, cut].astype(F32)


def spread_feed(place, *halves):
    return call(
        spread_feed_kernel,
        [(VMEM, like(128, 1024, dtype=F32))] * 2,
        [SMEM] + [VMEM] * 4,
        (place, *halves),
        limit=8,
        moved=2 * MIB,
    )


def after(value, *earlier):
    return lax.optimization_barrier((value, *earlier))[0]


def packed_layer(args):
    image_rows, text_rows, segment_ids, cotangent, *others = args
    weights, norms = others[:10], others[10:]
    chip, core, top = lax.axis_index("chip"), lax.axis_index("core"), lax.axis_index("hi")
    place = jnp.stack([chip, core, top, core * 2 + top % 2]).astype(jnp.int32)

    def swap(value):
        return lax.ppermute(value, "core", [(0, 1), (1, 0)])

    def across(value, bit):
        return lax.ppermute(value, "chip", [(i, i ^ bit) for i in range(4)])

    def shift(value, step):
        return lax.ppermute(value, "hi", [((i + step) % 4, i) for i in range(4)])

    def exchange(pieces, back):
        got = []
        for number, piece in enumerate(pieces):
            pairs = []
            for source_core in range(2):
                for source_top in range(4):
                    slot = source_top ^ number
                    source = source_core * 4 + source_top
                    target = (slot // 2) * 4 + source_core * 2 + slot % 2
                    pairs.append((target, source) if back else (source, target))
            got.append(lax.ppermute(piece, ("core", "hi"), pairs))
        return got

    ids_wide = jnp.pad(segment_ids.astype(BF)[:, None, :], ((0, 0), (0, 15), (0, 896)))
    *pieces, keep, sent = prepare(place, image_rows, text_rows, ids_wide, cotangent, weights)
    messages, cots = pieces[:4], pieces[4:]
    taken = swap(sent)
    *singles, near_first, near_second = join(keep, taken)

    def plane(near, cut):
        side, over = across(near, 1), across(near, 2)
        return side, over, across(side[:cut], 2), across(over[cut:], 1)

    def line(group, *earlier):
        part = after(singles[group], *earlier)
        return [shift(part, step) for step in range(1, 4)]

    lines = [line(0)]
    near = [plane(near_first, 256)]
    messages = exchange([after(m, *lines[0]) for m in messages], False)
    rest = stack(lines[0])
    far = [(rest, *plane(rest, 384))]
    lines.append(line(1, *messages))
    near.append(plane(after(near_second, *far[0][1:3]), 256))
    lines.append(line(2, *lines[1]))
    lines.append(line(3, *lines[2]))
    for group in range(1, 4):
        rest = stack(lines[group])
        rest = after(rest, *(near[1][:2] if group == 1 else far[group - 1][1:3]))
        far.append((rest, *plane(rest, 384)))
    cots = exchange([after(c, *lines[3]) for c in cots], False)

    def group_weights(group):
        side, over, low, high = near[group // 2]
        first = near_first if group < 2 else near_second
        return assemble(place, (first, side, over, high if group % 2 else low), far[group], (group % 2) * 256)

    gains = lax.all_gather(after(jnp.stack(norms), lines[0][0]), ("chip", "core"), axis=1, tiled=True)
    gain_one, bias_one, gain_two, bias_two, gain_three, bias_three = [gains[i : i + 1] for i in range(6)]

    rows_own, text = arrange(place, messages)
    rows_other = swap(rows_own)
    ids = messages[0][160, :128].astype(jnp.int32)
    caption = jnp.repeat(ids, 8)[None, :]
    ids = ids[:, None]
    w_self = group_weights(0)
    normed_one, qkv, self_mix, self_lse, mine = fused_self_forward(
        place, rows_own, rows_other, gain_one, bias_one, w_self
    )
    theirs = swap(mine)
    w_cross = group_weights(1)
    after_attn, normed_two, queries, keys, cross_mix, cross_lse, mine = fused_cross_forward(
        place, rows_own, rows_other, mine, theirs, gain_two, bias_two, text, ids, caption, w_cross
    )
    theirs = swap(mine)
    cot_own = stack([c[None] for c in cots])
    cot_other = swap(cot_own)
    *grads_one, after_cross, normed_three, cot, out_sum, back_sum = feed_first(
        place, after_attn, mine, theirs, gain_three, bias_three, cot_own, cot_other, group_weights(2)
    )
    *grads_two, out_keep, out_sent, mine = feed_second(
        place, normed_three, cot, out_sum, back_sum, group_weights(3)
    )

    def reduce_plane(grads):
        own, side, over, low, high = grads
        to_over, to_side = relay(over, side, across(low, 1), across(high, 2))
        return plane_sum(own, across(to_over, 2), across(to_side, 1))

    def reduce_line(sums):
        kept, *parts = sums
        mine, other = line_sum(place, kept, [shift(part, 3 - i) for i, part in enumerate(parts)])
        return mine, swap(other)

    theirs = swap(mine)
    out_theirs = swap(out_sent)
    grad_cross, part, norms_three, text_part, *grads_three = fused_cross_backward(
        place, after_cross, mine, theirs, cot, gain_three, w_cross, normed_two, text, queries, keys,
        cross_mix, cross_lse, ids, caption,
    )
    theirs = swap(part)
    grad_own, low_grad, norms_two, dqkv = fused_self_backward(
        place, after_attn, part, theirs, grad_cross, gain_two, w_self, qkv, self_mix, self_lse
    )
    grads_four = self_grads(place, normed_one, low_grad, dqkv, self_mix)
    kept, sent = self_back(place, dqkv, w_self)
    *input_pieces, norms_one = last_norm(place, rows_own, grad_own, kept, swap(sent), gain_one)

    feeds = [reduce_line(reduce_plane(grads)) for grads in (grads_one, grads_two)]
    feed_grads = spread_feed(place, *feeds[0], *feeds[1])
    cross_grads = spread(place, *reduce_line(reduce_plane(grads_three)))
    result, text_grad = land(place, exchange(finish(place, after_cross, out_keep, out_theirs, text_part), True))
    own_grads = spread(place, *reduce_line(reduce_plane(grads_four)))
    input_grad = land_wide(place, exchange(input_pieces, True))

    sums = jnp.concatenate([norms_one[:2], 0.5 * norms_two[:2], 0.5 * norms_three[:2]], 0)
    sums = sums + swap(sums)
    sums = sums + across(sums, 1)
    sums = sums + across(sums, 2)
    for bit in (1, 2):
        sums = sums + lax.ppermute(sums, "hi", [(i, i ^ bit) for i in range(4)])
    sums = lax.dynamic_slice_in_dim(sums, (chip * 2 + core) * 128, 128, 1)
    return (result, input_grad, text_grad, *own_grads, *cross_grads, *feed_grads, *[sums[i] for i in range(6)])


def solution(mesh):
    fsdp, tensor = mesh.shape["fsdp"], mesh.shape["tensor"]

    def run(*args):
        images = args[0].shape[0] // fsdp
        tops = 2 * images
        shape = {"chip": fsdp // 2, "core": 2, "hi": tops, "lo": tensor // tops}
        fine = Mesh(mesh.devices.reshape(tuple(shape.values())), tuple(shape))
        first, second = ("chip", "core"), ("hi", "lo")
        wide, weight, norm = P(first, second, None), P(first, second), P(first)
        outs = (wide,) * 3 + (weight,) * 10 + (norm,) * 6
        packed = (
            (fsdp, tensor, images) == (8, 4, 2)
            and args[0].shape[1:] == (1024, 1024)
            and args[1].shape[1:] == (128, 1024)
            and args[12].shape == (1024, 4096)
        )
        return jax.shard_map(
            lambda *local: packed_layer(local) if packed else layer(shape, local),
            mesh=fine,
            in_specs=(wide, wide, P(first, None), wide) + (weight,) * 10 + (norm,) * 6,
            out_specs=outs,
            check_vma=False,
        )(*args)

    return run
```

```python
import functools
import math

import jax
import jax.numpy as jnp
from jax import lax
from jax.experimental import pallas as pl
from jax.experimental.pallas import tpu as pltpu
from jax.sharding import Mesh
from jax.sharding import PartitionSpec as P

HD = 64
EPS = 1e-05
NEG = -1e30
LOG2E = math.log2(math.e)
BF = jnp.bfloat16
F32 = jnp.float32
NT = (((1,), (1,)), ((), ()))
TN = (((0,), (0,)), ((), ()))
NN = (((1,), (0,)), ((), ()))


def dot(left, right, dims=NN):
    return lax.dot_general(left, right, dims, preferred_element_type=F32)


def lane_head(shape, axis, head):
    return lax.broadcasted_iota(jnp.int32, shape, axis) // HD == head


def self_forward_kernel(q_ref, k_ref, v_ref, mix_ref, lse_ref, *, block):
    length = q_ref.shape[0]
    scale = LOG2E * HD**-0.5
    causal = lax.broadcasted_iota(jnp.int32, (block, block), 0) <= lax.broadcasted_iota(
        jnp.int32, (block, block), 1
    )
    for at in range(length // block):
        lo, hi = at * block, (at + 1) * block
        query = q_ref[lo:hi, :]
        mixes = []
        for head in range(2):
            one = jnp.where(lane_head((1, 2 * HD), 1, head), query, jnp.zeros_like(query))
            diag = jnp.where(causal, dot(k_ref[lo:hi, :], one, NT), NEG)
            peak = jnp.max(diag, 0, keepdims=True)
            if at:
                past = dot(k_ref[:lo, :], one, NT)
                peak = jnp.maximum(peak, jnp.max(past, 0, keepdims=True))
            weights = jnp.exp2((diag - peak) * scale)
            total = jnp.sum(weights, 0, keepdims=True)
            mixed = dot(v_ref[lo:hi, :], weights.astype(BF), TN)
            if at:
                weights = jnp.exp2((past - peak) * scale)
                total = total + jnp.sum(weights, 0, keepdims=True)
                mixed = mixed + dot(v_ref[:lo, :], weights.astype(BF), TN)
            mixes.append(mixed / total)
            lse_ref[0, head : head + 1, lo:hi] = peak * scale + jnp.log2(total)
        both = jnp.where(lane_head((2 * HD, 1), 0, 0), mixes[0], mixes[1])
        mix_ref[lo:hi, :] = both.T.astype(BF)


def self_backward_kernel(
    q_ref, k_ref, v_ref, mix_ref, grad_ref, lse_ref, dq_ref, dk_ref, dv_ref, dk_sum, dv_sum, *, block
):
    length = q_ref.shape[0]
    scale = LOG2E * HD**-0.5
    causal = lax.broadcasted_iota(jnp.int32, (block, block), 0) <= lax.broadcasted_iota(
        jnp.int32, (block, block), 1
    )
    dk_sum[...] = jnp.zeros_like(dk_sum)
    dv_sum[...] = jnp.zeros_like(dv_sum)
    for at in range(length // block):
        lo, hi = at * block, (at + 1) * block
        query = q_ref[lo:hi, :]
        grad = grad_ref[lo:hi, :]
        product = (grad.astype(F32) * mix_ref[lo:hi, :].astype(F32)).T
        grads = []
        for head in range(2):
            picked = lane_head((1, 2 * HD), 1, head)
            one = jnp.where(picked, query, jnp.zeros_like(query))
            one_grad = jnp.where(picked, grad, jnp.zeros_like(grad))
            delta = jnp.sum(product[head * HD : (head + 1) * HD], 0, keepdims=True)
            lse = lse_ref[0, head : head + 1, lo:hi]
            total = jnp.zeros((2 * HD, block), F32)
            for start, stop in ((0, lo), (lo, hi)):
                if start == stop:
                    continue
                keys = k_ref[start:stop, :]
                weights = jnp.exp2(dot(keys, one, NT) * scale - lse)
                if start == lo:
                    weights = jnp.where(causal, weights, 0.0)
                slope = dot(v_ref[start:stop, :], one_grad, NT)
                score_grad = (weights * (slope - delta)).astype(BF)
                dv_sum[start:stop, :] += dot(weights.astype(BF), one_grad)
                dk_sum[start:stop, :] += dot(score_grad, one)
                total = total + dot(keys, score_grad, TN)
            grads.append(total)
        both = jnp.where(lane_head((2 * HD, 1), 0, 0), grads[0], grads[1])
        dq_ref[lo:hi, :] = (both.T * HD**-0.5).astype(BF)
    dk_ref[...] = (dk_sum[...] * HD**-0.5).astype(BF)
    dv_ref[...] = dv_sum[...].astype(BF)


def cross_forward_kernel(q_ref, k_ref, v_ref, ids_ref, caption_ref, mix_ref, lse_ref, *, block):
    length = q_ref.shape[0]
    scale = LOG2E * HD**-0.5
    for at in range(length // block):
        lo, hi = at * block, (at + 1) * block
        query = q_ref[lo:hi, :]
        seen = ids_ref[...] == caption_ref[:, lo:hi]
        mixes = []
        for head in range(2):
            one = jnp.where(lane_head((1, 2 * HD), 1, head), query, jnp.zeros_like(query))
            scores = jnp.where(seen, dot(k_ref[...], one, NT), NEG)
            peak = jnp.max(scores, 0, keepdims=True)
            weights = jnp.exp2((scores - peak) * scale)
            total = jnp.sum(weights, 0, keepdims=True)
            mixes.append(dot(v_ref[...], weights.astype(BF), TN) / total)
            lse_ref[0, head : head + 1, lo:hi] = peak * scale + jnp.log2(total)
        both = jnp.where(lane_head((2 * HD, 1), 0, 0), mixes[0], mixes[1])
        mix_ref[lo:hi, :] = both.T.astype(BF)


def cross_backward_kernel(
    q_ref, k_ref, v_ref, mix_ref, grad_ref, lse_ref, ids_ref, caption_ref, dq_ref, dk_ref, dv_ref, *, block
):
    length = q_ref.shape[0]
    scale = LOG2E * HD**-0.5
    keys, values = k_ref[...], v_ref[...]
    dk_sum = jnp.zeros(keys.shape, F32)
    dv_sum = jnp.zeros(keys.shape, F32)
    for at in range(length // block):
        lo, hi = at * block, (at + 1) * block
        query = q_ref[lo:hi, :]
        grad = grad_ref[lo:hi, :]
        product = (grad.astype(F32) * mix_ref[lo:hi, :].astype(F32)).T
        seen = ids_ref[...] == caption_ref[:, lo:hi]
        grads = []
        for head in range(2):
            picked = lane_head((1, 2 * HD), 1, head)
            one = jnp.where(picked, query, jnp.zeros_like(query))
            one_grad = jnp.where(picked, grad, jnp.zeros_like(grad))
            delta = jnp.sum(product[head * HD : (head + 1) * HD], 0, keepdims=True)
            lse = lse_ref[0, head : head + 1, lo:hi]
            weights = jnp.where(seen, jnp.exp2(dot(keys, one, NT) * scale - lse), 0.0)
            slope = dot(values, one_grad, NT)
            score_grad = (weights * (slope - delta)).astype(BF)
            dv_sum = dv_sum + dot(weights.astype(BF), one_grad)
            dk_sum = dk_sum + dot(score_grad, one)
            grads.append(dot(keys, score_grad, TN))
        both = jnp.where(lane_head((2 * HD, 1), 0, 0), grads[0], grads[1])
        dq_ref[lo:hi, :] = (both.T * HD**-0.5).astype(BF)
    dk_ref[...] = (dk_sum * HD**-0.5).astype(BF)
    dv_ref[...] = dv_sum.astype(BF)


def feed_kernel(
    rows_ref, cot_ref, win_ref, wout_ref, out_in, back_in, gin_ref, gout_ref, out_ref, back_ref, rows_t, cot_t, *, first
):
    step = pl.program_id(0)

    @pl.when(step == 0)
    def _():
        rows_t[...] = rows_ref[...].T
        cot_t[...] = cot_ref[...].T
        if first:
            out_ref[...] = jnp.zeros_like(out_ref)
            back_ref[...] = jnp.zeros_like(back_ref)
        else:
            out_ref[...] = out_in[...]
            back_ref[...] = back_in[...]

    pre = dot(rows_ref[...], win_ref[...])
    square = pre * pre
    slope = math.sqrt(2.0 / math.pi)
    bent = jnp.tanh(pre * (slope + slope * 0.044715 * square))
    half = 0.5 * (1.0 + bent)
    act = (pre * half).astype(BF)
    out_ref[...] += dot(act, wout_ref[...], NT)
    gout_ref[...] = dot(cot_t[...], act).astype(BF)
    bend = half + pre * (0.5 * (1.0 - bent * bent)) * (slope + 3.0 * slope * 0.044715 * square)
    pre_grad = (dot(cot_ref[...], wout_ref[...]) * bend).astype(BF)
    gin_ref[...] = dot(rows_t[...], pre_grad).astype(BF)
    back_ref[...] += dot(pre_grad, win_ref[...], NT)


VMEM_LIMIT = 60 * 1024 * 1024


def params():
    return pltpu.CompilerParams(vmem_limit_bytes=VMEM_LIMIT)


def column(rows, offset):
    return pl.BlockSpec((rows, 2 * HD), lambda i: (0, offset + i))


def self_forward(packed):
    length, width = packed.shape
    pairs = width // (6 * HD)
    return pl.pallas_call(
        functools.partial(self_forward_kernel, block=256),
        grid=(pairs,),
        in_specs=[column(length, 0), column(length, pairs), column(length, 2 * pairs)],
        out_specs=[column(length, 0), pl.BlockSpec((1, 2, length), lambda i: (i, 0, 0))],
        out_shape=[
            jax.ShapeDtypeStruct((length, pairs * 2 * HD), BF),
            jax.ShapeDtypeStruct((pairs, 2, length), F32),
        ],
        compiler_params=params(),
        cost_estimate=pl.CostEstimate(
            flops=8 * pairs * length * length * 2 * HD * 2,
            bytes_accessed=8 * pairs * length * 2 * HD,
            transcendentals=2 * pairs * length * length,
        ),
    )(packed, packed, packed)


def self_backward(packed, mix, grad, lse):
    length, width = packed.shape
    pairs = width // (6 * HD)
    part = jax.ShapeDtypeStruct((length, pairs * 2 * HD), BF)
    return pl.pallas_call(
        functools.partial(self_backward_kernel, block=256),
        grid=(pairs,),
        in_specs=[
            column(length, 0),
            column(length, pairs),
            column(length, 2 * pairs),
            column(length, 0),
            column(length, 0),
            pl.BlockSpec((1, 2, length), lambda i: (i, 0, 0)),
        ],
        out_specs=[column(length, 0)] * 3,
        out_shape=[part] * 3,
        scratch_shapes=[pltpu.VMEM((length, 2 * HD), F32)] * 2,
        compiler_params=params(),
        cost_estimate=pl.CostEstimate(
            flops=20 * pairs * length * length * 2 * HD * 2,
            bytes_accessed=16 * pairs * length * 2 * HD,
            transcendentals=2 * pairs * length * length,
        ),
    )(packed, packed, packed, mix, grad, lse)


def cross_forward(queries, keys, ids, captions):
    length, width = queries.shape
    texts = keys.shape[0]
    pairs = width // (2 * HD)
    return pl.pallas_call(
        functools.partial(cross_forward_kernel, block=min(512, length)),
        grid=(pairs,),
        in_specs=[
            column(length, 0),
            column(texts, 0),
            column(texts, pairs),
            pl.BlockSpec((texts, 1), lambda i: (0, 0)),
            pl.BlockSpec((1, length), lambda i: (0, 0)),
        ],
        out_specs=[column(length, 0), pl.BlockSpec((1, 2, length), lambda i: (i, 0, 0))],
        out_shape=[
            jax.ShapeDtypeStruct((length, width), BF),
            jax.ShapeDtypeStruct((pairs, 2, length), F32),
        ],
        compiler_params=params(),
    )(queries, keys, keys, ids, captions)


def cross_backward(queries, keys, mix, grad, lse, ids, captions):
    length, width = queries.shape
    texts = keys.shape[0]
    pairs = width // (2 * HD)
    return pl.pallas_call(
        functools.partial(cross_backward_kernel, block=min(512, length)),
        grid=(pairs,),
        in_specs=[
            column(length, 0),
            column(texts, 0),
            column(texts, pairs),
            column(length, 0),
            column(length, 0),
            pl.BlockSpec((1, 2, length), lambda i: (i, 0, 0)),
            pl.BlockSpec((texts, 1), lambda i: (0, 0)),
            pl.BlockSpec((1, length), lambda i: (0, 0)),
        ],
        out_specs=[column(length, 0), column(texts, 0), column(texts, 0)],
        out_shape=[
            jax.ShapeDtypeStruct((length, width), BF),
            jax.ShapeDtypeStruct((texts, width), BF),
            jax.ShapeDtypeStruct((texts, width), BF),
        ],
        compiler_params=params(),
    )(queries, keys, keys, mix, grad, lse, ids, captions)


def feed(rows, cot, w_in, w_out, sums):
    length, width = rows.shape
    units = w_in.shape[1]
    block = min(256, units)
    whole = pl.BlockSpec((length, width), lambda i: (0, 0))
    cut = pl.BlockSpec((width, block), lambda i: (0, i))
    first = sums is None
    kernel = functools.partial(feed_kernel, first=first)
    operands = [rows, cot, w_in, w_out]
    specs = [whole, whole, cut, cut]
    if first:
        body = lambda a, b, c, d, *rest: kernel(a, b, c, d, None, None, *rest)
    else:
        body = kernel
        operands += list(sums)
        specs += [whole, whole]
    total = jax.ShapeDtypeStruct((length, width), F32)
    part = jax.ShapeDtypeStruct((width, units), BF)
    return pl.pallas_call(
        body,
        grid=(units // block,),
        in_specs=specs,
        out_specs=[cut, cut, whole, whole],
        out_shape=[part, part, total, total],
        scratch_shapes=[pltpu.VMEM((width, length), BF)] * 2,
        compiler_params=params(),
        cost_estimate=pl.CostEstimate(
            flops=12 * length * width * units,
            bytes_accessed=8 * width * units + 8 * length * width,
            transcendentals=length * units,
        ),
    )(*operands)


def norm_parts(values):
    center = values - jnp.mean(values, -1, keepdims=True)
    inverse = lax.rsqrt(jnp.mean(center * center, -1, keepdims=True) + EPS)
    return center * inverse, inverse


def layer_norm(values, gain, offset):
    return (norm_parts(values)[0] * gain + offset).astype(BF)


def norm_back(values, gain, grad):
    hat, inverse = norm_parts(values)
    scaled = grad * gain
    back = inverse * (
        scaled
        - jnp.mean(scaled, -1, keepdims=True)
        - hat * jnp.mean(scaled * hat, -1, keepdims=True)
    )
    lead = tuple(range(values.ndim - 1))
    return back, jnp.sum(grad * hat, lead), jnp.sum(grad, lead)


def layer(shape, args):
    chips, tops, lows = shape["chip"], shape["hi"], shape["lo"]
    (
        image_rows,
        text_rows,
        segment_ids,
        cotangent,
        query_weight,
        key_weight,
        value_weight,
        attn_output,
        cross_query,
        cross_key,
        cross_value,
        cross_output,
        hidden_in,
        hidden_out,
        *norms,
    ) = args
    images, rows, width = image_rows.shape
    texts = text_rows.shape[1]
    half_rows = rows // 2
    length = rows * lows * tops
    shard = query_weight.shape[0]
    chip, core = lax.axis_index("chip"), lax.axis_index("core")
    top = lax.axis_index("hi")
    own_slot = core * images + top % images

    def swap(value):
        return lax.ppermute(value, "core", [(0, 1), (1, 0)])

    def across(value, bit):
        return lax.ppermute(value, "chip", [(i, i ^ bit) for i in range(chips)])

    def shift(value, step):
        return lax.ppermute(value, "hi", [((i + step) % tops, i) for i in range(tops)])

    def matching(number, back):
        pairs = []
        for source_core in range(2):
            for source_top in range(tops):
                slot = source_top ^ number
                target = (slot // images) * tops + source_core * images + slot % images
                source = source_core * tops + source_top
                pairs.append((target, source) if back else (source, target))
        return pairs

    def to_image(piece_of):
        got = [
            lax.ppermute(piece_of(top ^ number), ("core", "hi"), matching(number, False))
            for number in range(tops)
        ]
        whole = jnp.stack(got)
        return jnp.stack(
            [lax.dynamic_index_in_dim(whole, own_slot ^ place, 0, False) for place in range(tops)]
        )

    def from_image(pieces):
        return [
            lax.ppermute(
                lax.dynamic_index_in_dim(pieces, own_slot ^ number, 0, False),
                ("core", "hi"),
                matching(number, True),
            )
            for number in range(tops)
        ]

    def image_piece(value):
        def piece(slot):
            return lax.dynamic_slice(
                value,
                (slot % images, (slot // images) * half_rows, 0),
                (1, half_rows, width),
            )[0]

        return piece

    def to_rows(pieces):
        got = jnp.stack(from_image(pieces))
        ordered = jnp.stack(
            [lax.dynamic_index_in_dim(got, top ^ slot, 0, False) for slot in range(tops)]
        )
        ordered = ordered.reshape(2, images, half_rows, width)
        return jnp.swapaxes(ordered, 0, 1).reshape(images, rows, width)

    def tp_gather(mine):
        if lows == 1:
            other = swap(mine)
            first = jnp.where(core == 0, mine, other)
            second = jnp.where(core == 0, other, mine)
            return jnp.stack([first, second], 1).reshape(length, width)
        every = lax.all_gather(mine, ("lo", "core"))
        every = every.reshape(lows * 2, tops, half_rows, width)
        return jnp.swapaxes(every, 0, 1).reshape(length, width)

    def tp_reduce(partial):
        if lows == 1:
            cut = partial.reshape(tops, 2, half_rows, width)
            sent = lax.dynamic_index_in_dim(cut, 1 - core, 1, False).astype(BF)
            kept = lax.dynamic_index_in_dim(cut, core, 1, False)
            return kept + swap(sent).astype(F32)
        cut = jnp.swapaxes(partial.astype(BF).reshape(tops, lows * 2, half_rows, width), 0, 1)
        cut = lax.psum_scatter(cut, ("lo", "core"), scatter_dimension=0, tiled=False)
        return cut.astype(F32)

    def core_half(weight, which):
        columns = weight.shape[1] // 2
        return lax.dynamic_slice_in_dim(weight, which * columns, columns, 1)

    def pack(which):
        feeds = [core_half(weight, which) for weight in (hidden_in, hidden_out)]
        cuts = feeds[0].shape[1] // 2
        groups = [
            [core_half(w, which) for w in (query_weight, key_weight, value_weight, attn_output)],
            [core_half(w, which) for w in (cross_query, cross_key, cross_value, cross_output)],
            [w[:, :cuts] for w in feeds],
            [w[:, cuts:] for w in feeds],
        ]
        return jnp.concatenate([w for group in groups for w in group], 1)

    kept = pack(core)
    taken = swap(pack(1 - core))
    own = jnp.concatenate(
        [jnp.where(core == 0, kept, taken), jnp.where(core == 0, taken, kept)], 0
    )
    block_rows = 2 * shard
    group_width = own.shape[1] // 4

    def plane_gather(piece):
        if chips != 4:
            return lax.all_gather(piece, "chip", axis=0, tiled=True)
        side = across(piece, 1)
        over = across(piece, 2)
        corner_low = across(side[:shard], 2)
        corner_high = across(over[shard:], 1)
        corner = jnp.concatenate([corner_low, corner_high], 0)
        pieces = jnp.stack([piece, side, over, corner])
        ordered = [lax.dynamic_index_in_dim(pieces, chip ^ place, 0, False) for place in range(4)]
        return jnp.concatenate(ordered, 0)

    def plane_scatter(grads):
        if chips != 4:
            return lax.psum_scatter(grads, "chip", scatter_dimension=0, tiled=True).astype(F32)

        def rows_of(place, low, count):
            return lax.dynamic_slice_in_dim(grads, (chip ^ place) * block_rows + low, count, 0)

        by_side = across(rows_of(3, 0, shard), 1)
        by_over = across(rows_of(3, shard, shard), 2)
        to_over = jnp.concatenate(
            [rows_of(2, 0, shard).astype(F32) + by_side.astype(F32), rows_of(2, shard, shard).astype(F32)], 0
        ).astype(BF)
        to_side = jnp.concatenate(
            [rows_of(1, 0, shard).astype(F32), rows_of(1, shard, shard).astype(F32) + by_over.astype(F32)], 0
        ).astype(BF)
        over, side = across(to_over, 2), across(to_side, 1)
        return rows_of(0, 0, block_rows).astype(F32) + over.astype(F32) + side.astype(F32)

    def top_scatter(pieces):
        total = pieces[0].astype(F32)
        for step in range(1, tops):
            total = total + shift(pieces[step].astype(BF), tops - step).astype(F32)
        return total

    def core_split(total):
        cut = total.reshape(2, shard, total.shape[1])
        mine = lax.dynamic_index_in_dim(cut, core, 0, False)
        other = swap(lax.dynamic_index_in_dim(cut, 1 - core, 0, False).astype(BF)).astype(F32)
        return jnp.where(core == 0, mine, other), jnp.where(core == 0, other, mine)

    own_wide = plane_gather(own)

    def fetch(group, count):
        part = own[:, group * group_width : (group + 1) * group_width]
        columns = group_width // count
        got = [shift(part, step).reshape(block_rows, count, 1, columns) for step in range(1, tops)]
        rest = jnp.concatenate(got, 2).reshape(block_rows, (tops - 1) * group_width)
        rest = plane_gather(rest).reshape(width, count, (tops - 1) * columns)
        near = own_wide[:, group * group_width : (group + 1) * group_width]
        near = near.reshape(width, count, columns)
        return [
            jnp.concatenate([near[:, one], rest[:, one]], 1) for one in range(count)
        ]

    def give(grads):
        count = len(grads)
        columns = grads[0].shape[1] // tops
        summed = plane_scatter(jnp.concatenate(grads, 1)).reshape(block_rows, count, tops, columns)
        pieces = [summed[:, :, step].reshape(block_rows, count * columns) for step in range(tops)]
        low, high = core_split(top_scatter(pieces))
        low, high = low.reshape(shard, count, columns), high.reshape(shard, count, columns)
        return [(low[:, one], high[:, one]) for one in range(count)]

    packed_norms = lax.all_gather(jnp.stack(norms), ("chip", "core"), axis=1, tiled=True)
    gain_one, bias_one, gain_two, bias_two, gain_three, bias_three = packed_norms

    w_query, w_key, w_value, w_out = fetch(0, 4)
    inputs = to_image(image_piece(image_rows)).astype(F32)
    c_query, c_key, c_value, c_out = fetch(1, 4)
    in_low, out_low = fetch(2, 2)
    in_high, out_high = fetch(3, 2)

    text = to_image(lambda slot: text_rows[slot % images])
    if lows > 1:
        text = lax.all_gather(text, "lo", axis=1)
    text = text.reshape(tops * lows * texts, width)
    other_ids = swap(segment_ids)
    ids = jnp.where(core == top // images, segment_ids, other_ids)
    ids = lax.dynamic_index_in_dim(ids, top % images, 0, False)
    captions = jnp.repeat(ids, length // ids.shape[0])[None, :]
    ids = ids[:, None]
    cot = to_image(image_piece(cotangent))

    full_one = tp_gather(layer_norm(inputs, gain_one, bias_one))
    packed = dot(full_one, jnp.concatenate([w_query, w_key, w_value], 1)).astype(BF)
    self_mix, self_lse = self_forward(packed)
    after_attn = inputs + tp_reduce(dot(self_mix, w_out, NT))
    full_two = tp_gather(layer_norm(after_attn, gain_two, bias_two))
    queries = dot(full_two, c_query).astype(BF)
    w_text = jnp.concatenate([c_key, c_value], 1)
    keys = dot(text, w_text).astype(BF)
    cross_mix, cross_lse = cross_forward(queries, keys, ids, captions)
    after_cross = after_attn + tp_reduce(dot(cross_mix, c_out, NT))
    full_three = tp_gather(layer_norm(after_cross, gain_three, bias_three))
    full_cot = tp_gather(cot)
    gin_low, gout_low, *sums = feed(full_three, full_cot, in_low, out_low, None)
    gin_high, gout_high, out_sum, back_sum = feed(full_three, full_cot, in_high, out_high, sums)
    low_grads = give([gin_low, gout_low])
    high_grads = give([gin_high, gout_high])
    result = to_rows((after_cross + tp_reduce(out_sum)).astype(BF))

    back_three, dgain_three, dbias_three = norm_back(after_cross, gain_three, tp_reduce(back_sum))
    grad_cross = cot.astype(F32) + back_three
    full_grad = tp_gather(grad_cross.astype(BF))
    mix_grad = dot(full_grad, c_out).astype(BF)
    dq, dk, dv = cross_backward(queries, keys, cross_mix, mix_grad, cross_lse, ids, captions)
    back_sum = dot(dq, c_query, NT)
    dkv = jnp.concatenate([dk, dv], 1)
    cross_grads = give(
        [
            dot(full_two, dq, TN).astype(BF),
            dot(text, dk, TN).astype(BF),
            dot(text, dv, TN).astype(BF),
            dot(full_grad, cross_mix, TN).astype(BF),
        ]
    )
    text_part = dot(dkv, w_text, NT).astype(BF).reshape(tops, lows, texts, width)
    if lows > 1:
        text_part = lax.psum_scatter(text_part, "lo", scatter_dimension=1, tiled=True)
    got = [part.astype(F32) for part in from_image(text_part[:, 0])]
    got = jnp.stack(got)
    got = [lax.dynamic_index_in_dim(got, top ^ slot, 0, False) for slot in range(tops)]
    text_grad = jnp.stack([got[i] + got[images + i] for i in range(images)])

    back_two, dgain_two, dbias_two = norm_back(after_attn, gain_two, tp_reduce(back_sum))
    grad_attn = grad_cross + back_two
    full_grad = tp_gather(grad_attn.astype(BF))
    mix_grad = dot(full_grad, w_out).astype(BF)
    dq, dk, dv = self_backward(packed, self_mix, mix_grad, self_lse)
    dqkv = jnp.concatenate([dq, dk, dv], 1)
    dwqkv = dot(full_one, dqkv, TN).astype(BF)
    span = dq.shape[1]
    self_grads = give(
        [
            dwqkv[:, :span],
            dwqkv[:, span : 2 * span],
            dwqkv[:, 2 * span :],
            dot(full_grad, self_mix, TN).astype(BF),
        ]
    )
    back_sum = dot(dqkv, jnp.concatenate([w_query, w_key, w_value], 1), NT)
    back_one, dgain_one, dbias_one = norm_back(inputs, gain_one, tp_reduce(back_sum))
    input_grad = to_rows((grad_attn + back_one).astype(BF)).astype(F32)

    norm_sums = lax.psum(
        jnp.stack([dgain_one, dbias_one, dgain_two, dbias_two, dgain_three, dbias_three]),
        ("chip", "core", "hi", "lo"),
    )
    norm_sums = lax.dynamic_slice_in_dim(norm_sums, (chip * 2 + core) * shard, shard, 1)

    feeds = [
        jnp.concatenate([low_grads[i][0], high_grads[i][0], low_grads[i][1], high_grads[i][1]], 1)
        for i in range(2)
    ]
    joined = [jnp.concatenate(pair, 1) for pair in (*self_grads, *cross_grads)]
    return (result, input_grad, text_grad, *joined, *feeds, *[norm_sums[i] for i in range(6)])


BLOCK = 256
ANY = pl.BlockSpec(memory_space=pltpu.HBM)
SMEM = pl.BlockSpec(memory_space=pltpu.SMEM)
VMEM = pl.BlockSpec(memory_space=pltpu.VMEM)
MIB = 1024 * 1024


def like(*shape, dtype=BF):
    return jax.ShapeDtypeStruct(shape, dtype)


def call(body, outs, ins, operands, scratch=(), limit=60, grid=None, flops=0, moved=0):
    single = not isinstance(outs, (list, tuple))
    extra = {} if grid is None else {"grid": grid}
    cost = pl.CostEstimate(flops=1, bytes_accessed=1, transcendentals=0)
    out_specs, out_shape = ([outs[0]], [outs[1]]) if single else ([o[0] for o in outs], [o[1] for o in outs])
    return list(pl.pallas_call(
        body,
        in_specs=ins,
        out_specs=out_specs,
        out_shape=out_shape,
        scratch_shapes=list(scratch),
        compiler_params=pltpu.CompilerParams(vmem_limit_bytes=limit * MIB),
        cost_estimate=cost,
        **extra,
    )(*operands))


def run_copies(copies, sems):
    started = [pltpu.make_async_copy(source, target, sems.at[i]) for i, (source, target) in enumerate(copies)]
    for copy in started:
        copy.start()
    for copy in started:
        copy.wait()


def at(offset, count, unit=128):
    return pl.ds(pl.multiple_of(offset, unit), count)


def prepare_kernel(place, image, text, ids, cot, norms, wq, wk, wv, wo, cq, ck, cv, co, win, wout, *outs):
    keep, sent, rows_keep, rows_sent, cot_keep, cot_sent, sems = outs
    core = place[1]
    copies = []
    for target, which in ((sent, 1 - core), (keep, core)):
        for group, weights in enumerate(((wq, wk, wv, wo), (cq, ck, cv, co))):
            for one, weight in enumerate(weights):
                copies.append(
                    (
                        weight.at[:, at(which * 128, 128)],
                        target.at[group * 128 : (group + 1) * 128, one * 128 : (one + 1) * 128],
                    )
                )
        for part in range(2):
            for one, weight in enumerate((win, wout)):
                copies.append(
                    (
                        weight.at[:, at(which * 512 + part * 256, 256)],
                        target.at[256 + part * 128 : 384 + part * 128, one * 256 : (one + 1) * 256],
                    )
                )
        copies.append((norms, target.at[512:528, :]))
    for target, cots, which in ((rows_sent, cot_sent, 1 - core), (rows_keep, cot_keep, core)):
        for one in range(2):
            copies.append((image.at[one, at(which * 128, 128), :], target.at[one]))
            copies.append((cot.at[one, at(which * 128, 128), :], cots.at[one, 0:128, :]))
            copies.append((text.at[one], cots.at[one, 128:160, :]))
            copies.append((ids.at[one], cots.at[one, 160:176, :]))
    run_copies(copies, sems)


def prepare(place, image, text, ids, cot, norms, weights):
    return call(
        prepare_kernel,
        [(VMEM, like(528, 512))] * 2 + [(VMEM, like(2, 128, 1024))] * 2 + [(VMEM, like(2, 176, 1024))] * 2,
        [SMEM] + [ANY] * 15,
        (place, image, text, ids, cot, norms, *weights),
        [pltpu.SemaphoreType.DMA((42,))],
    )


def pick_kernel(place, keep, taken, *outs):
    core, top = place[1], place[2]
    for step, out in enumerate(outs):
        image = (top + 4 - step) % 4

        @pl.when(image // 2 == core)
        def _():
            out[...] = keep[image % 2]

        @pl.when(image // 2 != core)
        def _():
            out[...] = taken[image % 2]


def pick(place, keep, taken):
    return call(
        pick_kernel,
        [(VMEM, like(*keep.shape[1:]))] * 4,
        [SMEM, VMEM, VMEM],
        (place, keep, taken),
    )


def join_kernel(*refs):
    keep, taken, singles, doubles, sems = refs[0], refs[1], refs[2:6], refs[6:8], refs[8]
    copies = []
    for group in range(4):
        for half, source in enumerate((keep, taken)):
            part = source.at[group * 128 : (group + 1) * 128, :]
            copies.append((part, singles[group].at[half * 128 : (half + 1) * 128, :]))
            low = (group % 2) * 256 + half * 128
            copies.append((part, doubles[group // 2].at[low : low + 128, :]))
    for half, source in enumerate((keep, taken)):
        low = 512 + half * 16
        copies.append((source.at[512:528, :], doubles[0].at[low : low + 16, :]))
    run_copies(copies, sems)


def join(keep, taken):
    return call(
        join_kernel,
        [(VMEM, like(256, 512))] * 4 + [(VMEM, like(544, 512)), (VMEM, like(512, 512))],
        [ANY] * 2,
        (keep, taken),
        [pltpu.SemaphoreType.DMA((18,))],
        limit=60,
    )


def stack_kernel(*refs):
    *parts, whole, sems = refs
    copies, low = [], 0
    for part in parts:
        copies.append((part, whole.at[low : low + part.shape[0]]))
        low += part.shape[0]
    run_copies(copies, sems)


def stack(parts):
    rows = sum(part.shape[0] for part in parts)
    return call(
        stack_kernel,
        [(VMEM, like(rows, *parts[0].shape[1:]))],
        [ANY] * len(parts),
        parts,
        [pltpu.SemaphoreType.DMA((len(parts),))],
        limit=60,
    )[0]


def arrange_kernel(place, *refs):
    messages, rows, text, sems = refs[:4], refs[4], refs[5], refs[6]
    copies = []
    for number, message in enumerate(messages):
        copies.append((message.at[0:128, :], rows.at[number]))
        copies.append((message.at[128:160, :], text.at[at((place[2] + number) % 4 * 32, 32, 32), :]))
    run_copies(copies, sems)


def arrange(place, messages):
    return call(
        arrange_kernel,
        [(VMEM, like(4, 128, 1024)), (VMEM, like(128, 1024))],
        [SMEM] + [ANY] * 4,
        (place, *messages),
        [pltpu.SemaphoreType.DMA((8,))],
    )


def turn_kernel(place, whole, rest, sems):
    run_copies(
        [(whole.at[(place[2] + step) % 4], rest.at[(step - 1) * 256 : step * 256, :]) for step in range(1, 4)], sems
    )


def turn(place, whole):
    return call(
        turn_kernel,
        [(VMEM, like(768, 512))],
        [SMEM, ANY],
        (place, whole),
        [pltpu.SemaphoreType.DMA((3,))],
    )[0]


def assemble_kernel(place, *refs, low, far_parts, norms):
    own, side, over, corner, rest, rside, rover = refs[:7]
    rcorner = refs[7 : 7 + far_parts]
    outs = refs[7 + far_parts :]
    whole, buffer, loads, stores = outs[0], outs[-3], outs[-2], outs[-1]
    chip, core = place[0], place[1]
    batches = []
    for source in range(4):
        copies = []
        for half in range(2):
            row = at((chip ^ source) * 256 + (core ^ half) * 128, 128)
            near = (own, side, over, corner)[source]
            first = half * 128 + (0 if source == 3 else low)
            copies.append((near.at[first : first + 128, :], buffer.at[row, 0:512]))
            for step in range(3):
                first = step * 256 + half * 128
                far = (rest, rside, rover, rcorner[first * far_parts // 768])[source]
                if source == 3:
                    first %= 768 // far_parts
                columns = slice((step + 1) * 512, (step + 2) * 512)
                copies.append((far.at[first : first + 128, :], buffer.at[row, columns]))
        batches.append([pltpu.make_async_copy(a, b, loads.at[source * 8 + i]) for i, (a, b) in enumerate(copies)])
    for batch in batches:
        for copy in batch:
            copy.start()
    stored = []
    if norms:
        pairs = []
        for source, piece in enumerate((own, side, over, outs[1])):
            for half in range(2):
                column = (chip ^ source) * 256 + (core ^ half) * 128
                first = (256 if source == 3 else 512) + half * 16
                pairs.append((piece.at[first : first + 16, 0:128], outs[2].at[:, at(column, 128)]))
        for i, (a, b) in enumerate(pairs):
            stored.append(pltpu.make_async_copy(a, b, stores.at[4 + i]))
            stored[-1].start()
    for source, batch in enumerate(batches):
        for copy in batch:
            copy.wait()
        rows = at((chip ^ source) * 256, 256)
        stored.append(pltpu.make_async_copy(buffer.at[rows, :], whole.at[rows, :], stores.at[source]))
        stored[-1].start()
    for copy in stored:
        copy.wait()


def assemble(place, near, far, low, norms=None):
    outs = [(ANY, like(1024, 2048))]
    operands = (place, *near, *far)
    if norms is not None:
        outs.append((VMEM, like(16, 1024)))
        operands += (norms,)

    def body(*refs):
        count = len(operands)
        if norms is None:
            assemble_kernel(*refs, low=low, far_parts=len(far) - 3, norms=False)
        else:
            assemble_kernel(
                *refs[: count - 1], refs[count], refs[count - 1], *refs[count + 1 :],
                low=low, far_parts=len(far) - 3, norms=True,
            )

    return call(
        body,
        outs,
        [SMEM] + [ANY] * (len(operands) - 1),
        operands,
        [pltpu.VMEM((1024, 2048), BF), pltpu.SemaphoreType.DMA((32,)), pltpu.SemaphoreType.DMA((12,))],
    )


def norm_row(norms, one):
    return norms[one : one + 1, :].astype(F32)


def normalized(values, gain, bias):
    center = values - jnp.mean(values, -1, keepdims=True)
    inverse = lax.rsqrt(jnp.mean(center * center, -1, keepdims=True) + EPS)
    return (center * inverse * gain + bias).astype(BF)


def columns_of(weights, one, count=128):
    return jnp.concatenate([weights[:, s * 512 + one * count : s * 512 + (one + 1) * count] for s in range(4)], 1)


def image_blocks(place, own, other):
    core, top = place[1], place[2]
    for number in range(4):
        yield (top + number) % 4 * 256 + core * 128, own, number
        yield (top + number) % 4 * 256 + (1 - core) * 128, other, number


def one_head(values, head):
    return jnp.where(lane_head((1, 2 * HD), 1, head), values, jnp.zeros_like(values))


def softmax_mix(scores, values):
    scale = LOG2E * HD**-0.5
    peak = jnp.max(scores[0], 0, keepdims=True)
    for part in scores[1:]:
        peak = jnp.maximum(peak, jnp.max(part, 0, keepdims=True))
    total, mixed = 0.0, 0.0
    for part, rows in zip(scores, values):
        weights = jnp.exp2((part - peak) * scale)
        total = total + jnp.sum(weights, 0, keepdims=True)
        mixed = mixed + dot(rows, weights.astype(BF), TN)
    return mixed / total, peak * scale + jnp.log2(total)


def causal_mask():
    return lax.broadcasted_iota(jnp.int32, (BLOCK, BLOCK), 0) <= lax.broadcasted_iota(
        jnp.int32, (BLOCK, BLOCK), 1
    )


def self_fwd_kernel(place, own, other, norms, weights, normed, qkv, mix, lse, part):
    gain, bias = norm_row(norms, 0), norm_row(norms, 1)
    for row, half, number in image_blocks(place, own, other):
        normed[at(row, 128), :] = normalized(half[number].astype(F32), gain, bias)
    w_in = jnp.concatenate([columns_of(weights, one) for one in range(3)], 1)
    for low in range(0, 1024, BLOCK):
        qkv[low : low + BLOCK, :] = dot(normed[low : low + BLOCK, :], w_in).astype(BF)
    causal = causal_mask()

    def pair_step(pair, carry):
        lanes = at(pair * 128, 128)
        k_lanes, v_lanes = at(512 + pair * 128, 128), at(1024 + pair * 128, 128)
        for low in range(0, 1024, BLOCK):
            high = low + BLOCK
            query = qkv[low:high, lanes]
            mixes = []
            for head in range(2):
                one = one_head(query, head)
                scores = [jnp.where(causal, dot(qkv[low:high, k_lanes], one, NT), NEG)]
                values = [qkv[low:high, v_lanes]]
                if low:
                    scores.append(dot(qkv[:low, k_lanes], one, NT))
                    values.append(qkv[:low, v_lanes])
                mixed, logsum = softmax_mix(scores, values)
                mixes.append(mixed)
                lse[pair, head : head + 1, low:high] = logsum
            both = jnp.where(lane_head((128, 1), 0, 0), mixes[0], mixes[1])
            mix[low:high, lanes] = both.T.astype(BF)
        return carry

    lax.fori_loop(0, 4, pair_step, 0)
    w_out = columns_of(weights, 3)
    for low in range(0, 1024, BLOCK):
        part[low : low + BLOCK, :] = dot(mix[low : low + BLOCK, :], w_out, NT).astype(BF)


def fused_self_forward(place, own, other, norms, weights):
    return call(
        self_fwd_kernel,
        [
            (VMEM, like(1024, 1024)),
            (VMEM, like(1024, 1536)),
            (VMEM, like(1024, 512)),
            (VMEM, like(4, 2, 1024, dtype=F32)),
            (VMEM, like(1024, 1024)),
        ],
        [SMEM] + [VMEM] * 4,
        (place, own, other, norms, weights),
        limit=60,
        flops=10 * 2**30,
        moved=14 * MIB,
    )


def cross_fwd_kernel(
    place, own, other, mine, theirs, norms, text, ids, caption, weights, after, normed, queries, keys, mix, lse, part
):
    gain, bias = norm_row(norms, 2), norm_row(norms, 3)
    for row, half, number in image_blocks(place, own, other):
        rows = at(row, 128)
        values = half[number].astype(F32) + (mine[rows, :].astype(F32) + theirs[rows, :].astype(F32))
        after[rows, :] = values
        normed[rows, :] = normalized(values, gain, bias)
    w_query = columns_of(weights, 0)
    for low in range(0, 1024, BLOCK):
        queries[low : low + BLOCK, :] = dot(normed[low : low + BLOCK, :], w_query).astype(BF)
    w_text = jnp.concatenate([columns_of(weights, 1), columns_of(weights, 2)], 1)
    keys[...] = dot(text[...], w_text).astype(BF)

    def pair_step(pair, carry):
        lanes, v_lanes = at(pair * 128, 128), at(512 + pair * 128, 128)
        for low in range(0, 1024, 512):
            high = low + 512
            query = queries[low:high, lanes]
            seen = ids[...] == caption[:, low:high]
            mixes = []
            for head in range(2):
                scores = jnp.where(seen, dot(keys[:, lanes], one_head(query, head), NT), NEG)
                mixed, logsum = softmax_mix([scores], [keys[:, v_lanes]])
                mixes.append(mixed)
                lse[pair, head : head + 1, low:high] = logsum
            both = jnp.where(lane_head((128, 1), 0, 0), mixes[0], mixes[1])
            mix[low:high, lanes] = both.T.astype(BF)
        return carry

    lax.fori_loop(0, 4, pair_step, 0)
    w_out = columns_of(weights, 3)
    for low in range(0, 1024, BLOCK):
        part[low : low + BLOCK, :] = dot(mix[low : low + BLOCK, :], w_out, NT).astype(BF)


def fused_cross_forward(place, own, other, mine, theirs, norms, text, ids, caption, weights):
    return call(
        cross_fwd_kernel,
        [
            (VMEM, like(1024, 1024, dtype=F32)),
            (VMEM, like(1024, 1024)),
            (VMEM, like(1024, 512)),
            (VMEM, like(128, 1024)),
            (VMEM, like(1024, 512)),
            (VMEM, like(4, 2, 1024, dtype=F32)),
            (VMEM, like(1024, 1024)),
        ],
        [SMEM] + [VMEM] * 9,
        (place, own, other, mine, theirs, norms, text, ids, caption, weights),
        limit=60,
        flops=5 * 2**30,
        moved=20 * MIB,
    )


def cut_grads(place, grads, columns, own, side, over, low, high):
    chip = place[0]
    own[:, columns] = grads[at(chip * 256, 256), :].astype(BF)
    side[:, columns] = grads[at((chip ^ 1) * 256, 256), :].astype(BF)
    over[:, columns] = grads[at((chip ^ 2) * 256, 256), :].astype(BF)
    low[:, columns] = grads[at((chip ^ 3) * 256, 128), :].astype(BF)
    high[:, columns] = grads[at((chip ^ 3) * 256 + 128, 128), :].astype(BF)


GRAD_SHAPES = [(256, 2048)] * 3 + [(128, 2048)] * 2


def feed_step(rows, cot, rows_t, cot_t, weights, out_sum, back_sum, grads):
    w_in, w_out = weights[:, :256], weights[:, 256:]
    slope = math.sqrt(2.0 / math.pi)
    acts, pre_grads = [], []
    for low in range(0, 1024, BLOCK):
        part = slice(low, low + BLOCK)
        pre = dot(rows[part, :], w_in)
        square = pre * pre
        bent = jnp.tanh(pre * (slope + slope * 0.044715 * square))
        half = 0.5 * (1.0 + bent)
        act = (pre * half).astype(BF)
        bend = half + pre * (0.5 * (1.0 - bent * bent)) * (slope + 3.0 * slope * 0.044715 * square)
        pre_grad = (dot(cot[part, :], w_out) * bend).astype(BF)
        out_sum[part, :] += dot(act, w_out, NT)
        back_sum[part, :] += dot(pre_grad, w_in, NT)
        acts.append(act)
        pre_grads.append(pre_grad)
    grads[:, :256] = dot(rows_t[...], jnp.concatenate(pre_grads, 0))
    grads[:, 256:] = dot(cot_t[...], jnp.concatenate(acts, 0))


def feed_first_kernel(
    place, after, mine, theirs, norms, cot_own, cot_other, weights,
    g_own, g_side, g_over, g_low, g_high, after_cross, normed, cot, out_sum, back_sum, rows_t, cot_t, grads,
):
    @pl.when(pl.program_id(0) == 0)
    def _():
        gain, bias = norm_row(norms, 4), norm_row(norms, 5)
        for low in range(0, 1024, 128):
            rows = slice(low, low + 128)
            values = after[rows, :] + (mine[rows, :].astype(F32) + theirs[rows, :].astype(F32))
            after_cross[rows, :] = values
            normed[rows, :] = normalized(values, gain, bias)
        for row, half, number in image_blocks(place, cot_own, cot_other):
            cot[at(row, 128), :] = half[number]
        rows_t[...] = normed[...].T
        cot_t[...] = cot[...].T
        out_sum[...] = jnp.zeros_like(out_sum)
        back_sum[...] = jnp.zeros_like(back_sum)

    feed_step(normed, cot, rows_t, cot_t, weights, out_sum, back_sum, grads)
    cut_grads(place, grads, slice(None), g_own, g_side, g_over, g_low, g_high)


def feed_second_kernel(
    place, normed, cot, out_in, back_in, weights,
    g_own, g_side, g_over, g_low, g_high, out_keep, out_sent, back, out_sum, back_sum, rows_t, cot_t, grads,
):
    step, core = pl.program_id(0), place[1]

    @pl.when(step == 0)
    def _():
        rows_t[...] = normed[...].T
        cot_t[...] = cot[...].T
        out_sum[...] = out_in[...]
        back_sum[...] = back_in[...]

    feed_step(normed, cot, rows_t, cot_t, weights, out_sum, back_sum, grads)
    cut_grads(place, grads, slice(None), g_own, g_side, g_over, g_low, g_high)

    @pl.when(step == 3)
    def _():
        back[...] = back_sum[...].astype(BF)
        for block in range(4):
            out_keep[block] = out_sum[at(block * 256 + core * 128, 128), :]
            out_sent[block] = out_sum[at(block * 256 + (1 - core) * 128, 128), :].astype(BF)


def once(*shape):
    zeros = (0,) * len(shape)
    return pl.BlockSpec(shape, lambda i: zeros, pipeline_mode=pl.Buffered(1))


def grad_outs():
    return [(pl.BlockSpec((rows, 512), lambda i: (0, i)), like(rows, n)) for rows, n in GRAD_SHAPES]


FEED_FLOPS = 13 * 2**30


def feed_first(place, after, mine, theirs, norms, cot_own, cot_other, weights):
    square = once(1024, 1024)
    return call(
        feed_first_kernel,
        grad_outs()
        + [
            (square, like(1024, 1024, dtype=F32)),
            (square, like(1024, 1024)),
            (square, like(1024, 1024)),
            (square, like(1024, 1024, dtype=F32)),
            (square, like(1024, 1024, dtype=F32)),
        ],
        [SMEM, square, square, square, once(16, 1024), once(4, 128, 1024), once(4, 128, 1024)]
        + [pl.BlockSpec((1024, 512), lambda i: (0, i))],
        (place, after, mine, theirs, norms, cot_own, cot_other, weights),
        [pltpu.VMEM((1024, 1024), BF)] * 2 + [pltpu.VMEM((1024, 512), F32)],
        limit=60,
        grid=(4,),
        flops=FEED_FLOPS,
        moved=30 * MIB,
    )


def feed_second(place, normed, cot, out_in, back_in, weights):
    square = once(1024, 1024)
    return call(
        feed_second_kernel,
        grad_outs()
        + [
            (once(4, 128, 1024), like(4, 128, 1024, dtype=F32)),
            (once(4, 128, 1024), like(4, 128, 1024)),
            (square, like(1024, 1024)),
        ],
        [SMEM, square, square, square, square, pl.BlockSpec((1024, 512), lambda i: (0, i))],
        (place, normed, cot, out_in, back_in, weights),
        [pltpu.VMEM((1024, 1024), F32)] * 2
        + [pltpu.VMEM((1024, 1024), BF)] * 2
        + [pltpu.VMEM((1024, 512), F32)],
        limit=60,
        grid=(4,),
        flops=FEED_FLOPS,
        moved=26 * MIB,
    )


def norm_backward(values, gain, grad):
    center = values - jnp.mean(values, -1, keepdims=True)
    inverse = lax.rsqrt(jnp.mean(center * center, -1, keepdims=True) + EPS)
    hat = center * inverse
    scaled = grad * gain
    back = inverse * (
        scaled - jnp.mean(scaled, -1, keepdims=True) - hat * jnp.mean(scaled * hat, -1, keepdims=True)
    )
    return back, grad * hat


def norm_block(values_of, mine, theirs, base_of, gain, norms, keep):
    gain = norm_row(*gain)
    gain_sum, bias_sum = jnp.zeros((8, 1024), F32), jnp.zeros((8, 1024), F32)
    for low in range(0, 1024, 128):
        rows = slice(low, low + 128)
        grad = mine[rows, :].astype(F32) + theirs[rows, :].astype(F32)
        back, term = norm_backward(values_of(rows), gain, grad)
        keep(rows, base_of(rows) + back)
        gain_sum = gain_sum + jnp.sum(term.reshape(16, 8, 1024), 0)
        bias_sum = bias_sum + jnp.sum(grad.reshape(16, 8, 1024), 0)
    norms[0:1, :] = jnp.sum(gain_sum, 0, keepdims=True)
    norms[1:2, :] = jnp.sum(bias_sum, 0, keepdims=True)


def head_grads(keys, values, one, one_grad, lse, delta, mask):
    weights = jnp.exp2(dot(keys, one, NT) * (LOG2E * HD**-0.5) - lse)
    if mask is not None:
        weights = jnp.where(mask, weights, 0.0)
    slope = dot(values, one_grad, NT)
    return weights.astype(BF), (weights * (slope - delta)).astype(BF)


def cross_bwd_kernel(
    place, after, mine, theirs, cot, gain, weights, normed, text, queries, keys, mix, lse, ids, caption,
    grad_cross, part, norms, text_part, g_own, g_side, g_over, g_low, g_high, low_grad, mix_grad, dq, dkv, grads,
):
    def keep(rows, value):
        grad_cross[rows, :] = value
        low_grad[rows, :] = value.astype(BF)

    norm_block(lambda rows: after[rows, :], mine, theirs, lambda rows: cot[rows, :].astype(F32), (gain, 4), norms, keep)
    w_out = columns_of(weights, 3)
    for low in range(0, 1024, BLOCK):
        mix_grad[low : low + BLOCK, :] = dot(low_grad[low : low + BLOCK, :], w_out).astype(BF)

    def pair_step(pair, carry):
        lanes, v_lanes = at(pair * 128, 128), at(512 + pair * 128, 128)
        dk_sum, dv_sum = jnp.zeros((128, 128), F32), jnp.zeros((128, 128), F32)
        for low in range(0, 1024, 512):
            high = low + 512
            query, grad = queries[low:high, lanes], mix_grad[low:high, lanes]
            product = (grad.astype(F32) * mix[low:high, lanes].astype(F32)).T
            seen = ids[...] == caption[:, low:high]
            back = []
            for head in range(2):
                one, one_grad = one_head(query, head), one_head(grad, head)
                delta = jnp.sum(product[head * HD : (head + 1) * HD], 0, keepdims=True)
                prob, score_grad = head_grads(
                    keys[:, lanes], keys[:, v_lanes], one, one_grad, lse[pair, head : head + 1, low:high], delta, seen
                )
                dv_sum = dv_sum + dot(prob, one_grad)
                dk_sum = dk_sum + dot(score_grad, one)
                back.append(dot(keys[:, lanes], score_grad, TN))
            both = jnp.where(lane_head((128, 1), 0, 0), back[0], back[1])
            dq[low:high, lanes] = (both.T * HD**-0.5).astype(BF)
        dkv[:, lanes] = (dk_sum * HD**-0.5).astype(BF)
        dkv[:, v_lanes] = dv_sum.astype(BF)
        return carry

    lax.fori_loop(0, 4, pair_step, 0)
    w_query = columns_of(weights, 0)
    for low in range(0, 1024, BLOCK):
        part[low : low + BLOCK, :] = dot(dq[low : low + BLOCK, :], w_query, NT).astype(BF)
    w_text = jnp.concatenate([columns_of(weights, 1), columns_of(weights, 2)], 1)
    text_part[...] = dot(dkv[...], w_text, NT).astype(BF)
    for one, (left, right) in enumerate(
        ((normed, dq[...]), (text, dkv[:, :512]), (text, dkv[:, 512:]), (low_grad, mix[...]))
    ):
        grads[...] = dot(left[...], right, TN)
        for s in range(4):
            columns = slice(s * 512 + one * 128, s * 512 + (one + 1) * 128)
            cut_grads(
                place, grads.at[:, s * 128 : (s + 1) * 128], columns, g_own, g_side, g_over, g_low, g_high
            )


def fused_cross_backward(place, after, mine, theirs, cot, gain, weights, normed, text, queries, keys, mix, lse, ids, caption):
    return call(
        cross_bwd_kernel,
        [
            (VMEM, like(1024, 1024, dtype=F32)),
            (VMEM, like(1024, 1024)),
            (VMEM, like(8, 1024, dtype=F32)),
            (VMEM, like(128, 1024)),
        ]
        + [(VMEM, like(*shape)) for shape in GRAD_SHAPES],
        [SMEM] + [VMEM] * 14,
        (place, after, mine, theirs, cot, gain, weights, normed, text, queries, keys, mix, lse, ids, caption),
        [
            pltpu.VMEM((1024, 1024), BF),
            pltpu.VMEM((1024, 512), BF),
            pltpu.VMEM((1024, 512), BF),
            pltpu.VMEM((128, 1024), BF),
            pltpu.VMEM((1024, 512), F32),
        ],
        limit=60,
        flops=9 * 2**30,
        moved=32 * MIB,
    )


def self_bwd_kernel(
    place, after, mine, theirs, base, gain, weights, qkv, mix, lse,
    grad_own, low_grad, norms, dqkv, mix_grad, dk_sum, dv_sum,
):
    core = place[1]

    def keep(rows, value):
        low_grad[rows, :] = value.astype(BF)

        @pl.when(core == (rows.start // 128) % 2)
        def _():
            grad_own[rows.start // 256] = value

    norm_block(lambda rows: after[rows, :], mine, theirs, lambda rows: base[rows, :], (gain, 2), norms, keep)
    w_out = columns_of(weights, 3)
    for low in range(0, 1024, BLOCK):
        mix_grad[low : low + BLOCK, :] = dot(low_grad[low : low + BLOCK, :], w_out).astype(BF)
    causal = causal_mask()

    def pair_step(pair, carry):
        lanes = at(pair * 128, 128)
        k_lanes, v_lanes = at(512 + pair * 128, 128), at(1024 + pair * 128, 128)
        dk_sum[...] = jnp.zeros_like(dk_sum)
        dv_sum[...] = jnp.zeros_like(dv_sum)
        for low in range(0, 1024, BLOCK):
            high = low + BLOCK
            query, grad = qkv[low:high, lanes], mix_grad[low:high, lanes]
            product = (grad.astype(F32) * mix[low:high, lanes].astype(F32)).T
            back = []
            for head in range(2):
                one, one_grad = one_head(query, head), one_head(grad, head)
                delta = jnp.sum(product[head * HD : (head + 1) * HD], 0, keepdims=True)
                total = jnp.zeros((128, BLOCK), F32)
                for start, stop in ((0, low), (low, high)):
                    if start == stop:
                        continue
                    prob, score_grad = head_grads(
                        qkv[start:stop, k_lanes],
                        qkv[start:stop, v_lanes],
                        one,
                        one_grad,
                        lse[pair, head : head + 1, low:high],
                        delta,
                        causal if start == low else None,
                    )
                    dv_sum[start:stop, :] += dot(prob, one_grad)
                    dk_sum[start:stop, :] += dot(score_grad, one)
                    total = total + dot(qkv[start:stop, k_lanes], score_grad, TN)
                back.append(total)
            both = jnp.where(lane_head((128, 1), 0, 0), back[0], back[1])
            dqkv[low:high, lanes] = (both.T * HD**-0.5).astype(BF)
        dqkv[:, k_lanes] = (dk_sum[...] * HD**-0.5).astype(BF)
        dqkv[:, v_lanes] = dv_sum[...].astype(BF)
        return carry

    lax.fori_loop(0, 4, pair_step, 0)


def fused_self_backward(place, after, mine, theirs, base, gain, weights, qkv, mix, lse):
    return call(
        self_bwd_kernel,
        [
            (VMEM, like(4, 128, 1024, dtype=F32)),
            (VMEM, like(1024, 1024)),
            (VMEM, like(8, 1024, dtype=F32)),
            (VMEM, like(1024, 1536)),
        ],
        [SMEM] + [VMEM] * 9,
        (place, after, mine, theirs, base, gain, weights, qkv, mix, lse),
        [pltpu.VMEM((1024, 512), BF), pltpu.VMEM((1024, 128), F32), pltpu.VMEM((1024, 128), F32)],
        limit=60,
        flops=9 * 2**30,
        moved=32 * MIB,
    )


def self_grads_kernel(place, normed, low_grad, dq, dk, dv, mix, g_own, g_side, g_over, g_low, g_high, rows_t, grad_t, grads):
    @pl.when(pl.program_id(0) == 0)
    def _():
        rows_t[...] = normed[...].T
        grad_t[...] = low_grad[...].T

    grads[:, :384] = dot(rows_t[...], jnp.concatenate([dq[...], dk[...], dv[...]], 1))
    grads[:, 384:] = dot(grad_t[...], mix[...])
    cut_grads(place, grads, slice(None), g_own, g_side, g_over, g_low, g_high)


def self_grads(place, normed, low_grad, dqkv, mix):
    square = once(1024, 1024)

    def cut(offset):
        return pl.BlockSpec((1024, 128), lambda i: (0, offset + i))

    return call(
        self_grads_kernel,
        grad_outs(),
        [SMEM, square, square, cut(0), cut(4), cut(8), cut(0)],
        (place, normed, low_grad, dqkv, dqkv, dqkv, mix),
        [pltpu.VMEM((1024, 1024), BF)] * 2 + [pltpu.VMEM((1024, 512), F32)],
        limit=60,
        grid=(4,),
        flops=4 * 2**30,
        moved=12 * MIB,
    )


def self_back_kernel(place, dqkv, weights, kept, sent):
    core = place[1]
    w_in = jnp.concatenate([columns_of(weights, one) for one in range(3)], 1)
    for block in range(4):
        for target, half in ((sent, 1 - core), (kept, core)):
            value = dot(dqkv[at(block * 256 + half * 128, 128), :], w_in, NT)
            target[block] = value.astype(target.dtype)


def self_back(place, dqkv, weights):
    return call(
        self_back_kernel,
        [(VMEM, like(4, 128, 1024, dtype=F32)), (VMEM, like(4, 128, 1024))],
        [SMEM, VMEM, VMEM],
        (place, dqkv, weights),
        limit=60,
        flops=3 * 2**30,
        moved=10 * MIB,
    )


def last_norm_kernel(place, rows, grad_own, mine, theirs, gain, text_part, *outs):
    pieces, norms = outs[:4], outs[4]
    gain_sum, bias_sum = jnp.zeros((8, 1024), F32), jnp.zeros((8, 1024), F32)
    for number in range(4):
        block = (place[2] + number) % 4
        grad = mine[block] + theirs[block].astype(F32)
        back, term = norm_backward(rows[number].astype(F32), norm_row(gain, 0), grad)
        pieces[-number % 4][0:128, :] = (grad_own[block] + back).astype(BF)
        pieces[-number % 4][128:160, :] = text_part[at(block * 32, 32, 32), :]
        gain_sum = gain_sum + jnp.sum(term.reshape(16, 8, 1024), 0)
        bias_sum = bias_sum + jnp.sum(grad.reshape(16, 8, 1024), 0)
    norms[0:1, :] = jnp.sum(gain_sum, 0, keepdims=True)
    norms[1:2, :] = jnp.sum(bias_sum, 0, keepdims=True)


def last_norm(place, rows, grad_own, mine, theirs, gain, text_part):
    return call(
        last_norm_kernel,
        [(VMEM, like(160, 1024))] * 4 + [(VMEM, like(8, 1024, dtype=F32))],
        [SMEM] + [VMEM] * 6,
        (place, rows, grad_own, mine, theirs, gain, text_part),
        limit=60,
        moved=8 * MIB,
    )


def finish_kernel(place, after, out_keep, theirs, *rest):
    messages, rows, sems = rest[:4], rest[4], rest[5]
    core, top = place[1], place[2]
    run_copies(
        [(after.at[at((top + 4 - n) % 4 * 256 + core * 128, 128), :], rows.at[n]) for n in range(4)], sems
    )
    for number in range(4):
        block = (top + 4 - number) % 4
        value = rows[number] + (out_keep[block] + theirs[block].astype(F32))
        messages[number][...] = value.astype(BF)


def finish(place, after, out_keep, theirs):
    return call(
        finish_kernel,
        [(VMEM, like(128, 1024))] * 4,
        [SMEM, ANY] + [VMEM] * 2,
        (place, after, out_keep, theirs),
        [pltpu.VMEM((4, 128, 1024), F32), pltpu.SemaphoreType.DMA((4,))],
        limit=60,
        moved=8 * MIB,
    )


def part_kernel(place, *refs):
    pieces, mine, sent = refs[:4], refs[4], refs[5]
    core, top = place[1], place[2]
    for step, piece in enumerate(pieces):
        image = (top + step) % 4

        @pl.when(image // 2 == core)
        def _():
            mine[image % 2] = piece[...]

        @pl.when(image // 2 != core)
        def _():
            sent[image % 2] = piece[...]


def part_images(place, pieces):
    return call(
        part_kernel,
        [(VMEM, like(2, *pieces[0].shape))] * 2,
        [SMEM] + [VMEM] * 4,
        (place, *pieces),
    )


def land_kernel(place, mine, taken, rows, *text):
    core = place[1]
    for one in range(2):
        rows[one, at(core * 128, 128), :] = mine[one, 0:128, :].astype(rows.dtype)
        rows[one, at((1 - core) * 128, 128), :] = taken[one, 0:128, :].astype(rows.dtype)
        if text:
            text[0][one] = mine[one, 128:160, :].astype(F32) + taken[one, 128:160, :].astype(F32)


def land(place, mine, taken, dtype):
    outs = [(VMEM, like(2, 256, 1024, dtype=dtype))]
    if mine.shape[1] > 128:
        outs.append((VMEM, like(2, 32, 1024, dtype=F32)))
    return call(land_kernel, outs, [SMEM, VMEM, VMEM], (place, mine, taken))


def relay_kernel(over, side, from_side, from_over, to_over, to_side):
    to_over[0:128, :] = (over[0:128, :].astype(F32) + from_side[...].astype(F32)).astype(BF)
    to_over[128:256, :] = over[128:256, :]
    to_side[0:128, :] = side[0:128, :]
    to_side[128:256, :] = (side[128:256, :].astype(F32) + from_over[...].astype(F32)).astype(BF)


def relay(over, side, from_side, from_over):
    return call(
        relay_kernel,
        [(VMEM, like(256, 2048))] * 2,
        [VMEM] * 4,
        (over, side, from_side, from_over),
        limit=60,
        moved=5 * MIB,
    )


def plane_sum_kernel(own, over, side, keep, *sent):
    for s in range(4):
        columns = slice(s * 512, (s + 1) * 512)
        total = own[:, columns].astype(F32) + over[:, columns].astype(F32) + side[:, columns].astype(F32)
        if s:
            sent[s - 1][...] = total.astype(BF)
        else:
            keep[...] = total


def plane_sum(own, over, side):
    return call(
        plane_sum_kernel,
        [(VMEM, like(256, 512, dtype=F32))] + [(VMEM, like(256, 512))] * 3,
        [VMEM] * 3,
        (own, over, side),
        limit=60,
        moved=5 * MIB,
    )


def plane_sum_whole_kernel(place, own, over, side, whole):
    for step in range(4):
        columns = slice(step * 512, (step + 1) * 512)
        total = own[:, columns].astype(F32) + over[:, columns].astype(F32) + side[:, columns].astype(F32)
        whole[at((place[2] + step) % 4 * 256, 256), :] = total.astype(BF)


def plane_sum_whole(place, own, over, side):
    return call(
        plane_sum_whole_kernel,
        [(VMEM, like(1024, 512))],
        [SMEM] + [VMEM] * 3,
        (place, own, over, side),
    )[0]


def line_sum_kernel(place, keep, one, two, three, mine, other):
    core = place[1]
    for target, half in ((other, 1 - core), (mine, core)):
        rows = at(half * 128, 128)
        total = keep[rows, :]
        for part in (one, two, three):
            total = total + part[rows, :].astype(F32)
        target[...] = total.astype(target.dtype)


def line_sum(place, keep, parts):
    return call(
        line_sum_kernel,
        [(VMEM, like(128, 512, dtype=F32)), (VMEM, like(128, 512))],
        [SMEM] + [VMEM] * 4,
        (place, keep, *parts),
        limit=60,
        moved=2 * MIB,
    )


def spread_kernel(place, mine, other, *outs):
    core, columns = place[1], mine.shape[1] // len(outs)
    for one, out in enumerate(outs):
        cut = slice(one * columns, (one + 1) * columns)
        out[:, at(core * columns, columns)] = mine[:, cut].astype(F32)
        out[:, at((1 - core) * columns, columns)] = other[:, cut].astype(F32)


def spread(place, mine, other):
    return call(
        spread_kernel,
        [(VMEM, like(128, 256, dtype=F32))] * 4,
        [SMEM] + [VMEM] * 2,
        (place, mine, other),
        limit=60,
        moved=MIB,
    )


def spread_feed_kernel(place, mine_one, other_one, mine_two, other_two, *outs):
    core = place[1]
    for part, (mine, other) in enumerate(((mine_one, other_one), (mine_two, other_two))):
        for one, out in enumerate(outs):
            cut = slice(one * 256, (one + 1) * 256)
            out[:, at(core * 512 + part * 256, 256)] = mine[:, cut].astype(F32)
            out[:, at((1 - core) * 512 + part * 256, 256)] = other[:, cut].astype(F32)


def spread_feed(place, *halves):
    return call(
        spread_feed_kernel,
        [(VMEM, like(128, 1024, dtype=F32))] * 2,
        [SMEM] + [VMEM] * 4,
        (place, *halves),
        limit=60,
        moved=2 * MIB,
    )


tie = lax.optimization_barrier


def packed_layer(args):
    image_rows, text_rows, segment_ids, cotangent, *others = args
    weights, norms = others[:10], others[10:]
    chip, core, top = lax.axis_index("chip"), lax.axis_index("core"), lax.axis_index("hi")
    place = jnp.stack([chip, core, top, core * 2 + top % 2]).astype(jnp.int32)

    def swap(value):
        return lax.ppermute(value, "core", [(0, 1), (1, 0)])

    def across(value, bit):
        return lax.ppermute(value, "chip", [(i, i ^ bit) for i in range(4)])

    def shift(value, step):
        return lax.ppermute(value, "hi", [((i + step) % 4, i) for i in range(4)])

    def line(part):
        return [shift(part, step) for step in range(1, 4)]

    def exchange(pieces):
        return [pieces[0]] + [shift(piece, step) for step, piece in enumerate(pieces) if step]

    def gather_line(part):
        return lax.all_gather(part, "hi")

    def sides(value):
        return [across(value, 1), across(value, 2)]

    def corners(pair, cut):
        return [across(pair[0][:cut], 2), across(pair[1][cut:], 1)]

    def grad_corners(grads):
        return [across(grads[3], 1), across(grads[4], 2)]

    def grad_sides(grads, got):
        to_over, to_side = relay(grads[2], grads[1], *got)
        return [across(to_over, 2), across(to_side, 1)]

    def halves(total):
        cut = total.reshape(2, 128, 512)
        sent = lax.dynamic_index_in_dim(cut, 1 - core, 0, False)
        return lax.dynamic_index_in_dim(cut, core, 0, False), swap(sent)

    ids_wide = jnp.pad(segment_ids.astype(BF)[:, None, :], ((0, 0), (0, 15), (0, 896)))
    norms_wide = jnp.pad(jnp.stack(norms).astype(BF), ((0, 10), (0, 384)))
    keep, sent, rows_keep, rows_sent, cot_keep, cot_sent = prepare(
        place, image_rows, text_rows, ids_wide, cotangent, norms_wide, weights
    )
    v = {"rows_keep": rows_keep, "cot_keep": cot_keep}
    v["taken"], v["rows_taken"], v["cot_taken"] = swap(sent), swap(rows_sent), swap(cot_sent)
    v = tie(v)
    v["singles"] = join(keep, v.pop("taken"))
    v["near_first"], v["near_second"] = v["singles"][4:]
    v["singles"] = v["singles"][:4]
    v = tie(v)

    v["line"] = line(v["singles"][0])
    v["near_one"] = sides(v["near_first"])
    v["pieces"] = pick(place, v.pop("rows_keep"), v.pop("rows_taken"))
    v["cot_pieces"] = pick(place, v.pop("cot_keep"), v.pop("cot_taken"))
    v = tie(v)

    v["rest_self"] = stack(v.pop("line"))
    v["far_self"] = sides(v["rest_self"])
    v["pieces"] = exchange(v["pieces"])
    line_cross = gather_line(v["singles"][1])
    v = tie(v)

    v["far_self"] += corners(v["far_self"], 384)
    v["near_one"] += corners(v["near_one"], 256)
    v["rows_own"] = stack([piece[None] for piece in v.pop("pieces")])
    v["rows_other"] = swap(v["rows_own"])
    v["rest_cross"] = turn(place, line_cross)
    v = tie(v)

    v["far_cross"] = sides(v["rest_cross"])
    v["cot_pieces"] = exchange(v["cot_pieces"])
    line_one = gather_line(v["singles"][2])
    near = v["near_one"]
    v["w_self"], v["norms"] = assemble(
        place, (v["near_first"], *near[:2], near[2]), (v.pop("rest_self"), *v.pop("far_self")), 0, near[3]
    )
    v["normed_one"], v["qkv"], v["self_mix"], v["self_lse"], v["mine"] = fused_self_forward(
        place, v["rows_own"], v["rows_other"], v["norms"], v["w_self"]
    )
    v = tie(v)

    v["theirs"] = swap(v["mine"])
    v["far_cross"] += corners(v["far_cross"], 384)
    cot_pieces = v.pop("cot_pieces")
    v["cot_own"], v["text"] = arrange(place, cot_pieces)
    v["cot_other"] = swap(v["cot_own"])
    ids = cot_pieces[0][160, :128].astype(jnp.int32)
    v["caption"] = jnp.repeat(ids, 8)[None, :]
    v["ids"] = ids[:, None]
    v["rest_one"] = turn(place, line_one)
    v = tie(v)

    v["far_one"] = sides(v["rest_one"])
    v["near_two"] = sides(v["near_second"])
    line_two = gather_line(v.pop("singles")[3])
    near = v.pop("near_one")
    (v["w_cross"],) = assemble(
        place, (v.pop("near_first"), *near[:2], near[3]), (v.pop("rest_cross"), *v.pop("far_cross")), 256
    )
    v["after_attn"], v["normed_two"], v["queries"], v["keys"], v["cross_mix"], v["cross_lse"], v["mine"] = (
        fused_cross_forward(
            place, v["rows_own"], v.pop("rows_other"), v["mine"], v["theirs"], v["norms"], v["text"], v["ids"],
            v["caption"], v["w_cross"],
        )
    )
    v = tie(v)

    v["theirs"] = swap(v["mine"])
    v["far_one"] += corners(v["far_one"], 384)
    v["near_two"] += corners(v["near_two"], 256)
    v["rest_two"] = turn(place, line_two)
    v = tie(v)

    v["far_two"] = [*sides(v["rest_two"]), across(v["rest_two"], 3)]
    near = v["near_two"]
    (w_one,) = assemble(
        place, (v["near_second"], *near[:2], near[2]), (v.pop("rest_one"), *v.pop("far_one")), 0
    )
    *v["grads_one"], v["after_cross"], v["normed_three"], v["cot"], v["out_sum"], v["back_sum"] = feed_first(
        place, v["after_attn"], v["mine"], v["theirs"], v["norms"], v.pop("cot_own"), v.pop("cot_other"), w_one
    )
    v = tie(v)

    v["got_one"] = grad_corners(v["grads_one"])
    near = v.pop("near_two")
    (w_two,) = assemble(
        place, (v.pop("near_second"), *near[:2], near[3]), (v.pop("rest_two"), *v.pop("far_two")), 256
    )
    *v["grads_two"], v["out_keep"], v["out_sent"], v["mine"] = feed_second(
        place, v.pop("normed_three"), v["cot"], v.pop("out_sum"), v.pop("back_sum"), w_two
    )
    v = tie(v)

    v["theirs"] = swap(v["mine"])
    v["sides_one"] = grad_sides(v["grads_one"], v.pop("got_one"))
    v["got_two"] = grad_corners(v["grads_two"])
    v["grad_cross"], v["part"], v["norms_three"], v["text_part"], *v["grads_three"] = fused_cross_backward(
        place, v["after_cross"], v.pop("mine"), v.pop("theirs"), v.pop("cot"), v["norms"], v.pop("w_cross"),
        v.pop("normed_two"), v.pop("text"), v.pop("queries"), v.pop("keys"), v.pop("cross_mix"),
        v.pop("cross_lse"), v.pop("ids"), v.pop("caption"),
    )
    v = tie(v)

    v["theirs"] = swap(v["part"])
    v["out_theirs"] = swap(v.pop("out_sent"))
    v["to_two"] = relay(v["grads_two"][2], v["grads_two"][1], *v.pop("got_two"))
    v["total_one"] = plane_sum_whole(place, v.pop("grads_one")[0], *v.pop("sides_one"))
    v = tie(v)

    to_two = v.pop("to_two")
    v["sides_two"] = [across(to_two[0], 2), across(to_two[1], 1)]
    v["got_three"] = grad_corners(v["grads_three"])
    line_one = lax.psum_scatter(v.pop("total_one"), "hi", scatter_dimension=0, tiled=True)
    v["grad_own"], v["low_grad"], v["norms_two"], v["dqkv"] = fused_self_backward(
        place, v.pop("after_attn"), v.pop("part"), v.pop("theirs"), v.pop("grad_cross"), v["norms"], v["w_self"],
        v.pop("qkv"), v["self_mix"], v.pop("self_lse"),
    )
    v = tie(v)

    v["sides_three"] = grad_sides(v["grads_three"], v.pop("got_three"))
    v["total_two"] = plane_sum_whole(place, v.pop("grads_two")[0], *v.pop("sides_two"))
    v["grads_four"] = self_grads(place, v.pop("normed_one"), v.pop("low_grad"), v["dqkv"], v.pop("self_mix"))
    v["pieces"] = finish(place, v.pop("after_cross"), v.pop("out_keep"), v.pop("out_theirs"))
    v = tie(v)

    v["got_four"] = grad_corners(v["grads_four"])
    line_two = lax.psum_scatter(v.pop("total_two"), "hi", scatter_dimension=0, tiled=True)
    pieces = exchange(v.pop("pieces"))
    v["kept"], v["sent"] = self_back(place, v.pop("dqkv"), v.pop("w_self"))
    v["theirs"] = swap(v.pop("sent"))
    v["feed_one"] = halves(line_one)
    v = tie(v)

    v["sides_four"] = grad_sides(v["grads_four"], v.pop("got_four"))
    *input_pieces, norms_one = last_norm(
        place, v.pop("rows_own"), v.pop("grad_own"), v.pop("kept"), v.pop("theirs"), v.pop("norms"), v.pop("text_part")
    )
    v["input_pieces"] = exchange(input_pieces)
    total_three = plane_sum_whole(place, v.pop("grads_three")[0], *v.pop("sides_three"))
    line_three = lax.psum_scatter(total_three, "hi", scatter_dimension=0, tiled=True)
    sums = jnp.concatenate([norms_one[:2], 0.5 * v.pop("norms_two")[:2], 0.5 * v.pop("norms_three")[:2]], 0)
    v["sums"] = sums + swap(sums)
    v["feed_two"] = halves(line_two)
    mine, sent = part_images(place, pieces)
    (v["result"],) = land(place, mine, swap(sent), BF)
    v = tie(v)

    sums_four = plane_sum(v.pop("grads_four")[0], *v.pop("sides_four"))
    v["line_four"] = [shift(piece, 3 - i) for i, piece in enumerate(sums_four[1:])]
    v["feed_grads"] = spread_feed(place, *v.pop("feed_one"), *v.pop("feed_two"))
    sums = v.pop("sums")
    sums = sums + across(sums, 1)
    v["sums"] = sums + across(sums, 2)
    mine, sent = part_images(place, v.pop("input_pieces"))
    v["input_grad"], v["text_grad"] = land(place, mine, swap(sent), F32)
    v["kept"] = sums_four[0]
    v = tie(v)

    kept, sent = line_sum(place, v.pop("kept"), v.pop("line_four"))
    own_grads = spread(place, kept, swap(sent))
    cross_grads = spread(place, *halves(line_three))
    sums = v.pop("sums")
    for bit in (1, 2):
        sums = sums + lax.ppermute(sums, "hi", [(i, i ^ bit) for i in range(4)])
    sums = lax.dynamic_slice_in_dim(sums, (chip * 2 + core) * 128, 128, 1)
    return (
        v["result"], v["input_grad"], v["text_grad"], *own_grads, *cross_grads, *v["feed_grads"],
        *[sums[i] for i in range(6)],
    )


def solution(mesh):
    fsdp, tensor = mesh.shape["fsdp"], mesh.shape["tensor"]

    def run(*args):
        images = args[0].shape[0] // fsdp
        tops = 2 * images
        shape = {"chip": fsdp // 2, "core": 2, "hi": tops, "lo": tensor // tops}
        fine = Mesh(mesh.devices.reshape(tuple(shape.values())), tuple(shape))
        first, second = ("chip", "core"), ("hi", "lo")
        wide, weight, norm = P(first, second, None), P(first, second), P(first)
        outs = (wide,) * 3 + (weight,) * 10 + (norm,) * 6
        packed = (
            (fsdp, tensor, images) == (8, 4, 2)
            and args[0].shape[1:] == (1024, 1024)
            and args[1].shape[1:] == (128, 1024)
            and args[12].shape == (1024, 4096)
        )
        return jax.shard_map(
            lambda *local: packed_layer(local) if packed else layer(shape, local),
            mesh=fine,
            in_specs=(wide, wide, P(first, None), wide) + (weight,) * 10 + (norm,) * 6,
            out_specs=outs,
            check_vma=False,
        )(*args)

    return run
```

```python
import functools
import math

import jax
import jax.numpy as jnp
from jax import lax
from jax.experimental import pallas as pl
from jax.experimental.pallas import tpu as pltpu
from jax.sharding import Mesh
from jax.sharding import PartitionSpec as P

HD = 64
EPS = 1e-05
NEG = -1e30
LOG2E = math.log2(math.e)
BF = jnp.bfloat16
F32 = jnp.float32
NT = (((1,), (1,)), ((), ()))
TN = (((0,), (0,)), ((), ()))
NN = (((1,), (0,)), ((), ()))


def dot(left, right, dims=NN):
    return lax.dot_general(left, right, dims, preferred_element_type=F32)


def lane_head(shape, axis, head):
    return lax.broadcasted_iota(jnp.int32, shape, axis) // HD == head


def self_forward_kernel(q_ref, k_ref, v_ref, mix_ref, lse_ref, *, block):
    length = q_ref.shape[0]
    scale = LOG2E * HD**-0.5
    causal = lax.broadcasted_iota(jnp.int32, (block, block), 0) <= lax.broadcasted_iota(
        jnp.int32, (block, block), 1
    )
    for at in range(length // block):
        lo, hi = at * block, (at + 1) * block
        query = q_ref[lo:hi, :]
        mixes = []
        for head in range(2):
            one = jnp.where(lane_head((1, 2 * HD), 1, head), query, jnp.zeros_like(query))
            diag = jnp.where(causal, dot(k_ref[lo:hi, :], one, NT), NEG)
            peak = jnp.max(diag, 0, keepdims=True)
            if at:
                past = dot(k_ref[:lo, :], one, NT)
                peak = jnp.maximum(peak, jnp.max(past, 0, keepdims=True))
            weights = jnp.exp2((diag - peak) * scale)
            total = jnp.sum(weights, 0, keepdims=True)
            mixed = dot(v_ref[lo:hi, :], weights.astype(BF), TN)
            if at:
                weights = jnp.exp2((past - peak) * scale)
                total = total + jnp.sum(weights, 0, keepdims=True)
                mixed = mixed + dot(v_ref[:lo, :], weights.astype(BF), TN)
            mixes.append(mixed / total)
            lse_ref[0, head : head + 1, lo:hi] = peak * scale + jnp.log2(total)
        both = jnp.where(lane_head((2 * HD, 1), 0, 0), mixes[0], mixes[1])
        mix_ref[lo:hi, :] = both.T.astype(BF)


def self_backward_kernel(
    q_ref, k_ref, v_ref, mix_ref, grad_ref, lse_ref, dq_ref, dk_ref, dv_ref, dk_sum, dv_sum, *, block
):
    length = q_ref.shape[0]
    scale = LOG2E * HD**-0.5
    causal = lax.broadcasted_iota(jnp.int32, (block, block), 0) <= lax.broadcasted_iota(
        jnp.int32, (block, block), 1
    )
    dk_sum[...] = jnp.zeros_like(dk_sum)
    dv_sum[...] = jnp.zeros_like(dv_sum)
    for at in range(length // block):
        lo, hi = at * block, (at + 1) * block
        query = q_ref[lo:hi, :]
        grad = grad_ref[lo:hi, :]
        product = (grad.astype(F32) * mix_ref[lo:hi, :].astype(F32)).T
        grads = []
        for head in range(2):
            picked = lane_head((1, 2 * HD), 1, head)
            one = jnp.where(picked, query, jnp.zeros_like(query))
            one_grad = jnp.where(picked, grad, jnp.zeros_like(grad))
            delta = jnp.sum(product[head * HD : (head + 1) * HD], 0, keepdims=True)
            lse = lse_ref[0, head : head + 1, lo:hi]
            total = jnp.zeros((2 * HD, block), F32)
            for start, stop in ((0, lo), (lo, hi)):
                if start == stop:
                    continue
                keys = k_ref[start:stop, :]
                weights = jnp.exp2(dot(keys, one, NT) * scale - lse)
                if start == lo:
                    weights = jnp.where(causal, weights, 0.0)
                slope = dot(v_ref[start:stop, :], one_grad, NT)
                score_grad = (weights * (slope - delta)).astype(BF)
                dv_sum[start:stop, :] += dot(weights.astype(BF), one_grad)
                dk_sum[start:stop, :] += dot(score_grad, one)
                total = total + dot(keys, score_grad, TN)
            grads.append(total)
        both = jnp.where(lane_head((2 * HD, 1), 0, 0), grads[0], grads[1])
        dq_ref[lo:hi, :] = (both.T * HD**-0.5).astype(BF)
    dk_ref[...] = (dk_sum[...] * HD**-0.5).astype(BF)
    dv_ref[...] = dv_sum[...].astype(BF)


def cross_forward_kernel(q_ref, k_ref, v_ref, ids_ref, caption_ref, mix_ref, lse_ref, *, block):
    length = q_ref.shape[0]
    scale = LOG2E * HD**-0.5
    for at in range(length // block):
        lo, hi = at * block, (at + 1) * block
        query = q_ref[lo:hi, :]
        seen = ids_ref[...] == caption_ref[:, lo:hi]
        mixes = []
        for head in range(2):
            one = jnp.where(lane_head((1, 2 * HD), 1, head), query, jnp.zeros_like(query))
            scores = jnp.where(seen, dot(k_ref[...], one, NT), NEG)
            peak = jnp.max(scores, 0, keepdims=True)
            weights = jnp.exp2((scores - peak) * scale)
            total = jnp.sum(weights, 0, keepdims=True)
            mixes.append(dot(v_ref[...], weights.astype(BF), TN) / total)
            lse_ref[0, head : head + 1, lo:hi] = peak * scale + jnp.log2(total)
        both = jnp.where(lane_head((2 * HD, 1), 0, 0), mixes[0], mixes[1])
        mix_ref[lo:hi, :] = both.T.astype(BF)


def cross_backward_kernel(
    q_ref, k_ref, v_ref, mix_ref, grad_ref, lse_ref, ids_ref, caption_ref, dq_ref, dk_ref, dv_ref, *, block
):
    length = q_ref.shape[0]
    scale = LOG2E * HD**-0.5
    keys, values = k_ref[...], v_ref[...]
    dk_sum = jnp.zeros(keys.shape, F32)
    dv_sum = jnp.zeros(keys.shape, F32)
    for at in range(length // block):
        lo, hi = at * block, (at + 1) * block
        query = q_ref[lo:hi, :]
        grad = grad_ref[lo:hi, :]
        product = (grad.astype(F32) * mix_ref[lo:hi, :].astype(F32)).T
        seen = ids_ref[...] == caption_ref[:, lo:hi]
        grads = []
        for head in range(2):
            picked = lane_head((1, 2 * HD), 1, head)
            one = jnp.where(picked, query, jnp.zeros_like(query))
            one_grad = jnp.where(picked, grad, jnp.zeros_like(grad))
            delta = jnp.sum(product[head * HD : (head + 1) * HD], 0, keepdims=True)
            lse = lse_ref[0, head : head + 1, lo:hi]
            weights = jnp.where(seen, jnp.exp2(dot(keys, one, NT) * scale - lse), 0.0)
            slope = dot(values, one_grad, NT)
            score_grad = (weights * (slope - delta)).astype(BF)
            dv_sum = dv_sum + dot(weights.astype(BF), one_grad)
            dk_sum = dk_sum + dot(score_grad, one)
            grads.append(dot(keys, score_grad, TN))
        both = jnp.where(lane_head((2 * HD, 1), 0, 0), grads[0], grads[1])
        dq_ref[lo:hi, :] = (both.T * HD**-0.5).astype(BF)
    dk_ref[...] = (dk_sum * HD**-0.5).astype(BF)
    dv_ref[...] = dv_sum.astype(BF)


def feed_kernel(
    rows_ref, cot_ref, win_ref, wout_ref, out_in, back_in, gin_ref, gout_ref, out_ref, back_ref, rows_t, cot_t, *, first
):
    step = pl.program_id(0)

    @pl.when(step == 0)
    def _():
        rows_t[...] = rows_ref[...].T
        cot_t[...] = cot_ref[...].T
        if first:
            out_ref[...] = jnp.zeros_like(out_ref)
            back_ref[...] = jnp.zeros_like(back_ref)
        else:
            out_ref[...] = out_in[...]
            back_ref[...] = back_in[...]

    pre = dot(rows_ref[...], win_ref[...])
    square = pre * pre
    slope = math.sqrt(2.0 / math.pi)
    bent = jnp.tanh(pre * (slope + slope * 0.044715 * square))
    half = 0.5 * (1.0 + bent)
    act = (pre * half).astype(BF)
    out_ref[...] += dot(act, wout_ref[...], NT)
    gout_ref[...] = dot(cot_t[...], act).astype(BF)
    bend = half + pre * (0.5 * (1.0 - bent * bent)) * (slope + 3.0 * slope * 0.044715 * square)
    pre_grad = (dot(cot_ref[...], wout_ref[...]) * bend).astype(BF)
    gin_ref[...] = dot(rows_t[...], pre_grad).astype(BF)
    back_ref[...] += dot(pre_grad, win_ref[...], NT)


VMEM_LIMIT = 60 * 1024 * 1024


def params():
    return pltpu.CompilerParams(vmem_limit_bytes=VMEM_LIMIT)


def column(rows, offset):
    return pl.BlockSpec((rows, 2 * HD), lambda i: (0, offset + i))


def self_forward(packed):
    length, width = packed.shape
    pairs = width // (6 * HD)
    return pl.pallas_call(
        functools.partial(self_forward_kernel, block=256),
        grid=(pairs,),
        in_specs=[column(length, 0), column(length, pairs), column(length, 2 * pairs)],
        out_specs=[column(length, 0), pl.BlockSpec((1, 2, length), lambda i: (i, 0, 0))],
        out_shape=[
            jax.ShapeDtypeStruct((length, pairs * 2 * HD), BF),
            jax.ShapeDtypeStruct((pairs, 2, length), F32),
        ],
        compiler_params=params(),
        cost_estimate=pl.CostEstimate(
            flops=8 * pairs * length * length * 2 * HD * 2,
            bytes_accessed=8 * pairs * length * 2 * HD,
            transcendentals=2 * pairs * length * length,
        ),
    )(packed, packed, packed)


def self_backward(packed, mix, grad, lse):
    length, width = packed.shape
    pairs = width // (6 * HD)
    part = jax.ShapeDtypeStruct((length, pairs * 2 * HD), BF)
    return pl.pallas_call(
        functools.partial(self_backward_kernel, block=256),
        grid=(pairs,),
        in_specs=[
            column(length, 0),
            column(length, pairs),
            column(length, 2 * pairs),
            column(length, 0),
            column(length, 0),
            pl.BlockSpec((1, 2, length), lambda i: (i, 0, 0)),
        ],
        out_specs=[column(length, 0)] * 3,
        out_shape=[part] * 3,
        scratch_shapes=[pltpu.VMEM((length, 2 * HD), F32)] * 2,
        compiler_params=params(),
        cost_estimate=pl.CostEstimate(
            flops=20 * pairs * length * length * 2 * HD * 2,
            bytes_accessed=16 * pairs * length * 2 * HD,
            transcendentals=2 * pairs * length * length,
        ),
    )(packed, packed, packed, mix, grad, lse)


def cross_forward(queries, keys, ids, captions):
    length, width = queries.shape
    texts = keys.shape[0]
    pairs = width // (2 * HD)
    return pl.pallas_call(
        functools.partial(cross_forward_kernel, block=min(512, length)),
        grid=(pairs,),
        in_specs=[
            column(length, 0),
            column(texts, 0),
            column(texts, pairs),
            pl.BlockSpec((texts, 1), lambda i: (0, 0)),
            pl.BlockSpec((1, length), lambda i: (0, 0)),
        ],
        out_specs=[column(length, 0), pl.BlockSpec((1, 2, length), lambda i: (i, 0, 0))],
        out_shape=[
            jax.ShapeDtypeStruct((length, width), BF),
            jax.ShapeDtypeStruct((pairs, 2, length), F32),
        ],
        compiler_params=params(),
    )(queries, keys, keys, ids, captions)


def cross_backward(queries, keys, mix, grad, lse, ids, captions):
    length, width = queries.shape
    texts = keys.shape[0]
    pairs = width // (2 * HD)
    return pl.pallas_call(
        functools.partial(cross_backward_kernel, block=min(512, length)),
        grid=(pairs,),
        in_specs=[
            column(length, 0),
            column(texts, 0),
            column(texts, pairs),
            column(length, 0),
            column(length, 0),
            pl.BlockSpec((1, 2, length), lambda i: (i, 0, 0)),
            pl.BlockSpec((texts, 1), lambda i: (0, 0)),
            pl.BlockSpec((1, length), lambda i: (0, 0)),
        ],
        out_specs=[column(length, 0), column(texts, 0), column(texts, 0)],
        out_shape=[
            jax.ShapeDtypeStruct((length, width), BF),
            jax.ShapeDtypeStruct((texts, width), BF),
            jax.ShapeDtypeStruct((texts, width), BF),
        ],
        compiler_params=params(),
    )(queries, keys, keys, mix, grad, lse, ids, captions)


def feed(rows, cot, w_in, w_out, sums):
    length, width = rows.shape
    units = w_in.shape[1]
    block = min(256, units)
    whole = pl.BlockSpec((length, width), lambda i: (0, 0))
    cut = pl.BlockSpec((width, block), lambda i: (0, i))
    first = sums is None
    kernel = functools.partial(feed_kernel, first=first)
    operands = [rows, cot, w_in, w_out]
    specs = [whole, whole, cut, cut]
    if first:
        body = lambda a, b, c, d, *rest: kernel(a, b, c, d, None, None, *rest)
    else:
        body = kernel
        operands += list(sums)
        specs += [whole, whole]
    total = jax.ShapeDtypeStruct((length, width), F32)
    part = jax.ShapeDtypeStruct((width, units), BF)
    return pl.pallas_call(
        body,
        grid=(units // block,),
        in_specs=specs,
        out_specs=[cut, cut, whole, whole],
        out_shape=[part, part, total, total],
        scratch_shapes=[pltpu.VMEM((width, length), BF)] * 2,
        compiler_params=params(),
        cost_estimate=pl.CostEstimate(
            flops=12 * length * width * units,
            bytes_accessed=8 * width * units + 8 * length * width,
            transcendentals=length * units,
        ),
    )(*operands)


def norm_parts(values):
    center = values - jnp.mean(values, -1, keepdims=True)
    inverse = lax.rsqrt(jnp.mean(center * center, -1, keepdims=True) + EPS)
    return center * inverse, inverse


def layer_norm(values, gain, offset):
    return (norm_parts(values)[0] * gain + offset).astype(BF)


def norm_back(values, gain, grad):
    hat, inverse = norm_parts(values)
    scaled = grad * gain
    back = inverse * (
        scaled
        - jnp.mean(scaled, -1, keepdims=True)
        - hat * jnp.mean(scaled * hat, -1, keepdims=True)
    )
    lead = tuple(range(values.ndim - 1))
    return back, jnp.sum(grad * hat, lead), jnp.sum(grad, lead)


def layer(shape, args):
    chips, tops, lows = shape["chip"], shape["hi"], shape["lo"]
    (
        image_rows,
        text_rows,
        segment_ids,
        cotangent,
        query_weight,
        key_weight,
        value_weight,
        attn_output,
        cross_query,
        cross_key,
        cross_value,
        cross_output,
        hidden_in,
        hidden_out,
        *norms,
    ) = args
    images, rows, width = image_rows.shape
    texts = text_rows.shape[1]
    half_rows = rows // 2
    length = rows * lows * tops
    shard = query_weight.shape[0]
    chip, core = lax.axis_index("chip"), lax.axis_index("core")
    top = lax.axis_index("hi")
    own_slot = core * images + top % images

    def swap(value):
        return lax.ppermute(value, "core", [(0, 1), (1, 0)])

    def across(value, bit):
        return lax.ppermute(value, "chip", [(i, i ^ bit) for i in range(chips)])

    def shift(value, step):
        return lax.ppermute(value, "hi", [((i + step) % tops, i) for i in range(tops)])

    def matching(number, back):
        pairs = []
        for source_core in range(2):
            for source_top in range(tops):
                slot = source_top ^ number
                target = (slot // images) * tops + source_core * images + slot % images
                source = source_core * tops + source_top
                pairs.append((target, source) if back else (source, target))
        return pairs

    def to_image(piece_of):
        got = [
            lax.ppermute(piece_of(top ^ number), ("core", "hi"), matching(number, False))
            for number in range(tops)
        ]
        whole = jnp.stack(got)
        return jnp.stack(
            [lax.dynamic_index_in_dim(whole, own_slot ^ place, 0, False) for place in range(tops)]
        )

    def from_image(pieces):
        return [
            lax.ppermute(
                lax.dynamic_index_in_dim(pieces, own_slot ^ number, 0, False),
                ("core", "hi"),
                matching(number, True),
            )
            for number in range(tops)
        ]

    def image_piece(value):
        def piece(slot):
            return lax.dynamic_slice(
                value,
                (slot % images, (slot // images) * half_rows, 0),
                (1, half_rows, width),
            )[0]

        return piece

    def to_rows(pieces):
        got = jnp.stack(from_image(pieces))
        ordered = jnp.stack(
            [lax.dynamic_index_in_dim(got, top ^ slot, 0, False) for slot in range(tops)]
        )
        ordered = ordered.reshape(2, images, half_rows, width)
        return jnp.swapaxes(ordered, 0, 1).reshape(images, rows, width)

    def tp_gather(mine):
        if lows == 1:
            other = swap(mine)
            first = jnp.where(core == 0, mine, other)
            second = jnp.where(core == 0, other, mine)
            return jnp.stack([first, second], 1).reshape(length, width)
        every = lax.all_gather(mine, ("lo", "core"))
        every = every.reshape(lows * 2, tops, half_rows, width)
        return jnp.swapaxes(every, 0, 1).reshape(length, width)

    def tp_reduce(partial):
        if lows == 1:
            cut = partial.reshape(tops, 2, half_rows, width)
            sent = lax.dynamic_index_in_dim(cut, 1 - core, 1, False).astype(BF)
            kept = lax.dynamic_index_in_dim(cut, core, 1, False)
            return kept + swap(sent).astype(F32)
        cut = jnp.swapaxes(partial.astype(BF).reshape(tops, lows * 2, half_rows, width), 0, 1)
        cut = lax.psum_scatter(cut, ("lo", "core"), scatter_dimension=0, tiled=False)
        return cut.astype(F32)

    def core_half(weight, which):
        columns = weight.shape[1] // 2
        return lax.dynamic_slice_in_dim(weight, which * columns, columns, 1)

    def pack(which):
        feeds = [core_half(weight, which) for weight in (hidden_in, hidden_out)]
        cuts = feeds[0].shape[1] // 2
        groups = [
            [core_half(w, which) for w in (query_weight, key_weight, value_weight, attn_output)],
            [core_half(w, which) for w in (cross_query, cross_key, cross_value, cross_output)],
            [w[:, :cuts] for w in feeds],
            [w[:, cuts:] for w in feeds],
        ]
        return jnp.concatenate([w for group in groups for w in group], 1)

    kept = pack(core)
    taken = swap(pack(1 - core))
    own = jnp.concatenate(
        [jnp.where(core == 0, kept, taken), jnp.where(core == 0, taken, kept)], 0
    )
    block_rows = 2 * shard
    group_width = own.shape[1] // 4

    def plane_gather(piece):
        if chips != 4:
            return lax.all_gather(piece, "chip", axis=0, tiled=True)
        side = across(piece, 1)
        over = across(piece, 2)
        corner_low = across(side[:shard], 2)
        corner_high = across(over[shard:], 1)
        corner = jnp.concatenate([corner_low, corner_high], 0)
        pieces = jnp.stack([piece, side, over, corner])
        ordered = [lax.dynamic_index_in_dim(pieces, chip ^ place, 0, False) for place in range(4)]
        return jnp.concatenate(ordered, 0)

    def plane_scatter(grads):
        if chips != 4:
            return lax.psum_scatter(grads, "chip", scatter_dimension=0, tiled=True).astype(F32)

        def rows_of(place, low, count):
            return lax.dynamic_slice_in_dim(grads, (chip ^ place) * block_rows + low, count, 0)

        by_side = across(rows_of(3, 0, shard), 1)
        by_over = across(rows_of(3, shard, shard), 2)
        to_over = jnp.concatenate(
            [rows_of(2, 0, shard).astype(F32) + by_side.astype(F32), rows_of(2, shard, shard).astype(F32)], 0
        ).astype(BF)
        to_side = jnp.concatenate(
            [rows_of(1, 0, shard).astype(F32), rows_of(1, shard, shard).astype(F32) + by_over.astype(F32)], 0
        ).astype(BF)
        over, side = across(to_over, 2), across(to_side, 1)
        return rows_of(0, 0, block_rows).astype(F32) + over.astype(F32) + side.astype(F32)

    def top_scatter(pieces):
        total = pieces[0].astype(F32)
        for step in range(1, tops):
            total = total + shift(pieces[step].astype(BF), tops - step).astype(F32)
        return total

    def core_split(total):
        cut = total.reshape(2, shard, total.shape[1])
        mine = lax.dynamic_index_in_dim(cut, core, 0, False)
        other = swap(lax.dynamic_index_in_dim(cut, 1 - core, 0, False).astype(BF)).astype(F32)
        return jnp.where(core == 0, mine, other), jnp.where(core == 0, other, mine)

    own_wide = plane_gather(own)

    def fetch(group, count):
        part = own[:, group * group_width : (group + 1) * group_width]
        columns = group_width // count
        got = [shift(part, step).reshape(block_rows, count, 1, columns) for step in range(1, tops)]
        rest = jnp.concatenate(got, 2).reshape(block_rows, (tops - 1) * group_width)
        rest = plane_gather(rest).reshape(width, count, (tops - 1) * columns)
        near = own_wide[:, group * group_width : (group + 1) * group_width]
        near = near.reshape(width, count, columns)
        return [
            jnp.concatenate([near[:, one], rest[:, one]], 1) for one in range(count)
        ]

    def give(grads):
        count = len(grads)
        columns = grads[0].shape[1] // tops
        summed = plane_scatter(jnp.concatenate(grads, 1)).reshape(block_rows, count, tops, columns)
        pieces = [summed[:, :, step].reshape(block_rows, count * columns) for step in range(tops)]
        low, high = core_split(top_scatter(pieces))
        low, high = low.reshape(shard, count, columns), high.reshape(shard, count, columns)
        return [(low[:, one], high[:, one]) for one in range(count)]

    packed_norms = lax.all_gather(jnp.stack(norms), ("chip", "core"), axis=1, tiled=True)
    gain_one, bias_one, gain_two, bias_two, gain_three, bias_three = packed_norms

    w_query, w_key, w_value, w_out = fetch(0, 4)
    inputs = to_image(image_piece(image_rows)).astype(F32)
    c_query, c_key, c_value, c_out = fetch(1, 4)
    in_low, out_low = fetch(2, 2)
    in_high, out_high = fetch(3, 2)

    text = to_image(lambda slot: text_rows[slot % images])
    if lows > 1:
        text = lax.all_gather(text, "lo", axis=1)
    text = text.reshape(tops * lows * texts, width)
    other_ids = swap(segment_ids)
    ids = jnp.where(core == top // images, segment_ids, other_ids)
    ids = lax.dynamic_index_in_dim(ids, top % images, 0, False)
    captions = jnp.repeat(ids, length // ids.shape[0])[None, :]
    ids = ids[:, None]
    cot = to_image(image_piece(cotangent))

    full_one = tp_gather(layer_norm(inputs, gain_one, bias_one))
    packed = dot(full_one, jnp.concatenate([w_query, w_key, w_value], 1)).astype(BF)
    self_mix, self_lse = self_forward(packed)
    after_attn = inputs + tp_reduce(dot(self_mix, w_out, NT))
    full_two = tp_gather(layer_norm(after_attn, gain_two, bias_two))
    queries = dot(full_two, c_query).astype(BF)
    w_text = jnp.concatenate([c_key, c_value], 1)
    keys = dot(text, w_text).astype(BF)
    cross_mix, cross_lse = cross_forward(queries, keys, ids, captions)
    after_cross = after_attn + tp_reduce(dot(cross_mix, c_out, NT))
    full_three = tp_gather(layer_norm(after_cross, gain_three, bias_three))
    full_cot = tp_gather(cot)
    gin_low, gout_low, *sums = feed(full_three, full_cot, in_low, out_low, None)
    gin_high, gout_high, out_sum, back_sum = feed(full_three, full_cot, in_high, out_high, sums)
    low_grads = give([gin_low, gout_low])
    high_grads = give([gin_high, gout_high])
    result = to_rows((after_cross + tp_reduce(out_sum)).astype(BF))

    back_three, dgain_three, dbias_three = norm_back(after_cross, gain_three, tp_reduce(back_sum))
    grad_cross = cot.astype(F32) + back_three
    full_grad = tp_gather(grad_cross.astype(BF))
    mix_grad = dot(full_grad, c_out).astype(BF)
    dq, dk, dv = cross_backward(queries, keys, cross_mix, mix_grad, cross_lse, ids, captions)
    back_sum = dot(dq, c_query, NT)
    dkv = jnp.concatenate([dk, dv], 1)
    cross_grads = give(
        [
            dot(full_two, dq, TN).astype(BF),
            dot(text, dk, TN).astype(BF),
            dot(text, dv, TN).astype(BF),
            dot(full_grad, cross_mix, TN).astype(BF),
        ]
    )
    text_part = dot(dkv, w_text, NT).astype(BF).reshape(tops, lows, texts, width)
    if lows > 1:
        text_part = lax.psum_scatter(text_part, "lo", scatter_dimension=1, tiled=True)
    got = [part.astype(F32) for part in from_image(text_part[:, 0])]
    got = jnp.stack(got)
    got = [lax.dynamic_index_in_dim(got, top ^ slot, 0, False) for slot in range(tops)]
    text_grad = jnp.stack([got[i] + got[images + i] for i in range(images)])

    back_two, dgain_two, dbias_two = norm_back(after_attn, gain_two, tp_reduce(back_sum))
    grad_attn = grad_cross + back_two
    full_grad = tp_gather(grad_attn.astype(BF))
    mix_grad = dot(full_grad, w_out).astype(BF)
    dq, dk, dv = self_backward(packed, self_mix, mix_grad, self_lse)
    dqkv = jnp.concatenate([dq, dk, dv], 1)
    dwqkv = dot(full_one, dqkv, TN).astype(BF)
    span = dq.shape[1]
    self_grads = give(
        [
            dwqkv[:, :span],
            dwqkv[:, span : 2 * span],
            dwqkv[:, 2 * span :],
            dot(full_grad, self_mix, TN).astype(BF),
        ]
    )
    back_sum = dot(dqkv, jnp.concatenate([w_query, w_key, w_value], 1), NT)
    back_one, dgain_one, dbias_one = norm_back(inputs, gain_one, tp_reduce(back_sum))
    input_grad = to_rows((grad_attn + back_one).astype(BF)).astype(F32)

    norm_sums = lax.psum(
        jnp.stack([dgain_one, dbias_one, dgain_two, dbias_two, dgain_three, dbias_three]),
        ("chip", "core", "hi", "lo"),
    )
    norm_sums = lax.dynamic_slice_in_dim(norm_sums, (chip * 2 + core) * shard, shard, 1)

    feeds = [
        jnp.concatenate([low_grads[i][0], high_grads[i][0], low_grads[i][1], high_grads[i][1]], 1)
        for i in range(2)
    ]
    joined = [jnp.concatenate(pair, 1) for pair in (*self_grads, *cross_grads)]
    return (result, input_grad, text_grad, *joined, *feeds, *[norm_sums[i] for i in range(6)])


BLOCK = 256
ANY = pl.BlockSpec(memory_space=pltpu.HBM)
SMEM = pl.BlockSpec(memory_space=pltpu.SMEM)
VMEM = pl.BlockSpec(memory_space=pltpu.VMEM)
MIB = 1024 * 1024


def like(*shape, dtype=BF):
    return jax.ShapeDtypeStruct(shape, dtype)


def call(body, outs, ins, operands, scratch=(), limit=60, grid=None, flops=0, moved=0):
    single = not isinstance(outs, (list, tuple))
    extra = {} if grid is None else {"grid": grid}
    cost = pl.CostEstimate(flops=1, bytes_accessed=1, transcendentals=0)
    out_specs, out_shape = ([outs[0]], [outs[1]]) if single else ([o[0] for o in outs], [o[1] for o in outs])
    return list(pl.pallas_call(
        body,
        in_specs=ins,
        out_specs=out_specs,
        out_shape=out_shape,
        scratch_shapes=list(scratch),
        compiler_params=pltpu.CompilerParams(vmem_limit_bytes=limit * MIB),
        cost_estimate=cost,
        **extra,
    )(*operands))


def run_copies(copies, sems):
    started = [pltpu.make_async_copy(source, target, sems.at[i]) for i, (source, target) in enumerate(copies)]
    for copy in started:
        copy.start()
    for copy in started:
        copy.wait()


def at(offset, count, unit=128):
    return pl.ds(pl.multiple_of(offset, unit), count)


def prepare_kernel(place, image, text, ids, cot, norms, wq, wk, wv, wo, cq, ck, cv, co, win, wout, *outs):
    keep, sent, rows_keep, rows_sent, cot_keep, cot_sent, text_pair, sems = outs
    core = place[1]
    copies = []
    for target, which in ((sent, 1 - core), (keep, core)):
        for group, weights in enumerate(((wq, wk, wv, wo), (cq, ck, cv, co))):
            for one, weight in enumerate(weights):
                copies.append(
                    (
                        weight.at[:, at(which * 128, 128)],
                        target.at[group * 128 : (group + 1) * 128, one * 128 : (one + 1) * 128],
                    )
                )
        for part in range(2):
            for one, weight in enumerate((win, wout)):
                copies.append(
                    (
                        weight.at[:, at(which * 512 + part * 256, 256)],
                        target.at[256 + part * 128 : 384 + part * 128, one * 256 : (one + 1) * 256],
                    )
                )
        copies.append((norms, target.at[512:528, :]))
    for target, cots, which in ((rows_sent, cot_sent, 1 - core), (rows_keep, cot_keep, core)):
        for one in range(2):
            copies.append((image.at[one, at(which * 128, 128), :], target.at[one]))
            copies.append((cot.at[one, at(which * 128, 128), :], cots.at[one]))
    for one in range(2):
        copies.append((text.at[one], text_pair.at[one, 0:32, :]))
        copies.append((ids.at[one], text_pair.at[one, 32:48, :]))
    run_copies(copies, sems)


def prepare(place, image, text, ids, cot, norms, weights):
    return call(
        prepare_kernel,
        [(VMEM, like(528, 512))] * 2 + [(VMEM, like(2, 128, 1024))] * 4 + [(VMEM, like(2, 48, 1024))],
        [SMEM] + [ANY] * 15,
        (place, image, text, ids, cot, norms, *weights),
        [pltpu.SemaphoreType.DMA((42,))],
    )


def pick_kernel(place, keep, taken, *outs):
    core, top = place[1], place[2]
    for step, out in enumerate(outs):
        image = (top + 4 - step) % 4

        @pl.when(image // 2 == core)
        def _():
            out[...] = keep[image % 2]

        @pl.when(image // 2 != core)
        def _():
            out[...] = taken[image % 2]


def pick(place, keep, taken):
    return call(
        pick_kernel,
        [(VMEM, like(*keep.shape[1:]))] * 4,
        [SMEM, VMEM, VMEM],
        (place, keep, taken),
    )


def join_kernel(place, keep, taken, *refs):
    singles, near, sems = refs[:4], refs[4], refs[5]
    copies = []
    for half, source in enumerate((keep, taken)):
        core = place[1] ^ half
        for group in range(4):
            part = source.at[group * 128 : (group + 1) * 128, :]
            copies.append((part, singles[group].at[at(core * 128, 128), :]))
        copies.append((source.at[0:128, :], near.at[at(core * 128, 128), :]))
        copies.append((source.at[512:528, :], near.at[at(256 + core * 16, 16, 16), :]))
    run_copies(copies, sems)


def join(place, keep, taken):
    return call(
        join_kernel,
        [(VMEM, like(256, 512))] * 4 + [(VMEM, like(288, 512))],
        [SMEM] + [ANY] * 2,
        (place, keep, taken),
        [pltpu.SemaphoreType.DMA((12,))],
    )


def stack_kernel(*refs):
    *parts, whole, sems = refs
    copies, low = [], 0
    for part in parts:
        copies.append((part, whole.at[low : low + part.shape[0]]))
        low += part.shape[0]
    run_copies(copies, sems)


def stack(parts):
    rows = sum(part.shape[0] for part in parts)
    return call(
        stack_kernel,
        [(VMEM, like(rows, *parts[0].shape[1:]))],
        [ANY] * len(parts),
        parts,
        [pltpu.SemaphoreType.DMA((len(parts),))],
        limit=60,
    )[0]


def arrange_kernel(place, *refs):
    messages, text, sems = refs[:4], refs[4], refs[5]
    run_copies(
        [(m.at[0:32, :], text.at[at((place[2] + i) % 4 * 32, 32, 32), :]) for i, m in enumerate(messages)], sems
    )


def arrange(place, messages):
    return call(
        arrange_kernel,
        [(VMEM, like(128, 1024))],
        [SMEM] + [ANY] * 4,
        (place, *messages),
        [pltpu.SemaphoreType.DMA((4,))],
    )[0]


def gather_copies(batches, buffer, whole, rows_of, loads, stores, extra=()):
    started = []
    for i, batch in enumerate(batches):
        copies = [pltpu.make_async_copy(a, b, loads.at[i * 8 + j]) for j, (a, b) in enumerate(batch)]
        for copy in copies:
            copy.start()
        started.append(copies)
    stored = [pltpu.make_async_copy(a, b, stores.at[4 + i]) for i, (a, b) in enumerate(extra)]
    for copy in stored:
        copy.start()
    for i, copies in enumerate(started):
        for copy in copies:
            copy.wait()
        rows = rows_of(i)
        stored.append(pltpu.make_async_copy(buffer.at[rows, :], whole.at[rows, :], stores.at[i]))
        stored[-1].start()
    for copy in stored:
        copy.wait()


def assemble_first_kernel(place, *refs):
    near, far = refs[:5], refs[5:10]
    whole, norms, buffer, loads, stores = refs[10:]
    chip, top = place[0], place[2]
    batches, extra = [], []
    for source in range(4):
        batch = []
        for half in range(2):
            row = at((chip ^ source) * 256 + half * 128, 128)
            piece, first = (near[source], half * 128) if source < 3 else (near[3 + half], 0)
            batch.append((piece.at[first : first + 128, :], buffer.at[row, at(top * 512, 512, 512)]))
            low = 256 + half * 16 if source < 3 else 128 + half * 16
            piece = near[source] if source < 3 else near[4]
            column = at((chip ^ source) * 256 + half * 128, 128)
            extra.append((piece.at[low : low + 16, 0:128], norms.at[:, column]))
            for step in range(3):
                first = step * 256 + half * 128
                piece = far[source] if source < 3 else far[3 + first // 384]
                first = first if source < 3 else first % 384
                columns = at((top + 1 + step) % 4 * 512, 512, 512)
                batch.append((piece.at[first : first + 128, :], buffer.at[row, columns]))
        batches.append(batch)
    gather_copies(batches, buffer, whole, lambda i: at((chip ^ i) * 256, 256), loads, stores, extra)


ASSEMBLE_SCRATCH = [
    pltpu.VMEM((1024, 2048), BF),
    pltpu.SemaphoreType.DMA((32,)),
    pltpu.SemaphoreType.DMA((12,)),
]


def assemble_first(place, near, far):
    return call(
        assemble_first_kernel,
        [(ANY, like(1024, 2048)), (VMEM, like(16, 1024))],
        [SMEM] + [ANY] * 10,
        (place, *near, *far),
        ASSEMBLE_SCRATCH,
    )


def assemble_kernel(place, own, side, over, low, high, whole, buffer, loads, stores):
    chip = place[0]
    batches = []
    for source in range(4):
        batch = []
        for top in range(4):
            piece = (own, side, over, low if top < 2 else high)[source]
            rows, columns = at((chip ^ source) * 256, 256), slice(top * 512, (top + 1) * 512)
            batch.append((piece.at[top % 2 if source == 3 else top], buffer.at[rows, columns]))
        batches.append(batch)
    gather_copies(batches, buffer, whole, lambda i: at((chip ^ i) * 256, 256), loads, stores)


def assemble(place, own, others):
    return call(
        assemble_kernel,
        [(ANY, like(1024, 2048))],
        [SMEM] + [ANY] * 5,
        (place, own, *others),
        ASSEMBLE_SCRATCH,
    )[0]


def norm_row(norms, one):
    return norms[one : one + 1, :].astype(F32)


def normalized(values, gain, bias):
    center = values - jnp.mean(values, -1, keepdims=True)
    inverse = lax.rsqrt(jnp.mean(center * center, -1, keepdims=True) + EPS)
    return (center * inverse * gain + bias).astype(BF)


def columns_of(weights, one, count=128):
    return jnp.concatenate([weights[:, s * 512 + one * count : s * 512 + (one + 1) * count] for s in range(4)], 1)


def image_blocks(place, own, other):
    core, top = place[1], place[2]
    for number in range(4):
        yield (top + number) % 4 * 256 + core * 128, own, number
        yield (top + number) % 4 * 256 + (1 - core) * 128, other, number


def one_head(values, head):
    return jnp.where(lane_head((1, 2 * HD), 1, head), values, jnp.zeros_like(values))


def softmax_mix(scores, values):
    scale = LOG2E * HD**-0.5
    peak = jnp.max(scores[0], 0, keepdims=True)
    for part in scores[1:]:
        peak = jnp.maximum(peak, jnp.max(part, 0, keepdims=True))
    total, mixed = 0.0, 0.0
    for part, rows in zip(scores, values):
        weights = jnp.exp2((part - peak) * scale)
        total = total + jnp.sum(weights, 0, keepdims=True)
        mixed = mixed + dot(rows, weights.astype(BF), TN)
    return mixed / total, peak * scale + jnp.log2(total)


def causal_mask():
    return lax.broadcasted_iota(jnp.int32, (BLOCK, BLOCK), 0) <= lax.broadcasted_iota(
        jnp.int32, (BLOCK, BLOCK), 1
    )


def self_fwd_kernel(place, own, other, norms, weights, normed, qkv, mix, lse, part):
    gain, bias = norm_row(norms, 0), norm_row(norms, 1)
    for row, half, number in image_blocks(place, own, other):
        normed[at(row, 128), :] = normalized(half[number].astype(F32), gain, bias)
    w_in = jnp.concatenate([columns_of(weights, one) for one in range(3)], 1)
    for low in range(0, 1024, BLOCK):
        qkv[low : low + BLOCK, :] = dot(normed[low : low + BLOCK, :], w_in).astype(BF)
    causal = causal_mask()

    def pair_step(pair, carry):
        lanes = at(pair * 128, 128)
        k_lanes, v_lanes = at(512 + pair * 128, 128), at(1024 + pair * 128, 128)
        for low in range(0, 1024, BLOCK):
            high = low + BLOCK
            query = qkv[low:high, lanes]
            mixes = []
            for head in range(2):
                one = one_head(query, head)
                scores = [jnp.where(causal, dot(qkv[low:high, k_lanes], one, NT), NEG)]
                values = [qkv[low:high, v_lanes]]
                if low:
                    scores.append(dot(qkv[:low, k_lanes], one, NT))
                    values.append(qkv[:low, v_lanes])
                mixed, logsum = softmax_mix(scores, values)
                mixes.append(mixed)
                lse[pair, head : head + 1, low:high] = logsum
            both = jnp.where(lane_head((128, 1), 0, 0), mixes[0], mixes[1])
            mix[low:high, lanes] = both.T.astype(BF)
        return carry

    lax.fori_loop(0, 4, pair_step, 0)
    w_out = columns_of(weights, 3)
    for low in range(0, 1024, BLOCK):
        part[low : low + BLOCK, :] = dot(mix[low : low + BLOCK, :], w_out, NT).astype(BF)


def fused_self_forward(place, own, other, norms, weights):
    return call(
        self_fwd_kernel,
        [
            (VMEM, like(1024, 1024)),
            (VMEM, like(1024, 1536)),
            (VMEM, like(1024, 512)),
            (VMEM, like(4, 2, 1024, dtype=F32)),
            (VMEM, like(1024, 1024)),
        ],
        [SMEM] + [VMEM] * 4,
        (place, own, other, norms, weights),
        limit=60,
        flops=10 * 2**30,
        moved=14 * MIB,
    )


def cross_fwd_kernel(
    place, own, other, mine, theirs, norms, text, ids, caption, weights, after, normed, queries, keys, mix, lse, part
):
    gain, bias = norm_row(norms, 2), norm_row(norms, 3)
    for row, half, number in image_blocks(place, own, other):
        rows = at(row, 128)
        values = half[number].astype(F32) + (mine[rows, :].astype(F32) + theirs[rows, :].astype(F32))
        after[rows, :] = values
        normed[rows, :] = normalized(values, gain, bias)
    w_query = columns_of(weights, 0)
    for low in range(0, 1024, BLOCK):
        queries[low : low + BLOCK, :] = dot(normed[low : low + BLOCK, :], w_query).astype(BF)
    w_text = jnp.concatenate([columns_of(weights, 1), columns_of(weights, 2)], 1)
    keys[...] = dot(text[...], w_text).astype(BF)

    def pair_step(pair, carry):
        lanes, v_lanes = at(pair * 128, 128), at(512 + pair * 128, 128)
        for low in range(0, 1024, 512):
            high = low + 512
            query = queries[low:high, lanes]
            seen = ids[...] == caption[:, low:high]
            mixes = []
            for head in range(2):
                scores = jnp.where(seen, dot(keys[:, lanes], one_head(query, head), NT), NEG)
                mixed, logsum = softmax_mix([scores], [keys[:, v_lanes]])
                mixes.append(mixed)
                lse[pair, head : head + 1, low:high] = logsum
            both = jnp.where(lane_head((128, 1), 0, 0), mixes[0], mixes[1])
            mix[low:high, lanes] = both.T.astype(BF)
        return carry

    lax.fori_loop(0, 4, pair_step, 0)
    w_out = columns_of(weights, 3)
    for low in range(0, 1024, BLOCK):
        part[low : low + BLOCK, :] = dot(mix[low : low + BLOCK, :], w_out, NT).astype(BF)


def fused_cross_forward(place, own, other, mine, theirs, norms, text, ids, caption, weights):
    return call(
        cross_fwd_kernel,
        [
            (VMEM, like(1024, 1024, dtype=F32)),
            (VMEM, like(1024, 1024)),
            (VMEM, like(1024, 512)),
            (VMEM, like(128, 1024)),
            (VMEM, like(1024, 512)),
            (VMEM, like(4, 2, 1024, dtype=F32)),
            (VMEM, like(1024, 1024)),
        ],
        [SMEM] + [VMEM] * 9,
        (place, own, other, mine, theirs, norms, text, ids, caption, weights),
        limit=60,
        flops=5 * 2**30,
        moved=20 * MIB,
    )


def cut_grads(place, grads, columns, own, side, over, low, high):
    chip = place[0]
    own[:, columns] = grads[at(chip * 256, 256), :].astype(BF)
    side[:, columns] = grads[at((chip ^ 1) * 256, 256), :].astype(BF)
    over[:, columns] = grads[at((chip ^ 2) * 256, 256), :].astype(BF)
    low[:, columns] = grads[at((chip ^ 3) * 256, 128), :].astype(BF)
    high[:, columns] = grads[at((chip ^ 3) * 256 + 128, 128), :].astype(BF)


GRAD_SHAPES = [(256, 2048)] * 3 + [(128, 2048)] * 2


def feed_step(rows, cot, rows_t, cot_t, weights, out_sum, back_sum, grads):
    w_in, w_out = weights[:, :256], weights[:, 256:]
    slope = math.sqrt(2.0 / math.pi)
    acts, pre_grads = [], []
    for low in range(0, 1024, BLOCK):
        part = slice(low, low + BLOCK)
        pre = dot(rows[part, :], w_in)
        square = pre * pre
        bent = jnp.tanh(pre * (slope + slope * 0.044715 * square))
        half = 0.5 * (1.0 + bent)
        act = (pre * half).astype(BF)
        bend = half + pre * (0.5 * (1.0 - bent * bent)) * (slope + 3.0 * slope * 0.044715 * square)
        pre_grad = (dot(cot[part, :], w_out) * bend).astype(BF)
        out_sum[part, :] += dot(act, w_out, NT)
        back_sum[part, :] += dot(pre_grad, w_in, NT)
        acts.append(act)
        pre_grads.append(pre_grad)
    grads[:, :256] = dot(rows_t[...], jnp.concatenate(pre_grads, 0))
    grads[:, 256:] = dot(cot_t[...], jnp.concatenate(acts, 0))


def feed_first_kernel(
    place, after, mine, theirs, norms, cot_own, cot_other, weights,
    g_whole, after_cross, normed, cot, out_sum, back_sum, rows_t, cot_t, grads,
):
    @pl.when(pl.program_id(0) == 0)
    def _():
        gain, bias = norm_row(norms, 4), norm_row(norms, 5)
        for low in range(0, 1024, 128):
            rows = slice(low, low + 128)
            values = after[rows, :] + (mine[rows, :].astype(F32) + theirs[rows, :].astype(F32))
            after_cross[rows, :] = values
            normed[rows, :] = normalized(values, gain, bias)
        for row, half, number in image_blocks(place, cot_own, cot_other):
            cot[at(row, 128), :] = half[number]
        rows_t[...] = normed[...].T
        cot_t[...] = cot[...].T
        out_sum[...] = jnp.zeros_like(out_sum)
        for block in range(4):
            rows = at(block * 256 + place[1] * 128, 128)
            out_sum[rows, :] = after_cross[rows, :]
        back_sum[...] = jnp.zeros_like(back_sum)

    feed_step(normed, cot, rows_t, cot_t, weights, out_sum, back_sum, grads)
    for chip in range(4):
        g_whole[chip, 0] = grads[chip * 256 : (chip + 1) * 256, :].astype(BF)


def feed_second_kernel(
    place, normed, cot, out_in, back_in, weights,
    g_own, g_side, g_over, g_low, g_high, out_keep, out_sent, back, out_sum, back_sum, rows_t, cot_t, grads,
):
    step, core = pl.program_id(0), place[1]

    @pl.when(step == 0)
    def _():
        rows_t[...] = normed[...].T
        cot_t[...] = cot[...].T
        out_sum[...] = out_in[...]
        back_sum[...] = back_in[...]

    feed_step(normed, cot, rows_t, cot_t, weights[:, 0].reshape(1024, 512), out_sum, back_sum, grads)
    cut_grads(place, grads, slice(None), g_own, g_side, g_over, g_low, g_high)

    @pl.when(step == 3)
    def _():
        back[...] = back_sum[...].astype(BF)
        for block in range(4):
            out_keep[block] = out_sum[at(block * 256 + core * 128, 128), :]
            out_sent[block] = out_sum[at(block * 256 + (1 - core) * 128, 128), :].astype(BF)


def once(*shape):
    zeros = (0,) * len(shape)
    return pl.BlockSpec(shape, lambda i: zeros, pipeline_mode=pl.Buffered(1))


def grad_outs():
    return [(pl.BlockSpec((rows, 512), lambda i: (0, i)), like(rows, n)) for rows, n in GRAD_SHAPES]


FEED_FLOPS = 13 * 2**30


def feed_first(place, after, mine, theirs, norms, cot_own, cot_other, weights):
    square = once(1024, 1024)
    return call(
        feed_first_kernel,
        [(pl.BlockSpec((4, 1, 256, 512), lambda i: (0, i, 0, 0)), like(4, 4, 256, 512))]
        + [
            (square, like(1024, 1024, dtype=F32)),
            (square, like(1024, 1024)),
            (square, like(1024, 1024)),
            (square, like(1024, 1024, dtype=F32)),
            (square, like(1024, 1024, dtype=F32)),
        ],
        [SMEM, square, square, square, once(16, 1024), once(4, 128, 1024), once(4, 128, 1024)]
        + [pl.BlockSpec((1024, 512), lambda i: (0, i))],
        (place, after, mine, theirs, norms, cot_own, cot_other, weights),
        [pltpu.VMEM((1024, 1024), BF)] * 2 + [pltpu.VMEM((1024, 512), F32)],
        limit=60,
        grid=(4,),
        flops=FEED_FLOPS,
        moved=30 * MIB,
    )


def feed_second(place, normed, cot, out_in, back_in, weights):
    square = once(1024, 1024)
    return call(
        feed_second_kernel,
        grad_outs()
        + [
            (once(4, 128, 1024), like(4, 128, 1024, dtype=F32)),
            (once(4, 128, 1024), like(4, 128, 1024)),
            (square, like(1024, 1024)),
        ],
        [SMEM, square, square, square, square, pl.BlockSpec((4, 1, 256, 512), lambda i: (0, i, 0, 0))],
        (place, normed, cot, out_in, back_in, weights),
        [pltpu.VMEM((1024, 1024), F32)] * 2
        + [pltpu.VMEM((1024, 1024), BF)] * 2
        + [pltpu.VMEM((1024, 512), F32)],
        limit=60,
        grid=(4,),
        flops=FEED_FLOPS,
        moved=26 * MIB,
    )


def norm_backward(values, gain, grad):
    center = values - jnp.mean(values, -1, keepdims=True)
    inverse = lax.rsqrt(jnp.mean(center * center, -1, keepdims=True) + EPS)
    hat = center * inverse
    scaled = grad * gain
    back = inverse * (
        scaled - jnp.mean(scaled, -1, keepdims=True) - hat * jnp.mean(scaled * hat, -1, keepdims=True)
    )
    return back, grad * hat


def norm_block(values_of, mine, theirs, base_of, gain, norms, keep):
    gain = norm_row(*gain)
    gain_sum, bias_sum = jnp.zeros((8, 1024), F32), jnp.zeros((8, 1024), F32)
    for low in range(0, 1024, 128):
        rows = slice(low, low + 128)
        grad = mine[rows, :].astype(F32) + theirs[rows, :].astype(F32)
        back, term = norm_backward(values_of(rows), gain, grad)
        keep(rows, base_of(rows) + back)
        gain_sum = gain_sum + jnp.sum(term.reshape(16, 8, 1024), 0)
        bias_sum = bias_sum + jnp.sum(grad.reshape(16, 8, 1024), 0)
    norms[0:1, :] = jnp.sum(gain_sum, 0, keepdims=True)
    norms[1:2, :] = jnp.sum(bias_sum, 0, keepdims=True)


def head_grads(keys, values, one, one_grad, lse, delta, mask):
    weights = jnp.exp2(dot(keys, one, NT) * (LOG2E * HD**-0.5) - lse)
    if mask is not None:
        weights = jnp.where(mask, weights, 0.0)
    slope = dot(values, one_grad, NT)
    return weights.astype(BF), (weights * (slope - delta)).astype(BF)


def cross_bwd_kernel(
    place, after, mine, theirs, cot, gain, weights, normed, text, queries, keys, mix, lse, ids, caption,
    grad_cross, part, norms, text_part, g_own, g_side, g_over, g_low, g_high, low_grad, mix_grad, dq, dkv, grads,
):
    def keep(rows, value):
        grad_cross[rows, :] = value
        low_grad[rows, :] = value.astype(BF)

    norm_block(lambda rows: after[rows, :], mine, theirs, lambda rows: cot[rows, :].astype(F32), (gain, 4), norms, keep)
    w_out = columns_of(weights, 3)
    for low in range(0, 1024, BLOCK):
        mix_grad[low : low + BLOCK, :] = dot(low_grad[low : low + BLOCK, :], w_out).astype(BF)

    def pair_step(pair, carry):
        lanes, v_lanes = at(pair * 128, 128), at(512 + pair * 128, 128)
        dk_sum, dv_sum = jnp.zeros((128, 128), F32), jnp.zeros((128, 128), F32)
        for low in range(0, 1024, 512):
            high = low + 512
            query, grad = queries[low:high, lanes], mix_grad[low:high, lanes]
            product = (grad.astype(F32) * mix[low:high, lanes].astype(F32)).T
            seen = ids[...] == caption[:, low:high]
            back = []
            for head in range(2):
                one, one_grad = one_head(query, head), one_head(grad, head)
                delta = jnp.sum(product[head * HD : (head + 1) * HD], 0, keepdims=True)
                prob, score_grad = head_grads(
                    keys[:, lanes], keys[:, v_lanes], one, one_grad, lse[pair, head : head + 1, low:high], delta, seen
                )
                dv_sum = dv_sum + dot(prob, one_grad)
                dk_sum = dk_sum + dot(score_grad, one)
                back.append(dot(keys[:, lanes], score_grad, TN))
            both = jnp.where(lane_head((128, 1), 0, 0), back[0], back[1])
            dq[low:high, lanes] = (both.T * HD**-0.5).astype(BF)
        dkv[:, lanes] = (dk_sum * HD**-0.5).astype(BF)
        dkv[:, v_lanes] = dv_sum.astype(BF)
        return carry

    lax.fori_loop(0, 4, pair_step, 0)
    w_query = columns_of(weights, 0)
    for low in range(0, 1024, BLOCK):
        part[low : low + BLOCK, :] = dot(dq[low : low + BLOCK, :], w_query, NT).astype(BF)
    w_text = jnp.concatenate([columns_of(weights, 1), columns_of(weights, 2)], 1)
    text_part[...] = dot(dkv[...], w_text, NT).astype(BF)
    for one, (left, right) in enumerate(
        ((normed, dq[...]), (text, dkv[:, :512]), (text, dkv[:, 512:]), (low_grad, mix[...]))
    ):
        grads[...] = dot(left[...], right, TN)
        for s in range(4):
            columns = slice(s * 512 + one * 128, s * 512 + (one + 1) * 128)
            cut_grads(
                place, grads.at[:, s * 128 : (s + 1) * 128], columns, g_own, g_side, g_over, g_low, g_high
            )


def fused_cross_backward(place, after, mine, theirs, cot, gain, weights, normed, text, queries, keys, mix, lse, ids, caption):
    return call(
        cross_bwd_kernel,
        [
            (VMEM, like(1024, 1024, dtype=F32)),
            (VMEM, like(1024, 1024)),
            (VMEM, like(8, 1024, dtype=F32)),
            (VMEM, like(128, 1024)),
        ]
        + [(VMEM, like(*shape)) for shape in GRAD_SHAPES],
        [SMEM] + [VMEM] * 14,
        (place, after, mine, theirs, cot, gain, weights, normed, text, queries, keys, mix, lse, ids, caption),
        [
            pltpu.VMEM((1024, 1024), BF),
            pltpu.VMEM((1024, 512), BF),
            pltpu.VMEM((1024, 512), BF),
            pltpu.VMEM((128, 1024), BF),
            pltpu.VMEM((1024, 512), F32),
        ],
        limit=60,
        flops=9 * 2**30,
        moved=32 * MIB,
    )


def self_bwd_kernel(
    place, after, mine, theirs, base, gain, weights, qkv, mix, lse,
    grad_own, low_grad, norms, dqkv, mix_grad, dk_sum, dv_sum,
):
    core = place[1]

    def keep(rows, value):
        low_grad[rows, :] = value.astype(BF)

        @pl.when(core == (rows.start // 128) % 2)
        def _():
            grad_own[rows.start // 256] = value

    norm_block(lambda rows: after[rows, :], mine, theirs, lambda rows: base[rows, :], (gain, 2), norms, keep)
    w_out = columns_of(weights, 3)
    for low in range(0, 1024, BLOCK):
        mix_grad[low : low + BLOCK, :] = dot(low_grad[low : low + BLOCK, :], w_out).astype(BF)
    causal = causal_mask()

    def pair_step(pair, carry):
        lanes = at(pair * 128, 128)
        k_lanes, v_lanes = at(512 + pair * 128, 128), at(1024 + pair * 128, 128)
        dk_sum[...] = jnp.zeros_like(dk_sum)
        dv_sum[...] = jnp.zeros_like(dv_sum)
        for low in range(0, 1024, BLOCK):
            high = low + BLOCK
            query, grad = qkv[low:high, lanes], mix_grad[low:high, lanes]
            product = (grad.astype(F32) * mix[low:high, lanes].astype(F32)).T
            back = []
            for head in range(2):
                one, one_grad = one_head(query, head), one_head(grad, head)
                delta = jnp.sum(product[head * HD : (head + 1) * HD], 0, keepdims=True)
                total = jnp.zeros((128, BLOCK), F32)
                for start, stop in ((0, low), (low, high)):
                    if start == stop:
                        continue
                    prob, score_grad = head_grads(
                        qkv[start:stop, k_lanes],
                        qkv[start:stop, v_lanes],
                        one,
                        one_grad,
                        lse[pair, head : head + 1, low:high],
                        delta,
                        causal if start == low else None,
                    )
                    dv_sum[start:stop, :] += dot(prob, one_grad)
                    dk_sum[start:stop, :] += dot(score_grad, one)
                    total = total + dot(qkv[start:stop, k_lanes], score_grad, TN)
                back.append(total)
            both = jnp.where(lane_head((128, 1), 0, 0), back[0], back[1])
            dqkv[low:high, lanes] = (both.T * HD**-0.5).astype(BF)
        dqkv[:, k_lanes] = (dk_sum[...] * HD**-0.5).astype(BF)
        dqkv[:, v_lanes] = dv_sum[...].astype(BF)
        return carry

    lax.fori_loop(0, 4, pair_step, 0)


def fused_self_backward(place, after, mine, theirs, base, gain, weights, qkv, mix, lse):
    return call(
        self_bwd_kernel,
        [
            (VMEM, like(4, 128, 1024, dtype=F32)),
            (VMEM, like(1024, 1024)),
            (VMEM, like(8, 1024, dtype=F32)),
            (VMEM, like(1024, 1536)),
        ],
        [SMEM] + [VMEM] * 9,
        (place, after, mine, theirs, base, gain, weights, qkv, mix, lse),
        [pltpu.VMEM((1024, 512), BF), pltpu.VMEM((1024, 128), F32), pltpu.VMEM((1024, 128), F32)],
        limit=60,
        flops=9 * 2**30,
        moved=32 * MIB,
    )


def self_grads_kernel(place, normed, low_grad, dq, dk, dv, mix, g_own, g_side, g_over, g_low, g_high, rows_t, grad_t, grads):
    @pl.when(pl.program_id(0) == 0)
    def _():
        rows_t[...] = normed[...].T
        grad_t[...] = low_grad[...].T

    grads[:, :384] = dot(rows_t[...], jnp.concatenate([dq[...], dk[...], dv[...]], 1))
    grads[:, 384:] = dot(grad_t[...], mix[...])
    cut_grads(place, grads, slice(None), g_own, g_side, g_over, g_low, g_high)


def self_grads(place, normed, low_grad, dqkv, mix):
    square = once(1024, 1024)

    def cut(offset):
        return pl.BlockSpec((1024, 128), lambda i: (0, offset + i))

    return call(
        self_grads_kernel,
        grad_outs(),
        [SMEM, square, square, cut(0), cut(4), cut(8), cut(0)],
        (place, normed, low_grad, dqkv, dqkv, dqkv, mix),
        [pltpu.VMEM((1024, 1024), BF)] * 2 + [pltpu.VMEM((1024, 512), F32)],
        limit=60,
        grid=(4,),
        flops=4 * 2**30,
        moved=12 * MIB,
    )


def self_back_kernel(place, dqkv, weights, kept, sent):
    core = place[1]
    w_in = jnp.concatenate([columns_of(weights, one) for one in range(3)], 1)
    for block in range(4):
        for target, half in ((sent, 1 - core), (kept, core)):
            value = dot(dqkv[at(block * 256 + half * 128, 128), :], w_in, NT)
            target[block] = value.astype(target.dtype)


def self_back(place, dqkv, weights):
    return call(
        self_back_kernel,
        [(VMEM, like(4, 128, 1024, dtype=F32)), (VMEM, like(4, 128, 1024))],
        [SMEM, VMEM, VMEM],
        (place, dqkv, weights),
        limit=60,
        flops=3 * 2**30,
        moved=10 * MIB,
    )


def last_norm_kernel(place, rows, grad_own, mine, theirs, gain, text_part, sums_two, sums_three, *pieces):
    gain_sum, bias_sum = jnp.zeros((8, 1024), F32), jnp.zeros((8, 1024), F32)
    for number in range(4):
        block = (place[2] + number) % 4
        grad = mine[block] + theirs[block].astype(F32)
        back, term = norm_backward(rows[number].astype(F32), norm_row(gain, 0), grad)
        pieces[-number % 4][0:128, :] = (grad_own[block] + back).astype(BF)
        pieces[-number % 4][128:160, :] = text_part[at(block * 32, 32, 32), :]
        gain_sum = gain_sum + jnp.sum(term.reshape(16, 8, 1024), 0)
        bias_sum = bias_sum + jnp.sum(grad.reshape(16, 8, 1024), 0)
    sums = [jnp.sum(gain_sum, 0, keepdims=True), jnp.sum(bias_sum, 0, keepdims=True)]
    sums += [0.5 * sums_two[0:2, :], 0.5 * sums_three[0:2, :], jnp.zeros((10, 1024), F32)]
    sums = jnp.concatenate(sums, 0).astype(BF)
    for piece in pieces:
        piece[160:176, :] = sums


def last_norm(place, rows, grad_own, mine, theirs, gain, text_part, sums_two, sums_three):
    return call(
        last_norm_kernel,
        [(VMEM, like(176, 1024))] * 4,
        [SMEM] + [VMEM] * 8,
        (place, rows, grad_own, mine, theirs, gain, text_part, sums_two, sums_three),
    )


def finish_kernel(place, out_keep, theirs, *pieces):
    for number, piece in enumerate(pieces):
        block = (place[2] + 4 - number) % 4
        piece[...] = (out_keep[block] + theirs[block].astype(F32)).astype(BF)


def finish(place, out_keep, theirs):
    return call(
        finish_kernel,
        [(VMEM, like(128, 1024))] * 4,
        [SMEM] + [VMEM] * 2,
        (place, out_keep, theirs),
    )


def part_kernel(place, *refs):
    pieces, mine, sent = refs[:4], refs[4], refs[5]
    core, top = place[1], place[2]
    for step, piece in enumerate(pieces):
        image = (top + step) % 4

        @pl.when(image // 2 == core)
        def _():
            mine[image % 2] = piece[...]

        @pl.when(image // 2 != core)
        def _():
            sent[image % 2] = piece[...]

    if pieces[0].shape[0] > 160:
        total = 0.0
        for piece in pieces:
            total = total + piece[160:176, :].astype(F32)
        mine[0, 160:176, :] = total.astype(BF)
        sent[0, 160:176, :] = total.astype(BF)


def part_images(place, pieces):
    return call(
        part_kernel,
        [(VMEM, like(2, *pieces[0].shape))] * 2,
        [SMEM] + [VMEM] * 4,
        (place, *pieces),
    )


def land_kernel(place, mine, taken, rows, *more):
    core = place[1]
    for one in range(2):
        rows[one, at(core * 128, 128), :] = mine[one, 0:128, :].astype(rows.dtype)
        rows[one, at((1 - core) * 128, 128), :] = taken[one, 0:128, :].astype(rows.dtype)
        if more:
            more[0][one] = mine[one, 128:160, :].astype(F32) + taken[one, 128:160, :].astype(F32)
    if more:
        more[1][...] = mine[0, 160:168, :].astype(F32) + taken[0, 160:168, :].astype(F32)


def land(place, mine, taken, dtype):
    outs = [(VMEM, like(2, 256, 1024, dtype=dtype))]
    if mine.shape[1] > 128:
        outs += [(VMEM, like(2, 32, 1024, dtype=F32)), (VMEM, like(8, 1024, dtype=F32))]
    return call(land_kernel, outs, [SMEM, VMEM, VMEM], (place, mine, taken))


def relay_kernel(over, side, from_side, from_over, to_over, to_side):
    to_over[0:128, :] = (over[0:128, :].astype(F32) + from_side[...].astype(F32)).astype(BF)
    to_over[128:256, :] = over[128:256, :]
    to_side[0:128, :] = side[0:128, :]
    to_side[128:256, :] = (side[128:256, :].astype(F32) + from_over[...].astype(F32)).astype(BF)


def relay(over, side, from_side, from_over):
    return call(
        relay_kernel,
        [(VMEM, like(256, 2048))] * 2,
        [VMEM] * 4,
        (over, side, from_side, from_over),
        limit=60,
        moved=5 * MIB,
    )


def plane_sum_kernel(place, own, over, side, keep, *sent):
    for s in range(4):
        columns = at((place[2] + s) % 4 * 512, 512, 512)
        total = own[:, columns].astype(F32) + over[:, columns].astype(F32) + side[:, columns].astype(F32)
        if s:
            sent[s - 1][...] = total.astype(BF)
        else:
            keep[...] = total


def plane_sum(place, own, over, side):
    return call(
        plane_sum_kernel,
        [(VMEM, like(256, 512, dtype=F32))] + [(VMEM, like(256, 512))] * 3,
        [SMEM] + [VMEM] * 3,
        (place, own, over, side),
        limit=60,
        moved=5 * MIB,
    )


def plane_sum_whole_kernel(own, over, side, whole):
    for step in range(4):
        columns = slice(step * 512, (step + 1) * 512)
        total = own[:, columns].astype(F32) + over[:, columns].astype(F32) + side[:, columns].astype(F32)
        whole[step * 256 : (step + 1) * 256, :] = total.astype(BF)


def plane_sum_whole(own, over, side):
    return call(
        plane_sum_whole_kernel,
        [(VMEM, like(1024, 512))],
        [VMEM] * 3,
        (own, over, side),
    )[0]


def line_sum_kernel(place, keep, one, two, three, mine, other):
    core = place[1]
    for target, half in ((other, 1 - core), (mine, core)):
        rows = at(half * 128, 128)
        total = keep[rows, :]
        for part in (one, two, three):
            total = total + part[rows, :].astype(F32)
        target[...] = total.astype(target.dtype)


def line_sum(place, keep, parts):
    return call(
        line_sum_kernel,
        [(VMEM, like(128, 512, dtype=F32)), (VMEM, like(128, 512))],
        [SMEM] + [VMEM] * 4,
        (place, keep, *parts),
        limit=60,
        moved=2 * MIB,
    )


def spread_kernel(place, mine, other, *outs):
    core, columns = place[1], mine.shape[1] // len(outs)
    for one, out in enumerate(outs):
        cut = slice(one * columns, (one + 1) * columns)
        out[:, at(core * columns, columns)] = mine[:, cut].astype(F32)
        out[:, at((1 - core) * columns, columns)] = other[:, cut].astype(F32)


def spread(place, mine, other):
    return call(
        spread_kernel,
        [(VMEM, like(128, 256, dtype=F32))] * 4,
        [SMEM] + [VMEM] * 2,
        (place, mine, other),
        limit=60,
        moved=MIB,
    )


def spread_feed_kernel(place, mine_one, other_one, mine_two, other_two, *outs):
    core = place[1]
    for part, (mine, other) in enumerate(((mine_one, other_one), (mine_two, other_two))):
        for one, out in enumerate(outs):
            cut = slice(one * 256, (one + 1) * 256)
            out[:, at(core * 512 + part * 256, 256)] = mine[:, cut].astype(F32)
            out[:, at((1 - core) * 512 + part * 256, 256)] = other[:, cut].astype(F32)


def spread_feed(place, *halves):
    return call(
        spread_feed_kernel,
        [(VMEM, like(128, 1024, dtype=F32))] * 2,
        [SMEM] + [VMEM] * 4,
        (place, *halves),
        limit=60,
        moved=2 * MIB,
    )


tie = lax.optimization_barrier


def packed_layer(args):
    image_rows, text_rows, segment_ids, cotangent, *others = args
    weights, norms = others[:10], others[10:]
    chip, core, top = lax.axis_index("chip"), lax.axis_index("core"), lax.axis_index("hi")
    place = jnp.stack([chip, core, top, core * 2 + top % 2]).astype(jnp.int32)

    def swap(value):
        return lax.ppermute(value, "core", [(0, 1), (1, 0)])

    def across(value, bit):
        return lax.ppermute(value, "chip", [(i, i ^ bit) for i in range(4)])

    def shift(value, step):
        return lax.ppermute(value, "hi", [((i + step) % 4, i) for i in range(4)])

    def line(part):
        return [shift(part, step) for step in range(1, 4)]

    def exchange(pieces):
        return [pieces[0]] + [shift(piece, step) for step, piece in enumerate(pieces) if step]

    def gather_line(part):
        return lax.all_gather(part, "hi")

    def sides(value):
        return [across(value, 1), across(value, 2)]

    def corners(pair, cut):
        return [across(pair[0][:cut], 2), across(pair[1][cut:], 1)]

    def grad_corners(grads):
        return [across(grads[3], 1), across(grads[4], 2)]

    def grad_sides(grads, got):
        to_over, to_side = relay(grads[2], grads[1], *got)
        return [across(to_over, 2), across(to_side, 1)]

    def halves(total):
        cut = total.reshape(2, 128, 512)
        sent = lax.dynamic_index_in_dim(cut, 1 - core, 0, False)
        return lax.dynamic_index_in_dim(cut, core, 0, False), swap(sent)

    ids_wide = jnp.pad(segment_ids.astype(BF)[:, None, :], ((0, 0), (0, 15), (0, 896)))
    norms_wide = jnp.pad(jnp.stack(norms).astype(BF), ((0, 10), (0, 384)))
    keep, sent, rows_keep, rows_sent, cot_keep, cot_sent, text_pair = prepare(
        place, image_rows, text_rows, ids_wide, cotangent, norms_wide, weights
    )
    v = {"rows_keep": rows_keep, "cot_keep": cot_keep, "text_pair": text_pair}
    v["taken"], v["rows_taken"], v["cot_taken"] = swap(sent), swap(rows_sent), swap(cot_sent)
    v["text_taken"] = swap(text_pair)
    v = tie(v)
    *v["singles"], v["near"] = join(place, keep, v.pop("taken"))
    v = tie(v)

    v["near"] = [v["near"], *sides(v["near"])]
    lines = line(v["singles"][0])
    v["pieces"] = pick(place, v.pop("rows_keep"), v.pop("rows_taken"))
    v["cot_pieces"] = pick(place, v.pop("cot_keep"), v.pop("cot_taken"))
    v["text_pieces"] = pick(place, v.pop("text_pair"), v.pop("text_taken"))
    v = tie(v)
    v["near"] += corners(v["near"][1:], 128)
    v["line"] = lines
    v = tie(v)

    rest = stack(v.pop("line"))
    v["far_self"] = [rest, *sides(rest)]
    pieces = exchange(v.pop("pieces"))
    line_cross = gather_line(v["singles"][1])
    v = tie(v)
    v["far_self"] += corners(v["far_self"][1:], 384)
    v["pieces"], v["line_cross"] = pieces, line_cross
    v = tie(v)
    v["rows_own"] = stack([piece[None] for piece in v.pop("pieces")])
    v["rows_other"] = swap(v["rows_own"])
    v["w_self"], v["norms"] = assemble_first(place, v.pop("near"), v.pop("far_self"))
    line_one = gather_line(v["singles"][2])
    v = tie(v)

    v["far_cross"] = sides(v["line_cross"])
    v["text_pieces"] = exchange(v["text_pieces"])
    v["line_one"] = line_one
    v["normed_one"], v["qkv"], v["self_mix"], v["self_lse"], v["mine"] = fused_self_forward(
        place, v["rows_own"], v["rows_other"], v["norms"], v["w_self"]
    )
    v = tie(v)

    v["theirs"] = swap(v["mine"])
    v["far_cross"] += corners(v["far_cross"], 2)
    line_two = gather_line(v.pop("singles")[3])
    text_pieces = v.pop("text_pieces")
    v["text"] = arrange(place, text_pieces)
    ids = text_pieces[0][32, :128].astype(jnp.int32)
    v["caption"] = jnp.repeat(ids, 8)[None, :]
    v["ids"] = ids[:, None]
    v = tie(v)

    v["far_one"] = sides(v["line_one"])
    v["line_two"] = line_two
    v["cot_pieces"] = exchange(v["cot_pieces"])
    v["w_cross"] = assemble(place, v.pop("line_cross"), v.pop("far_cross"))
    v["after_attn"], v["normed_two"], v["queries"], v["keys"], v["cross_mix"], v["cross_lse"], v["mine"] = (
        fused_cross_forward(
            place, v["rows_own"], v.pop("rows_other"), v["mine"], v["theirs"], v["norms"], v["text"], v["ids"],
            v["caption"], v["w_cross"],
        )
    )
    v = tie(v)

    v["theirs"] = swap(v["mine"])
    v["far_one"] += corners(v["far_one"], 2)
    v["cot_own"] = stack([piece[None] for piece in v.pop("cot_pieces")])
    v["cot_other"] = swap(v["cot_own"])
    w_two = lax.all_gather(v.pop("line_two"), "chip")
    v = tie(v)

    v["w_two"] = w_two
    w_one = assemble(place, v.pop("line_one"), v.pop("far_one"))
    v["grads_one"], v["after_cross"], v["normed_three"], v["cot"], v["out_sum"], v["back_sum"] = feed_first(
        place, v["after_attn"], v["mine"], v["theirs"], v["norms"], v.pop("cot_own"), v.pop("cot_other"), w_one
    )
    v = tie(v)

    total_one = lax.psum_scatter(v.pop("grads_one"), "chip", scatter_dimension=0, tiled=False)
    *v["grads_two"], v["out_keep"], v["out_sent"], v["mine"] = feed_second(
        place, v.pop("normed_three"), v["cot"], v.pop("out_sum"), v.pop("back_sum"), v.pop("w_two")
    )
    v = tie(v)

    v["theirs"] = swap(v["mine"])
    v["out_theirs"] = swap(v.pop("out_sent"))
    v = tie(v)
    v["got_two"] = grad_corners(v["grads_two"])
    v["pieces"] = exchange(finish(place, v.pop("out_keep"), v.pop("out_theirs")))
    v["grad_cross"], v["part"], v["norms_three"], v["text_part"], *v["grads_three"] = fused_cross_backward(
        place, v.pop("after_cross"), v.pop("mine"), v.pop("theirs"), v.pop("cot"), v["norms"], v.pop("w_cross"),
        v.pop("normed_two"), v.pop("text"), v.pop("queries"), v.pop("keys"), v.pop("cross_mix"),
        v.pop("cross_lse"), v.pop("ids"), v.pop("caption"),
    )
    v = tie(v)

    v["theirs"] = swap(v["part"])
    v["total_one"] = total_one
    v["to_two"] = relay(v["grads_two"][2], v["grads_two"][1], *v.pop("got_two"))
    v = tie(v)

    to_two = v.pop("to_two")
    v["sides_two"] = [across(to_two[0], 2), across(to_two[1], 1)]
    v["got_three"] = grad_corners(v["grads_three"])
    v["line_one"] = lax.psum_scatter(v.pop("total_one"), "hi", scatter_dimension=0, tiled=False)
    v["grad_own"], v["low_grad"], v["norms_two"], v["dqkv"] = fused_self_backward(
        place, v.pop("after_attn"), v.pop("part"), v.pop("theirs"), v.pop("grad_cross"), v["norms"], v["w_self"],
        v.pop("qkv"), v["self_mix"], v.pop("self_lse"),
    )
    v = tie(v)

    v["sides_three"] = grad_sides(v["grads_three"], v.pop("got_three"))
    total_two = plane_sum_whole(v.pop("grads_two")[0], *v.pop("sides_two"))
    line_two = lax.psum_scatter(total_two, "hi", scatter_dimension=0, tiled=True)
    v["grads_four"] = self_grads(place, v.pop("normed_one"), v.pop("low_grad"), v["dqkv"], v.pop("self_mix"))
    mine, sent = part_images(place, v.pop("pieces"))
    (v["result"],) = land(place, mine, swap(sent), BF)
    v["feed_one"] = halves(v.pop("line_one"))
    v = tie(v)

    v["got_four"] = grad_corners(v["grads_four"])
    total_three, dqkv = tie((plane_sum_whole(v.pop("grads_three")[0], *v.pop("sides_three")), v.pop("dqkv")))
    line_three = lax.psum_scatter(total_three, "hi", scatter_dimension=0, tiled=True)
    v["line_two"] = line_two
    v["kept"], v["sent"] = self_back(place, dqkv, v.pop("w_self"))
    v = tie(v)

    v["sides_four"] = grad_sides(v["grads_four"], v.pop("got_four"))
    pieces = last_norm(
        place, v.pop("rows_own"), v.pop("grad_own"), v.pop("kept"), swap(v.pop("sent")), v.pop("norms"),
        v.pop("text_part"), v.pop("norms_two"), v.pop("norms_three"),
    )
    input_pieces = exchange(pieces)
    v = tie(v)

    v["kept"], *sums_four = plane_sum(place, v.pop("grads_four")[0], *v.pop("sides_four"))
    v["line_four"] = [shift(piece, 3 - i) for i, piece in enumerate(sums_four)]
    v["feed_grads"] = spread_feed(place, *v.pop("feed_one"), *halves(v.pop("line_two")))
    later = tie((place, sums_four))[0]
    mine, sent = part_images(later, input_pieces)
    v["input_grad"], v["text_grad"], sums = land(place, mine, swap(sent), F32)
    sums = sums + across(sums, 1)
    sums = sums + across(sums, 2)
    v["sums"] = lax.dynamic_slice_in_dim(sums, (chip * 2 + core) * 128, 128, 1)
    v["cross_grads"] = spread(place, *halves(line_three))
    v = tie(v)

    kept, sent = line_sum(place, v.pop("kept"), v.pop("line_four"))
    own_grads = spread(place, kept, swap(sent))
    return (
        v["result"], v["input_grad"], v["text_grad"], *own_grads, *v["cross_grads"], *v["feed_grads"],
        *[v["sums"][i] for i in range(6)],
    )


def solution(mesh):
    fsdp, tensor = mesh.shape["fsdp"], mesh.shape["tensor"]

    def run(*args):
        images = args[0].shape[0] // fsdp
        tops = 2 * images
        shape = {"chip": fsdp // 2, "core": 2, "hi": tops, "lo": tensor // tops}
        fine = Mesh(mesh.devices.reshape(tuple(shape.values())), tuple(shape))
        first, second = ("chip", "core"), ("hi", "lo")
        wide, weight, norm = P(first, second, None), P(first, second), P(first)
        outs = (wide,) * 3 + (weight,) * 10 + (norm,) * 6
        packed = (
            (fsdp, tensor, images) == (8, 4, 2)
            and args[0].shape[1:] == (1024, 1024)
            and args[1].shape[1:] == (128, 1024)
            and args[12].shape == (1024, 4096)
        )
        return jax.shard_map(
            lambda *local: packed_layer(local) if packed else layer(shape, local),
            mesh=fine,
            in_specs=(wide, wide, P(first, None), wide) + (weight,) * 10 + (norm,) * 6,
            out_specs=outs,
            check_vma=False,
        )(*args)

    return run
```

```python
import functools
import math

import jax
import jax.numpy as jnp
from jax import lax
from jax.experimental import pallas as pl
from jax.experimental.pallas import tpu as pltpu
from jax.sharding import Mesh
from jax.sharding import PartitionSpec as P

HD = 64
EPS = 1e-05
NEG = -1e30
LOG2E = math.log2(math.e)
BF = jnp.bfloat16
F32 = jnp.float32
NT = (((1,), (1,)), ((), ()))
TN = (((0,), (0,)), ((), ()))
NN = (((1,), (0,)), ((), ()))


def dot(left, right, dims=NN):
    return lax.dot_general(left, right, dims, preferred_element_type=F32)


def lane_head(shape, axis, head):
    return lax.broadcasted_iota(jnp.int32, shape, axis) // HD == head


def self_forward_kernel(q_ref, k_ref, v_ref, mix_ref, lse_ref, *, block):
    length = q_ref.shape[0]
    scale = LOG2E * HD**-0.5
    causal = lax.broadcasted_iota(jnp.int32, (block, block), 0) <= lax.broadcasted_iota(
        jnp.int32, (block, block), 1
    )
    for at in range(length // block):
        lo, hi = at * block, (at + 1) * block
        query = q_ref[lo:hi, :]
        mixes = []
        for head in range(2):
            one = jnp.where(lane_head((1, 2 * HD), 1, head), query, jnp.zeros_like(query))
            diag = jnp.where(causal, dot(k_ref[lo:hi, :], one, NT), NEG)
            peak = jnp.max(diag, 0, keepdims=True)
            if at:
                past = dot(k_ref[:lo, :], one, NT)
                peak = jnp.maximum(peak, jnp.max(past, 0, keepdims=True))
            weights = jnp.exp2((diag - peak) * scale)
            total = jnp.sum(weights, 0, keepdims=True)
            mixed = dot(v_ref[lo:hi, :], weights.astype(BF), TN)
            if at:
                weights = jnp.exp2((past - peak) * scale)
                total = total + jnp.sum(weights, 0, keepdims=True)
                mixed = mixed + dot(v_ref[:lo, :], weights.astype(BF), TN)
            mixes.append(mixed / total)
            lse_ref[0, head : head + 1, lo:hi] = peak * scale + jnp.log2(total)
        both = jnp.where(lane_head((2 * HD, 1), 0, 0), mixes[0], mixes[1])
        mix_ref[lo:hi, :] = both.T.astype(BF)


def self_backward_kernel(
    q_ref, k_ref, v_ref, mix_ref, grad_ref, lse_ref, dq_ref, dk_ref, dv_ref, dk_sum, dv_sum, *, block
):
    length = q_ref.shape[0]
    scale = LOG2E * HD**-0.5
    causal = lax.broadcasted_iota(jnp.int32, (block, block), 0) <= lax.broadcasted_iota(
        jnp.int32, (block, block), 1
    )
    dk_sum[...] = jnp.zeros_like(dk_sum)
    dv_sum[...] = jnp.zeros_like(dv_sum)
    for at in range(length // block):
        lo, hi = at * block, (at + 1) * block
        query = q_ref[lo:hi, :]
        grad = grad_ref[lo:hi, :]
        product = (grad.astype(F32) * mix_ref[lo:hi, :].astype(F32)).T
        grads = []
        for head in range(2):
            picked = lane_head((1, 2 * HD), 1, head)
            one = jnp.where(picked, query, jnp.zeros_like(query))
            one_grad = jnp.where(picked, grad, jnp.zeros_like(grad))
            delta = jnp.sum(product[head * HD : (head + 1) * HD], 0, keepdims=True)
            lse = lse_ref[0, head : head + 1, lo:hi]
            total = jnp.zeros((2 * HD, block), F32)
            for start, stop in ((0, lo), (lo, hi)):
                if start == stop:
                    continue
                keys = k_ref[start:stop, :]
                weights = jnp.exp2(dot(keys, one, NT) * scale - lse)
                if start == lo:
                    weights = jnp.where(causal, weights, 0.0)
                slope = dot(v_ref[start:stop, :], one_grad, NT)
                score_grad = (weights * (slope - delta)).astype(BF)
                dv_sum[start:stop, :] += dot(weights.astype(BF), one_grad)
                dk_sum[start:stop, :] += dot(score_grad, one)
                total = total + dot(keys, score_grad, TN)
            grads.append(total)
        both = jnp.where(lane_head((2 * HD, 1), 0, 0), grads[0], grads[1])
        dq_ref[lo:hi, :] = (both.T * HD**-0.5).astype(BF)
    dk_ref[...] = (dk_sum[...] * HD**-0.5).astype(BF)
    dv_ref[...] = dv_sum[...].astype(BF)


def cross_forward_kernel(q_ref, k_ref, v_ref, ids_ref, caption_ref, mix_ref, lse_ref, *, block):
    length = q_ref.shape[0]
    scale = LOG2E * HD**-0.5
    for at in range(length // block):
        lo, hi = at * block, (at + 1) * block
        query = q_ref[lo:hi, :]
        seen = ids_ref[...] == caption_ref[:, lo:hi]
        mixes = []
        for head in range(2):
            one = jnp.where(lane_head((1, 2 * HD), 1, head), query, jnp.zeros_like(query))
            scores = jnp.where(seen, dot(k_ref[...], one, NT), NEG)
            peak = jnp.max(scores, 0, keepdims=True)
            weights = jnp.exp2((scores - peak) * scale)
            total = jnp.sum(weights, 0, keepdims=True)
            mixes.append(dot(v_ref[...], weights.astype(BF), TN) / total)
            lse_ref[0, head : head + 1, lo:hi] = peak * scale + jnp.log2(total)
        both = jnp.where(lane_head((2 * HD, 1), 0, 0), mixes[0], mixes[1])
        mix_ref[lo:hi, :] = both.T.astype(BF)


def cross_backward_kernel(
    q_ref, k_ref, v_ref, mix_ref, grad_ref, lse_ref, ids_ref, caption_ref, dq_ref, dk_ref, dv_ref, *, block
):
    length = q_ref.shape[0]
    scale = LOG2E * HD**-0.5
    keys, values = k_ref[...], v_ref[...]
    dk_sum = jnp.zeros(keys.shape, F32)
    dv_sum = jnp.zeros(keys.shape, F32)
    for at in range(length // block):
        lo, hi = at * block, (at + 1) * block
        query = q_ref[lo:hi, :]
        grad = grad_ref[lo:hi, :]
        product = (grad.astype(F32) * mix_ref[lo:hi, :].astype(F32)).T
        seen = ids_ref[...] == caption_ref[:, lo:hi]
        grads = []
        for head in range(2):
            picked = lane_head((1, 2 * HD), 1, head)
            one = jnp.where(picked, query, jnp.zeros_like(query))
            one_grad = jnp.where(picked, grad, jnp.zeros_like(grad))
            delta = jnp.sum(product[head * HD : (head + 1) * HD], 0, keepdims=True)
            lse = lse_ref[0, head : head + 1, lo:hi]
            weights = jnp.where(seen, jnp.exp2(dot(keys, one, NT) * scale - lse), 0.0)
            slope = dot(values, one_grad, NT)
            score_grad = (weights * (slope - delta)).astype(BF)
            dv_sum = dv_sum + dot(weights.astype(BF), one_grad)
            dk_sum = dk_sum + dot(score_grad, one)
            grads.append(dot(keys, score_grad, TN))
        both = jnp.where(lane_head((2 * HD, 1), 0, 0), grads[0], grads[1])
        dq_ref[lo:hi, :] = (both.T * HD**-0.5).astype(BF)
    dk_ref[...] = (dk_sum * HD**-0.5).astype(BF)
    dv_ref[...] = dv_sum.astype(BF)


def feed_kernel(
    rows_ref, cot_ref, win_ref, wout_ref, out_in, back_in, gin_ref, gout_ref, out_ref, back_ref, rows_t, cot_t, *, first
):
    step = pl.program_id(0)

    @pl.when(step == 0)
    def _():
        rows_t[...] = rows_ref[...].T
        cot_t[...] = cot_ref[...].T
        if first:
            out_ref[...] = jnp.zeros_like(out_ref)
            back_ref[...] = jnp.zeros_like(back_ref)
        else:
            out_ref[...] = out_in[...]
            back_ref[...] = back_in[...]

    pre = dot(rows_ref[...], win_ref[...])
    square = pre * pre
    slope = math.sqrt(2.0 / math.pi)
    bent = jnp.tanh(pre * (slope + slope * 0.044715 * square))
    half = 0.5 * (1.0 + bent)
    act = (pre * half).astype(BF)
    out_ref[...] += dot(act, wout_ref[...], NT)
    gout_ref[...] = dot(cot_t[...], act).astype(BF)
    bend = half + pre * (0.5 * (1.0 - bent * bent)) * (slope + 3.0 * slope * 0.044715 * square)
    pre_grad = (dot(cot_ref[...], wout_ref[...]) * bend).astype(BF)
    gin_ref[...] = dot(rows_t[...], pre_grad).astype(BF)
    back_ref[...] += dot(pre_grad, win_ref[...], NT)


VMEM_LIMIT = 60 * 1024 * 1024


def params():
    return pltpu.CompilerParams(vmem_limit_bytes=VMEM_LIMIT)


def column(rows, offset):
    return pl.BlockSpec((rows, 2 * HD), lambda i: (0, offset + i))


def self_forward(packed):
    length, width = packed.shape
    pairs = width // (6 * HD)
    return pl.pallas_call(
        functools.partial(self_forward_kernel, block=256),
        grid=(pairs,),
        in_specs=[column(length, 0), column(length, pairs), column(length, 2 * pairs)],
        out_specs=[column(length, 0), pl.BlockSpec((1, 2, length), lambda i: (i, 0, 0))],
        out_shape=[
            jax.ShapeDtypeStruct((length, pairs * 2 * HD), BF),
            jax.ShapeDtypeStruct((pairs, 2, length), F32),
        ],
        compiler_params=params(),
        cost_estimate=pl.CostEstimate(
            flops=8 * pairs * length * length * 2 * HD * 2,
            bytes_accessed=8 * pairs * length * 2 * HD,
            transcendentals=2 * pairs * length * length,
        ),
    )(packed, packed, packed)


def self_backward(packed, mix, grad, lse):
    length, width = packed.shape
    pairs = width // (6 * HD)
    part = jax.ShapeDtypeStruct((length, pairs * 2 * HD), BF)
    return pl.pallas_call(
        functools.partial(self_backward_kernel, block=256),
        grid=(pairs,),
        in_specs=[
            column(length, 0),
            column(length, pairs),
            column(length, 2 * pairs),
            column(length, 0),
            column(length, 0),
            pl.BlockSpec((1, 2, length), lambda i: (i, 0, 0)),
        ],
        out_specs=[column(length, 0)] * 3,
        out_shape=[part] * 3,
        scratch_shapes=[pltpu.VMEM((length, 2 * HD), F32)] * 2,
        compiler_params=params(),
        cost_estimate=pl.CostEstimate(
            flops=20 * pairs * length * length * 2 * HD * 2,
            bytes_accessed=16 * pairs * length * 2 * HD,
            transcendentals=2 * pairs * length * length,
        ),
    )(packed, packed, packed, mix, grad, lse)


def cross_forward(queries, keys, ids, captions):
    length, width = queries.shape
    texts = keys.shape[0]
    pairs = width // (2 * HD)
    return pl.pallas_call(
        functools.partial(cross_forward_kernel, block=min(512, length)),
        grid=(pairs,),
        in_specs=[
            column(length, 0),
            column(texts, 0),
            column(texts, pairs),
            pl.BlockSpec((texts, 1), lambda i: (0, 0)),
            pl.BlockSpec((1, length), lambda i: (0, 0)),
        ],
        out_specs=[column(length, 0), pl.BlockSpec((1, 2, length), lambda i: (i, 0, 0))],
        out_shape=[
            jax.ShapeDtypeStruct((length, width), BF),
            jax.ShapeDtypeStruct((pairs, 2, length), F32),
        ],
        compiler_params=params(),
    )(queries, keys, keys, ids, captions)


def cross_backward(queries, keys, mix, grad, lse, ids, captions):
    length, width = queries.shape
    texts = keys.shape[0]
    pairs = width // (2 * HD)
    return pl.pallas_call(
        functools.partial(cross_backward_kernel, block=min(512, length)),
        grid=(pairs,),
        in_specs=[
            column(length, 0),
            column(texts, 0),
            column(texts, pairs),
            column(length, 0),
            column(length, 0),
            pl.BlockSpec((1, 2, length), lambda i: (i, 0, 0)),
            pl.BlockSpec((texts, 1), lambda i: (0, 0)),
            pl.BlockSpec((1, length), lambda i: (0, 0)),
        ],
        out_specs=[column(length, 0), column(texts, 0), column(texts, 0)],
        out_shape=[
            jax.ShapeDtypeStruct((length, width), BF),
            jax.ShapeDtypeStruct((texts, width), BF),
            jax.ShapeDtypeStruct((texts, width), BF),
        ],
        compiler_params=params(),
    )(queries, keys, keys, mix, grad, lse, ids, captions)


def feed(rows, cot, w_in, w_out, sums):
    length, width = rows.shape
    units = w_in.shape[1]
    block = min(256, units)
    whole = pl.BlockSpec((length, width), lambda i: (0, 0))
    cut = pl.BlockSpec((width, block), lambda i: (0, i))
    first = sums is None
    kernel = functools.partial(feed_kernel, first=first)
    operands = [rows, cot, w_in, w_out]
    specs = [whole, whole, cut, cut]
    if first:
        body = lambda a, b, c, d, *rest: kernel(a, b, c, d, None, None, *rest)
    else:
        body = kernel
        operands += list(sums)
        specs += [whole, whole]
    total = jax.ShapeDtypeStruct((length, width), F32)
    part = jax.ShapeDtypeStruct((width, units), BF)
    return pl.pallas_call(
        body,
        grid=(units // block,),
        in_specs=specs,
        out_specs=[cut, cut, whole, whole],
        out_shape=[part, part, total, total],
        scratch_shapes=[pltpu.VMEM((width, length), BF)] * 2,
        compiler_params=params(),
        cost_estimate=pl.CostEstimate(
            flops=12 * length * width * units,
            bytes_accessed=8 * width * units + 8 * length * width,
            transcendentals=length * units,
        ),
    )(*operands)


def norm_parts(values):
    center = values - jnp.mean(values, -1, keepdims=True)
    inverse = lax.rsqrt(jnp.mean(center * center, -1, keepdims=True) + EPS)
    return center * inverse, inverse


def layer_norm(values, gain, offset):
    return (norm_parts(values)[0] * gain + offset).astype(BF)


def norm_back(values, gain, grad):
    hat, inverse = norm_parts(values)
    scaled = grad * gain
    back = inverse * (
        scaled
        - jnp.mean(scaled, -1, keepdims=True)
        - hat * jnp.mean(scaled * hat, -1, keepdims=True)
    )
    lead = tuple(range(values.ndim - 1))
    return back, jnp.sum(grad * hat, lead), jnp.sum(grad, lead)


def layer(shape, args):
    chips, tops, lows = shape["chip"], shape["hi"], shape["lo"]
    (
        image_rows,
        text_rows,
        segment_ids,
        cotangent,
        query_weight,
        key_weight,
        value_weight,
        attn_output,
        cross_query,
        cross_key,
        cross_value,
        cross_output,
        hidden_in,
        hidden_out,
        *norms,
    ) = args
    images, rows, width = image_rows.shape
    texts = text_rows.shape[1]
    half_rows = rows // 2
    length = rows * lows * tops
    shard = query_weight.shape[0]
    chip, core = lax.axis_index("chip"), lax.axis_index("core")
    top = lax.axis_index("hi")
    own_slot = core * images + top % images

    def swap(value):
        return lax.ppermute(value, "core", [(0, 1), (1, 0)])

    def across(value, bit):
        return lax.ppermute(value, "chip", [(i, i ^ bit) for i in range(chips)])

    def shift(value, step):
        return lax.ppermute(value, "hi", [((i + step) % tops, i) for i in range(tops)])

    def matching(number, back):
        pairs = []
        for source_core in range(2):
            for source_top in range(tops):
                slot = source_top ^ number
                target = (slot // images) * tops + source_core * images + slot % images
                source = source_core * tops + source_top
                pairs.append((target, source) if back else (source, target))
        return pairs

    def to_image(piece_of):
        got = [
            lax.ppermute(piece_of(top ^ number), ("core", "hi"), matching(number, False))
            for number in range(tops)
        ]
        whole = jnp.stack(got)
        return jnp.stack(
            [lax.dynamic_index_in_dim(whole, own_slot ^ place, 0, False) for place in range(tops)]
        )

    def from_image(pieces):
        return [
            lax.ppermute(
                lax.dynamic_index_in_dim(pieces, own_slot ^ number, 0, False),
                ("core", "hi"),
                matching(number, True),
            )
            for number in range(tops)
        ]

    def image_piece(value):
        def piece(slot):
            return lax.dynamic_slice(
                value,
                (slot % images, (slot // images) * half_rows, 0),
                (1, half_rows, width),
            )[0]

        return piece

    def to_rows(pieces):
        got = jnp.stack(from_image(pieces))
        ordered = jnp.stack(
            [lax.dynamic_index_in_dim(got, top ^ slot, 0, False) for slot in range(tops)]
        )
        ordered = ordered.reshape(2, images, half_rows, width)
        return jnp.swapaxes(ordered, 0, 1).reshape(images, rows, width)

    def tp_gather(mine):
        if lows == 1:
            other = swap(mine)
            first = jnp.where(core == 0, mine, other)
            second = jnp.where(core == 0, other, mine)
            return jnp.stack([first, second], 1).reshape(length, width)
        every = lax.all_gather(mine, ("lo", "core"))
        every = every.reshape(lows * 2, tops, half_rows, width)
        return jnp.swapaxes(every, 0, 1).reshape(length, width)

    def tp_reduce(partial):
        if lows == 1:
            cut = partial.reshape(tops, 2, half_rows, width)
            sent = lax.dynamic_index_in_dim(cut, 1 - core, 1, False).astype(BF)
            kept = lax.dynamic_index_in_dim(cut, core, 1, False)
            return kept + swap(sent).astype(F32)
        cut = jnp.swapaxes(partial.astype(BF).reshape(tops, lows * 2, half_rows, width), 0, 1)
        cut = lax.psum_scatter(cut, ("lo", "core"), scatter_dimension=0, tiled=False)
        return cut.astype(F32)

    def core_half(weight, which):
        columns = weight.shape[1] // 2
        return lax.dynamic_slice_in_dim(weight, which * columns, columns, 1)

    def pack(which):
        feeds = [core_half(weight, which) for weight in (hidden_in, hidden_out)]
        cuts = feeds[0].shape[1] // 2
        groups = [
            [core_half(w, which) for w in (query_weight, key_weight, value_weight, attn_output)],
            [core_half(w, which) for w in (cross_query, cross_key, cross_value, cross_output)],
            [w[:, :cuts] for w in feeds],
            [w[:, cuts:] for w in feeds],
        ]
        return jnp.concatenate([w for group in groups for w in group], 1)

    kept = pack(core)
    taken = swap(pack(1 - core))
    own = jnp.concatenate(
        [jnp.where(core == 0, kept, taken), jnp.where(core == 0, taken, kept)], 0
    )
    block_rows = 2 * shard
    group_width = own.shape[1] // 4

    def plane_gather(piece):
        if chips != 4:
            return lax.all_gather(piece, "chip", axis=0, tiled=True)
        side = across(piece, 1)
        over = across(piece, 2)
        corner_low = across(side[:shard], 2)
        corner_high = across(over[shard:], 1)
        corner = jnp.concatenate([corner_low, corner_high], 0)
        pieces = jnp.stack([piece, side, over, corner])
        ordered = [lax.dynamic_index_in_dim(pieces, chip ^ place, 0, False) for place in range(4)]
        return jnp.concatenate(ordered, 0)

    def plane_scatter(grads):
        if chips != 4:
            return lax.psum_scatter(grads, "chip", scatter_dimension=0, tiled=True).astype(F32)

        def rows_of(place, low, count):
            return lax.dynamic_slice_in_dim(grads, (chip ^ place) * block_rows + low, count, 0)

        by_side = across(rows_of(3, 0, shard), 1)
        by_over = across(rows_of(3, shard, shard), 2)
        to_over = jnp.concatenate(
            [rows_of(2, 0, shard).astype(F32) + by_side.astype(F32), rows_of(2, shard, shard).astype(F32)], 0
        ).astype(BF)
        to_side = jnp.concatenate(
            [rows_of(1, 0, shard).astype(F32), rows_of(1, shard, shard).astype(F32) + by_over.astype(F32)], 0
        ).astype(BF)
        over, side = across(to_over, 2), across(to_side, 1)
        return rows_of(0, 0, block_rows).astype(F32) + over.astype(F32) + side.astype(F32)

    def top_scatter(pieces):
        total = pieces[0].astype(F32)
        for step in range(1, tops):
            total = total + shift(pieces[step].astype(BF), tops - step).astype(F32)
        return total

    def core_split(total):
        cut = total.reshape(2, shard, total.shape[1])
        mine = lax.dynamic_index_in_dim(cut, core, 0, False)
        other = swap(lax.dynamic_index_in_dim(cut, 1 - core, 0, False).astype(BF)).astype(F32)
        return jnp.where(core == 0, mine, other), jnp.where(core == 0, other, mine)

    own_wide = plane_gather(own)

    def fetch(group, count):
        part = own[:, group * group_width : (group + 1) * group_width]
        columns = group_width // count
        got = [shift(part, step).reshape(block_rows, count, 1, columns) for step in range(1, tops)]
        rest = jnp.concatenate(got, 2).reshape(block_rows, (tops - 1) * group_width)
        rest = plane_gather(rest).reshape(width, count, (tops - 1) * columns)
        near = own_wide[:, group * group_width : (group + 1) * group_width]
        near = near.reshape(width, count, columns)
        return [
            jnp.concatenate([near[:, one], rest[:, one]], 1) for one in range(count)
        ]

    def give(grads):
        count = len(grads)
        columns = grads[0].shape[1] // tops
        summed = plane_scatter(jnp.concatenate(grads, 1)).reshape(block_rows, count, tops, columns)
        pieces = [summed[:, :, step].reshape(block_rows, count * columns) for step in range(tops)]
        low, high = core_split(top_scatter(pieces))
        low, high = low.reshape(shard, count, columns), high.reshape(shard, count, columns)
        return [(low[:, one], high[:, one]) for one in range(count)]

    packed_norms = lax.all_gather(jnp.stack(norms), ("chip", "core"), axis=1, tiled=True)
    gain_one, bias_one, gain_two, bias_two, gain_three, bias_three = packed_norms

    w_query, w_key, w_value, w_out = fetch(0, 4)
    inputs = to_image(image_piece(image_rows)).astype(F32)
    c_query, c_key, c_value, c_out = fetch(1, 4)
    in_low, out_low = fetch(2, 2)
    in_high, out_high = fetch(3, 2)

    text = to_image(lambda slot: text_rows[slot % images])
    if lows > 1:
        text = lax.all_gather(text, "lo", axis=1)
    text = text.reshape(tops * lows * texts, width)
    other_ids = swap(segment_ids)
    ids = jnp.where(core == top // images, segment_ids, other_ids)
    ids = lax.dynamic_index_in_dim(ids, top % images, 0, False)
    captions = jnp.repeat(ids, length // ids.shape[0])[None, :]
    ids = ids[:, None]
    cot = to_image(image_piece(cotangent))

    full_one = tp_gather(layer_norm(inputs, gain_one, bias_one))
    packed = dot(full_one, jnp.concatenate([w_query, w_key, w_value], 1)).astype(BF)
    self_mix, self_lse = self_forward(packed)
    after_attn = inputs + tp_reduce(dot(self_mix, w_out, NT))
    full_two = tp_gather(layer_norm(after_attn, gain_two, bias_two))
    queries = dot(full_two, c_query).astype(BF)
    w_text = jnp.concatenate([c_key, c_value], 1)
    keys = dot(text, w_text).astype(BF)
    cross_mix, cross_lse = cross_forward(queries, keys, ids, captions)
    after_cross = after_attn + tp_reduce(dot(cross_mix, c_out, NT))
    full_three = tp_gather(layer_norm(after_cross, gain_three, bias_three))
    full_cot = tp_gather(cot)
    gin_low, gout_low, *sums = feed(full_three, full_cot, in_low, out_low, None)
    gin_high, gout_high, out_sum, back_sum = feed(full_three, full_cot, in_high, out_high, sums)
    low_grads = give([gin_low, gout_low])
    high_grads = give([gin_high, gout_high])
    result = to_rows((after_cross + tp_reduce(out_sum)).astype(BF))

    back_three, dgain_three, dbias_three = norm_back(after_cross, gain_three, tp_reduce(back_sum))
    grad_cross = cot.astype(F32) + back_three
    full_grad = tp_gather(grad_cross.astype(BF))
    mix_grad = dot(full_grad, c_out).astype(BF)
    dq, dk, dv = cross_backward(queries, keys, cross_mix, mix_grad, cross_lse, ids, captions)
    back_sum = dot(dq, c_query, NT)
    dkv = jnp.concatenate([dk, dv], 1)
    cross_grads = give(
        [
            dot(full_two, dq, TN).astype(BF),
            dot(text, dk, TN).astype(BF),
            dot(text, dv, TN).astype(BF),
            dot(full_grad, cross_mix, TN).astype(BF),
        ]
    )
    text_part = dot(dkv, w_text, NT).astype(BF).reshape(tops, lows, texts, width)
    if lows > 1:
        text_part = lax.psum_scatter(text_part, "lo", scatter_dimension=1, tiled=True)
    got = [part.astype(F32) for part in from_image(text_part[:, 0])]
    got = jnp.stack(got)
    got = [lax.dynamic_index_in_dim(got, top ^ slot, 0, False) for slot in range(tops)]
    text_grad = jnp.stack([got[i] + got[images + i] for i in range(images)])

    back_two, dgain_two, dbias_two = norm_back(after_attn, gain_two, tp_reduce(back_sum))
    grad_attn = grad_cross + back_two
    full_grad = tp_gather(grad_attn.astype(BF))
    mix_grad = dot(full_grad, w_out).astype(BF)
    dq, dk, dv = self_backward(packed, self_mix, mix_grad, self_lse)
    dqkv = jnp.concatenate([dq, dk, dv], 1)
    dwqkv = dot(full_one, dqkv, TN).astype(BF)
    span = dq.shape[1]
    self_grads = give(
        [
            dwqkv[:, :span],
            dwqkv[:, span : 2 * span],
            dwqkv[:, 2 * span :],
            dot(full_grad, self_mix, TN).astype(BF),
        ]
    )
    back_sum = dot(dqkv, jnp.concatenate([w_query, w_key, w_value], 1), NT)
    back_one, dgain_one, dbias_one = norm_back(inputs, gain_one, tp_reduce(back_sum))
    input_grad = to_rows((grad_attn + back_one).astype(BF)).astype(F32)

    norm_sums = lax.psum(
        jnp.stack([dgain_one, dbias_one, dgain_two, dbias_two, dgain_three, dbias_three]),
        ("chip", "core", "hi", "lo"),
    )
    norm_sums = lax.dynamic_slice_in_dim(norm_sums, (chip * 2 + core) * shard, shard, 1)

    feeds = [
        jnp.concatenate([low_grads[i][0], high_grads[i][0], low_grads[i][1], high_grads[i][1]], 1)
        for i in range(2)
    ]
    joined = [jnp.concatenate(pair, 1) for pair in (*self_grads, *cross_grads)]
    return (result, input_grad, text_grad, *joined, *feeds, *[norm_sums[i] for i in range(6)])


BLOCK = 256
ANY = pl.BlockSpec(memory_space=pltpu.HBM)
SMEM = pl.BlockSpec(memory_space=pltpu.SMEM)
VMEM = pl.BlockSpec(memory_space=pltpu.VMEM)
LATE = object()
MIB = 1024 * 1024


def like(*shape, dtype=BF):
    return jax.ShapeDtypeStruct(shape, dtype)


class Late:
    def __init__(self, source, target, sem):
        self.ref, self.copy = target, pltpu.make_async_copy(source, target, sem)
        self.copy.start()

    def ready(self):
        if self.copy is not None:
            self.copy.wait()
            self.copy = None
        return self.ref


class Early:
    def __init__(self, source, target, sem):
        self.ref, self.copy, self.sent = source, pltpu.make_async_copy(source, target, sem), False

    def send(self):
        self.copy.start()
        self.sent = True


def call_overlapped(body, outs, ins, operands, scratch=(), limit=60):
    late_ins = [i for i, spec in enumerate(ins) if spec is LATE]
    late_outs = [i for i, (spec, _) in enumerate(outs) if spec is LATE]
    buffers = [pltpu.VMEM(operands[i].shape, operands[i].dtype) for i in late_ins]
    buffers += [pltpu.VMEM(outs[i][1].shape, outs[i][1].dtype) for i in late_outs]
    count = len(buffers)

    def wrapped(*refs):
        refs = list(refs)
        sems = refs.pop()
        extra = refs[len(refs) - count :]
        refs = refs[: len(refs) - count]
        loads = [Late(refs[i], extra[n], sems.at[n]) for n, i in enumerate(late_ins)]
        for load, i in zip(loads, late_ins):
            refs[i] = load
        stores = []
        for n, i in enumerate(late_outs):
            place = len(ins) + i
            stores.append(Early(extra[len(late_ins) + n], refs[place], sems.at[len(late_ins) + n]))
            refs[place] = stores[-1]
        body(*refs)
        for load in loads:
            load.ready()
        for store in stores:
            if not store.sent:
                store.send()
        for store in stores:
            store.copy.wait()

    return call(
        wrapped,
        [(ANY if spec is LATE else spec, shape) for spec, shape in outs],
        [ANY if spec is LATE else spec for spec in ins],
        operands,
        [*scratch, *buffers, pltpu.SemaphoreType.DMA((max(count, 1),))],
        limit,
    )


def call(body, outs, ins, operands, scratch=(), limit=60, grid=None, flops=0, moved=0):
    single = not isinstance(outs, (list, tuple))
    extra = {} if grid is None else {"grid": grid}
    cost = pl.CostEstimate(flops=1, bytes_accessed=1, transcendentals=0)
    out_specs, out_shape = ([outs[0]], [outs[1]]) if single else ([o[0] for o in outs], [o[1] for o in outs])
    return list(pl.pallas_call(
        body,
        in_specs=ins,
        out_specs=out_specs,
        out_shape=out_shape,
        scratch_shapes=list(scratch),
        compiler_params=pltpu.CompilerParams(vmem_limit_bytes=limit * MIB),
        cost_estimate=cost,
        **extra,
    )(*operands))


def run_copies(copies, sems):
    started = [pltpu.make_async_copy(source, target, sems.at[i]) for i, (source, target) in enumerate(copies)]
    for copy in started:
        copy.start()
    for copy in started:
        copy.wait()


def at(offset, count, unit=128):
    return pl.ds(pl.multiple_of(offset, unit), count)


def prepare_kernel(place, image, text, ids, cot, norms, wq, wk, wv, wo, cq, ck, cv, co, win, wout, *outs):
    keep, sent, rows_keep, rows_sent, cot_keep, cot_sent, text_pair, sems = outs
    core = place[1]
    copies = []
    for target, which in ((sent, 1 - core), (keep, core)):
        for group, weights in enumerate(((wq, wk, wv, wo), (cq, ck, cv, co))):
            for one, weight in enumerate(weights):
                copies.append(
                    (
                        weight.at[:, at(which * 128, 128)],
                        target.at[group * 128 : (group + 1) * 128, one * 128 : (one + 1) * 128],
                    )
                )
        for part in range(2):
            for one, weight in enumerate((win, wout)):
                copies.append(
                    (
                        weight.at[:, at(which * 512 + part * 256, 256)],
                        target.at[256 + part * 128 : 384 + part * 128, one * 256 : (one + 1) * 256],
                    )
                )
        copies.append((norms, target.at[512:528, :]))
    for target, cots, which in ((rows_sent, cot_sent, 1 - core), (rows_keep, cot_keep, core)):
        for one in range(2):
            copies.append((image.at[one, at(which * 128, 128), :], target.at[one]))
            copies.append((cot.at[one, at(which * 128, 128), :], cots.at[one]))
    for one in range(2):
        copies.append((text.at[one], text_pair.at[one, 0:32, :]))
        copies.append((ids.at[one], text_pair.at[one, 32:48, :]))
    run_copies(copies, sems)


def prepare(place, image, text, ids, cot, norms, weights):
    return call(
        prepare_kernel,
        [(VMEM, like(528, 512))] * 2 + [(VMEM, like(2, 128, 1024))] * 4 + [(VMEM, like(2, 48, 1024))],
        [SMEM] + [ANY] * 15,
        (place, image, text, ids, cot, norms, *weights),
        [pltpu.SemaphoreType.DMA((42,))],
    )


def pick_kernel(place, keep, taken, *outs):
    core, top = place[1], place[2]
    for step, out in enumerate(outs):
        image = (top + 4 - step) % 4

        @pl.when(image // 2 == core)
        def _():
            out[...] = keep[image % 2]

        @pl.when(image // 2 != core)
        def _():
            out[...] = taken[image % 2]


def pick(place, keep, taken):
    return call(
        pick_kernel,
        [(VMEM, like(*keep.shape[1:]))] * 4,
        [SMEM, VMEM, VMEM],
        (place, keep, taken),
    )


def join_kernel(place, keep, taken, *refs):
    singles, near, sems = refs[:4], refs[4], refs[5]
    copies = []
    for half, source in enumerate((keep, taken)):
        core = place[1] ^ half
        for group in range(4):
            part = source.at[group * 128 : (group + 1) * 128, :]
            copies.append((part, singles[group].at[at(core * 128, 128), :]))
        copies.append((source.at[0:128, :], near.at[at(core * 128, 128), :]))
        copies.append((source.at[512:528, :], near.at[at(256 + core * 16, 16, 16), :]))
    run_copies(copies, sems)


def join(place, keep, taken):
    return call(
        join_kernel,
        [(VMEM, like(256, 512))] * 4 + [(VMEM, like(288, 512))],
        [SMEM] + [ANY] * 2,
        (place, keep, taken),
        [pltpu.SemaphoreType.DMA((12,))],
    )


def stack_kernel(*refs):
    *parts, whole, sems = refs
    copies, low = [], 0
    for part in parts:
        copies.append((part, whole.at[low : low + part.shape[0]]))
        low += part.shape[0]
    run_copies(copies, sems)


def stack(parts):
    rows = sum(part.shape[0] for part in parts)
    return call(
        stack_kernel,
        [(VMEM, like(rows, *parts[0].shape[1:]))],
        [ANY] * len(parts),
        parts,
        [pltpu.SemaphoreType.DMA((len(parts),))],
        limit=60,
    )[0]


def arrange_kernel(place, *refs):
    messages, text, sems = refs[:4], refs[4], refs[5]
    run_copies(
        [(m.at[0:32, :], text.at[at((place[2] + i) % 4 * 32, 32, 32), :]) for i, m in enumerate(messages)], sems
    )


def arrange(place, messages):
    return call(
        arrange_kernel,
        [(VMEM, like(128, 1024))],
        [SMEM] + [ANY] * 4,
        (place, *messages),
        [pltpu.SemaphoreType.DMA((4,))],
    )[0]


def gather_copies(batches, buffer, whole, rows_of, loads, stores, extra=()):
    started = []
    for i, batch in enumerate(batches):
        copies = [pltpu.make_async_copy(a, b, loads.at[i * 8 + j]) for j, (a, b) in enumerate(batch)]
        for copy in copies:
            copy.start()
        started.append(copies)
    stored = [pltpu.make_async_copy(a, b, stores.at[4 + i]) for i, (a, b) in enumerate(extra)]
    for copy in stored:
        copy.start()
    for i, copies in enumerate(started):
        for copy in copies:
            copy.wait()
        rows = rows_of(i)
        stored.append(pltpu.make_async_copy(buffer.at[rows, :], whole.at[rows, :], stores.at[i]))
        stored[-1].start()
    for copy in stored:
        copy.wait()


def assemble_first_kernel(place, *refs):
    near, far = refs[:5], refs[5:10]
    whole, norms, buffer, loads, stores = refs[10:]
    chip, top = place[0], place[2]
    batches, extra = [], []
    for source in range(4):
        batch = []
        for half in range(2):
            row = at((chip ^ source) * 256 + half * 128, 128)
            piece, first = (near[source], half * 128) if source < 3 else (near[3 + half], 0)
            batch.append((piece.at[first : first + 128, :], buffer.at[row, at(top * 512, 512, 512)]))
            low = 256 + half * 16 if source < 3 else 128 + half * 16
            piece = near[source] if source < 3 else near[4]
            column = at((chip ^ source) * 256 + half * 128, 128)
            extra.append((piece.at[low : low + 16, 0:128], norms.at[:, column]))
            for step in range(3):
                first = step * 256 + half * 128
                piece = far[source] if source < 3 else far[3 + first // 384]
                first = first if source < 3 else first % 384
                columns = at((top + 1 + step) % 4 * 512, 512, 512)
                batch.append((piece.at[first : first + 128, :], buffer.at[row, columns]))
        batches.append(batch)
    gather_copies(batches, buffer, whole, lambda i: at((chip ^ i) * 256, 256), loads, stores, extra)


ASSEMBLE_SCRATCH = [
    pltpu.VMEM((1024, 2048), BF),
    pltpu.SemaphoreType.DMA((32,)),
    pltpu.SemaphoreType.DMA((12,)),
]


def assemble_first(place, near, far):
    return call(
        assemble_first_kernel,
        [(ANY, like(1024, 2048)), (VMEM, like(16, 1024))],
        [SMEM] + [ANY] * 10,
        (place, *near, *far),
        ASSEMBLE_SCRATCH,
    )


def assemble_kernel(place, own, side, over, low, high, whole, buffer, loads, stores):
    chip = place[0]
    batches = []
    for source in range(4):
        batch = []
        for top in range(4):
            piece = (own, side, over, low if top < 2 else high)[source]
            rows, columns = at((chip ^ source) * 256, 256), slice(top * 512, (top + 1) * 512)
            batch.append((piece.at[top % 2 if source == 3 else top], buffer.at[rows, columns]))
        batches.append(batch)
    gather_copies(batches, buffer, whole, lambda i: at((chip ^ i) * 256, 256), loads, stores)


def assemble(place, own, others):
    return call(
        assemble_kernel,
        [(ANY, like(1024, 2048))],
        [SMEM] + [ANY] * 5,
        (place, own, *others),
        ASSEMBLE_SCRATCH,
    )[0]


def norm_row(norms, one):
    return norms[one : one + 1, :].astype(F32)


def normalized(values, gain, bias):
    center = values - jnp.mean(values, -1, keepdims=True)
    inverse = lax.rsqrt(jnp.mean(center * center, -1, keepdims=True) + EPS)
    return (center * inverse * gain + bias).astype(BF)


def columns_of(weights, one, count=128):
    return jnp.concatenate([weights[:, s * 512 + one * count : s * 512 + (one + 1) * count] for s in range(4)], 1)


def project_into(target, rows, weights, dims=NN, step=512):
    count = weights.shape[0] if dims == NT else weights.shape[1]
    for low in range(0, count, step):
        part = weights[low : low + step, :] if dims == NT else weights[:, low : low + step]
        target[:, low : low + step] = dot(rows, part, dims).astype(target.dtype)


def image_blocks(place, own, other):
    core, top = place[1], place[2]
    for number in range(4):
        yield (top + number) % 4 * 256 + core * 128, own, number
        yield (top + number) % 4 * 256 + (1 - core) * 128, other, number


def one_head(values, head):
    return jnp.where(lane_head((1, 2 * HD), 1, head), values, jnp.zeros_like(values))


def both_heads(values):
    return jnp.concatenate([one_head(values, 0), one_head(values, 1)], 0)


def pick_heads(values):
    count = values.shape[1] // 2
    return jnp.where(lane_head((128, 1), 0, 0), values[:, :count], values[:, count:]).T


def causal_pair(count):
    rows = lax.broadcasted_iota(jnp.int32, (count, 2 * count), 0)
    columns = lax.broadcasted_iota(jnp.int32, (count, 2 * count), 1)
    return rows <= jnp.where(columns >= count, columns - count, columns)


def twice(row):
    return jnp.concatenate([row, row], 1)


def softmax_mix(scores, values):
    scale = LOG2E * HD**-0.5
    peak = jnp.max(scores[0], 0, keepdims=True)
    for part in scores[1:]:
        peak = jnp.maximum(peak, jnp.max(part, 0, keepdims=True))
    total, mixed = 0.0, 0.0
    for part, rows in zip(scores, values):
        weights = jnp.exp2((part - peak) * scale)
        total = total + jnp.sum(weights, 0, keepdims=True)
        mixed = mixed + dot(rows, weights.astype(BF), TN)
    return mixed / total, peak * scale + jnp.log2(total)


def causal_mask():
    return lax.broadcasted_iota(jnp.int32, (BLOCK, BLOCK), 0) <= lax.broadcasted_iota(
        jnp.int32, (BLOCK, BLOCK), 1
    )


def self_fwd_kernel(place, own, other, norms, weights, normed, qkv, mix, lse, part):
    gain, bias = norm_row(norms, 0), norm_row(norms, 1)
    for row, half, number in image_blocks(place, own, other):
        normed[at(row, 128), :] = normalized(half[number].astype(F32), gain, bias)
    for one in range(3):
        qkv[:, one * 512 : (one + 1) * 512] = dot(normed[...], columns_of(weights, one)).astype(BF)
    causal = causal_pair(512)

    def pair_step(pair, carry):
        lanes = at(pair * 128, 128)
        k_lanes, v_lanes = at(512 + pair * 128, 128), at(1024 + pair * 128, 128)
        for low in range(0, 1024, 512):
            high = low + 512
            both = both_heads(qkv[low:high, lanes])
            scores = [jnp.where(causal, dot(qkv[low:high, k_lanes], both, NT), NEG)]
            values = [qkv[low:high, v_lanes]]
            if low:
                scores.append(dot(qkv[:low, k_lanes], both, NT))
                values.append(qkv[:low, v_lanes])
            mixed, logsum = softmax_mix(scores, values)
            for head in range(2):
                lse[pair, head : head + 1, low:high] = logsum[:, head * 512 : (head + 1) * 512]
            mix[low:high, lanes] = pick_heads(mixed).astype(BF)
        return carry

    lax.fori_loop(0, 4, pair_step, 0)
    project_into(part, mix[...], columns_of(weights, 3), NT)


def fused_self_forward(place, own, other, norms, weights):
    return call(
        self_fwd_kernel,
        [
            (VMEM, like(1024, 1024)),
            (VMEM, like(1024, 1536)),
            (VMEM, like(1024, 512)),
            (VMEM, like(4, 2, 1024, dtype=F32)),
            (VMEM, like(1024, 1024)),
        ],
        [SMEM, VMEM, VMEM, VMEM, VMEM],
        (place, own, other, norms, weights),
    )


def cross_fwd_kernel(
    place, own, other, mine, theirs, norms, text, ids, caption, weights, after, normed, queries, keys, mix, lse, part
):
    gain, bias = norm_row(norms, 2), norm_row(norms, 3)
    for row, half, number in image_blocks(place, own, other):
        rows = at(row, 128)
        values = half[number].astype(F32) + (mine[rows, :].astype(F32) + theirs[rows, :].astype(F32))
        after[rows, :] = values
        normed[rows, :] = normalized(values, gain, bias)
    project_into(queries, normed[...], columns_of(weights, 0))
    w_text = jnp.concatenate([columns_of(weights, 1), columns_of(weights, 2)], 1)
    keys[...] = dot(text[...], w_text).astype(BF)

    def pair_step(pair, carry):
        lanes, v_lanes = at(pair * 128, 128), at(512 + pair * 128, 128)
        seen = twice(ids[...] == caption[...])
        scores = jnp.where(seen, dot(keys[:, lanes], both_heads(queries[:, lanes]), NT), NEG)
        mixed, logsum = softmax_mix([scores], [keys[:, v_lanes]])
        for head in range(2):
            lse[pair, head : head + 1, :] = logsum[:, head * 1024 : (head + 1) * 1024]
        mix[:, lanes] = pick_heads(mixed).astype(BF)
        return carry

    lax.fori_loop(0, 4, pair_step, 0)
    project_into(part, mix[...], columns_of(weights, 3), NT)


def fused_cross_forward(place, own, other, mine, theirs, norms, text, ids, caption, weights):
    return call(
        cross_fwd_kernel,
        [
            (VMEM, like(1024, 1024, dtype=F32)),
            (VMEM, like(1024, 1024)),
            (VMEM, like(1024, 512)),
            (VMEM, like(128, 1024)),
            (VMEM, like(1024, 512)),
            (VMEM, like(4, 2, 1024, dtype=F32)),
            (VMEM, like(1024, 1024)),
        ],
        [SMEM] + [VMEM] * 8 + [VMEM],
        (place, own, other, mine, theirs, norms, text, ids, caption, weights),
    )


def cut_grads(place, grads, columns, own, side, over, low, high):
    chip = place[0]
    own[:, columns] = grads[at(chip * 256, 256), :].astype(BF)
    side[:, columns] = grads[at((chip ^ 1) * 256, 256), :].astype(BF)
    over[:, columns] = grads[at((chip ^ 2) * 256, 256), :].astype(BF)
    low[:, columns] = grads[at((chip ^ 3) * 256, 128), :].astype(BF)
    high[:, columns] = grads[at((chip ^ 3) * 256 + 128, 128), :].astype(BF)


GRAD_SHAPES = [(256, 2048)] * 3 + [(128, 2048)] * 2


def feed_step(rows, cot, rows_t, cot_t, weights, out_sum, back_sum, grads):
    w_in = jnp.concatenate([weights[0][:, :256], weights[1][:, :256]], 1)
    w_out = jnp.concatenate([weights[0][:, 256:], weights[1][:, 256:]], 1)
    slope = math.sqrt(2.0 / math.pi)
    pre = dot(rows[...], w_in)
    square = pre * pre
    bent = jnp.tanh(pre * (slope + slope * 0.044715 * square))
    half = 0.5 * (1.0 + bent)
    act = (pre * half).astype(BF)
    bend = half + pre * (0.5 * (1.0 - bent * bent)) * (slope + 3.0 * slope * 0.044715 * square)
    pre_grad = (dot(cot[...], w_out) * bend).astype(BF)
    for low in range(0, 1024, 512):
        part = slice(low, low + 512)
        out_sum[:, part] += dot(act, w_out[part, :], NT)
        back_sum[:, part] += dot(pre_grad, w_in[part, :], NT)
    for block in range(2):
        part = slice(block * 256, (block + 1) * 256)
        grads[:, block * 512 : block * 512 + 256] = dot(rows_t[...], pre_grad[:, part])
        grads[:, block * 512 + 256 : (block + 1) * 512] = dot(cot_t[...], act[:, part])


def feed_first_kernel(
    place, after, mine, theirs, norms, cot_own, cot_other, weights,
    g_whole, after_out, normed_out, cot_out, out_sum, back, after_cross, normed, cot, back_sum, rows_t, cot_t, grads, sems,
):
    step = pl.program_id(0)
    pairs = ((after_cross, after_out), (normed, normed_out), (cot, cot_out))
    stores = [pltpu.make_async_copy(a, b, sems.at[i]) for i, (a, b) in enumerate(pairs)]

    @pl.when(step == 0)
    def _():
        gain, bias = norm_row(norms, 4), norm_row(norms, 5)
        for low in range(0, 1024, 128):
            rows = slice(low, low + 128)
            values = after[rows, :] + (mine[rows, :].astype(F32) + theirs[rows, :].astype(F32))
            after_cross[rows, :] = values
            normed[rows, :] = normalized(values, gain, bias)
        for row, half, number in image_blocks(place, cot_own, cot_other):
            cot[at(row, 128), :] = half[number]
        for store in stores:
            store.start()
        rows_t[...] = normed[...].T
        cot_t[...] = cot[...].T
        out_sum[...] = jnp.zeros_like(out_sum)
        for block in range(4):
            rows = at(block * 256 + place[1] * 128, 128)
            out_sum[rows, :] = after_cross[rows, :]
        back_sum[...] = jnp.zeros_like(back_sum)

    feed_step(
        normed, cot, rows_t, cot_t, (weights[:, :512], weights[:, 512:]), out_sum, back_sum, grads
    )
    for chip in range(4):
        for block in range(2):
            part = grads[chip * 256 : (chip + 1) * 256, block * 512 : (block + 1) * 512]
            g_whole[chip, block] = part.astype(BF)

    @pl.when(step == 1)
    def _():
        back[...] = back_sum[...].astype(BF)
        for store in stores:
            store.wait()


def feed_second_kernel(
    place, normed, cot, out_in, back_in, weights,
    g_own, g_side, g_over, g_low, g_high, out_keep, out_sent, back, out_sum, back_sum, rows_t, cot_t, grads,
):
    step, core = pl.program_id(0), place[1]

    @pl.when(step == 0)
    def _():
        rows_t[...] = normed[...].T
        cot_t[...] = cot[...].T
        out_sum[...] = out_in[...]
        back_sum[...] = back_in[...].astype(F32)

    blocks = [weights[:, block].reshape(1024, 512) for block in range(2)]
    feed_step(normed, cot, rows_t, cot_t, blocks, out_sum, back_sum, grads)
    cut_grads(place, grads, slice(None), g_own, g_side, g_over, g_low, g_high)

    @pl.when(step == 1)
    def _():
        back[...] = back_sum[...].astype(BF)
        for block in range(4):
            out_keep[block] = out_sum[at(block * 256 + core * 128, 128), :]
            out_sent[block] = out_sum[at(block * 256 + (1 - core) * 128, 128), :].astype(BF)


def once(*shape):
    zeros = (0,) * len(shape)
    return pl.BlockSpec(shape, lambda i: zeros, pipeline_mode=pl.Buffered(1))


def grad_outs(width=512):
    return [(pl.BlockSpec((rows, width), lambda i: (0, i)), like(rows, n)) for rows, n in GRAD_SHAPES]


FEED_FLOPS = 13 * 2**30


def feed_first(place, after, mine, theirs, norms, cot_own, cot_other, weights):
    square = once(1024, 1024)
    return call(
        feed_first_kernel,
        [(pl.BlockSpec((4, 2, 256, 512), lambda i: (0, i, 0, 0)), like(4, 4, 256, 512))]
        + [
            (ANY, like(1024, 1024, dtype=F32)),
            (ANY, like(1024, 1024)),
            (ANY, like(1024, 1024)),
            (square, like(1024, 1024, dtype=F32)),
            (square, like(1024, 1024)),
        ],
        [SMEM, square, square, square, once(16, 1024), once(4, 128, 1024), once(4, 128, 1024)]
        + [pl.BlockSpec((1024, 1024), lambda i: (0, i))],
        (place, after, mine, theirs, norms, cot_own, cot_other, weights),
        [pltpu.VMEM((1024, 1024), F32)]
        + [pltpu.VMEM((1024, 1024), BF)] * 2
        + [pltpu.VMEM((1024, 1024), F32)]
        + [pltpu.VMEM((1024, 1024), BF)] * 2
        + [pltpu.VMEM((1024, 1024), F32), pltpu.SemaphoreType.DMA((3,))],
        limit=60,
        grid=(2,),
        flops=FEED_FLOPS,
        moved=30 * MIB,
    )


def feed_second(place, normed, cot, out_in, back_in, weights):
    square = once(1024, 1024)
    return call(
        feed_second_kernel,
        grad_outs(1024)
        + [
            (once(4, 128, 1024), like(4, 128, 1024, dtype=F32)),
            (once(4, 128, 1024), like(4, 128, 1024)),
            (square, like(1024, 1024)),
        ],
        [SMEM, square, square, square, square, pl.BlockSpec((4, 2, 256, 512), lambda i: (0, i, 0, 0))],
        (place, normed, cot, out_in, back_in, weights),
        [pltpu.VMEM((1024, 1024), F32)] * 2
        + [pltpu.VMEM((1024, 1024), BF)] * 2
        + [pltpu.VMEM((1024, 1024), F32)],
        limit=60,
        grid=(2,),
        flops=FEED_FLOPS,
        moved=26 * MIB,
    )


def norm_backward(values, gain, grad):
    center = values - jnp.mean(values, -1, keepdims=True)
    inverse = lax.rsqrt(jnp.mean(center * center, -1, keepdims=True) + EPS)
    hat = center * inverse
    scaled = grad * gain
    back = inverse * (
        scaled - jnp.mean(scaled, -1, keepdims=True) - hat * jnp.mean(scaled * hat, -1, keepdims=True)
    )
    return back, grad * hat


def norm_block(values_of, mine, theirs, base_of, gain, norms, keep):
    gain = norm_row(*gain)
    gain_sum, bias_sum = jnp.zeros((8, 1024), F32), jnp.zeros((8, 1024), F32)
    for low in range(0, 1024, 128):
        rows = slice(low, low + 128)
        grad = mine[rows, :].astype(F32) + theirs[rows, :].astype(F32)
        back, term = norm_backward(values_of(rows), gain, grad)
        keep(rows, base_of(rows) + back)
        gain_sum = gain_sum + jnp.sum(term.reshape(16, 8, 1024), 0)
        bias_sum = bias_sum + jnp.sum(grad.reshape(16, 8, 1024), 0)
    norms[0:1, :] = jnp.sum(gain_sum, 0, keepdims=True)
    norms[1:2, :] = jnp.sum(bias_sum, 0, keepdims=True)


def pair_row(lse, pair, low, high):
    return jnp.concatenate([lse[pair, 0:1, low:high], lse[pair, 1:2, low:high]], 1)


def pair_delta(grad, mix):
    product = (grad.astype(F32) * mix.astype(F32)).T
    return jnp.concatenate([jnp.sum(product[:HD], 0, keepdims=True), jnp.sum(product[HD:], 0, keepdims=True)], 1)


def head_grads(keys, values, one, one_grad, lse, delta, mask):
    weights = jnp.exp2(dot(keys, one, NT) * (LOG2E * HD**-0.5) - lse)
    if mask is not None:
        weights = jnp.where(mask, weights, 0.0)
    slope = dot(values, one_grad, NT)
    return weights.astype(BF), (weights * (slope - delta)).astype(BF)


def cross_bwd_kernel(
    place, after, mine, theirs, cot, gain, weights, normed, text, queries, keys, mix, lse, ids, caption,
    grad_out, part_out, norms, text_part, g_own, g_side, g_over, g_low, g_high, low_grad, mix_grad, dq, dkv, grads,
):
    grad_cross, part = grad_out.ref, part_out.ref

    def keep(rows, value):
        grad_cross[rows, :] = value
        low_grad[rows, :] = value.astype(BF)

    norm_block(lambda rows: after[rows, :], mine, theirs, lambda rows: cot[rows, :].astype(F32), (gain, 4), norms, keep)
    grad_out.send()
    weights, queries, keys, mix = weights.ready(), queries.ready(), keys.ready(), mix.ready()
    project_into(mix_grad, low_grad[...], columns_of(weights, 3))

    def pair_step(pair, carry):
        lanes, v_lanes = at(pair * 128, 128), at(512 + pair * 128, 128)
        query, grad = both_heads(queries[:, lanes]), both_heads(mix_grad[:, lanes])
        prob, score_grad = head_grads(
            keys[:, lanes],
            keys[:, v_lanes],
            query,
            grad,
            pair_row(lse, pair, 0, 1024),
            pair_delta(mix_grad[:, lanes], mix[:, lanes]),
            twice(ids[...] == caption[...]),
        )
        dv_sum, dk_sum = dot(prob, grad), dot(score_grad, query)
        dq[:, lanes] = (pick_heads(dot(keys[:, lanes], score_grad, TN)) * HD**-0.5).astype(BF)
        dkv[:, lanes] = (dk_sum * HD**-0.5).astype(BF)
        dkv[:, v_lanes] = dv_sum.astype(BF)
        return carry

    lax.fori_loop(0, 4, pair_step, 0)
    project_into(part, dq[...], columns_of(weights, 0), NT)
    part_out.send()
    normed = normed.ready()
    w_text = jnp.concatenate([columns_of(weights, 1), columns_of(weights, 2)], 1)
    text_part[...] = dot(dkv[...], w_text, NT).astype(BF)
    for one, (left, right) in enumerate(
        ((normed, dq[...]), (text, dkv[:, :512]), (text, dkv[:, 512:]), (low_grad, mix[...]))
    ):
        grads[...] = dot(left[...], right, TN)
        for s in range(4):
            columns = slice(s * 512 + one * 128, s * 512 + (one + 1) * 128)
            cut_grads(
                place, grads.at[:, s * 128 : (s + 1) * 128], columns, g_own, g_side, g_over, g_low, g_high
            )


def fused_cross_backward(place, after, mine, theirs, cot, gain, weights, normed, text, queries, keys, mix, lse, ids, caption):
    return call_overlapped(
        cross_bwd_kernel,
        [
            (LATE, like(1024, 1024, dtype=F32)),
            (LATE, like(1024, 1024)),
            (VMEM, like(8, 1024, dtype=F32)),
            (VMEM, like(128, 1024)),
        ]
        + [(VMEM, like(*shape)) for shape in GRAD_SHAPES],
        [SMEM] + [VMEM] * 5 + [LATE, LATE, VMEM, LATE, LATE, LATE, VMEM, VMEM, VMEM],
        (place, after, mine, theirs, cot, gain, weights, normed, text, queries, keys, mix, lse, ids, caption),
        [
            pltpu.VMEM((1024, 1024), BF),
            pltpu.VMEM((1024, 512), BF),
            pltpu.VMEM((1024, 512), BF),
            pltpu.VMEM((128, 1024), BF),
            pltpu.VMEM((1024, 512), F32),
        ],
    )


def self_bwd_kernel(
    place, after, mine, theirs, base, gain, weights, qkv, mix, lse,
    grad_out, low_out, norms, dqkv, mix_grad, dk_sum, dv_sum,
):
    core = place[1]
    grad_own, low_grad = grad_out.ref, low_out.ref

    def keep(rows, value):
        low_grad[rows, :] = value.astype(BF)

        @pl.when(core == (rows.start // 128) % 2)
        def _():
            grad_own[rows.start // 256] = value

    norm_block(lambda rows: after[rows, :], mine, theirs, lambda rows: base[rows, :], (gain, 2), norms, keep)
    grad_out.send()
    low_out.send()
    weights, qkv, mix = weights.ready(), qkv.ready(), mix.ready()
    project_into(mix_grad, low_grad[...], columns_of(weights, 3))
    causal = causal_pair(512)

    def pair_step(pair, carry):
        lanes = at(pair * 128, 128)
        k_lanes, v_lanes = at(512 + pair * 128, 128), at(1024 + pair * 128, 128)
        for low in range(0, 1024, 512):
            high = low + 512
            query, grad = both_heads(qkv[low:high, lanes]), both_heads(mix_grad[low:high, lanes])
            delta = pair_delta(mix_grad[low:high, lanes], mix[low:high, lanes])
            logsum = pair_row(lse, pair, low, high)
            total = 0.0
            for start in range(0, high, 512):
                rows = slice(start, start + 512)
                keys = qkv[rows, k_lanes]
                prob, score_grad = head_grads(
                    keys, qkv[rows, v_lanes], query, grad, logsum, delta, causal if start == low else None
                )
                dv, dk = dot(prob, grad), dot(score_grad, query)
                if start == low:
                    dv_sum[rows, :], dk_sum[rows, :] = dv, dk
                else:
                    dv_sum[rows, :] += dv
                    dk_sum[rows, :] += dk
                total = total + dot(keys, score_grad, TN)
            dqkv[low:high, lanes] = (pick_heads(total) * HD**-0.5).astype(BF)
        dqkv[:, k_lanes] = (dk_sum[...] * HD**-0.5).astype(BF)
        dqkv[:, v_lanes] = dv_sum[...].astype(BF)
        return carry

    lax.fori_loop(0, 4, pair_step, 0)


def fused_self_backward(place, after, mine, theirs, base, gain, weights, qkv, mix, lse):
    return call_overlapped(
        self_bwd_kernel,
        [
            (LATE, like(4, 128, 1024, dtype=F32)),
            (LATE, like(1024, 1024)),
            (VMEM, like(8, 1024, dtype=F32)),
            (VMEM, like(1024, 1536)),
        ],
        [SMEM] + [VMEM] * 5 + [LATE] * 3 + [VMEM],
        (place, after, mine, theirs, base, gain, weights, qkv, mix, lse),
        [pltpu.VMEM((1024, 512), BF), pltpu.VMEM((1024, 128), F32), pltpu.VMEM((1024, 128), F32)],
    )


def self_grads_kernel(place, normed, low_grad, dq, dk, dv, mix, g_own, g_side, g_over, g_low, g_high, rows_t, grad_t, grads):
    @pl.when(pl.program_id(0) == 0)
    def _():
        rows_t[...] = normed[...].T
        grad_t[...] = low_grad[...].T

    grads[:, :384] = dot(rows_t[...], jnp.concatenate([dq[...], dk[...], dv[...]], 1))
    grads[:, 384:] = dot(grad_t[...], mix[...])
    cut_grads(place, grads, slice(None), g_own, g_side, g_over, g_low, g_high)


def self_grads(place, normed, low_grad, dqkv, mix):
    square = once(1024, 1024)

    def cut(offset):
        return pl.BlockSpec((1024, 128), lambda i: (0, offset + i))

    return call(
        self_grads_kernel,
        grad_outs(),
        [SMEM, square, square, cut(0), cut(4), cut(8), cut(0)],
        (place, normed, low_grad, dqkv, dqkv, dqkv, mix),
        [pltpu.VMEM((1024, 1024), BF)] * 2 + [pltpu.VMEM((1024, 512), F32)],
        limit=60,
        grid=(4,),
        flops=4 * 2**30,
        moved=12 * MIB,
    )


def self_back_kernel(place, dqkv, weights, kept, sent):
    core = place[1]
    w_in = jnp.concatenate([columns_of(weights, one) for one in range(3)], 1)
    for target, half in ((sent, 1 - core), (kept, core)):
        rows = jnp.concatenate([dqkv[at(block * 256 + half * 128, 128), :] for block in range(4)], 0)
        for low in range(0, 1024, 512):
            value = dot(rows, w_in[low : low + 512, :], NT).astype(target.dtype)
            target[:, :, low : low + 512] = value.reshape(4, 128, 512)


def self_back(place, dqkv, weights):
    return call(
        self_back_kernel,
        [(VMEM, like(4, 128, 1024, dtype=F32)), (VMEM, like(4, 128, 1024))],
        [SMEM, VMEM, VMEM],
        (place, dqkv, weights),
        limit=60,
        flops=3 * 2**30,
        moved=10 * MIB,
    )


def last_norm_kernel(place, rows, grad_own, mine, theirs, gain, text_part, sums_two, sums_three, *pieces):
    gain_sum, bias_sum = jnp.zeros((8, 1024), F32), jnp.zeros((8, 1024), F32)
    for number in range(4):
        block = (place[2] + number) % 4
        grad = mine[block] + theirs[block].astype(F32)
        back, term = norm_backward(rows[number].astype(F32), norm_row(gain, 0), grad)
        pieces[-number % 4][0:128, :] = (grad_own[block] + back).astype(BF)
        pieces[-number % 4][128:160, :] = text_part[at(block * 32, 32, 32), :]
        gain_sum = gain_sum + jnp.sum(term.reshape(16, 8, 1024), 0)
        bias_sum = bias_sum + jnp.sum(grad.reshape(16, 8, 1024), 0)
    sums = [jnp.sum(gain_sum, 0, keepdims=True), jnp.sum(bias_sum, 0, keepdims=True)]
    sums += [0.5 * sums_two[0:2, :], 0.5 * sums_three[0:2, :], jnp.zeros((10, 1024), F32)]
    sums = jnp.concatenate(sums, 0).astype(BF)
    for piece in pieces:
        piece[160:176, :] = sums


def last_norm(place, rows, grad_own, mine, theirs, gain, text_part, sums_two, sums_three):
    return call(
        last_norm_kernel,
        [(VMEM, like(176, 1024))] * 4,
        [SMEM] + [VMEM] * 8,
        (place, rows, grad_own, mine, theirs, gain, text_part, sums_two, sums_three),
    )


def finish_kernel(place, out_keep, theirs, *pieces):
    for number, piece in enumerate(pieces):
        block = (place[2] + 4 - number) % 4
        piece[...] = (out_keep[block] + theirs[block].astype(F32)).astype(BF)


def finish(place, out_keep, theirs):
    return call(
        finish_kernel,
        [(VMEM, like(128, 1024))] * 4,
        [SMEM] + [VMEM] * 2,
        (place, out_keep, theirs),
    )


def part_kernel(place, *refs):
    pieces, mine, sent = refs[:4], refs[4], refs[5]
    core, top = place[1], place[2]
    for step, piece in enumerate(pieces):
        image = (top + step) % 4

        @pl.when(image // 2 == core)
        def _():
            mine[image % 2] = piece[...]

        @pl.when(image // 2 != core)
        def _():
            sent[image % 2] = piece[...]

    if pieces[0].shape[0] > 160:
        total = 0.0
        for piece in pieces:
            total = total + piece[160:176, :].astype(F32)
        mine[0, 160:176, :] = total.astype(BF)
        sent[0, 160:176, :] = total.astype(BF)


def part_images(place, pieces):
    return call(
        part_kernel,
        [(VMEM, like(2, *pieces[0].shape))] * 2,
        [SMEM] + [VMEM] * 4,
        (place, *pieces),
    )


def land_kernel(place, mine, taken, rows, *more):
    core = place[1]
    for one in range(2):
        rows[one, at(core * 128, 128), :] = mine[one, 0:128, :].astype(rows.dtype)
        rows[one, at((1 - core) * 128, 128), :] = taken[one, 0:128, :].astype(rows.dtype)
        if more:
            more[0][one] = mine[one, 128:160, :].astype(F32) + taken[one, 128:160, :].astype(F32)
    if more:
        more[1][...] = mine[0, 160:168, :].astype(F32) + taken[0, 160:168, :].astype(F32)


def land(place, mine, taken, dtype):
    outs = [(VMEM, like(2, 256, 1024, dtype=dtype))]
    if mine.shape[1] > 128:
        outs += [(VMEM, like(2, 32, 1024, dtype=F32)), (VMEM, like(8, 1024, dtype=F32))]
    return call(land_kernel, outs, [SMEM, VMEM, VMEM], (place, mine, taken))


def relay_kernel(over, side, from_side, from_over, to_over, to_side):
    to_over[0:128, :] = (over[0:128, :].astype(F32) + from_side[...].astype(F32)).astype(BF)
    to_over[128:256, :] = over[128:256, :]
    to_side[0:128, :] = side[0:128, :]
    to_side[128:256, :] = (side[128:256, :].astype(F32) + from_over[...].astype(F32)).astype(BF)


def relay(over, side, from_side, from_over):
    return call(
        relay_kernel,
        [(VMEM, like(256, 2048))] * 2,
        [VMEM] * 4,
        (over, side, from_side, from_over),
        limit=60,
        moved=5 * MIB,
    )


def plane_sum_kernel(place, own, over, side, keep, *sent):
    for s in range(4):
        columns = at((place[2] + s) % 4 * 512, 512, 512)
        total = own[:, columns].astype(F32) + over[:, columns].astype(F32) + side[:, columns].astype(F32)
        if s:
            sent[s - 1][...] = total.astype(BF)
        else:
            keep[...] = total


def plane_sum(place, own, over, side):
    return call(
        plane_sum_kernel,
        [(VMEM, like(256, 512, dtype=F32))] + [(VMEM, like(256, 512))] * 3,
        [SMEM] + [VMEM] * 3,
        (place, own, over, side),
        limit=60,
        moved=5 * MIB,
    )


def plane_sum_whole_kernel(own, over, side, whole):
    for step in range(4):
        columns = slice(step * 512, (step + 1) * 512)
        total = own[:, columns].astype(F32) + over[:, columns].astype(F32) + side[:, columns].astype(F32)
        whole[step * 256 : (step + 1) * 256, :] = total.astype(BF)


def plane_sum_whole(own, over, side):
    return call(
        plane_sum_whole_kernel,
        [(VMEM, like(1024, 512))],
        [VMEM] * 3,
        (own, over, side),
    )[0]


def line_sum_kernel(place, keep, one, two, three, mine, other):
    core = place[1]
    for target, half in ((other, 1 - core), (mine, core)):
        rows = at(half * 128, 128)
        total = keep[rows, :]
        for part in (one, two, three):
            total = total + part[rows, :].astype(F32)
        target[...] = total.astype(target.dtype)


def line_sum(place, keep, parts):
    return call(
        line_sum_kernel,
        [(VMEM, like(128, 512, dtype=F32)), (VMEM, like(128, 512))],
        [SMEM] + [VMEM] * 4,
        (place, keep, *parts),
        limit=60,
        moved=2 * MIB,
    )


def spread_kernel(place, mine, other, *outs):
    core, columns = place[1], mine.shape[1] // len(outs)
    for one, out in enumerate(outs):
        cut = slice(one * columns, (one + 1) * columns)
        out[:, at(core * columns, columns)] = mine[:, cut].astype(F32)
        out[:, at((1 - core) * columns, columns)] = other[:, cut].astype(F32)


def spread(place, mine, other):
    return call(
        spread_kernel,
        [(VMEM, like(128, 256, dtype=F32))] * 4,
        [SMEM] + [VMEM] * 2,
        (place, mine, other),
        limit=60,
        moved=MIB,
    )


def spread_feed_kernel(place, mine_one, other_one, mine_two, other_two, *outs):
    core = place[1]
    for part, (mine, other) in enumerate(((mine_one, other_one), (mine_two, other_two))):
        for one, out in enumerate(outs):
            cut = slice(one * 256, (one + 1) * 256)
            out[:, at(core * 512 + part * 256, 256)] = mine[:, cut].astype(F32)
            out[:, at((1 - core) * 512 + part * 256, 256)] = other[:, cut].astype(F32)


def spread_feed(place, *halves):
    return call(
        spread_feed_kernel,
        [(VMEM, like(128, 1024, dtype=F32))] * 2,
        [SMEM] + [VMEM] * 4,
        (place, *halves),
        limit=60,
        moved=2 * MIB,
    )


tie = lax.optimization_barrier


def packed_layer(args):
    image_rows, text_rows, segment_ids, cotangent, *others = args
    weights, norms = others[:10], others[10:]
    chip, core, top = lax.axis_index("chip"), lax.axis_index("core"), lax.axis_index("hi")
    place = jnp.stack([chip, core, top, core * 2 + top % 2]).astype(jnp.int32)

    def swap(value):
        return lax.ppermute(value, "core", [(0, 1), (1, 0)])

    def across(value, bit):
        return lax.ppermute(value, "chip", [(i, i ^ bit) for i in range(4)])

    def shift(value, step):
        return lax.ppermute(value, "hi", [((i + step) % 4, i) for i in range(4)])

    def line(part):
        return [shift(part, step) for step in range(1, 4)]

    def exchange(pieces):
        return [pieces[0]] + [shift(piece, step) for step, piece in enumerate(pieces) if step]

    def gather_line(part):
        return lax.all_gather(part, "hi")

    def sides(value):
        return [across(value, 1), across(value, 2)]

    def corners(pair, cut):
        return [across(pair[0][:cut], 2), across(pair[1][cut:], 1)]

    def grad_corners(grads):
        return [across(grads[3], 1), across(grads[4], 2)]

    def grad_sides(grads, got):
        to_over, to_side = relay(grads[2], grads[1], *got)
        return [across(to_over, 2), across(to_side, 1)]

    def halves(total):
        cut = total.reshape(2, 128, 512)
        sent = lax.dynamic_index_in_dim(cut, 1 - core, 0, False)
        return lax.dynamic_index_in_dim(cut, core, 0, False), swap(sent)

    ids_wide = jnp.pad(segment_ids.astype(BF)[:, None, :], ((0, 0), (0, 15), (0, 896)))
    norms_wide = jnp.pad(jnp.stack(norms).astype(BF), ((0, 10), (0, 384)))
    keep, sent, rows_keep, rows_sent, cot_keep, cot_sent, text_pair = prepare(
        place, image_rows, text_rows, ids_wide, cotangent, norms_wide, weights
    )
    v = {"rows_keep": rows_keep, "cot_keep": cot_keep, "text_pair": text_pair}
    v["taken"], v["rows_taken"], v["cot_taken"] = swap(sent), swap(rows_sent), swap(cot_sent)
    v["text_taken"] = swap(text_pair)
    v = tie(v)
    *v["singles"], v["near"] = join(place, keep, v.pop("taken"))
    v = tie(v)

    v["near"] = [v["near"], *sides(v["near"])]
    lines = line(v["singles"][0])
    v["pieces"] = pick(place, v.pop("rows_keep"), v.pop("rows_taken"))
    v["cot_pieces"] = pick(place, v.pop("cot_keep"), v.pop("cot_taken"))
    v["text_pieces"] = pick(place, v.pop("text_pair"), v.pop("text_taken"))
    v = tie(v)
    v["near"] += corners(v["near"][1:], 128)
    v["line"] = lines
    v = tie(v)

    rest = stack(v.pop("line"))
    v["far_self"] = [rest, *sides(rest)]
    pieces = exchange(v.pop("pieces"))
    line_cross = gather_line(v["singles"][1])
    v = tie(v)
    v["far_self"] += corners(v["far_self"][1:], 384)
    v["pieces"], v["line_cross"] = pieces, line_cross
    v = tie(v)
    v["rows_own"] = stack([piece[None] for piece in v.pop("pieces")])
    v["rows_other"] = swap(v["rows_own"])
    v["w_self"], v["norms"] = assemble_first(place, v.pop("near"), v.pop("far_self"))
    line_one = gather_line(v["singles"][2])
    v = tie(v)

    v["far_cross"] = sides(v["line_cross"])
    v["text_pieces"] = exchange(v["text_pieces"])
    v["line_one"] = line_one
    v["normed_one"], v["qkv"], v["self_mix"], v["self_lse"], v["mine"] = fused_self_forward(
        place, v["rows_own"], v["rows_other"], v["norms"], v["w_self"]
    )
    v = tie(v)

    v["theirs"] = swap(v["mine"])
    v["far_cross"] += corners(v["far_cross"], 2)
    line_two = gather_line(v.pop("singles")[3])
    text_pieces = v.pop("text_pieces")
    v["text"] = arrange(place, text_pieces)
    ids = text_pieces[0][32, :128].astype(jnp.int32)
    v["caption"] = jnp.repeat(ids, 8)[None, :]
    v["ids"] = ids[:, None]
    v = tie(v)

    v["far_one"] = sides(v["line_one"])
    v["line_two"] = line_two
    v["cot_pieces"] = exchange(v["cot_pieces"])
    v["w_cross"] = assemble(place, v.pop("line_cross"), v.pop("far_cross"))
    v["after_attn"], v["normed_two"], v["queries"], v["keys"], v["cross_mix"], v["cross_lse"], v["mine"] = (
        fused_cross_forward(
            place, v["rows_own"], v.pop("rows_other"), v["mine"], v["theirs"], v["norms"], v["text"], v["ids"],
            v["caption"], v["w_cross"],
        )
    )
    v = tie(v)

    v["theirs"] = swap(v["mine"])
    v["far_one"] += corners(v["far_one"], 2)
    v["cot_own"] = stack([piece[None] for piece in v.pop("cot_pieces")])
    v["cot_other"] = swap(v["cot_own"])
    w_two = lax.all_gather(v.pop("line_two"), "chip")
    v = tie(v)

    v["w_two"] = w_two
    w_one = assemble(place, v.pop("line_one"), v.pop("far_one"))
    v["grads_one"], v["after_cross"], v["normed_three"], v["cot"], v["out_sum"], v["back_sum"] = feed_first(
        place, v["after_attn"], v["mine"], v["theirs"], v["norms"], v.pop("cot_own"), v.pop("cot_other"), w_one
    )
    v = tie(v)

    total_one = lax.psum_scatter(v.pop("grads_one"), "chip", scatter_dimension=0, tiled=False)
    *v["grads_two"], v["out_keep"], v["out_sent"], v["mine"] = feed_second(
        place, v.pop("normed_three"), v["cot"], v.pop("out_sum"), v.pop("back_sum"), v.pop("w_two")
    )
    v = tie(v)

    v["theirs"] = swap(v["mine"])
    v["out_theirs"] = swap(v.pop("out_sent"))
    v = tie(v)
    v["got_two"] = grad_corners(v["grads_two"])
    v["pieces"] = exchange(finish(place, v.pop("out_keep"), v.pop("out_theirs")))
    v["grad_cross"], v["part"], v["norms_three"], v["text_part"], *v["grads_three"] = fused_cross_backward(
        place, v.pop("after_cross"), v.pop("mine"), v.pop("theirs"), v.pop("cot"), v["norms"], v.pop("w_cross"),
        v.pop("normed_two"), v.pop("text"), v.pop("queries"), v.pop("keys"), v.pop("cross_mix"),
        v.pop("cross_lse"), v.pop("ids"), v.pop("caption"),
    )
    v = tie(v)

    v["theirs"] = swap(v["part"])
    v["total_one"] = total_one
    v["to_two"] = relay(v["grads_two"][2], v["grads_two"][1], *v.pop("got_two"))
    v = tie(v)

    to_two = v.pop("to_two")
    v["sides_two"] = [across(to_two[0], 2), across(to_two[1], 1)]
    v["got_three"] = grad_corners(v["grads_three"])
    v["line_one"] = lax.psum_scatter(v.pop("total_one"), "hi", scatter_dimension=0, tiled=False)
    v["grad_own"], v["low_grad"], v["norms_two"], v["dqkv"] = fused_self_backward(
        place, v.pop("after_attn"), v.pop("part"), v.pop("theirs"), v.pop("grad_cross"), v["norms"], v["w_self"],
        v.pop("qkv"), v["self_mix"], v.pop("self_lse"),
    )
    v = tie(v)

    v["sides_three"] = grad_sides(v["grads_three"], v.pop("got_three"))
    total_two = plane_sum_whole(v.pop("grads_two")[0], *v.pop("sides_two"))
    line_two = lax.psum_scatter(total_two, "hi", scatter_dimension=0, tiled=True)
    v["grads_four"] = self_grads(place, v.pop("normed_one"), v.pop("low_grad"), v["dqkv"], v.pop("self_mix"))
    mine, sent = part_images(place, v.pop("pieces"))
    (v["result"],) = land(place, mine, swap(sent), BF)
    v["feed_one"] = halves(v.pop("line_one"))
    v = tie(v)

    v["got_four"] = grad_corners(v["grads_four"])
    total_three, dqkv = tie((plane_sum_whole(v.pop("grads_three")[0], *v.pop("sides_three")), v.pop("dqkv")))
    line_three = lax.psum_scatter(total_three, "hi", scatter_dimension=0, tiled=True)
    v["line_two"] = line_two
    v["kept"], v["sent"] = self_back(place, dqkv, v.pop("w_self"))
    v = tie(v)

    v["sides_four"] = grad_sides(v["grads_four"], v.pop("got_four"))
    pieces = last_norm(
        place, v.pop("rows_own"), v.pop("grad_own"), v.pop("kept"), swap(v.pop("sent")), v.pop("norms"),
        v.pop("text_part"), v.pop("norms_two"), v.pop("norms_three"),
    )
    input_pieces = exchange(pieces)
    v = tie(v)

    v["kept"], *sums_four = plane_sum(place, v.pop("grads_four")[0], *v.pop("sides_four"))
    v["line_four"] = [shift(piece, 3 - i) for i, piece in enumerate(sums_four)]
    v["feed_grads"] = spread_feed(place, *v.pop("feed_one"), *halves(v.pop("line_two")))
    later = tie((place, sums_four))[0]
    mine, sent = part_images(later, input_pieces)
    v["input_grad"], v["text_grad"], sums = land(place, mine, swap(sent), F32)
    sums = sums + across(sums, 1)
    sums = sums + across(sums, 2)
    v["sums"] = lax.dynamic_slice_in_dim(sums, (chip * 2 + core) * 128, 128, 1)
    v["cross_grads"] = spread(place, *halves(line_three))
    v = tie(v)

    kept, sent = line_sum(place, v.pop("kept"), v.pop("line_four"))
    own_grads = spread(place, kept, swap(sent))
    return (
        v["result"], v["input_grad"], v["text_grad"], *own_grads, *v["cross_grads"], *v["feed_grads"],
        *[v["sums"][i] for i in range(6)],
    )


def solution(mesh):
    fsdp, tensor = mesh.shape["fsdp"], mesh.shape["tensor"]

    def run(*args):
        images = args[0].shape[0] // fsdp
        tops = 2 * images
        shape = {"chip": fsdp // 2, "core": 2, "hi": tops, "lo": tensor // tops}
        fine = Mesh(mesh.devices.reshape(tuple(shape.values())), tuple(shape))
        first, second = ("chip", "core"), ("hi", "lo")
        wide, weight, norm = P(first, second, None), P(first, second), P(first)
        outs = (wide,) * 3 + (weight,) * 10 + (norm,) * 6
        packed = (
            (fsdp, tensor, images) == (8, 4, 2)
            and args[0].shape[1:] == (1024, 1024)
            and args[1].shape[1:] == (128, 1024)
            and args[12].shape == (1024, 4096)
        )
        return jax.shard_map(
            lambda *local: packed_layer(local) if packed else layer(shape, local),
            mesh=fine,
            in_specs=(wide, wide, P(first, None), wide) + (weight,) * 10 + (norm,) * 6,
            out_specs=outs,
            check_vma=False,
        )(*args)

    return run
```

```python
import functools
import math

import jax
import jax.numpy as jnp
from jax import lax
from jax.experimental import pallas as pl
from jax.experimental.pallas import tpu as pltpu
from jax.sharding import Mesh
from jax.sharding import PartitionSpec as P

HD = 64
EPS = 1e-05
NEG = -1e30
LOG2E = math.log2(math.e)
BF = jnp.bfloat16
F32 = jnp.float32
NT = (((1,), (1,)), ((), ()))
TN = (((0,), (0,)), ((), ()))
NN = (((1,), (0,)), ((), ()))


def dot(left, right, dims=NN):
    return lax.dot_general(left, right, dims, preferred_element_type=F32)


def lane_head(shape, axis, head):
    return lax.broadcasted_iota(jnp.int32, shape, axis) // HD == head


def self_forward_kernel(q_ref, k_ref, v_ref, mix_ref, lse_ref, *, block):
    length = q_ref.shape[0]
    scale = LOG2E * HD**-0.5
    causal = lax.broadcasted_iota(jnp.int32, (block, block), 0) <= lax.broadcasted_iota(
        jnp.int32, (block, block), 1
    )
    for at in range(length // block):
        lo, hi = at * block, (at + 1) * block
        query = q_ref[lo:hi, :]
        mixes = []
        for head in range(2):
            one = jnp.where(lane_head((1, 2 * HD), 1, head), query, jnp.zeros_like(query))
            diag = jnp.where(causal, dot(k_ref[lo:hi, :], one, NT), NEG)
            peak = jnp.max(diag, 0, keepdims=True)
            if at:
                past = dot(k_ref[:lo, :], one, NT)
                peak = jnp.maximum(peak, jnp.max(past, 0, keepdims=True))
            weights = jnp.exp2((diag - peak) * scale)
            total = jnp.sum(weights, 0, keepdims=True)
            mixed = dot(v_ref[lo:hi, :], weights.astype(BF), TN)
            if at:
                weights = jnp.exp2((past - peak) * scale)
                total = total + jnp.sum(weights, 0, keepdims=True)
                mixed = mixed + dot(v_ref[:lo, :], weights.astype(BF), TN)
            mixes.append(mixed / total)
            lse_ref[0, head : head + 1, lo:hi] = peak * scale + jnp.log2(total)
        both = jnp.where(lane_head((2 * HD, 1), 0, 0), mixes[0], mixes[1])
        mix_ref[lo:hi, :] = both.T.astype(BF)


def self_backward_kernel(
    q_ref, k_ref, v_ref, mix_ref, grad_ref, lse_ref, dq_ref, dk_ref, dv_ref, dk_sum, dv_sum, *, block
):
    length = q_ref.shape[0]
    scale = LOG2E * HD**-0.5
    causal = lax.broadcasted_iota(jnp.int32, (block, block), 0) <= lax.broadcasted_iota(
        jnp.int32, (block, block), 1
    )
    dk_sum[...] = jnp.zeros_like(dk_sum)
    dv_sum[...] = jnp.zeros_like(dv_sum)
    for at in range(length // block):
        lo, hi = at * block, (at + 1) * block
        query = q_ref[lo:hi, :]
        grad = grad_ref[lo:hi, :]
        product = (grad.astype(F32) * mix_ref[lo:hi, :].astype(F32)).T
        grads = []
        for head in range(2):
            picked = lane_head((1, 2 * HD), 1, head)
            one = jnp.where(picked, query, jnp.zeros_like(query))
            one_grad = jnp.where(picked, grad, jnp.zeros_like(grad))
            delta = jnp.sum(product[head * HD : (head + 1) * HD], 0, keepdims=True)
            lse = lse_ref[0, head : head + 1, lo:hi]
            total = jnp.zeros((2 * HD, block), F32)
            for start, stop in ((0, lo), (lo, hi)):
                if start == stop:
                    continue
                keys = k_ref[start:stop, :]
                weights = jnp.exp2(dot(keys, one, NT) * scale - lse)
                if start == lo:
                    weights = jnp.where(causal, weights, 0.0)
                slope = dot(v_ref[start:stop, :], one_grad, NT)
                score_grad = (weights * (slope - delta)).astype(BF)
                dv_sum[start:stop, :] += dot(weights.astype(BF), one_grad)
                dk_sum[start:stop, :] += dot(score_grad, one)
                total = total + dot(keys, score_grad, TN)
            grads.append(total)
        both = jnp.where(lane_head((2 * HD, 1), 0, 0), grads[0], grads[1])
        dq_ref[lo:hi, :] = (both.T * HD**-0.5).astype(BF)
    dk_ref[...] = (dk_sum[...] * HD**-0.5).astype(BF)
    dv_ref[...] = dv_sum[...].astype(BF)


def cross_forward_kernel(q_ref, k_ref, v_ref, ids_ref, caption_ref, mix_ref, lse_ref, *, block):
    length = q_ref.shape[0]
    scale = LOG2E * HD**-0.5
    for at in range(length // block):
        lo, hi = at * block, (at + 1) * block
        query = q_ref[lo:hi, :]
        seen = ids_ref[...] == caption_ref[:, lo:hi]
        mixes = []
        for head in range(2):
            one = jnp.where(lane_head((1, 2 * HD), 1, head), query, jnp.zeros_like(query))
            scores = jnp.where(seen, dot(k_ref[...], one, NT), NEG)
            peak = jnp.max(scores, 0, keepdims=True)
            weights = jnp.exp2((scores - peak) * scale)
            total = jnp.sum(weights, 0, keepdims=True)
            mixes.append(dot(v_ref[...], weights.astype(BF), TN) / total)
            lse_ref[0, head : head + 1, lo:hi] = peak * scale + jnp.log2(total)
        both = jnp.where(lane_head((2 * HD, 1), 0, 0), mixes[0], mixes[1])
        mix_ref[lo:hi, :] = both.T.astype(BF)


def cross_backward_kernel(
    q_ref, k_ref, v_ref, mix_ref, grad_ref, lse_ref, ids_ref, caption_ref, dq_ref, dk_ref, dv_ref, *, block
):
    length = q_ref.shape[0]
    scale = LOG2E * HD**-0.5
    keys, values = k_ref[...], v_ref[...]
    dk_sum = jnp.zeros(keys.shape, F32)
    dv_sum = jnp.zeros(keys.shape, F32)
    for at in range(length // block):
        lo, hi = at * block, (at + 1) * block
        query = q_ref[lo:hi, :]
        grad = grad_ref[lo:hi, :]
        product = (grad.astype(F32) * mix_ref[lo:hi, :].astype(F32)).T
        seen = ids_ref[...] == caption_ref[:, lo:hi]
        grads = []
        for head in range(2):
            picked = lane_head((1, 2 * HD), 1, head)
            one = jnp.where(picked, query, jnp.zeros_like(query))
            one_grad = jnp.where(picked, grad, jnp.zeros_like(grad))
            delta = jnp.sum(product[head * HD : (head + 1) * HD], 0, keepdims=True)
            lse = lse_ref[0, head : head + 1, lo:hi]
            weights = jnp.where(seen, jnp.exp2(dot(keys, one, NT) * scale - lse), 0.0)
            slope = dot(values, one_grad, NT)
            score_grad = (weights * (slope - delta)).astype(BF)
            dv_sum = dv_sum + dot(weights.astype(BF), one_grad)
            dk_sum = dk_sum + dot(score_grad, one)
            grads.append(dot(keys, score_grad, TN))
        both = jnp.where(lane_head((2 * HD, 1), 0, 0), grads[0], grads[1])
        dq_ref[lo:hi, :] = (both.T * HD**-0.5).astype(BF)
    dk_ref[...] = (dk_sum * HD**-0.5).astype(BF)
    dv_ref[...] = dv_sum.astype(BF)


def feed_kernel(
    rows_ref, cot_ref, win_ref, wout_ref, out_in, back_in, gin_ref, gout_ref, out_ref, back_ref, rows_t, cot_t, *, first
):
    step = pl.program_id(0)

    @pl.when(step == 0)
    def _():
        rows_t[...] = rows_ref[...].T
        cot_t[...] = cot_ref[...].T
        if first:
            out_ref[...] = jnp.zeros_like(out_ref)
            back_ref[...] = jnp.zeros_like(back_ref)
        else:
            out_ref[...] = out_in[...]
            back_ref[...] = back_in[...]

    pre = dot(rows_ref[...], win_ref[...])
    square = pre * pre
    slope = math.sqrt(2.0 / math.pi)
    bent = jnp.tanh(pre * (slope + slope * 0.044715 * square))
    half = 0.5 * (1.0 + bent)
    act = (pre * half).astype(BF)
    out_ref[...] += dot(act, wout_ref[...], NT)
    gout_ref[...] = dot(cot_t[...], act).astype(BF)
    bend = half + pre * (0.5 * (1.0 - bent * bent)) * (slope + 3.0 * slope * 0.044715 * square)
    pre_grad = (dot(cot_ref[...], wout_ref[...]) * bend).astype(BF)
    gin_ref[...] = dot(rows_t[...], pre_grad).astype(BF)
    back_ref[...] += dot(pre_grad, win_ref[...], NT)


VMEM_LIMIT = 60 * 1024 * 1024


def params():
    return pltpu.CompilerParams(vmem_limit_bytes=VMEM_LIMIT)


def column(rows, offset):
    return pl.BlockSpec((rows, 2 * HD), lambda i: (0, offset + i))


def self_forward(packed):
    length, width = packed.shape
    pairs = width // (6 * HD)
    return pl.pallas_call(
        functools.partial(self_forward_kernel, block=256),
        grid=(pairs,),
        in_specs=[column(length, 0), column(length, pairs), column(length, 2 * pairs)],
        out_specs=[column(length, 0), pl.BlockSpec((1, 2, length), lambda i: (i, 0, 0))],
        out_shape=[
            jax.ShapeDtypeStruct((length, pairs * 2 * HD), BF),
            jax.ShapeDtypeStruct((pairs, 2, length), F32),
        ],
        compiler_params=params(),
        cost_estimate=pl.CostEstimate(
            flops=8 * pairs * length * length * 2 * HD * 2,
            bytes_accessed=8 * pairs * length * 2 * HD,
            transcendentals=2 * pairs * length * length,
        ),
    )(packed, packed, packed)


def self_backward(packed, mix, grad, lse):
    length, width = packed.shape
    pairs = width // (6 * HD)
    part = jax.ShapeDtypeStruct((length, pairs * 2 * HD), BF)
    return pl.pallas_call(
        functools.partial(self_backward_kernel, block=256),
        grid=(pairs,),
        in_specs=[
            column(length, 0),
            column(length, pairs),
            column(length, 2 * pairs),
            column(length, 0),
            column(length, 0),
            pl.BlockSpec((1, 2, length), lambda i: (i, 0, 0)),
        ],
        out_specs=[column(length, 0)] * 3,
        out_shape=[part] * 3,
        scratch_shapes=[pltpu.VMEM((length, 2 * HD), F32)] * 2,
        compiler_params=params(),
        cost_estimate=pl.CostEstimate(
            flops=20 * pairs * length * length * 2 * HD * 2,
            bytes_accessed=16 * pairs * length * 2 * HD,
            transcendentals=2 * pairs * length * length,
        ),
    )(packed, packed, packed, mix, grad, lse)


def cross_forward(queries, keys, ids, captions):
    length, width = queries.shape
    texts = keys.shape[0]
    pairs = width // (2 * HD)
    return pl.pallas_call(
        functools.partial(cross_forward_kernel, block=min(512, length)),
        grid=(pairs,),
        in_specs=[
            column(length, 0),
            column(texts, 0),
            column(texts, pairs),
            pl.BlockSpec((texts, 1), lambda i: (0, 0)),
            pl.BlockSpec((1, length), lambda i: (0, 0)),
        ],
        out_specs=[column(length, 0), pl.BlockSpec((1, 2, length), lambda i: (i, 0, 0))],
        out_shape=[
            jax.ShapeDtypeStruct((length, width), BF),
            jax.ShapeDtypeStruct((pairs, 2, length), F32),
        ],
        compiler_params=params(),
    )(queries, keys, keys, ids, captions)


def cross_backward(queries, keys, mix, grad, lse, ids, captions):
    length, width = queries.shape
    texts = keys.shape[0]
    pairs = width // (2 * HD)
    return pl.pallas_call(
        functools.partial(cross_backward_kernel, block=min(512, length)),
        grid=(pairs,),
        in_specs=[
            column(length, 0),
            column(texts, 0),
            column(texts, pairs),
            column(length, 0),
            column(length, 0),
            pl.BlockSpec((1, 2, length), lambda i: (i, 0, 0)),
            pl.BlockSpec((texts, 1), lambda i: (0, 0)),
            pl.BlockSpec((1, length), lambda i: (0, 0)),
        ],
        out_specs=[column(length, 0), column(texts, 0), column(texts, 0)],
        out_shape=[
            jax.ShapeDtypeStruct((length, width), BF),
            jax.ShapeDtypeStruct((texts, width), BF),
            jax.ShapeDtypeStruct((texts, width), BF),
        ],
        compiler_params=params(),
    )(queries, keys, keys, mix, grad, lse, ids, captions)


def feed(rows, cot, w_in, w_out, sums):
    length, width = rows.shape
    units = w_in.shape[1]
    block = min(256, units)
    whole = pl.BlockSpec((length, width), lambda i: (0, 0))
    cut = pl.BlockSpec((width, block), lambda i: (0, i))
    first = sums is None
    kernel = functools.partial(feed_kernel, first=first)
    operands = [rows, cot, w_in, w_out]
    specs = [whole, whole, cut, cut]
    if first:
        body = lambda a, b, c, d, *rest: kernel(a, b, c, d, None, None, *rest)
    else:
        body = kernel
        operands += list(sums)
        specs += [whole, whole]
    total = jax.ShapeDtypeStruct((length, width), F32)
    part = jax.ShapeDtypeStruct((width, units), BF)
    return pl.pallas_call(
        body,
        grid=(units // block,),
        in_specs=specs,
        out_specs=[cut, cut, whole, whole],
        out_shape=[part, part, total, total],
        scratch_shapes=[pltpu.VMEM((width, length), BF)] * 2,
        compiler_params=params(),
        cost_estimate=pl.CostEstimate(
            flops=12 * length * width * units,
            bytes_accessed=8 * width * units + 8 * length * width,
            transcendentals=length * units,
        ),
    )(*operands)


def norm_parts(values):
    center = values - jnp.mean(values, -1, keepdims=True)
    inverse = lax.rsqrt(jnp.mean(center * center, -1, keepdims=True) + EPS)
    return center * inverse, inverse


def layer_norm(values, gain, offset):
    return (norm_parts(values)[0] * gain + offset).astype(BF)


def norm_back(values, gain, grad):
    hat, inverse = norm_parts(values)
    scaled = grad * gain
    back = inverse * (
        scaled
        - jnp.mean(scaled, -1, keepdims=True)
        - hat * jnp.mean(scaled * hat, -1, keepdims=True)
    )
    lead = tuple(range(values.ndim - 1))
    return back, jnp.sum(grad * hat, lead), jnp.sum(grad, lead)


def layer(shape, args):
    chips, tops, lows = shape["chip"], shape["hi"], shape["lo"]
    (
        image_rows,
        text_rows,
        segment_ids,
        cotangent,
        query_weight,
        key_weight,
        value_weight,
        attn_output,
        cross_query,
        cross_key,
        cross_value,
        cross_output,
        hidden_in,
        hidden_out,
        *norms,
    ) = args
    images, rows, width = image_rows.shape
    texts = text_rows.shape[1]
    half_rows = rows // 2
    length = rows * lows * tops
    shard = query_weight.shape[0]
    chip, core = lax.axis_index("chip"), lax.axis_index("core")
    top = lax.axis_index("hi")
    own_slot = core * images + top % images

    def swap(value):
        return lax.ppermute(value, "core", [(0, 1), (1, 0)])

    def across(value, bit):
        return lax.ppermute(value, "chip", [(i, i ^ bit) for i in range(chips)])

    def shift(value, step):
        return lax.ppermute(value, "hi", [((i + step) % tops, i) for i in range(tops)])

    def matching(number, back):
        pairs = []
        for source_core in range(2):
            for source_top in range(tops):
                slot = source_top ^ number
                target = (slot // images) * tops + source_core * images + slot % images
                source = source_core * tops + source_top
                pairs.append((target, source) if back else (source, target))
        return pairs

    def to_image(piece_of):
        got = [
            lax.ppermute(piece_of(top ^ number), ("core", "hi"), matching(number, False))
            for number in range(tops)
        ]
        whole = jnp.stack(got)
        return jnp.stack(
            [lax.dynamic_index_in_dim(whole, own_slot ^ place, 0, False) for place in range(tops)]
        )

    def from_image(pieces):
        return [
            lax.ppermute(
                lax.dynamic_index_in_dim(pieces, own_slot ^ number, 0, False),
                ("core", "hi"),
                matching(number, True),
            )
            for number in range(tops)
        ]

    def image_piece(value):
        def piece(slot):
            return lax.dynamic_slice(
                value,
                (slot % images, (slot // images) * half_rows, 0),
                (1, half_rows, width),
            )[0]

        return piece

    def to_rows(pieces):
        got = jnp.stack(from_image(pieces))
        ordered = jnp.stack(
            [lax.dynamic_index_in_dim(got, top ^ slot, 0, False) for slot in range(tops)]
        )
        ordered = ordered.reshape(2, images, half_rows, width)
        return jnp.swapaxes(ordered, 0, 1).reshape(images, rows, width)

    def tp_gather(mine):
        if lows == 1:
            other = swap(mine)
            first = jnp.where(core == 0, mine, other)
            second = jnp.where(core == 0, other, mine)
            return jnp.stack([first, second], 1).reshape(length, width)
        every = lax.all_gather(mine, ("lo", "core"))
        every = every.reshape(lows * 2, tops, half_rows, width)
        return jnp.swapaxes(every, 0, 1).reshape(length, width)

    def tp_reduce(partial):
        if lows == 1:
            cut = partial.reshape(tops, 2, half_rows, width)
            sent = lax.dynamic_index_in_dim(cut, 1 - core, 1, False).astype(BF)
            kept = lax.dynamic_index_in_dim(cut, core, 1, False)
            return kept + swap(sent).astype(F32)
        cut = jnp.swapaxes(partial.astype(BF).reshape(tops, lows * 2, half_rows, width), 0, 1)
        cut = lax.psum_scatter(cut, ("lo", "core"), scatter_dimension=0, tiled=False)
        return cut.astype(F32)

    def core_half(weight, which):
        columns = weight.shape[1] // 2
        return lax.dynamic_slice_in_dim(weight, which * columns, columns, 1)

    def pack(which):
        feeds = [core_half(weight, which) for weight in (hidden_in, hidden_out)]
        cuts = feeds[0].shape[1] // 2
        groups = [
            [core_half(w, which) for w in (query_weight, key_weight, value_weight, attn_output)],
            [core_half(w, which) for w in (cross_query, cross_key, cross_value, cross_output)],
            [w[:, :cuts] for w in feeds],
            [w[:, cuts:] for w in feeds],
        ]
        return jnp.concatenate([w for group in groups for w in group], 1)

    kept = pack(core)
    taken = swap(pack(1 - core))
    own = jnp.concatenate(
        [jnp.where(core == 0, kept, taken), jnp.where(core == 0, taken, kept)], 0
    )
    block_rows = 2 * shard
    group_width = own.shape[1] // 4

    def plane_gather(piece):
        if chips != 4:
            return lax.all_gather(piece, "chip", axis=0, tiled=True)
        side = across(piece, 1)
        over = across(piece, 2)
        corner_low = across(side[:shard], 2)
        corner_high = across(over[shard:], 1)
        corner = jnp.concatenate([corner_low, corner_high], 0)
        pieces = jnp.stack([piece, side, over, corner])
        ordered = [lax.dynamic_index_in_dim(pieces, chip ^ place, 0, False) for place in range(4)]
        return jnp.concatenate(ordered, 0)

    def plane_scatter(grads):
        if chips != 4:
            return lax.psum_scatter(grads, "chip", scatter_dimension=0, tiled=True).astype(F32)

        def rows_of(place, low, count):
            return lax.dynamic_slice_in_dim(grads, (chip ^ place) * block_rows + low, count, 0)

        by_side = across(rows_of(3, 0, shard), 1)
        by_over = across(rows_of(3, shard, shard), 2)
        to_over = jnp.concatenate(
            [rows_of(2, 0, shard).astype(F32) + by_side.astype(F32), rows_of(2, shard, shard).astype(F32)], 0
        ).astype(BF)
        to_side = jnp.concatenate(
            [rows_of(1, 0, shard).astype(F32), rows_of(1, shard, shard).astype(F32) + by_over.astype(F32)], 0
        ).astype(BF)
        over, side = across(to_over, 2), across(to_side, 1)
        return rows_of(0, 0, block_rows).astype(F32) + over.astype(F32) + side.astype(F32)

    def top_scatter(pieces):
        total = pieces[0].astype(F32)
        for step in range(1, tops):
            total = total + shift(pieces[step].astype(BF), tops - step).astype(F32)
        return total

    def core_split(total):
        cut = total.reshape(2, shard, total.shape[1])
        mine = lax.dynamic_index_in_dim(cut, core, 0, False)
        other = swap(lax.dynamic_index_in_dim(cut, 1 - core, 0, False).astype(BF)).astype(F32)
        return jnp.where(core == 0, mine, other), jnp.where(core == 0, other, mine)

    own_wide = plane_gather(own)

    def fetch(group, count):
        part = own[:, group * group_width : (group + 1) * group_width]
        columns = group_width // count
        got = [shift(part, step).reshape(block_rows, count, 1, columns) for step in range(1, tops)]
        rest = jnp.concatenate(got, 2).reshape(block_rows, (tops - 1) * group_width)
        rest = plane_gather(rest).reshape(width, count, (tops - 1) * columns)
        near = own_wide[:, group * group_width : (group + 1) * group_width]
        near = near.reshape(width, count, columns)
        return [
            jnp.concatenate([near[:, one], rest[:, one]], 1) for one in range(count)
        ]

    def give(grads):
        count = len(grads)
        columns = grads[0].shape[1] // tops
        summed = plane_scatter(jnp.concatenate(grads, 1)).reshape(block_rows, count, tops, columns)
        pieces = [summed[:, :, step].reshape(block_rows, count * columns) for step in range(tops)]
        low, high = core_split(top_scatter(pieces))
        low, high = low.reshape(shard, count, columns), high.reshape(shard, count, columns)
        return [(low[:, one], high[:, one]) for one in range(count)]

    packed_norms = lax.all_gather(jnp.stack(norms), ("chip", "core"), axis=1, tiled=True)
    gain_one, bias_one, gain_two, bias_two, gain_three, bias_three = packed_norms

    w_query, w_key, w_value, w_out = fetch(0, 4)
    inputs = to_image(image_piece(image_rows)).astype(F32)
    c_query, c_key, c_value, c_out = fetch(1, 4)
    in_low, out_low = fetch(2, 2)
    in_high, out_high = fetch(3, 2)

    text = to_image(lambda slot: text_rows[slot % images])
    if lows > 1:
        text = lax.all_gather(text, "lo", axis=1)
    text = text.reshape(tops * lows * texts, width)
    other_ids = swap(segment_ids)
    ids = jnp.where(core == top // images, segment_ids, other_ids)
    ids = lax.dynamic_index_in_dim(ids, top % images, 0, False)
    captions = jnp.repeat(ids, length // ids.shape[0])[None, :]
    ids = ids[:, None]
    cot = to_image(image_piece(cotangent))

    full_one = tp_gather(layer_norm(inputs, gain_one, bias_one))
    packed = dot(full_one, jnp.concatenate([w_query, w_key, w_value], 1)).astype(BF)
    self_mix, self_lse = self_forward(packed)
    after_attn = inputs + tp_reduce(dot(self_mix, w_out, NT))
    full_two = tp_gather(layer_norm(after_attn, gain_two, bias_two))
    queries = dot(full_two, c_query).astype(BF)
    w_text = jnp.concatenate([c_key, c_value], 1)
    keys = dot(text, w_text).astype(BF)
    cross_mix, cross_lse = cross_forward(queries, keys, ids, captions)
    after_cross = after_attn + tp_reduce(dot(cross_mix, c_out, NT))
    full_three = tp_gather(layer_norm(after_cross, gain_three, bias_three))
    full_cot = tp_gather(cot)
    gin_low, gout_low, *sums = feed(full_three, full_cot, in_low, out_low, None)
    gin_high, gout_high, out_sum, back_sum = feed(full_three, full_cot, in_high, out_high, sums)
    low_grads = give([gin_low, gout_low])
    high_grads = give([gin_high, gout_high])
    result = to_rows((after_cross + tp_reduce(out_sum)).astype(BF))

    back_three, dgain_three, dbias_three = norm_back(after_cross, gain_three, tp_reduce(back_sum))
    grad_cross = cot.astype(F32) + back_three
    full_grad = tp_gather(grad_cross.astype(BF))
    mix_grad = dot(full_grad, c_out).astype(BF)
    dq, dk, dv = cross_backward(queries, keys, cross_mix, mix_grad, cross_lse, ids, captions)
    back_sum = dot(dq, c_query, NT)
    dkv = jnp.concatenate([dk, dv], 1)
    cross_grads = give(
        [
            dot(full_two, dq, TN).astype(BF),
            dot(text, dk, TN).astype(BF),
            dot(text, dv, TN).astype(BF),
            dot(full_grad, cross_mix, TN).astype(BF),
        ]
    )
    text_part = dot(dkv, w_text, NT).astype(BF).reshape(tops, lows, texts, width)
    if lows > 1:
        text_part = lax.psum_scatter(text_part, "lo", scatter_dimension=1, tiled=True)
    got = [part.astype(F32) for part in from_image(text_part[:, 0])]
    got = jnp.stack(got)
    got = [lax.dynamic_index_in_dim(got, top ^ slot, 0, False) for slot in range(tops)]
    text_grad = jnp.stack([got[i] + got[images + i] for i in range(images)])

    back_two, dgain_two, dbias_two = norm_back(after_attn, gain_two, tp_reduce(back_sum))
    grad_attn = grad_cross + back_two
    full_grad = tp_gather(grad_attn.astype(BF))
    mix_grad = dot(full_grad, w_out).astype(BF)
    dq, dk, dv = self_backward(packed, self_mix, mix_grad, self_lse)
    dqkv = jnp.concatenate([dq, dk, dv], 1)
    dwqkv = dot(full_one, dqkv, TN).astype(BF)
    span = dq.shape[1]
    self_grads = give(
        [
            dwqkv[:, :span],
            dwqkv[:, span : 2 * span],
            dwqkv[:, 2 * span :],
            dot(full_grad, self_mix, TN).astype(BF),
        ]
    )
    back_sum = dot(dqkv, jnp.concatenate([w_query, w_key, w_value], 1), NT)
    back_one, dgain_one, dbias_one = norm_back(inputs, gain_one, tp_reduce(back_sum))
    input_grad = to_rows((grad_attn + back_one).astype(BF)).astype(F32)

    norm_sums = lax.psum(
        jnp.stack([dgain_one, dbias_one, dgain_two, dbias_two, dgain_three, dbias_three]),
        ("chip", "core", "hi", "lo"),
    )
    norm_sums = lax.dynamic_slice_in_dim(norm_sums, (chip * 2 + core) * shard, shard, 1)

    feeds = [
        jnp.concatenate([low_grads[i][0], high_grads[i][0], low_grads[i][1], high_grads[i][1]], 1)
        for i in range(2)
    ]
    joined = [jnp.concatenate(pair, 1) for pair in (*self_grads, *cross_grads)]
    return (result, input_grad, text_grad, *joined, *feeds, *[norm_sums[i] for i in range(6)])


BLOCK = 256
ANY = pl.BlockSpec(memory_space=pl.ANY)
HBM = pl.BlockSpec(memory_space=pltpu.HBM)
SMEM = pl.BlockSpec(memory_space=pltpu.SMEM)
VMEM = pl.BlockSpec(memory_space=pltpu.VMEM)
LATE = object()
MIB = 1024 * 1024


def like(*shape, dtype=BF):
    return jax.ShapeDtypeStruct(shape, dtype)


class Late:
    def __init__(self, source, target, sem):
        self.ref, self.copy = target, pltpu.make_async_copy(source, target, sem)
        self.copy.start()

    def ready(self):
        if self.copy is not None:
            self.copy.wait()
            self.copy = None
        return self.ref


class Early:
    def __init__(self, source, target, sem):
        self.ref, self.copy, self.sent = source, pltpu.make_async_copy(source, target, sem), False

    def send(self):
        self.copy.start()
        self.sent = True


def call_overlapped(body, outs, ins, operands, scratch=(), limit=60):
    late_ins = [i for i, spec in enumerate(ins) if spec is LATE]
    late_outs = [i for i, (spec, _) in enumerate(outs) if spec is LATE]
    buffers = [pltpu.VMEM(operands[i].shape, operands[i].dtype) for i in late_ins]
    buffers += [pltpu.VMEM(outs[i][1].shape, outs[i][1].dtype) for i in late_outs]
    count = len(buffers)

    def wrapped(*refs):
        refs = list(refs)
        sems = refs.pop()
        extra = refs[len(refs) - count :]
        refs = refs[: len(refs) - count]
        loads = [Late(refs[i], extra[n], sems.at[n]) for n, i in enumerate(late_ins)]
        for load, i in zip(loads, late_ins):
            refs[i] = load
        stores = []
        for n, i in enumerate(late_outs):
            place = len(ins) + i
            stores.append(Early(extra[len(late_ins) + n], refs[place], sems.at[len(late_ins) + n]))
            refs[place] = stores[-1]
        body(*refs)
        for load in loads:
            load.ready()
        for store in stores:
            if not store.sent:
                store.send()
        for store in stores:
            store.copy.wait()

    return call(
        wrapped,
        [(HBM if spec is LATE else spec, shape) for spec, shape in outs],
        [ANY if spec is LATE else spec for spec in ins],
        operands,
        [*scratch, *buffers, pltpu.SemaphoreType.DMA((max(count, 1),))],
        limit,
    )


def call(body, outs, ins, operands, scratch=(), limit=60, grid=None, flops=0, moved=0):
    single = not isinstance(outs, (list, tuple))
    extra = {} if grid is None else {"grid": grid}
    cost = pl.CostEstimate(flops=1, bytes_accessed=1, transcendentals=0)
    out_specs, out_shape = ([outs[0]], [outs[1]]) if single else ([o[0] for o in outs], [o[1] for o in outs])
    return list(pl.pallas_call(
        body,
        in_specs=ins,
        out_specs=out_specs,
        out_shape=out_shape,
        scratch_shapes=list(scratch),
        compiler_params=pltpu.CompilerParams(vmem_limit_bytes=limit * MIB),
        cost_estimate=cost,
        **extra,
    )(*operands))


def run_copies(copies, sems):
    started = [pltpu.make_async_copy(source, target, sems.at[i]) for i, (source, target) in enumerate(copies)]
    for copy in started:
        copy.start()
    for copy in started:
        copy.wait()


def at(offset, count, unit=128):
    return pl.ds(pl.multiple_of(offset, unit), count)


def prepare_kernel(place, norms, wq, wk, wv, wo, cq, ck, cv, co, win, wout, keep, sent, sems):
    core = place[1]
    copies = []
    for target, which in ((sent, 1 - core), (keep, core)):
        for group, weights in enumerate(((wq, wk, wv, wo), (cq, ck, cv, co))):
            for one, weight in enumerate(weights):
                copies.append(
                    (
                        weight.at[:, at(which * 128, 128)],
                        target.at[group * 128 : (group + 1) * 128, one * 128 : (one + 1) * 128],
                    )
                )
        for part in range(2):
            for one, weight in enumerate((win, wout)):
                copies.append(
                    (
                        weight.at[:, at(which * 512 + part * 256, 256)],
                        target.at[256 + part * 128 : 384 + part * 128, one * 256 : (one + 1) * 256],
                    )
                )
        rows = jnp.concatenate([norms[...], jnp.zeros((10, 128), F32)], 0).astype(BF)
        target[512:528, :] = jnp.concatenate([rows] * 4, 1)
    run_copies(copies, sems)


def prepare(place, norms, weights):
    return call(
        prepare_kernel,
        [(VMEM, like(528, 512))] * 2,
        [SMEM, VMEM] + [ANY] * 10,
        (place, norms, *weights),
        [pltpu.SemaphoreType.DMA((24,))],
    )


def prepare_rows_kernel(place, ids, image, text, cot, *outs):
    rows_keep, rows_sent, cot_keep, cot_sent, text_pair, sems = outs
    core = place[1]
    copies = []
    for target, cots, which in ((rows_sent, cot_sent, 1 - core), (rows_keep, cot_keep, core)):
        for one in range(2):
            copies.append((image.at[one, at(which * 128, 128), :], target.at[one]))
            copies.append((cot.at[one, at(which * 128, 128), :], cots.at[one]))
    for one in range(2):
        copies.append((text.at[one], text_pair.at[one, 0:32, :]))
        row = jnp.concatenate([ids[one : one + 1, :].astype(F32), jnp.zeros((1, 896), F32)], 1)
        text_pair[one, 32:48, :] = jnp.concatenate([row] * 16, 0).astype(BF)
    run_copies(copies, sems)


def prepare_rows(place, ids, image, text, cot):
    return call(
        prepare_rows_kernel,
        [(VMEM, like(2, 128, 1024))] * 4 + [(VMEM, like(2, 48, 1024))],
        [SMEM, VMEM] + [ANY] * 3,
        (place, ids, image, text, cot),
        [pltpu.SemaphoreType.DMA((10,))],
    )


def pick_kernel(place, keep, taken, *outs):
    core, top = place[1], place[2]
    for step, out in enumerate(outs):
        image = (top + 4 - step) % 4

        @pl.when(image // 2 == core)
        def _():
            out[...] = keep[image % 2]

        @pl.when(image // 2 != core)
        def _():
            out[...] = taken[image % 2]


def pick(place, keep, taken):
    return call(
        pick_kernel,
        [(VMEM, like(*keep.shape[1:]))] * 4,
        [SMEM, VMEM, VMEM],
        (place, keep, taken),
    )


def join_kernel(place, keep, taken, *refs):
    singles, near, sems = refs[:4], refs[4], refs[5]
    copies = []
    for half, source in enumerate((keep, taken)):
        core = place[1] ^ half
        for group in range(4):
            part = source.at[group * 128 : (group + 1) * 128, :]
            copies.append((part, singles[group].at[at(core * 128, 128), :]))
        copies.append((source.at[0:128, :], near.at[at(core * 128, 128), :]))
        copies.append((source.at[512:528, :], near.at[at(256 + core * 16, 16, 16), :]))
    run_copies(copies, sems)


def join(place, keep, taken):
    return call(
        join_kernel,
        [(VMEM, like(256, 512))] * 4 + [(VMEM, like(288, 512))],
        [SMEM] + [ANY] * 2,
        (place, keep, taken),
        [pltpu.SemaphoreType.DMA((12,))],
    )


def stack_kernel(*refs):
    *parts, whole, sems = refs
    copies, low = [], 0
    for part in parts:
        copies.append((part, whole.at[low : low + part.shape[0]]))
        low += part.shape[0]
    run_copies(copies, sems)


def stack(parts):
    rows = sum(part.shape[0] for part in parts)
    return call(
        stack_kernel,
        [(VMEM, like(rows, *parts[0].shape[1:]))],
        [ANY] * len(parts),
        parts,
        [pltpu.SemaphoreType.DMA((len(parts),))],
        limit=60,
    )[0]


def join_pieces_kernel(place, *refs):
    pieces, whole, sems = refs[:4], refs[4], refs[5]
    run_copies([(piece, whole.at[i]) for i, piece in enumerate(pieces)], sems)


def join_pieces(place, pieces):
    return call(
        join_pieces_kernel,
        [(VMEM, like(4, *pieces[0].shape))],
        [SMEM] + [ANY] * 4,
        (place, *pieces),
        [pltpu.SemaphoreType.DMA((4,))],
    )[0]


def arrange_kernel(place, *refs):
    messages, text, sems = refs[:4], refs[4], refs[5]
    run_copies(
        [(m.at[0:32, :], text.at[at((place[2] + i) % 4 * 32, 32, 32), :]) for i, m in enumerate(messages)], sems
    )


def arrange(place, messages):
    return call(
        arrange_kernel,
        [(VMEM, like(128, 1024))],
        [SMEM] + [ANY] * 4,
        (place, *messages),
        [pltpu.SemaphoreType.DMA((4,))],
    )[0]


def started(pairs, sems):
    copies = [pltpu.make_async_copy(source, target, sems.at[i]) for i, (source, target) in enumerate(pairs)]
    for copy in copies:
        copy.start()
    return copies


def wait_all(copies):
    for copy in copies:
        copy.wait()


def first_pieces(place, near, far, buffer, norms):
    chip, top = place[0], place[2]
    weights, rows = [], []
    for source in range(4):
        for half in range(2):
            row = at((chip ^ source) * 256 + half * 128, 128)
            piece, first = (near[source], half * 128) if source < 3 else (near[3 + half], 0)
            weights.append((piece.at[first : first + 128, :], buffer.at[row, at(top * 512, 512, 512)]))
            low = 256 + half * 16 if source < 3 else 128 + half * 16
            piece = near[source] if source < 3 else near[4]
            column = at((chip ^ source) * 256 + half * 128, 128)
            rows.append((piece.at[low : low + 16, 0:128], norms.at[:, column]))
            for step in range(3):
                first = step * 256 + half * 128
                piece = far[source] if source < 3 else far[3 + first // 384]
                first = first if source < 3 else first % 384
                columns = at((top + 1 + step) % 4 * 512, 512, 512)
                weights.append((piece.at[first : first + 128, :], buffer.at[row, columns]))
    return weights, rows


def later_pieces(place, own, side, over, low, high, buffer):
    chip = place[0]
    weights = []
    for source in range(4):
        for top in range(4):
            piece = (own, side, over, low if top < 2 else high)[source]
            rows, columns = at((chip ^ source) * 256, 256), slice(top * 512, (top + 1) * 512)
            weights.append((piece.at[top % 2 if source == 3 else top], buffer.at[rows, columns]))
    return weights


def norm_row(norms, one):
    return norms[one : one + 1, :].astype(F32)


def normalized(values, gain, bias):
    center = values - jnp.mean(values, -1, keepdims=True)
    inverse = lax.rsqrt(jnp.mean(center * center, -1, keepdims=True) + EPS)
    return (center * inverse * gain + bias).astype(BF)


def columns_of(weights, one, count=128):
    return jnp.concatenate([weights[:, s * 512 + one * count : s * 512 + (one + 1) * count] for s in range(4)], 1)


def project_into(target, rows, weights, dims=NN, step=512):
    count = weights.shape[0] if dims == NT else weights.shape[1]
    for low in range(0, count, step):
        part = weights[low : low + step, :] if dims == NT else weights[:, low : low + step]
        target[:, low : low + step] = dot(rows, part, dims).astype(target.dtype)


def image_blocks(place, own, other):
    core, top = place[1], place[2]
    for number in range(4):
        yield (top + number) % 4 * 256 + core * 128, own, number
        yield (top + number) % 4 * 256 + (1 - core) * 128, other, number


def one_head(values, head):
    return jnp.where(lane_head((1, 2 * HD), 1, head), values, jnp.zeros_like(values))


def both_heads(values):
    return jnp.concatenate([one_head(values, 0), one_head(values, 1)], 0)


def pick_heads(values):
    count = values.shape[1] // 2
    return jnp.where(lane_head((128, 1), 0, 0), values[:, :count], values[:, count:]).T


def causal_pair(count):
    rows = lax.broadcasted_iota(jnp.int32, (count, 2 * count), 0)
    columns = lax.broadcasted_iota(jnp.int32, (count, 2 * count), 1)
    return rows <= jnp.where(columns >= count, columns - count, columns)


def twice(row):
    return jnp.concatenate([row, row], 1)


def softmax_mix(scores, values):
    scale = LOG2E * HD**-0.5
    peak = jnp.max(scores[0], 0, keepdims=True)
    for part in scores[1:]:
        peak = jnp.maximum(peak, jnp.max(part, 0, keepdims=True))
    total, mixed = 0.0, 0.0
    for part, rows in zip(scores, values):
        weights = jnp.exp2((part - peak) * scale)
        total = total + jnp.sum(weights, 0, keepdims=True)
        mixed = mixed + dot(rows, weights.astype(BF), TN)
    return mixed / total, peak * scale + jnp.log2(total)


def causal_mask():
    return lax.broadcasted_iota(jnp.int32, (BLOCK, BLOCK), 0) <= lax.broadcasted_iota(
        jnp.int32, (BLOCK, BLOCK), 1
    )


def self_fwd_kernel(place, own, other, *refs):
    near, far = refs[:5], refs[5:10]
    whole, norms, normed, qkv, mix, lse, part, weights, loads, store = refs[10:]
    pieces, rows = first_pieces(place, near, far, weights, norms)
    copies = started(rows + pieces, loads)
    wait_all(copies[: len(rows)])
    gain, bias = norm_row(norms, 0), norm_row(norms, 1)
    for row, half, number in image_blocks(place, own, other):
        normed[at(row, 128), :] = normalized(half[number].astype(F32), gain, bias)
    wait_all(copies[len(rows) :])
    (stored,) = started([(weights, whole)], store)
    for one in range(3):
        qkv[:, one * 512 : (one + 1) * 512] = dot(normed[...], columns_of(weights, one)).astype(BF)
    causal = causal_pair(512)

    def pair_step(pair, carry):
        lanes = at(pair * 128, 128)
        k_lanes, v_lanes = at(512 + pair * 128, 128), at(1024 + pair * 128, 128)
        for low in range(0, 1024, 512):
            high = low + 512
            both = both_heads(qkv[low:high, lanes])
            scores = [jnp.where(causal, dot(qkv[low:high, k_lanes], both, NT), NEG)]
            values = [qkv[low:high, v_lanes]]
            if low:
                scores.append(dot(qkv[:low, k_lanes], both, NT))
                values.append(qkv[:low, v_lanes])
            mixed, logsum = softmax_mix(scores, values)
            for head in range(2):
                lse[pair, head : head + 1, low:high] = logsum[:, head * 512 : (head + 1) * 512]
            mix[low:high, lanes] = pick_heads(mixed).astype(BF)
        return carry

    lax.fori_loop(0, 4, pair_step, 0)
    project_into(part, mix[...], columns_of(weights, 3), NT)
    stored.wait()


def fused_self_forward(place, own, other, near, far):
    return call(
        self_fwd_kernel,
        [
            (HBM, like(1024, 2048)),
            (VMEM, like(16, 1024)),
            (VMEM, like(1024, 1024)),
            (VMEM, like(1024, 1536)),
            (VMEM, like(1024, 512)),
            (VMEM, like(4, 2, 1024, dtype=F32)),
            (VMEM, like(1024, 1024)),
        ],
        [SMEM, VMEM, VMEM] + [ANY] * 10,
        (place, own, other, *near, *far),
        [pltpu.VMEM((1024, 2048), BF), pltpu.SemaphoreType.DMA((40,)), pltpu.SemaphoreType.DMA((1,))],
    )


def cross_fwd_kernel(
    place, own, other, mine, theirs, norms, text, ids, caption, *refs
):
    pieces = refs[:5]
    whole, after, normed, queries, keys, mix, lse, part, weights, loads, store = refs[5:]
    copies = started(later_pieces(place, *pieces, weights), loads)
    gain, bias = norm_row(norms, 2), norm_row(norms, 3)
    for row, half, number in image_blocks(place, own, other):
        rows = at(row, 128)
        values = half[number].astype(F32) + (mine[rows, :].astype(F32) + theirs[rows, :].astype(F32))
        after[rows, :] = values
        normed[rows, :] = normalized(values, gain, bias)
    wait_all(copies)
    (stored,) = started([(weights, whole)], store)
    project_into(queries, normed[...], columns_of(weights, 0))
    w_text = jnp.concatenate([columns_of(weights, 1), columns_of(weights, 2)], 1)
    keys[...] = dot(text[...], w_text).astype(BF)

    def pair_step(pair, carry):
        lanes, v_lanes = at(pair * 128, 128), at(512 + pair * 128, 128)
        seen = twice(ids[...] == caption[...])
        scores = jnp.where(seen, dot(keys[:, lanes], both_heads(queries[:, lanes]), NT), NEG)
        mixed, logsum = softmax_mix([scores], [keys[:, v_lanes]])
        for head in range(2):
            lse[pair, head : head + 1, :] = logsum[:, head * 1024 : (head + 1) * 1024]
        mix[:, lanes] = pick_heads(mixed).astype(BF)
        return carry

    lax.fori_loop(0, 4, pair_step, 0)
    project_into(part, mix[...], columns_of(weights, 3), NT)
    stored.wait()


def fused_cross_forward(place, own, other, mine, theirs, norms, text, ids, caption, pieces):
    return call(
        cross_fwd_kernel,
        [
            (HBM, like(1024, 2048)),
            (VMEM, like(1024, 1024, dtype=F32)),
            (VMEM, like(1024, 1024)),
            (VMEM, like(1024, 512)),
            (VMEM, like(128, 1024)),
            (VMEM, like(1024, 512)),
            (VMEM, like(4, 2, 1024, dtype=F32)),
            (VMEM, like(1024, 1024)),
        ],
        [SMEM] + [VMEM] * 8 + [ANY] * 5,
        (place, own, other, mine, theirs, norms, text, ids, caption, *pieces),
        [pltpu.VMEM((1024, 2048), BF), pltpu.SemaphoreType.DMA((16,)), pltpu.SemaphoreType.DMA((1,))],
    )


def cut_grads(place, grads, columns, own, side, over, low, high):
    chip = place[0]
    own[:, columns] = grads[at(chip * 256, 256), :].astype(BF)
    side[:, columns] = grads[at((chip ^ 1) * 256, 256), :].astype(BF)
    over[:, columns] = grads[at((chip ^ 2) * 256, 256), :].astype(BF)
    low[:, columns] = grads[at((chip ^ 3) * 256, 128), :].astype(BF)
    high[:, columns] = grads[at((chip ^ 3) * 256 + 128, 128), :].astype(BF)


GRAD_SHAPES = [(256, 2048)] * 3 + [(128, 2048)] * 2


def feed_step(rows, cot, rows_t, cot_t, weights, out_sum, back_sum, grads):
    w_in = jnp.concatenate([weights[0][:, :256], weights[1][:, :256]], 1)
    w_out = jnp.concatenate([weights[0][:, 256:], weights[1][:, 256:]], 1)
    slope = math.sqrt(2.0 / math.pi)
    pre = dot(rows[...], w_in)
    square = pre * pre
    bent = jnp.tanh(pre * (slope + slope * 0.044715 * square))
    half = 0.5 * (1.0 + bent)
    act = (pre * half).astype(BF)
    bend = half + pre * (0.5 * (1.0 - bent * bent)) * (slope + 3.0 * slope * 0.044715 * square)
    pre_grad = (dot(cot[...], w_out) * bend).astype(BF)
    for low in range(0, 1024, 512):
        part = slice(low, low + 512)
        out_sum[:, part] += dot(act, w_out[part, :], NT)
        back_sum[:, part] += dot(pre_grad, w_in[part, :], NT)
    for block in range(2):
        part = slice(block * 256, (block + 1) * 256)
        grads[:, block * 512 : block * 512 + 256] = dot(rows_t[...], pre_grad[:, part])
        grads[:, block * 512 + 256 : (block + 1) * 512] = dot(cot_t[...], act[:, part])


def feed_first_kernel(
    place, after, mine, theirs, norms, cot_own, cot_other, p_own, p_side, p_over, p_low, p_high,
    g_whole, after_out, normed_out, cot_out, out_sum, back, after_cross, normed, cot, back_sum, rows_t, cot_t, grads,
    weights, sems, loads,
):
    step = pl.program_id(0)
    pairs = ((after_cross, after_out), (normed, normed_out), (cot, cot_out))
    stores = [pltpu.make_async_copy(a, b, sems.at[i]) for i, (a, b) in enumerate(pairs)]

    @pl.when(step == 0)
    def _():
        copies = started(later_pieces(place, p_own, p_side, p_over, p_low, p_high, weights), loads)
        gain, bias = norm_row(norms, 4), norm_row(norms, 5)
        for low in range(0, 1024, 128):
            rows = slice(low, low + 128)
            values = after[rows, :] + (mine[rows, :].astype(F32) + theirs[rows, :].astype(F32))
            after_cross[rows, :] = values
            normed[rows, :] = normalized(values, gain, bias)
        for row, half, number in image_blocks(place, cot_own, cot_other):
            cot[at(row, 128), :] = half[number]
        for store in stores:
            store.start()
        rows_t[...] = normed[...].T
        cot_t[...] = cot[...].T
        out_sum[...] = jnp.zeros_like(out_sum)
        for block in range(4):
            rows = at(block * 256 + place[1] * 128, 128)
            out_sum[rows, :] = after_cross[rows, :]
        back_sum[...] = jnp.zeros_like(back_sum)
        wait_all(copies)

    blocks = [weights[:, at(step * 1024 + block * 512, 512, 512)] for block in range(2)]
    feed_step(normed, cot, rows_t, cot_t, blocks, out_sum, back_sum, grads)
    for chip in range(4):
        for block in range(2):
            part = grads[chip * 256 : (chip + 1) * 256, block * 512 : (block + 1) * 512]
            g_whole[chip, block] = part.astype(BF)

    @pl.when(step == 1)
    def _():
        back[...] = back_sum[...].astype(BF)
        for store in stores:
            store.wait()


def feed_second_kernel(
    place, normed, cot, out_in, back_in, weights,
    g_own, g_side, g_over, g_low, g_high, out_keep, out_sent, back, out_sum, back_sum, rows_t, cot_t, grads,
):
    step, core = pl.program_id(0), place[1]

    @pl.when(step == 0)
    def _():
        rows_t[...] = normed[...].T
        cot_t[...] = cot[...].T
        out_sum[...] = out_in[...]
        back_sum[...] = back_in[...].astype(F32)

    blocks = [weights[:, block].reshape(1024, 512) for block in range(2)]
    feed_step(normed, cot, rows_t, cot_t, blocks, out_sum, back_sum, grads)
    cut_grads(place, grads, slice(None), g_own, g_side, g_over, g_low, g_high)

    @pl.when(step == 1)
    def _():
        back[...] = back_sum[...].astype(BF)
        for block in range(4):
            out_keep[block] = out_sum[at(block * 256 + core * 128, 128), :]
            out_sent[block] = out_sum[at(block * 256 + (1 - core) * 128, 128), :].astype(BF)


def once(*shape):
    zeros = (0,) * len(shape)
    return pl.BlockSpec(shape, lambda i: zeros, pipeline_mode=pl.Buffered(1))


def grad_outs(width=512):
    return [(pl.BlockSpec((rows, width), lambda i: (0, i)), like(rows, n)) for rows, n in GRAD_SHAPES]


FEED_FLOPS = 13 * 2**30


def feed_first(place, after, mine, theirs, norms, cot_own, cot_other, pieces):
    square = once(1024, 1024)
    return call(
        feed_first_kernel,
        [(pl.BlockSpec((4, 2, 256, 512), lambda i: (0, i, 0, 0)), like(4, 4, 256, 512))]
        + [
            (HBM, like(1024, 1024, dtype=F32)),
            (HBM, like(1024, 1024)),
            (HBM, like(1024, 1024)),
            (square, like(1024, 1024, dtype=F32)),
            (square, like(1024, 1024)),
        ],
        [SMEM, square, square, square, once(16, 1024), once(4, 128, 1024), once(4, 128, 1024)]
        + [ANY] * 5,
        (place, after, mine, theirs, norms, cot_own, cot_other, *pieces),
        [pltpu.VMEM((1024, 1024), F32)]
        + [pltpu.VMEM((1024, 1024), BF)] * 2
        + [pltpu.VMEM((1024, 1024), F32)]
        + [pltpu.VMEM((1024, 1024), BF)] * 2
        + [pltpu.VMEM((1024, 1024), F32), pltpu.VMEM((1024, 2048), BF)]
        + [pltpu.SemaphoreType.DMA((3,)), pltpu.SemaphoreType.DMA((16,))],
        limit=60,
        grid=(2,),
        flops=FEED_FLOPS,
        moved=30 * MIB,
    )


def feed_second(place, normed, cot, out_in, back_in, weights):
    square = once(1024, 1024)
    return call(
        feed_second_kernel,
        grad_outs(1024)
        + [
            (once(4, 128, 1024), like(4, 128, 1024, dtype=F32)),
            (once(4, 128, 1024), like(4, 128, 1024)),
            (square, like(1024, 1024)),
        ],
        [SMEM, square, square, square, square, pl.BlockSpec((4, 2, 256, 512), lambda i: (0, i, 0, 0))],
        (place, normed, cot, out_in, back_in, weights),
        [pltpu.VMEM((1024, 1024), F32)] * 2
        + [pltpu.VMEM((1024, 1024), BF)] * 2
        + [pltpu.VMEM((1024, 1024), F32)],
        limit=60,
        grid=(2,),
        flops=FEED_FLOPS,
        moved=26 * MIB,
    )


def norm_backward(values, gain, grad):
    center = values - jnp.mean(values, -1, keepdims=True)
    inverse = lax.rsqrt(jnp.mean(center * center, -1, keepdims=True) + EPS)
    hat = center * inverse
    scaled = grad * gain
    back = inverse * (
        scaled - jnp.mean(scaled, -1, keepdims=True) - hat * jnp.mean(scaled * hat, -1, keepdims=True)
    )
    return back, grad * hat


def norm_block(values_of, mine, theirs, base_of, gain, norms, keep):
    gain = norm_row(*gain)
    gain_sum, bias_sum = jnp.zeros((8, 1024), F32), jnp.zeros((8, 1024), F32)
    for low in range(0, 1024, 128):
        rows = slice(low, low + 128)
        grad = mine[rows, :].astype(F32) + theirs[rows, :].astype(F32)
        back, term = norm_backward(values_of(rows), gain, grad)
        keep(rows, base_of(rows) + back)
        gain_sum = gain_sum + jnp.sum(term.reshape(16, 8, 1024), 0)
        bias_sum = bias_sum + jnp.sum(grad.reshape(16, 8, 1024), 0)
    norms[0:1, :] = jnp.sum(gain_sum, 0, keepdims=True)
    norms[1:2, :] = jnp.sum(bias_sum, 0, keepdims=True)


def pair_row(lse, pair, low, high):
    return jnp.concatenate([lse[pair, 0:1, low:high], lse[pair, 1:2, low:high]], 1)


def pair_delta(grad, mix):
    product = (grad.astype(F32) * mix.astype(F32)).T
    return jnp.concatenate([jnp.sum(product[:HD], 0, keepdims=True), jnp.sum(product[HD:], 0, keepdims=True)], 1)


def head_grads(keys, values, one, one_grad, lse, delta, mask):
    weights = jnp.exp2(dot(keys, one, NT) * (LOG2E * HD**-0.5) - lse)
    if mask is not None:
        weights = jnp.where(mask, weights, 0.0)
    slope = dot(values, one_grad, NT)
    return weights.astype(BF), (weights * (slope - delta)).astype(BF)


def cross_bwd_kernel(
    place, after, mine, theirs, cot, gain, weights, normed, text, queries, keys, mix, lse, ids, caption,
    grad_out, part_out, norms, text_part, g_own, g_side, g_over, g_low, g_high, low_grad, mix_grad, dq, dkv, grads,
):
    grad_cross, part = grad_out.ref, part_out.ref

    def keep(rows, value):
        grad_cross[rows, :] = value
        low_grad[rows, :] = value.astype(BF)

    norm_block(lambda rows: after[rows, :], mine, theirs, lambda rows: cot[rows, :].astype(F32), (gain, 4), norms, keep)
    grad_out.send()
    weights, queries, keys, mix = weights.ready(), queries.ready(), keys.ready(), mix.ready()
    project_into(mix_grad, low_grad[...], columns_of(weights, 3))

    def pair_step(pair, carry):
        lanes, v_lanes = at(pair * 128, 128), at(512 + pair * 128, 128)
        query, grad = both_heads(queries[:, lanes]), both_heads(mix_grad[:, lanes])
        prob, score_grad = head_grads(
            keys[:, lanes],
            keys[:, v_lanes],
            query,
            grad,
            pair_row(lse, pair, 0, 1024),
            pair_delta(mix_grad[:, lanes], mix[:, lanes]),
            twice(ids[...] == caption[...]),
        )
        dv_sum, dk_sum = dot(prob, grad), dot(score_grad, query)
        dq[:, lanes] = (pick_heads(dot(keys[:, lanes], score_grad, TN)) * HD**-0.5).astype(BF)
        dkv[:, lanes] = (dk_sum * HD**-0.5).astype(BF)
        dkv[:, v_lanes] = dv_sum.astype(BF)
        return carry

    lax.fori_loop(0, 4, pair_step, 0)
    project_into(part, dq[...], columns_of(weights, 0), NT)
    part_out.send()
    normed = normed.ready()
    w_text = jnp.concatenate([columns_of(weights, 1), columns_of(weights, 2)], 1)
    text_part[...] = dot(dkv[...], w_text, NT).astype(BF)
    for one, (left, right) in enumerate(
        ((normed, dq[...]), (text, dkv[:, :512]), (text, dkv[:, 512:]), (low_grad, mix[...]))
    ):
        grads[...] = dot(left[...], right, TN)
        for s in range(4):
            columns = slice(s * 512 + one * 128, s * 512 + (one + 1) * 128)
            cut_grads(
                place, grads.at[:, s * 128 : (s + 1) * 128], columns, g_own, g_side, g_over, g_low, g_high
            )


def fused_cross_backward(place, after, mine, theirs, cot, gain, weights, normed, text, queries, keys, mix, lse, ids, caption):
    return call_overlapped(
        cross_bwd_kernel,
        [
            (LATE, like(1024, 1024, dtype=F32)),
            (LATE, like(1024, 1024)),
            (VMEM, like(8, 1024, dtype=F32)),
            (VMEM, like(128, 1024)),
        ]
        + [(VMEM, like(*shape)) for shape in GRAD_SHAPES],
        [SMEM] + [VMEM] * 5 + [LATE, LATE, VMEM, LATE, LATE, LATE, VMEM, VMEM, VMEM],
        (place, after, mine, theirs, cot, gain, weights, normed, text, queries, keys, mix, lse, ids, caption),
        [
            pltpu.VMEM((1024, 1024), BF),
            pltpu.VMEM((1024, 512), BF),
            pltpu.VMEM((1024, 512), BF),
            pltpu.VMEM((128, 1024), BF),
            pltpu.VMEM((1024, 512), F32),
        ],
    )


def self_bwd_kernel(
    place, after, mine, theirs, base, gain, weights, qkv, mix, lse,
    grad_out, low_out, norms, dqkv, mix_grad, dk_sum, dv_sum,
):
    core = place[1]
    grad_own, low_grad = grad_out.ref, low_out.ref

    def keep(rows, value):
        low_grad[rows, :] = value.astype(BF)

        @pl.when(core == (rows.start // 128) % 2)
        def _():
            grad_own[rows.start // 256] = value

    norm_block(lambda rows: after[rows, :], mine, theirs, lambda rows: base[rows, :], (gain, 2), norms, keep)
    grad_out.send()
    low_out.send()
    weights, qkv, mix = weights.ready(), qkv.ready(), mix.ready()
    project_into(mix_grad, low_grad[...], columns_of(weights, 3))
    causal = causal_pair(512)

    def pair_step(pair, carry):
        lanes = at(pair * 128, 128)
        k_lanes, v_lanes = at(512 + pair * 128, 128), at(1024 + pair * 128, 128)
        for low in range(0, 1024, 512):
            high = low + 512
            query, grad = both_heads(qkv[low:high, lanes]), both_heads(mix_grad[low:high, lanes])
            delta = pair_delta(mix_grad[low:high, lanes], mix[low:high, lanes])
            logsum = pair_row(lse, pair, low, high)
            total = 0.0
            for start in range(0, high, 512):
                rows = slice(start, start + 512)
                keys = qkv[rows, k_lanes]
                prob, score_grad = head_grads(
                    keys, qkv[rows, v_lanes], query, grad, logsum, delta, causal if start == low else None
                )
                dv, dk = dot(prob, grad), dot(score_grad, query)
                if start == low:
                    dv_sum[rows, :], dk_sum[rows, :] = dv, dk
                else:
                    dv_sum[rows, :] += dv
                    dk_sum[rows, :] += dk
                total = total + dot(keys, score_grad, TN)
            dqkv[low:high, lanes] = (pick_heads(total) * HD**-0.5).astype(BF)
        dqkv[:, k_lanes] = (dk_sum[...] * HD**-0.5).astype(BF)
        dqkv[:, v_lanes] = dv_sum[...].astype(BF)
        return carry

    lax.fori_loop(0, 4, pair_step, 0)


def fused_self_backward(place, after, mine, theirs, base, gain, weights, qkv, mix, lse):
    return call_overlapped(
        self_bwd_kernel,
        [
            (LATE, like(4, 128, 1024, dtype=F32)),
            (LATE, like(1024, 1024)),
            (VMEM, like(8, 1024, dtype=F32)),
            (VMEM, like(1024, 1536)),
        ],
        [SMEM] + [VMEM] * 5 + [LATE] * 3 + [VMEM],
        (place, after, mine, theirs, base, gain, weights, qkv, mix, lse),
        [pltpu.VMEM((1024, 512), BF), pltpu.VMEM((1024, 128), F32), pltpu.VMEM((1024, 128), F32)],
    )


def self_grads_kernel(place, normed, low_grad, dq, dk, dv, mix, g_own, g_side, g_over, g_low, g_high, rows_t, grad_t, grads):
    @pl.when(pl.program_id(0) == 0)
    def _():
        rows_t[...] = normed[...].T
        grad_t[...] = low_grad[...].T

    grads[:, :384] = dot(rows_t[...], jnp.concatenate([dq[...], dk[...], dv[...]], 1))
    grads[:, 384:] = dot(grad_t[...], mix[...])
    cut_grads(place, grads, slice(None), g_own, g_side, g_over, g_low, g_high)


def self_grads(place, normed, low_grad, dqkv, mix):
    square = once(1024, 1024)

    def cut(offset):
        return pl.BlockSpec((1024, 128), lambda i: (0, offset + i))

    return call(
        self_grads_kernel,
        grad_outs(),
        [SMEM, square, square, cut(0), cut(4), cut(8), cut(0)],
        (place, normed, low_grad, dqkv, dqkv, dqkv, mix),
        [pltpu.VMEM((1024, 1024), BF)] * 2 + [pltpu.VMEM((1024, 512), F32)],
        limit=60,
        grid=(4,),
        flops=4 * 2**30,
        moved=12 * MIB,
    )


def self_back_kernel(place, dqkv, weights, kept, sent):
    core = place[1]
    w_in = jnp.concatenate([columns_of(weights, one) for one in range(3)], 1)
    for target, half in ((sent, 1 - core), (kept, core)):
        rows = jnp.concatenate([dqkv[at(block * 256 + half * 128, 128), :] for block in range(4)], 0)
        for low in range(0, 1024, 512):
            value = dot(rows, w_in[low : low + 512, :], NT).astype(target.dtype)
            target[:, :, low : low + 512] = value.reshape(4, 128, 512)


def self_back(place, dqkv, weights):
    return call(
        self_back_kernel,
        [(VMEM, like(4, 128, 1024, dtype=F32)), (VMEM, like(4, 128, 1024))],
        [SMEM, VMEM, VMEM],
        (place, dqkv, weights),
        limit=60,
        flops=3 * 2**30,
        moved=10 * MIB,
    )


def last_norm_kernel(place, rows, grad_own, mine, theirs, gain, text_part, sums_two, sums_three, *pieces):
    gain_sum, bias_sum = jnp.zeros((8, 1024), F32), jnp.zeros((8, 1024), F32)
    for number in range(4):
        block = (place[2] + number) % 4
        grad = mine[block] + theirs[block].astype(F32)
        back, term = norm_backward(rows[number].astype(F32), norm_row(gain, 0), grad)
        pieces[-number % 4][0:128, :] = (grad_own[block] + back).astype(BF)
        pieces[-number % 4][128:160, :] = text_part[at(block * 32, 32, 32), :]
        gain_sum = gain_sum + jnp.sum(term.reshape(16, 8, 1024), 0)
        bias_sum = bias_sum + jnp.sum(grad.reshape(16, 8, 1024), 0)
    sums = [jnp.sum(gain_sum, 0, keepdims=True), jnp.sum(bias_sum, 0, keepdims=True)]
    sums += [0.5 * sums_two[0:2, :], 0.5 * sums_three[0:2, :], jnp.zeros((10, 1024), F32)]
    sums = jnp.concatenate(sums, 0).astype(BF)
    for piece in pieces:
        piece[160:176, :] = sums


def last_norm(place, rows, grad_own, mine, theirs, gain, text_part, sums_two, sums_three):
    return call(
        last_norm_kernel,
        [(VMEM, like(176, 1024))] * 4,
        [SMEM] + [VMEM] * 8,
        (place, rows, grad_own, mine, theirs, gain, text_part, sums_two, sums_three),
    )


def finish_kernel(place, out_keep, theirs, *pieces):
    for number, piece in enumerate(pieces):
        block = (place[2] + 4 - number) % 4
        piece[...] = (out_keep[block] + theirs[block].astype(F32)).astype(BF)


def finish(place, out_keep, theirs):
    return call(
        finish_kernel,
        [(VMEM, like(128, 1024))] * 4,
        [SMEM] + [VMEM] * 2,
        (place, out_keep, theirs),
    )


def part_kernel(place, *refs):
    pieces, mine, sent = refs[:4], refs[4], refs[5]
    core, top = place[1], place[2]
    for step, piece in enumerate(pieces):
        image = (top + step) % 4

        @pl.when(image // 2 == core)
        def _():
            mine[image % 2] = piece[...]

        @pl.when(image // 2 != core)
        def _():
            sent[image % 2] = piece[...]

    if pieces[0].shape[0] > 160:
        total = 0.0
        for piece in pieces:
            total = total + piece[160:176, :].astype(F32)
        mine[0, 160:176, :] = total.astype(BF)
        sent[0, 160:176, :] = total.astype(BF)


def part_images(place, pieces):
    return call(
        part_kernel,
        [(VMEM, like(2, *pieces[0].shape))] * 2,
        [SMEM] + [VMEM] * 4,
        (place, *pieces),
    )


def land_kernel(place, mine, taken, rows, *more):
    core = place[1]
    for one in range(2):
        rows[one, at(core * 128, 128), :] = mine[one, 0:128, :].astype(rows.dtype)
        rows[one, at((1 - core) * 128, 128), :] = taken[one, 0:128, :].astype(rows.dtype)
        if more:
            more[0][one] = mine[one, 128:160, :].astype(F32) + taken[one, 128:160, :].astype(F32)
    if more:
        more[1][...] = mine[0, 160:168, :].astype(F32) + taken[0, 160:168, :].astype(F32)


def land(place, mine, taken, dtype):
    outs = [(VMEM, like(2, 256, 1024, dtype=dtype))]
    if mine.shape[1] > 128:
        outs += [(VMEM, like(2, 32, 1024, dtype=F32)), (VMEM, like(8, 1024, dtype=F32))]
    return call(land_kernel, outs, [SMEM, VMEM, VMEM], (place, mine, taken))


def relay_kernel(over, side, from_side, from_over, to_over, to_side):
    to_over[0:128, :] = (over[0:128, :].astype(F32) + from_side[...].astype(F32)).astype(BF)
    to_over[128:256, :] = over[128:256, :]
    to_side[0:128, :] = side[0:128, :]
    to_side[128:256, :] = (side[128:256, :].astype(F32) + from_over[...].astype(F32)).astype(BF)


def relay(over, side, from_side, from_over):
    return call(
        relay_kernel,
        [(VMEM, like(256, 2048))] * 2,
        [VMEM] * 4,
        (over, side, from_side, from_over),
        limit=60,
        moved=5 * MIB,
    )


def plane_sum_kernel(place, own, over, side, keep, *sent):
    for s in range(4):
        columns = at((place[2] + s) % 4 * 512, 512, 512)
        total = own[:, columns].astype(F32) + over[:, columns].astype(F32) + side[:, columns].astype(F32)
        if s:
            sent[s - 1][...] = total.astype(BF)
        else:
            keep[...] = total


def plane_sum(place, own, over, side):
    return call(
        plane_sum_kernel,
        [(VMEM, like(256, 512, dtype=F32))] + [(VMEM, like(256, 512))] * 3,
        [SMEM] + [VMEM] * 3,
        (place, own, over, side),
        limit=60,
        moved=5 * MIB,
    )


def plane_sum_whole_kernel(own, over, side, whole):
    for step in range(4):
        columns = slice(step * 512, (step + 1) * 512)
        total = own[:, columns].astype(F32) + over[:, columns].astype(F32) + side[:, columns].astype(F32)
        whole[step * 256 : (step + 1) * 256, :] = total.astype(BF)


def plane_sum_whole(own, over, side):
    return call(
        plane_sum_whole_kernel,
        [(VMEM, like(1024, 512))],
        [VMEM] * 3,
        (own, over, side),
    )[0]


def line_sum_kernel(place, keep, one, two, three, mine, other):
    core = place[1]
    for target, half in ((other, 1 - core), (mine, core)):
        rows = at(half * 128, 128)
        total = keep[rows, :]
        for part in (one, two, three):
            total = total + part[rows, :].astype(F32)
        target[...] = total.astype(target.dtype)


def line_sum(place, keep, parts):
    return call(
        line_sum_kernel,
        [(VMEM, like(128, 512, dtype=F32)), (VMEM, like(128, 512))],
        [SMEM] + [VMEM] * 4,
        (place, keep, *parts),
        limit=60,
        moved=2 * MIB,
    )


def spread_kernel(place, mine, other, *outs):
    core, columns = place[1], mine.shape[1] // len(outs)
    for one, out in enumerate(outs):
        cut = slice(one * columns, (one + 1) * columns)
        out[:, at(core * columns, columns)] = mine[:, cut].astype(F32)
        out[:, at((1 - core) * columns, columns)] = other[:, cut].astype(F32)


def spread(place, mine, other):
    return call(
        spread_kernel,
        [(VMEM, like(128, 256, dtype=F32))] * 4,
        [SMEM] + [VMEM] * 2,
        (place, mine, other),
        limit=60,
        moved=MIB,
    )


def spread_feed_kernel(place, mine_one, other_one, mine_two, other_two, *outs):
    core = place[1]
    for part, (mine, other) in enumerate(((mine_one, other_one), (mine_two, other_two))):
        for one, out in enumerate(outs):
            cut = slice(one * 256, (one + 1) * 256)
            out[:, at(core * 512 + part * 256, 256)] = mine[:, cut].astype(F32)
            out[:, at((1 - core) * 512 + part * 256, 256)] = other[:, cut].astype(F32)


def spread_feed(place, *halves):
    return call(
        spread_feed_kernel,
        [(VMEM, like(128, 1024, dtype=F32))] * 2,
        [SMEM] + [VMEM] * 4,
        (place, *halves),
        limit=60,
        moved=2 * MIB,
    )


tie = lax.optimization_barrier


def packed_layer(args):
    image_rows, text_rows, segment_ids, cotangent, *others = args
    weights, norms = others[:10], others[10:]
    chip, core, top = lax.axis_index("chip"), lax.axis_index("core"), lax.axis_index("hi")
    place = jnp.stack([chip, core, top, core * 2 + top % 2]).astype(jnp.int32)

    def swap(value):
        return lax.ppermute(value, "core", [(0, 1), (1, 0)])

    def across(value, bit):
        return lax.ppermute(value, "chip", [(i, i ^ bit) for i in range(4)])

    def shift(value, step):
        return lax.ppermute(value, "hi", [((i + step) % 4, i) for i in range(4)])

    def line(part):
        return [shift(part, step) for step in range(1, 4)]

    def exchange(pieces):
        return [pieces[0]] + [shift(piece, step) for step, piece in enumerate(pieces) if step]

    def gather_line(part):
        return lax.all_gather(part, "hi")

    def sides(value):
        return [across(value, 1), across(value, 2)]

    def corners(pair, cut):
        return [across(pair[0][:cut], 2), across(pair[1][cut:], 1)]

    def grad_corners(grads):
        return [across(grads[3], 1), across(grads[4], 2)]

    def grad_sides(grads, got, later):
        to_over, to_side, later = tie((*relay(grads[2], grads[1], *got), later))
        return [across(to_over, 2), across(to_side, 1)], later

    def halves(total):
        cut = total.reshape(2, 128, 512)
        sent = lax.dynamic_index_in_dim(cut, 1 - core, 0, False)
        return lax.dynamic_index_in_dim(cut, core, 0, False), swap(sent)

    keep, sent = prepare(place, jnp.stack(norms), weights)
    v = {"taken": swap(sent)}
    v["rows_keep"], v["rows_sent"], v["cot_keep"], v["cot_sent"], v["text_pair"] = prepare_rows(
        place, segment_ids, image_rows, text_rows, cotangent
    )
    v = tie(v)
    *v["singles"], v["near"] = join(place, keep, v.pop("taken"))
    v["rows_taken"], v["cot_taken"] = swap(v.pop("rows_sent")), swap(v.pop("cot_sent"))
    v["text_taken"] = swap(v["text_pair"])
    v = tie(v)

    v["near"] = [v["near"], *sides(v["near"])]
    lines = line(v["singles"][0])
    v["pieces"] = pick(place, v.pop("rows_keep"), v.pop("rows_taken"))
    v["cot_pieces"] = pick(place, v.pop("cot_keep"), v.pop("cot_taken"))
    v["text_pieces"] = pick(place, v.pop("text_pair"), v.pop("text_taken"))
    v = tie(v)
    v["near"] += corners(v["near"][1:], 128)
    v["line"] = lines
    v = tie(v)

    rest = stack(v.pop("line"))
    v["far_self"] = [rest, *sides(rest)]
    v["two_on"] = shift(v["pieces"][2], 2)
    line_cross = gather_line(v["singles"][1])
    v = tie(v)
    v["far_self"] += corners(v["far_self"][1:], 384)
    pieces = v.pop("pieces")
    v["pieces"] = [pieces[0], shift(pieces[1], 1), v.pop("two_on"), shift(pieces[3], 3)]
    v["line_cross"] = line_cross
    v = tie(v)
    v["rows_own"] = stack([piece[None] for piece in v.pop("pieces")])
    v["rows_other"] = swap(v["rows_own"])
    line_one = gather_line(v["singles"][2])
    v = tie(v)

    v["far_cross"] = sides(v["line_cross"])
    text_pieces, cot_pieces = v.pop("text_pieces"), v.pop("cot_pieces")
    v["text_near"] = [text_pieces[0], shift(text_pieces[1], 1), shift(text_pieces[3], 3)]
    v["text_two"], v["cot_two"] = text_pieces[2], shift(cot_pieces[2], 2)
    v["cot_near"] = [cot_pieces[0], cot_pieces[1], cot_pieces[3]]
    v["line_one"] = line_one
    v["w_self"], v["norms"], v["normed_one"], v["qkv"], v["self_mix"], v["self_lse"], v["mine"] = (
        fused_self_forward(place, v["rows_own"], v["rows_other"], v.pop("near"), v.pop("far_self"))
    )
    v = tie(v)

    v["theirs"] = swap(v["mine"])
    v["far_cross"] += corners(v["far_cross"], 2)
    line_two = gather_line(v.pop("singles")[3])
    text_near, text_two = v.pop("text_near"), shift(v.pop("text_two"), 2)
    text_pieces = [text_near[0], text_near[1], text_two, text_near[2]]
    v["text"] = arrange(place, text_pieces)
    ids = text_pieces[0][32, :128].astype(jnp.int32)
    v["caption"] = jnp.repeat(ids, 8)[None, :]
    v["ids"] = ids[:, None]
    v = tie(v)

    v["far_one"] = sides(v["line_one"])
    near, one_on, three_on = v.pop("cot_near")
    cot_pieces = [near, shift(one_on, 1), v.pop("cot_two"), shift(three_on, 3)]
    v["line_two"] = line_two
    v["w_cross"], v["after_attn"], v["normed_two"], v["queries"], v["keys"], v["cross_mix"], v["cross_lse"], v["mine"] = (
        fused_cross_forward(
            place, v["rows_own"], v.pop("rows_other"), v["mine"], v["theirs"], v["norms"], v["text"], v["ids"],
            v["caption"], (v.pop("line_cross"), *v.pop("far_cross")),
        )
    )
    v["cot_own"] = join_pieces(place, cot_pieces)
    v = tie(v)

    v["theirs"] = swap(v["mine"])
    low, high, line_two = tie((v["far_one"][0][:2], v["far_one"][1][2:], v.pop("line_two")))
    v["far_one"] += [across(low, 2), across(high, 1)]
    v["cot_other"] = swap(v["cot_own"])
    w_two = lax.all_gather(line_two, "chip")
    v = tie(v)

    v["w_two"] = w_two
    pieces = (v.pop("line_one"), *v.pop("far_one"))
    v["grads_one"], v["after_cross"], v["normed_three"], v["cot"], v["out_sum"], v["back_sum"] = feed_first(
        place, v["after_attn"], v["mine"], v["theirs"], v["norms"], v.pop("cot_own"), v.pop("cot_other"), pieces
    )
    v = tie(v)

    total_one = lax.psum_scatter(v.pop("grads_one"), "chip", scatter_dimension=0, tiled=False)
    *v["grads_two"], v["out_keep"], v["out_sent"], v["mine"] = feed_second(
        place, v.pop("normed_three"), v["cot"], v.pop("out_sum"), v.pop("back_sum"), v.pop("w_two")
    )
    v = tie(v)

    v["theirs"] = swap(v["mine"])
    v["out_theirs"] = swap(v.pop("out_sent"))
    v = tie(v)
    v["got_two"] = grad_corners(v["grads_two"])
    v["pieces"] = exchange(finish(place, v.pop("out_keep"), v.pop("out_theirs")))
    v["grad_cross"], v["part"], v["norms_three"], v["text_part"], *v["grads_three"] = fused_cross_backward(
        place, v.pop("after_cross"), v.pop("mine"), v.pop("theirs"), v.pop("cot"), v["norms"], v.pop("w_cross"),
        v.pop("normed_two"), v.pop("text"), v.pop("queries"), v.pop("keys"), v.pop("cross_mix"),
        v.pop("cross_lse"), v.pop("ids"), v.pop("caption"),
    )
    v = tie(v)

    v["theirs"] = swap(v["part"])
    v["total_one"] = total_one
    v["to_two"] = relay(v["grads_two"][2], v["grads_two"][1], *v.pop("got_two"))
    v = tie(v)

    to_two = v.pop("to_two")
    v["sides_two"] = [across(to_two[0], 2), across(to_two[1], 1)]
    v["got_three"] = grad_corners(v["grads_three"])
    v["line_one"] = lax.psum_scatter(v.pop("total_one"), "hi", scatter_dimension=0, tiled=False)
    v["grad_own"], v["low_grad"], v["norms_two"], v["dqkv"] = fused_self_backward(
        place, v.pop("after_attn"), v.pop("part"), v.pop("theirs"), v.pop("grad_cross"), v["norms"], v["w_self"],
        v.pop("qkv"), v["self_mix"], v.pop("self_lse"),
    )
    v = tie(v)

    v["sides_three"], sides_two = grad_sides(v["grads_three"], v.pop("got_three"), v.pop("sides_two"))
    total_two = plane_sum_whole(v.pop("grads_two")[0], *sides_two)
    line_two = lax.psum_scatter(total_two, "hi", scatter_dimension=0, tiled=True)
    v["grads_four"] = self_grads(place, v.pop("normed_one"), v.pop("low_grad"), v["dqkv"], v.pop("self_mix"))
    mine, sent = part_images(place, v.pop("pieces"))
    (v["result"],) = land(place, mine, swap(sent), BF)
    v["feed_one"] = halves(v.pop("line_one"))
    v = tie(v)

    v["got_four"] = grad_corners(v["grads_four"])
    total_three, dqkv = tie((plane_sum_whole(v.pop("grads_three")[0], *v.pop("sides_three")), v.pop("dqkv")))
    line_three = lax.psum_scatter(total_three, "hi", scatter_dimension=0, tiled=True)
    v["line_two"] = line_two
    v["kept"], v["sent"] = self_back(place, dqkv, v.pop("w_self"))
    v = tie(v)

    v["sides_four"], _ = grad_sides(v["grads_four"], v.pop("got_four"), place)
    pieces = last_norm(
        place, v.pop("rows_own"), v.pop("grad_own"), v.pop("kept"), swap(v.pop("sent")), v.pop("norms"),
        v.pop("text_part"), v.pop("norms_two"), v.pop("norms_three"),
    )
    input_pieces = exchange(pieces)
    v = tie(v)

    v["kept"], *sums_four = plane_sum(place, v.pop("grads_four")[0], *v.pop("sides_four"))
    v["line_four"] = [shift(piece, 3 - i) for i, piece in enumerate(sums_four)]
    v["feed_grads"] = spread_feed(place, *v.pop("feed_one"), *halves(v.pop("line_two")))
    later = tie((place, sums_four))[0]
    mine, sent = part_images(later, input_pieces)
    v["input_grad"], v["text_grad"], sums = land(place, mine, swap(sent), F32)
    sums = sums + across(sums, 1)
    sums = sums + across(sums, 2)
    v["sums"] = lax.dynamic_slice_in_dim(sums, (chip * 2 + core) * 128, 128, 1)
    v["cross_grads"] = spread(place, *halves(line_three))
    v = tie(v)

    kept, sent = line_sum(place, v.pop("kept"), v.pop("line_four"))
    own_grads = spread(place, kept, swap(sent))
    return (
        v["result"], v["input_grad"], v["text_grad"], *own_grads, *v["cross_grads"], *v["feed_grads"],
        *[v["sums"][i] for i in range(6)],
    )


def solution(mesh):
    fsdp, tensor = mesh.shape["fsdp"], mesh.shape["tensor"]

    def run(*args):
        images = args[0].shape[0] // fsdp
        tops = 2 * images
        shape = {"chip": fsdp // 2, "core": 2, "hi": tops, "lo": tensor // tops}
        fine = Mesh(mesh.devices.reshape(tuple(shape.values())), tuple(shape))
        first, second = ("chip", "core"), ("hi", "lo")
        wide, weight, norm = P(first, second, None), P(first, second), P(first)
        outs = (wide,) * 3 + (weight,) * 10 + (norm,) * 6
        packed = (
            (fsdp, tensor, images) == (8, 4, 2)
            and args[0].shape[1:] == (1024, 1024)
            and args[1].shape[1:] == (128, 1024)
            and args[12].shape == (1024, 4096)
        )
        return jax.shard_map(
            lambda *local: packed_layer(local) if packed else layer(shape, local),
            mesh=fine,
            in_specs=(wide, wide, P(first, None), wide) + (weight,) * 10 + (norm,) * 6,
            out_specs=outs,
            check_vma=False,
        )(*args)

    return run
```

```python
import functools
import math

import jax
import jax.numpy as jnp
from jax import lax
from jax.experimental import pallas as pl
from jax.experimental.pallas import tpu as pltpu
from jax.sharding import Mesh
from jax.sharding import PartitionSpec as P

HD = 64
EPS = 1e-05
NEG = -1e30
LOG2E = math.log2(math.e)
BF = jnp.bfloat16
F32 = jnp.float32
NT = (((1,), (1,)), ((), ()))
TN = (((0,), (0,)), ((), ()))
NN = (((1,), (0,)), ((), ()))


def dot(left, right, dims=NN):
    return lax.dot_general(left, right, dims, preferred_element_type=F32)


def lane_head(shape, axis, head):
    return lax.broadcasted_iota(jnp.int32, shape, axis) // HD == head


def self_forward_kernel(q_ref, k_ref, v_ref, mix_ref, lse_ref, *, block):
    length = q_ref.shape[0]
    scale = LOG2E * HD**-0.5
    causal = lax.broadcasted_iota(jnp.int32, (block, block), 0) <= lax.broadcasted_iota(
        jnp.int32, (block, block), 1
    )
    for at in range(length // block):
        lo, hi = at * block, (at + 1) * block
        query = q_ref[lo:hi, :]
        mixes = []
        for head in range(2):
            one = jnp.where(lane_head((1, 2 * HD), 1, head), query, jnp.zeros_like(query))
            diag = jnp.where(causal, dot(k_ref[lo:hi, :], one, NT), NEG)
            peak = jnp.max(diag, 0, keepdims=True)
            if at:
                past = dot(k_ref[:lo, :], one, NT)
                peak = jnp.maximum(peak, jnp.max(past, 0, keepdims=True))
            weights = jnp.exp2((diag - peak) * scale)
            total = jnp.sum(weights, 0, keepdims=True)
            mixed = dot(v_ref[lo:hi, :], weights.astype(BF), TN)
            if at:
                weights = jnp.exp2((past - peak) * scale)
                total = total + jnp.sum(weights, 0, keepdims=True)
                mixed = mixed + dot(v_ref[:lo, :], weights.astype(BF), TN)
            mixes.append(mixed / total)
            lse_ref[0, head : head + 1, lo:hi] = peak * scale + jnp.log2(total)
        both = jnp.where(lane_head((2 * HD, 1), 0, 0), mixes[0], mixes[1])
        mix_ref[lo:hi, :] = both.T.astype(BF)


def self_backward_kernel(
    q_ref, k_ref, v_ref, mix_ref, grad_ref, lse_ref, dq_ref, dk_ref, dv_ref, dk_sum, dv_sum, *, block
):
    length = q_ref.shape[0]
    scale = LOG2E * HD**-0.5
    causal = lax.broadcasted_iota(jnp.int32, (block, block), 0) <= lax.broadcasted_iota(
        jnp.int32, (block, block), 1
    )
    dk_sum[...] = jnp.zeros_like(dk_sum)
    dv_sum[...] = jnp.zeros_like(dv_sum)
    for at in range(length // block):
        lo, hi = at * block, (at + 1) * block
        query = q_ref[lo:hi, :]
        grad = grad_ref[lo:hi, :]
        product = (grad.astype(F32) * mix_ref[lo:hi, :].astype(F32)).T
        grads = []
        for head in range(2):
            picked = lane_head((1, 2 * HD), 1, head)
            one = jnp.where(picked, query, jnp.zeros_like(query))
            one_grad = jnp.where(picked, grad, jnp.zeros_like(grad))
            delta = jnp.sum(product[head * HD : (head + 1) * HD], 0, keepdims=True)
            lse = lse_ref[0, head : head + 1, lo:hi]
            total = jnp.zeros((2 * HD, block), F32)
            for start, stop in ((0, lo), (lo, hi)):
                if start == stop:
                    continue
                keys = k_ref[start:stop, :]
                weights = jnp.exp2(dot(keys, one, NT) * scale - lse)
                if start == lo:
                    weights = jnp.where(causal, weights, 0.0)
                slope = dot(v_ref[start:stop, :], one_grad, NT)
                score_grad = (weights * (slope - delta)).astype(BF)
                dv_sum[start:stop, :] += dot(weights.astype(BF), one_grad)
                dk_sum[start:stop, :] += dot(score_grad, one)
                total = total + dot(keys, score_grad, TN)
            grads.append(total)
        both = jnp.where(lane_head((2 * HD, 1), 0, 0), grads[0], grads[1])
        dq_ref[lo:hi, :] = (both.T * HD**-0.5).astype(BF)
    dk_ref[...] = (dk_sum[...] * HD**-0.5).astype(BF)
    dv_ref[...] = dv_sum[...].astype(BF)


def cross_forward_kernel(q_ref, k_ref, v_ref, ids_ref, caption_ref, mix_ref, lse_ref, *, block):
    length = q_ref.shape[0]
    scale = LOG2E * HD**-0.5
    for at in range(length // block):
        lo, hi = at * block, (at + 1) * block
        query = q_ref[lo:hi, :]
        seen = ids_ref[...] == caption_ref[:, lo:hi]
        mixes = []
        for head in range(2):
            one = jnp.where(lane_head((1, 2 * HD), 1, head), query, jnp.zeros_like(query))
            scores = jnp.where(seen, dot(k_ref[...], one, NT), NEG)
            peak = jnp.max(scores, 0, keepdims=True)
            weights = jnp.exp2((scores - peak) * scale)
            total = jnp.sum(weights, 0, keepdims=True)
            mixes.append(dot(v_ref[...], weights.astype(BF), TN) / total)
            lse_ref[0, head : head + 1, lo:hi] = peak * scale + jnp.log2(total)
        both = jnp.where(lane_head((2 * HD, 1), 0, 0), mixes[0], mixes[1])
        mix_ref[lo:hi, :] = both.T.astype(BF)


def cross_backward_kernel(
    q_ref, k_ref, v_ref, mix_ref, grad_ref, lse_ref, ids_ref, caption_ref, dq_ref, dk_ref, dv_ref, *, block
):
    length = q_ref.shape[0]
    scale = LOG2E * HD**-0.5
    keys, values = k_ref[...], v_ref[...]
    dk_sum = jnp.zeros(keys.shape, F32)
    dv_sum = jnp.zeros(keys.shape, F32)
    for at in range(length // block):
        lo, hi = at * block, (at + 1) * block
        query = q_ref[lo:hi, :]
        grad = grad_ref[lo:hi, :]
        product = (grad.astype(F32) * mix_ref[lo:hi, :].astype(F32)).T
        seen = ids_ref[...] == caption_ref[:, lo:hi]
        grads = []
        for head in range(2):
            picked = lane_head((1, 2 * HD), 1, head)
            one = jnp.where(picked, query, jnp.zeros_like(query))
            one_grad = jnp.where(picked, grad, jnp.zeros_like(grad))
            delta = jnp.sum(product[head * HD : (head + 1) * HD], 0, keepdims=True)
            lse = lse_ref[0, head : head + 1, lo:hi]
            weights = jnp.where(seen, jnp.exp2(dot(keys, one, NT) * scale - lse), 0.0)
            slope = dot(values, one_grad, NT)
            score_grad = (weights * (slope - delta)).astype(BF)
            dv_sum = dv_sum + dot(weights.astype(BF), one_grad)
            dk_sum = dk_sum + dot(score_grad, one)
            grads.append(dot(keys, score_grad, TN))
        both = jnp.where(lane_head((2 * HD, 1), 0, 0), grads[0], grads[1])
        dq_ref[lo:hi, :] = (both.T * HD**-0.5).astype(BF)
    dk_ref[...] = (dk_sum * HD**-0.5).astype(BF)
    dv_ref[...] = dv_sum.astype(BF)


def feed_kernel(
    rows_ref, cot_ref, win_ref, wout_ref, out_in, back_in, gin_ref, gout_ref, out_ref, back_ref, rows_t, cot_t, *, first
):
    step = pl.program_id(0)

    @pl.when(step == 0)
    def _():
        rows_t[...] = rows_ref[...].T
        cot_t[...] = cot_ref[...].T
        if first:
            out_ref[...] = jnp.zeros_like(out_ref)
            back_ref[...] = jnp.zeros_like(back_ref)
        else:
            out_ref[...] = out_in[...]
            back_ref[...] = back_in[...]

    pre = dot(rows_ref[...], win_ref[...])
    square = pre * pre
    slope = math.sqrt(2.0 / math.pi)
    bent = jnp.tanh(pre * (slope + slope * 0.044715 * square))
    half = 0.5 * (1.0 + bent)
    act = (pre * half).astype(BF)
    out_ref[...] += dot(act, wout_ref[...], NT)
    gout_ref[...] = dot(cot_t[...], act).astype(BF)
    bend = half + pre * (0.5 * (1.0 - bent * bent)) * (slope + 3.0 * slope * 0.044715 * square)
    pre_grad = (dot(cot_ref[...], wout_ref[...]) * bend).astype(BF)
    gin_ref[...] = dot(rows_t[...], pre_grad).astype(BF)
    back_ref[...] += dot(pre_grad, win_ref[...], NT)


VMEM_LIMIT = 60 * 1024 * 1024


def params():
    return pltpu.CompilerParams(vmem_limit_bytes=VMEM_LIMIT)


def column(rows, offset):
    return pl.BlockSpec((rows, 2 * HD), lambda i: (0, offset + i))


def self_forward(packed):
    length, width = packed.shape
    pairs = width // (6 * HD)
    return pl.pallas_call(
        functools.partial(self_forward_kernel, block=256),
        grid=(pairs,),
        in_specs=[column(length, 0), column(length, pairs), column(length, 2 * pairs)],
        out_specs=[column(length, 0), pl.BlockSpec((1, 2, length), lambda i: (i, 0, 0))],
        out_shape=[
            jax.ShapeDtypeStruct((length, pairs * 2 * HD), BF),
            jax.ShapeDtypeStruct((pairs, 2, length), F32),
        ],
        compiler_params=params(),
        cost_estimate=pl.CostEstimate(
            flops=8 * pairs * length * length * 2 * HD * 2,
            bytes_accessed=8 * pairs * length * 2 * HD,
            transcendentals=2 * pairs * length * length,
        ),
    )(packed, packed, packed)


def self_backward(packed, mix, grad, lse):
    length, width = packed.shape
    pairs = width // (6 * HD)
    part = jax.ShapeDtypeStruct((length, pairs * 2 * HD), BF)
    return pl.pallas_call(
        functools.partial(self_backward_kernel, block=256),
        grid=(pairs,),
        in_specs=[
            column(length, 0),
            column(length, pairs),
            column(length, 2 * pairs),
            column(length, 0),
            column(length, 0),
            pl.BlockSpec((1, 2, length), lambda i: (i, 0, 0)),
        ],
        out_specs=[column(length, 0)] * 3,
        out_shape=[part] * 3,
        scratch_shapes=[pltpu.VMEM((length, 2 * HD), F32)] * 2,
        compiler_params=params(),
        cost_estimate=pl.CostEstimate(
            flops=20 * pairs * length * length * 2 * HD * 2,
            bytes_accessed=16 * pairs * length * 2 * HD,
            transcendentals=2 * pairs * length * length,
        ),
    )(packed, packed, packed, mix, grad, lse)


def cross_forward(queries, keys, ids, captions):
    length, width = queries.shape
    texts = keys.shape[0]
    pairs = width // (2 * HD)
    return pl.pallas_call(
        functools.partial(cross_forward_kernel, block=min(512, length)),
        grid=(pairs,),
        in_specs=[
            column(length, 0),
            column(texts, 0),
            column(texts, pairs),
            pl.BlockSpec((texts, 1), lambda i: (0, 0)),
            pl.BlockSpec((1, length), lambda i: (0, 0)),
        ],
        out_specs=[column(length, 0), pl.BlockSpec((1, 2, length), lambda i: (i, 0, 0))],
        out_shape=[
            jax.ShapeDtypeStruct((length, width), BF),
            jax.ShapeDtypeStruct((pairs, 2, length), F32),
        ],
        compiler_params=params(),
    )(queries, keys, keys, ids, captions)


def cross_backward(queries, keys, mix, grad, lse, ids, captions):
    length, width = queries.shape
    texts = keys.shape[0]
    pairs = width // (2 * HD)
    return pl.pallas_call(
        functools.partial(cross_backward_kernel, block=min(512, length)),
        grid=(pairs,),
        in_specs=[
            column(length, 0),
            column(texts, 0),
            column(texts, pairs),
            column(length, 0),
            column(length, 0),
            pl.BlockSpec((1, 2, length), lambda i: (i, 0, 0)),
            pl.BlockSpec((texts, 1), lambda i: (0, 0)),
            pl.BlockSpec((1, length), lambda i: (0, 0)),
        ],
        out_specs=[column(length, 0), column(texts, 0), column(texts, 0)],
        out_shape=[
            jax.ShapeDtypeStruct((length, width), BF),
            jax.ShapeDtypeStruct((texts, width), BF),
            jax.ShapeDtypeStruct((texts, width), BF),
        ],
        compiler_params=params(),
    )(queries, keys, keys, mix, grad, lse, ids, captions)


def feed(rows, cot, w_in, w_out, sums):
    length, width = rows.shape
    units = w_in.shape[1]
    block = min(256, units)
    whole = pl.BlockSpec((length, width), lambda i: (0, 0))
    cut = pl.BlockSpec((width, block), lambda i: (0, i))
    first = sums is None
    kernel = functools.partial(feed_kernel, first=first)
    operands = [rows, cot, w_in, w_out]
    specs = [whole, whole, cut, cut]
    if first:
        body = lambda a, b, c, d, *rest: kernel(a, b, c, d, None, None, *rest)
    else:
        body = kernel
        operands += list(sums)
        specs += [whole, whole]
    total = jax.ShapeDtypeStruct((length, width), F32)
    part = jax.ShapeDtypeStruct((width, units), BF)
    return pl.pallas_call(
        body,
        grid=(units // block,),
        in_specs=specs,
        out_specs=[cut, cut, whole, whole],
        out_shape=[part, part, total, total],
        scratch_shapes=[pltpu.VMEM((width, length), BF)] * 2,
        compiler_params=params(),
        cost_estimate=pl.CostEstimate(
            flops=12 * length * width * units,
            bytes_accessed=8 * width * units + 8 * length * width,
            transcendentals=length * units,
        ),
    )(*operands)


def norm_parts(values):
    center = values - jnp.mean(values, -1, keepdims=True)
    inverse = lax.rsqrt(jnp.mean(center * center, -1, keepdims=True) + EPS)
    return center * inverse, inverse


def layer_norm(values, gain, offset):
    return (norm_parts(values)[0] * gain + offset).astype(BF)


def norm_back(values, gain, grad):
    hat, inverse = norm_parts(values)
    scaled = grad * gain
    back = inverse * (
        scaled
        - jnp.mean(scaled, -1, keepdims=True)
        - hat * jnp.mean(scaled * hat, -1, keepdims=True)
    )
    lead = tuple(range(values.ndim - 1))
    return back, jnp.sum(grad * hat, lead), jnp.sum(grad, lead)


def layer(shape, args):
    chips, tops, lows = shape["chip"], shape["hi"], shape["lo"]
    (
        image_rows,
        text_rows,
        segment_ids,
        cotangent,
        query_weight,
        key_weight,
        value_weight,
        attn_output,
        cross_query,
        cross_key,
        cross_value,
        cross_output,
        hidden_in,
        hidden_out,
        *norms,
    ) = args
    images, rows, width = image_rows.shape
    texts = text_rows.shape[1]
    half_rows = rows // 2
    length = rows * lows * tops
    shard = query_weight.shape[0]
    chip, core = lax.axis_index("chip"), lax.axis_index("core")
    top = lax.axis_index("hi")
    own_slot = core * images + top % images

    def swap(value):
        return lax.ppermute(value, "core", [(0, 1), (1, 0)])

    def across(value, bit):
        return lax.ppermute(value, "chip", [(i, i ^ bit) for i in range(chips)])

    def shift(value, step):
        return lax.ppermute(value, "hi", [((i + step) % tops, i) for i in range(tops)])

    def matching(number, back):
        pairs = []
        for source_core in range(2):
            for source_top in range(tops):
                slot = source_top ^ number
                target = (slot // images) * tops + source_core * images + slot % images
                source = source_core * tops + source_top
                pairs.append((target, source) if back else (source, target))
        return pairs

    def to_image(piece_of):
        got = [
            lax.ppermute(piece_of(top ^ number), ("core", "hi"), matching(number, False))
            for number in range(tops)
        ]
        whole = jnp.stack(got)
        return jnp.stack(
            [lax.dynamic_index_in_dim(whole, own_slot ^ place, 0, False) for place in range(tops)]
        )

    def from_image(pieces):
        return [
            lax.ppermute(
                lax.dynamic_index_in_dim(pieces, own_slot ^ number, 0, False),
                ("core", "hi"),
                matching(number, True),
            )
            for number in range(tops)
        ]

    def image_piece(value):
        def piece(slot):
            return lax.dynamic_slice(
                value,
                (slot % images, (slot // images) * half_rows, 0),
                (1, half_rows, width),
            )[0]

        return piece

    def to_rows(pieces):
        got = jnp.stack(from_image(pieces))
        ordered = jnp.stack(
            [lax.dynamic_index_in_dim(got, top ^ slot, 0, False) for slot in range(tops)]
        )
        ordered = ordered.reshape(2, images, half_rows, width)
        return jnp.swapaxes(ordered, 0, 1).reshape(images, rows, width)

    def tp_gather(mine):
        if lows == 1:
            other = swap(mine)
            first = jnp.where(core == 0, mine, other)
            second = jnp.where(core == 0, other, mine)
            return jnp.stack([first, second], 1).reshape(length, width)
        every = lax.all_gather(mine, ("lo", "core"))
        every = every.reshape(lows * 2, tops, half_rows, width)
        return jnp.swapaxes(every, 0, 1).reshape(length, width)

    def tp_reduce(partial):
        if lows == 1:
            cut = partial.reshape(tops, 2, half_rows, width)
            sent = lax.dynamic_index_in_dim(cut, 1 - core, 1, False).astype(BF)
            kept = lax.dynamic_index_in_dim(cut, core, 1, False)
            return kept + swap(sent).astype(F32)
        cut = jnp.swapaxes(partial.astype(BF).reshape(tops, lows * 2, half_rows, width), 0, 1)
        cut = lax.psum_scatter(cut, ("lo", "core"), scatter_dimension=0, tiled=False)
        return cut.astype(F32)

    def core_half(weight, which):
        columns = weight.shape[1] // 2
        return lax.dynamic_slice_in_dim(weight, which * columns, columns, 1)

    def pack(which):
        feeds = [core_half(weight, which) for weight in (hidden_in, hidden_out)]
        cuts = feeds[0].shape[1] // 2
        groups = [
            [core_half(w, which) for w in (query_weight, key_weight, value_weight, attn_output)],
            [core_half(w, which) for w in (cross_query, cross_key, cross_value, cross_output)],
            [w[:, :cuts] for w in feeds],
            [w[:, cuts:] for w in feeds],
        ]
        return jnp.concatenate([w for group in groups for w in group], 1)

    kept = pack(core)
    taken = swap(pack(1 - core))
    own = jnp.concatenate(
        [jnp.where(core == 0, kept, taken), jnp.where(core == 0, taken, kept)], 0
    )
    block_rows = 2 * shard
    group_width = own.shape[1] // 4

    def plane_gather(piece):
        if chips != 4:
            return lax.all_gather(piece, "chip", axis=0, tiled=True)
        side = across(piece, 1)
        over = across(piece, 2)
        corner_low = across(side[:shard], 2)
        corner_high = across(over[shard:], 1)
        corner = jnp.concatenate([corner_low, corner_high], 0)
        pieces = jnp.stack([piece, side, over, corner])
        ordered = [lax.dynamic_index_in_dim(pieces, chip ^ place, 0, False) for place in range(4)]
        return jnp.concatenate(ordered, 0)

    def plane_scatter(grads):
        if chips != 4:
            return lax.psum_scatter(grads, "chip", scatter_dimension=0, tiled=True).astype(F32)

        def rows_of(place, low, count):
            return lax.dynamic_slice_in_dim(grads, (chip ^ place) * block_rows + low, count, 0)

        by_side = across(rows_of(3, 0, shard), 1)
        by_over = across(rows_of(3, shard, shard), 2)
        to_over = jnp.concatenate(
            [rows_of(2, 0, shard).astype(F32) + by_side.astype(F32), rows_of(2, shard, shard).astype(F32)], 0
        ).astype(BF)
        to_side = jnp.concatenate(
            [rows_of(1, 0, shard).astype(F32), rows_of(1, shard, shard).astype(F32) + by_over.astype(F32)], 0
        ).astype(BF)
        over, side = across(to_over, 2), across(to_side, 1)
        return rows_of(0, 0, block_rows).astype(F32) + over.astype(F32) + side.astype(F32)

    def top_scatter(pieces):
        total = pieces[0].astype(F32)
        for step in range(1, tops):
            total = total + shift(pieces[step].astype(BF), tops - step).astype(F32)
        return total

    def core_split(total):
        cut = total.reshape(2, shard, total.shape[1])
        mine = lax.dynamic_index_in_dim(cut, core, 0, False)
        other = swap(lax.dynamic_index_in_dim(cut, 1 - core, 0, False).astype(BF)).astype(F32)
        return jnp.where(core == 0, mine, other), jnp.where(core == 0, other, mine)

    own_wide = plane_gather(own)

    def fetch(group, count):
        part = own[:, group * group_width : (group + 1) * group_width]
        columns = group_width // count
        got = [shift(part, step).reshape(block_rows, count, 1, columns) for step in range(1, tops)]
        rest = jnp.concatenate(got, 2).reshape(block_rows, (tops - 1) * group_width)
        rest = plane_gather(rest).reshape(width, count, (tops - 1) * columns)
        near = own_wide[:, group * group_width : (group + 1) * group_width]
        near = near.reshape(width, count, columns)
        return [
            jnp.concatenate([near[:, one], rest[:, one]], 1) for one in range(count)
        ]

    def give(grads):
        count = len(grads)
        columns = grads[0].shape[1] // tops
        summed = plane_scatter(jnp.concatenate(grads, 1)).reshape(block_rows, count, tops, columns)
        pieces = [summed[:, :, step].reshape(block_rows, count * columns) for step in range(tops)]
        low, high = core_split(top_scatter(pieces))
        low, high = low.reshape(shard, count, columns), high.reshape(shard, count, columns)
        return [(low[:, one], high[:, one]) for one in range(count)]

    packed_norms = lax.all_gather(jnp.stack(norms), ("chip", "core"), axis=1, tiled=True)
    gain_one, bias_one, gain_two, bias_two, gain_three, bias_three = packed_norms

    w_query, w_key, w_value, w_out = fetch(0, 4)
    inputs = to_image(image_piece(image_rows)).astype(F32)
    c_query, c_key, c_value, c_out = fetch(1, 4)
    in_low, out_low = fetch(2, 2)
    in_high, out_high = fetch(3, 2)

    text = to_image(lambda slot: text_rows[slot % images])
    if lows > 1:
        text = lax.all_gather(text, "lo", axis=1)
    text = text.reshape(tops * lows * texts, width)
    other_ids = swap(segment_ids)
    ids = jnp.where(core == top // images, segment_ids, other_ids)
    ids = lax.dynamic_index_in_dim(ids, top % images, 0, False)
    captions = jnp.repeat(ids, length // ids.shape[0])[None, :]
    ids = ids[:, None]
    cot = to_image(image_piece(cotangent))

    full_one = tp_gather(layer_norm(inputs, gain_one, bias_one))
    packed = dot(full_one, jnp.concatenate([w_query, w_key, w_value], 1)).astype(BF)
    self_mix, self_lse = self_forward(packed)
    after_attn = inputs + tp_reduce(dot(self_mix, w_out, NT))
    full_two = tp_gather(layer_norm(after_attn, gain_two, bias_two))
    queries = dot(full_two, c_query).astype(BF)
    w_text = jnp.concatenate([c_key, c_value], 1)
    keys = dot(text, w_text).astype(BF)
    cross_mix, cross_lse = cross_forward(queries, keys, ids, captions)
    after_cross = after_attn + tp_reduce(dot(cross_mix, c_out, NT))
    full_three = tp_gather(layer_norm(after_cross, gain_three, bias_three))
    full_cot = tp_gather(cot)
    gin_low, gout_low, *sums = feed(full_three, full_cot, in_low, out_low, None)
    gin_high, gout_high, out_sum, back_sum = feed(full_three, full_cot, in_high, out_high, sums)
    low_grads = give([gin_low, gout_low])
    high_grads = give([gin_high, gout_high])
    result = to_rows((after_cross + tp_reduce(out_sum)).astype(BF))

    back_three, dgain_three, dbias_three = norm_back(after_cross, gain_three, tp_reduce(back_sum))
    grad_cross = cot.astype(F32) + back_three
    full_grad = tp_gather(grad_cross.astype(BF))
    mix_grad = dot(full_grad, c_out).astype(BF)
    dq, dk, dv = cross_backward(queries, keys, cross_mix, mix_grad, cross_lse, ids, captions)
    back_sum = dot(dq, c_query, NT)
    dkv = jnp.concatenate([dk, dv], 1)
    cross_grads = give(
        [
            dot(full_two, dq, TN).astype(BF),
            dot(text, dk, TN).astype(BF),
            dot(text, dv, TN).astype(BF),
            dot(full_grad, cross_mix, TN).astype(BF),
        ]
    )
    text_part = dot(dkv, w_text, NT).astype(BF).reshape(tops, lows, texts, width)
    if lows > 1:
        text_part = lax.psum_scatter(text_part, "lo", scatter_dimension=1, tiled=True)
    got = [part.astype(F32) for part in from_image(text_part[:, 0])]
    got = jnp.stack(got)
    got = [lax.dynamic_index_in_dim(got, top ^ slot, 0, False) for slot in range(tops)]
    text_grad = jnp.stack([got[i] + got[images + i] for i in range(images)])

    back_two, dgain_two, dbias_two = norm_back(after_attn, gain_two, tp_reduce(back_sum))
    grad_attn = grad_cross + back_two
    full_grad = tp_gather(grad_attn.astype(BF))
    mix_grad = dot(full_grad, w_out).astype(BF)
    dq, dk, dv = self_backward(packed, self_mix, mix_grad, self_lse)
    dqkv = jnp.concatenate([dq, dk, dv], 1)
    dwqkv = dot(full_one, dqkv, TN).astype(BF)
    span = dq.shape[1]
    self_grads = give(
        [
            dwqkv[:, :span],
            dwqkv[:, span : 2 * span],
            dwqkv[:, 2 * span :],
            dot(full_grad, self_mix, TN).astype(BF),
        ]
    )
    back_sum = dot(dqkv, jnp.concatenate([w_query, w_key, w_value], 1), NT)
    back_one, dgain_one, dbias_one = norm_back(inputs, gain_one, tp_reduce(back_sum))
    input_grad = to_rows((grad_attn + back_one).astype(BF)).astype(F32)

    norm_sums = lax.psum(
        jnp.stack([dgain_one, dbias_one, dgain_two, dbias_two, dgain_three, dbias_three]),
        ("chip", "core", "hi", "lo"),
    )
    norm_sums = lax.dynamic_slice_in_dim(norm_sums, (chip * 2 + core) * shard, shard, 1)

    feeds = [
        jnp.concatenate([low_grads[i][0], high_grads[i][0], low_grads[i][1], high_grads[i][1]], 1)
        for i in range(2)
    ]
    joined = [jnp.concatenate(pair, 1) for pair in (*self_grads, *cross_grads)]
    return (result, input_grad, text_grad, *joined, *feeds, *[norm_sums[i] for i in range(6)])


BLOCK = 256
ANY = pl.BlockSpec(memory_space=pl.ANY)
HBM = pl.BlockSpec(memory_space=pltpu.HBM)
SMEM = pl.BlockSpec(memory_space=pltpu.SMEM)
VMEM = pl.BlockSpec(memory_space=pltpu.VMEM)
LATE, ROWS = object(), object()
MIB = 1024 * 1024


def like(*shape, dtype=BF):
    return jax.ShapeDtypeStruct(shape, dtype)


class Late:
    def __init__(self, source, target, sems, chunks=1):
        self.ref, self.rows, self.waited = target, target.shape[0] // chunks, [False] * chunks
        self.copies = []
        for i in range(chunks):
            part = slice(i * self.rows, (i + 1) * self.rows)
            self.copies.append(pltpu.make_async_copy(source.at[part], target.at[part], sems.at[i]))

    def start(self, chunk):
        self.copies[chunk].start()

    def need(self, row):
        chunk = row // self.rows
        if not self.waited[chunk]:
            self.copies[chunk].wait()
            self.waited[chunk] = True
        return self.ref

    def ready(self):
        for chunk in range(len(self.copies)):
            self.need(chunk * self.rows)
        return self.ref


def start_chunks(loads):
    for chunk in range(max((len(load.copies) for load in loads), default=0)):
        for load in loads:
            if chunk < len(load.copies):
                load.start(chunk)


class Early:
    def __init__(self, source, target, sem):
        self.ref, self.copy, self.sent = source, pltpu.make_async_copy(source, target, sem), False

    def send(self):
        self.copy.start()
        self.sent = True


def call_overlapped(body, outs, ins, operands, scratch=(), limit=60):
    late_ins = [i for i, spec in enumerate(ins) if spec in (LATE, ROWS)]
    late_outs = [i for i, (spec, _) in enumerate(outs) if spec is LATE]
    buffers = [pltpu.VMEM(operands[i].shape, operands[i].dtype) for i in late_ins]
    buffers += [pltpu.VMEM(outs[i][1].shape, outs[i][1].dtype) for i in late_outs]
    count = len(buffers)

    def wrapped(*refs):
        refs = list(refs)
        sems, load_sems = refs.pop(), refs.pop()
        extra = refs[len(refs) - count :]
        refs = refs[: len(refs) - count]
        loads = [
            Late(refs[i], extra[n], load_sems.at[n], 4 if ins[i] is ROWS else 1)
            for n, i in enumerate(late_ins)
        ]
        start_chunks([load for load in loads if len(load.copies) > 1])
        start_chunks([load for load in loads if len(load.copies) == 1])
        for load, i in zip(loads, late_ins):
            refs[i] = load
        stores = []
        for n, i in enumerate(late_outs):
            place = len(ins) + i
            stores.append(Early(extra[len(late_ins) + n], refs[place], sems.at[n]))
            refs[place] = stores[-1]
        body(*refs)
        for load in loads:
            load.ready()
        for store in stores:
            if not store.sent:
                store.send()
        for store in stores:
            store.copy.wait()

    return call(
        wrapped,
        [(HBM if spec is LATE else spec, shape) for spec, shape in outs],
        [ANY if spec in (LATE, ROWS) else spec for spec in ins],
        operands,
        [
            *scratch,
            *buffers,
            pltpu.SemaphoreType.DMA((max(len(late_ins), 1), 4)),
            pltpu.SemaphoreType.DMA((max(len(late_outs), 1),)),
        ],
        limit,
    )


def call(body, outs, ins, operands, scratch=(), limit=60, grid=None, flops=0, moved=0):
    single = not isinstance(outs, (list, tuple))
    extra = {} if grid is None else {"grid": grid}
    cost = pl.CostEstimate(flops=1, bytes_accessed=1, transcendentals=0)
    out_specs, out_shape = ([outs[0]], [outs[1]]) if single else ([o[0] for o in outs], [o[1] for o in outs])
    return list(pl.pallas_call(
        body,
        in_specs=ins,
        out_specs=out_specs,
        out_shape=out_shape,
        scratch_shapes=list(scratch),
        compiler_params=pltpu.CompilerParams(vmem_limit_bytes=limit * MIB),
        cost_estimate=cost,
        **extra,
    )(*operands))


def run_copies(copies, sems):
    started = [pltpu.make_async_copy(source, target, sems.at[i]) for i, (source, target) in enumerate(copies)]
    for copy in started:
        copy.start()
    for copy in started:
        copy.wait()


def at(offset, count, unit=128):
    return pl.ds(pl.multiple_of(offset, unit), count)


def prepare_kernel(place, norms, wq, wk, wv, wo, cq, ck, cv, co, win, wout, keep, sent, sems):
    core = place[1]
    copies = []
    for target, which in ((sent, 1 - core), (keep, core)):
        for group, weights in enumerate(((wq, wk, wv, wo), (cq, ck, cv, co))):
            for one, weight in enumerate(weights):
                copies.append(
                    (
                        weight.at[:, at(which * 128, 128)],
                        target.at[group * 128 : (group + 1) * 128, one * 128 : (one + 1) * 128],
                    )
                )
        for part in range(2):
            for one, weight in enumerate((win, wout)):
                copies.append(
                    (
                        weight.at[:, at(which * 512 + part * 256, 256)],
                        target.at[256 + part * 128 : 384 + part * 128, one * 256 : (one + 1) * 256],
                    )
                )
        rows = jnp.concatenate([norms[...], jnp.zeros((10, 128), F32)], 0).astype(BF)
        target[512:528, :] = jnp.concatenate([rows] * 4, 1)
    run_copies(copies, sems)


def prepare(place, norms, weights):
    return call(
        prepare_kernel,
        [(VMEM, like(528, 512))] * 2,
        [SMEM, VMEM] + [ANY] * 10,
        (place, norms, *weights),
        [pltpu.SemaphoreType.DMA((24,))],
    )


def prepare_rows_kernel(place, ids, image, text, cot, *outs):
    rows_keep, rows_sent, cot_keep, cot_sent, text_pair, sems = outs
    core = place[1]
    copies = []
    for target, cots, which in ((rows_sent, cot_sent, 1 - core), (rows_keep, cot_keep, core)):
        for one in range(2):
            copies.append((image.at[one, at(which * 128, 128), :], target.at[one]))
            copies.append((cot.at[one, at(which * 128, 128), :], cots.at[one]))
    for one in range(2):
        copies.append((text.at[one], text_pair.at[one, 0:32, :]))
        row = jnp.concatenate([ids[one : one + 1, :].astype(F32), jnp.zeros((1, 896), F32)], 1)
        text_pair[one, 32:48, :] = jnp.concatenate([row] * 16, 0).astype(BF)
    run_copies(copies, sems)


def prepare_rows(place, ids, image, text, cot):
    return call(
        prepare_rows_kernel,
        [(VMEM, like(2, 128, 1024))] * 4 + [(VMEM, like(2, 48, 1024))],
        [SMEM, VMEM] + [ANY] * 3,
        (place, ids, image, text, cot),
        [pltpu.SemaphoreType.DMA((10,))],
    )


def pick_kernel(place, keep, taken, *outs):
    core, top = place[1], place[2]
    for step, out in enumerate(outs):
        image = (top + 4 - step) % 4

        @pl.when(image // 2 == core)
        def _():
            out[...] = keep[image % 2]

        @pl.when(image // 2 != core)
        def _():
            out[...] = taken[image % 2]


def pick(place, keep, taken):
    return call(
        pick_kernel,
        [(VMEM, like(*keep.shape[1:]))] * 4,
        [SMEM, VMEM, VMEM],
        (place, keep, taken),
    )


def join_kernel(place, keep, taken, *refs):
    singles, near, sems = refs[:4], refs[4], refs[5]
    copies = []
    for half, source in enumerate((keep, taken)):
        core = place[1] ^ half
        for group in range(4):
            part = source.at[group * 128 : (group + 1) * 128, :]
            copies.append((part, singles[group].at[at(core * 128, 128), :]))
        copies.append((source.at[0:128, :], near.at[at(core * 128, 128), :]))
        copies.append((source.at[512:528, :], near.at[at(256 + core * 16, 16, 16), :]))
    run_copies(copies, sems)


def join(place, keep, taken):
    return call(
        join_kernel,
        [(VMEM, like(256, 512))] * 4 + [(VMEM, like(288, 512))],
        [SMEM] + [ANY] * 2,
        (place, keep, taken),
        [pltpu.SemaphoreType.DMA((12,))],
    )


def stack_kernel(*refs):
    *parts, whole, sems = refs
    copies, low = [], 0
    for part in parts:
        copies.append((part, whole.at[low : low + part.shape[0]]))
        low += part.shape[0]
    run_copies(copies, sems)


def stack(parts):
    rows = sum(part.shape[0] for part in parts)
    return call(
        stack_kernel,
        [(VMEM, like(rows, *parts[0].shape[1:]))],
        [ANY] * len(parts),
        parts,
        [pltpu.SemaphoreType.DMA((len(parts),))],
        limit=60,
    )[0]


def join_pieces_kernel(place, *refs):
    pieces, whole, sems = refs[:4], refs[4], refs[5]
    run_copies([(piece, whole.at[i]) for i, piece in enumerate(pieces)], sems)


def join_pieces(place, pieces):
    return call(
        join_pieces_kernel,
        [(VMEM, like(4, *pieces[0].shape))],
        [SMEM] + [ANY] * 4,
        (place, *pieces),
        [pltpu.SemaphoreType.DMA((4,))],
    )[0]


def arrange_kernel(place, *refs):
    messages, text, sems = refs[:4], refs[4], refs[5]
    run_copies(
        [(m.at[0:32, :], text.at[at((place[2] + i) % 4 * 32, 32, 32), :]) for i, m in enumerate(messages)], sems
    )


def arrange(place, messages):
    return call(
        arrange_kernel,
        [(VMEM, like(128, 1024))],
        [SMEM] + [ANY] * 4,
        (place, *messages),
        [pltpu.SemaphoreType.DMA((4,))],
    )[0]


def started(pairs, sems):
    copies = [pltpu.make_async_copy(source, target, sems.at[i]) for i, (source, target) in enumerate(pairs)]
    for copy in copies:
        copy.start()
    return copies


def wait_all(copies):
    for copy in copies:
        copy.wait()


def first_pieces(place, near, far, buffer, norms):
    chip, top = place[0], place[2]
    weights, rows = [], []
    for source in range(4):
        for half in range(2):
            row = at((chip ^ source) * 256 + half * 128, 128)
            piece, first = (near[source], half * 128) if source < 3 else (near[3 + half], 0)
            weights.append((piece.at[first : first + 128, :], buffer.at[row, at(top * 512, 512, 512)]))
            low = 256 + half * 16 if source < 3 else 128 + half * 16
            piece = near[source] if source < 3 else near[4]
            column = at((chip ^ source) * 256 + half * 128, 128)
            rows.append((piece.at[low : low + 16, 0:128], norms.at[:, column]))
            for step in range(3):
                first = step * 256 + half * 128
                piece = far[source] if source < 3 else far[3 + first // 384]
                first = first if source < 3 else first % 384
                columns = at((top + 1 + step) % 4 * 512, 512, 512)
                weights.append((piece.at[first : first + 128, :], buffer.at[row, columns]))
    return weights, rows


def later_pieces(place, pieces, buffer):
    groups = (pieces[:1], pieces[1:-3], pieces[-3:-2], pieces[-2:])
    chip = place[0]
    weights = []
    for source, parts in enumerate(groups):
        for top in range(4):
            part, each = parts[top * len(parts) // 4], 4 // len(parts)
            rows, columns = at((chip ^ source) * 256, 256), slice(top * 512, (top + 1) * 512)
            weights.append((part.at[top % each], buffer.at[rows, columns]))
    return weights


def norm_row(norms, one):
    return norms[one : one + 1, :].astype(F32)


def normalized(values, gain, bias):
    center = values - jnp.mean(values, -1, keepdims=True)
    inverse = lax.rsqrt(jnp.mean(center * center, -1, keepdims=True) + EPS)
    return (center * inverse * gain + bias).astype(BF)


def columns_of(weights, one, count=128):
    return jnp.concatenate([weights[:, s * 512 + one * count : s * 512 + (one + 1) * count] for s in range(4)], 1)


def project_into(target, rows, weights, dims=NN, step=512):
    count = weights.shape[0] if dims == NT else weights.shape[1]
    for low in range(0, count, step):
        part = weights[low : low + step, :] if dims == NT else weights[:, low : low + step]
        target[:, low : low + step] = dot(rows, part, dims).astype(target.dtype)


def image_blocks(place, own, other):
    core, top = place[1], place[2]
    for number in range(4):
        yield (top + number) % 4 * 256 + core * 128, own, number
        yield (top + number) % 4 * 256 + (1 - core) * 128, other, number


def one_head(values, head):
    return jnp.where(lane_head((1, 2 * HD), 1, head), values, jnp.zeros_like(values))


def both_heads(values):
    return jnp.concatenate([one_head(values, 0), one_head(values, 1)], 0)


def pick_heads(values):
    count = values.shape[1] // 2
    return jnp.where(lane_head((128, 1), 0, 0), values[:, :count], values[:, count:]).T


def causal_pair(count):
    rows = lax.broadcasted_iota(jnp.int32, (count, 2 * count), 0)
    columns = lax.broadcasted_iota(jnp.int32, (count, 2 * count), 1)
    return rows <= jnp.where(columns >= count, columns - count, columns)


def twice(row):
    return jnp.concatenate([row, row], 1)


def softmax_mix(scores, values):
    scale = LOG2E * HD**-0.5
    peak = jnp.max(scores[0], 0, keepdims=True)
    for part in scores[1:]:
        peak = jnp.maximum(peak, jnp.max(part, 0, keepdims=True))
    total, mixed = 0.0, 0.0
    for part, rows in zip(scores, values):
        weights = jnp.exp2((part - peak) * scale)
        total = total + jnp.sum(weights, 0, keepdims=True)
        mixed = mixed + dot(rows, weights.astype(BF), TN)
    return mixed / total, peak * scale + jnp.log2(total)


def causal_mask():
    return lax.broadcasted_iota(jnp.int32, (BLOCK, BLOCK), 0) <= lax.broadcasted_iota(
        jnp.int32, (BLOCK, BLOCK), 1
    )


def self_fwd_kernel(place, own, other, *refs):
    near, far = refs[:5], refs[5:10]
    whole, norms, normed, qkv, mix, lse, part, weights, loads, store = refs[10:]
    pieces, rows = first_pieces(place, near, far, weights, norms)
    copies = started(rows + pieces, loads)
    wait_all(copies[: len(rows)])
    gain, bias = norm_row(norms, 0), norm_row(norms, 1)
    for row, half, number in image_blocks(place, own, other):
        normed[at(row, 128), :] = normalized(half[number].astype(F32), gain, bias)
    wait_all(copies[len(rows) :])
    (stored,) = started([(weights, whole)], store)
    for one in range(3):
        qkv[:, one * 512 : (one + 1) * 512] = dot(normed[...], columns_of(weights, one)).astype(BF)
    causal = causal_pair(512)

    def pair_step(pair, carry):
        lanes = at(pair * 128, 128)
        k_lanes, v_lanes = at(512 + pair * 128, 128), at(1024 + pair * 128, 128)
        for low in range(0, 1024, 512):
            high = low + 512
            both = both_heads(qkv[low:high, lanes])
            scores = [jnp.where(causal, dot(qkv[low:high, k_lanes], both, NT), NEG)]
            values = [qkv[low:high, v_lanes]]
            if low:
                scores.append(dot(qkv[:low, k_lanes], both, NT))
                values.append(qkv[:low, v_lanes])
            mixed, logsum = softmax_mix(scores, values)
            for head in range(2):
                lse[pair, head : head + 1, low:high] = logsum[:, head * 512 : (head + 1) * 512]
            mix[low:high, lanes] = pick_heads(mixed).astype(BF)
        return carry

    lax.fori_loop(0, 4, pair_step, 0)
    project_into(part, mix[...], columns_of(weights, 3), NT)
    stored.wait()


def fused_self_forward(place, own, other, near, far):
    return call(
        self_fwd_kernel,
        [
            (HBM, like(1024, 2048)),
            (VMEM, like(16, 1024)),
            (VMEM, like(1024, 1024)),
            (VMEM, like(1024, 1536)),
            (VMEM, like(1024, 512)),
            (VMEM, like(4, 2, 1024, dtype=F32)),
            (VMEM, like(1024, 1024)),
        ],
        [SMEM, VMEM, VMEM] + [ANY] * 10,
        (place, own, other, *near, *far),
        [pltpu.VMEM((1024, 2048), BF), pltpu.SemaphoreType.DMA((40,)), pltpu.SemaphoreType.DMA((1,))],
    )


def cross_fwd_kernel(
    place, own, other, mine_in, theirs_in, norms, text, ids, caption, *refs
):
    pieces = refs[:5]
    whole, after, normed, queries, keys, mix, lse, part, weights, mine, theirs, loads, store, row_sems = refs[5:]
    late = [
        Late(source, target, row_sems.at[i], 4)
        for i, (source, target) in enumerate(((mine_in, mine), (theirs_in, theirs)))
    ]
    start_chunks(late)
    copies = started(later_pieces(place, pieces, weights), loads)
    gain, bias = norm_row(norms, 2), norm_row(norms, 3)
    core, top = place[1], place[2]
    for block in range(4):
        for load in late:
            load.need(block * 256)
        for half, which in ((own, core), (other, 1 - core)):
            rows = at(block * 256 + which * 128, 128)
            values = half[(block + 4 - top) % 4].astype(F32)
            values = values + (mine[rows, :].astype(F32) + theirs[rows, :].astype(F32))
            after[rows, :] = values
            normed[rows, :] = normalized(values, gain, bias)
    wait_all(copies)
    (stored,) = started([(weights, whole)], store)
    project_into(queries, normed[...], columns_of(weights, 0))
    w_text = jnp.concatenate([columns_of(weights, 1), columns_of(weights, 2)], 1)
    keys[...] = dot(text[...], w_text).astype(BF)

    def pair_step(pair, carry):
        lanes, v_lanes = at(pair * 128, 128), at(512 + pair * 128, 128)
        seen = twice(ids[...] == caption[...])
        scores = jnp.where(seen, dot(keys[:, lanes], both_heads(queries[:, lanes]), NT), NEG)
        mixed, logsum = softmax_mix([scores], [keys[:, v_lanes]])
        for head in range(2):
            lse[pair, head : head + 1, :] = logsum[:, head * 1024 : (head + 1) * 1024]
        mix[:, lanes] = pick_heads(mixed).astype(BF)
        return carry

    lax.fori_loop(0, 4, pair_step, 0)
    project_into(part, mix[...], columns_of(weights, 3), NT)
    stored.wait()


def fused_cross_forward(place, own, other, mine, theirs, norms, text, ids, caption, pieces):
    return call(
        cross_fwd_kernel,
        [
            (HBM, like(1024, 2048)),
            (VMEM, like(1024, 1024, dtype=F32)),
            (VMEM, like(1024, 1024)),
            (VMEM, like(1024, 512)),
            (VMEM, like(128, 1024)),
            (VMEM, like(1024, 512)),
            (VMEM, like(4, 2, 1024, dtype=F32)),
            (VMEM, like(1024, 1024)),
        ],
        [SMEM, VMEM, VMEM, ANY, ANY] + [VMEM] * 4 + [ANY] * 5,
        (place, own, other, mine, theirs, norms, text, ids, caption, *pieces),
        [pltpu.VMEM((1024, 2048), BF)]
        + [pltpu.VMEM((1024, 1024), BF)] * 2
        + [pltpu.SemaphoreType.DMA((16,)), pltpu.SemaphoreType.DMA((1,)), pltpu.SemaphoreType.DMA((2, 4))],
    )


def cut_grads(place, grads, columns, own, side, over, low, high):
    chip = place[0]
    own[:, columns] = grads[at(chip * 256, 256), :].astype(BF)
    side[:, columns] = grads[at((chip ^ 1) * 256, 256), :].astype(BF)
    over[:, columns] = grads[at((chip ^ 2) * 256, 256), :].astype(BF)
    low[:, columns] = grads[at((chip ^ 3) * 256, 128), :].astype(BF)
    high[:, columns] = grads[at((chip ^ 3) * 256 + 128, 128), :].astype(BF)


GRAD_SHAPES = [(256, 2048)] * 3 + [(128, 2048)] * 2


def feed_step(rows, cot, rows_t, cot_t, weights, out_sum, back_sum, grads):
    w_in = jnp.concatenate([weights[0][:, :256], weights[1][:, :256]], 1)
    w_out = jnp.concatenate([weights[0][:, 256:], weights[1][:, 256:]], 1)
    slope = math.sqrt(2.0 / math.pi)
    pre = dot(rows[...], w_in)
    square = pre * pre
    bent = jnp.tanh(pre * (slope + slope * 0.044715 * square))
    half = 0.5 * (1.0 + bent)
    act = (pre * half).astype(BF)
    bend = half + pre * (0.5 * (1.0 - bent * bent)) * (slope + 3.0 * slope * 0.044715 * square)
    pre_grad = (dot(cot[...], w_out) * bend).astype(BF)
    for low in range(0, 1024, 512):
        part = slice(low, low + 512)
        out_sum[:, part] += dot(act, w_out[part, :], NT)
        back_sum[:, part] += dot(pre_grad, w_in[part, :], NT)
    for block in range(2):
        part = slice(block * 256, (block + 1) * 256)
        grads[:, block * 512 : block * 512 + 256] = dot(rows_t[...], pre_grad[:, part])
        grads[:, block * 512 + 256 : (block + 1) * 512] = dot(cot_t[...], act[:, part])


def feed_first_kernel(
    place, after_in, mine_in, theirs_in, norms, cot_own, cot_other, *refs
):
    pieces = refs[:6]
    g_whole, after_out, normed_out, cot_out, out_sum, back = refs[6:12]
    after_cross, normed, cot, back_sum, rows_t, cot_t, grads, weights, after, mine, theirs, sems, loads, row_sems = refs[12:]
    step = pl.program_id(0)
    pairs = ((after_cross, after_out), (normed, normed_out), (cot, cot_out))
    stores = [pltpu.make_async_copy(a, b, sems.at[i]) for i, (a, b) in enumerate(pairs)]

    @pl.when(step == 0)
    def _():
        arrays = ((after_in, after), (mine_in, mine), (theirs_in, theirs))
        late = [Late(source, target, row_sems.at[i], 4) for i, (source, target) in enumerate(arrays)]
        start_chunks(late)
        copies = started(later_pieces(place, pieces, weights), loads)
        gain, bias = norm_row(norms, 4), norm_row(norms, 5)
        for low in range(0, 1024, 128):
            for load in late:
                load.need(low)
            rows = slice(low, low + 128)
            values = after[rows, :] + (mine[rows, :].astype(F32) + theirs[rows, :].astype(F32))
            after_cross[rows, :] = values
            normed[rows, :] = normalized(values, gain, bias)
        for row, half, number in image_blocks(place, cot_own, cot_other):
            cot[at(row, 128), :] = half[number]
        for store in stores:
            store.start()
        rows_t[...] = normed[...].T
        cot_t[...] = cot[...].T
        out_sum[...] = jnp.zeros_like(out_sum)
        for block in range(4):
            rows = at(block * 256 + place[1] * 128, 128)
            out_sum[rows, :] = after_cross[rows, :]
        back_sum[...] = jnp.zeros_like(back_sum)
        wait_all(copies)

    blocks = [weights[:, at(step * 1024 + block * 512, 512, 512)] for block in range(2)]
    feed_step(normed, cot, rows_t, cot_t, blocks, out_sum, back_sum, grads)
    for chip in range(4):
        for block in range(2):
            part = grads[chip * 256 : (chip + 1) * 256, block * 512 : (block + 1) * 512]
            g_whole[chip, block] = part.astype(BF)

    @pl.when(step == 1)
    def _():
        back[...] = back_sum[...].astype(BF)
        for store in stores:
            store.wait()


def feed_second_kernel(
    place, normed, cot, out_in, back_in, weights,
    g_own, g_side, g_over, g_low, g_high, out_keep, out_sent, back, out_sum, back_sum, rows_t, cot_t, grads,
):
    step, core = pl.program_id(0), place[1]

    @pl.when(step == 0)
    def _():
        rows_t[...] = normed[...].T
        cot_t[...] = cot[...].T
        out_sum[...] = out_in[...]
        back_sum[...] = back_in[...].astype(F32)

    blocks = [weights[:, block].reshape(1024, 512) for block in range(2)]
    feed_step(normed, cot, rows_t, cot_t, blocks, out_sum, back_sum, grads)
    cut_grads(place, grads, slice(None), g_own, g_side, g_over, g_low, g_high)

    @pl.when(step == 1)
    def _():
        back[...] = back_sum[...].astype(BF)
        for block in range(4):
            out_keep[block] = out_sum[at(block * 256 + core * 128, 128), :]
            out_sent[block] = out_sum[at(block * 256 + (1 - core) * 128, 128), :].astype(BF)


def once(*shape):
    zeros = (0,) * len(shape)
    return pl.BlockSpec(shape, lambda i: zeros, pipeline_mode=pl.Buffered(1))


def grad_outs(width=512):
    return [(pl.BlockSpec((rows, width), lambda i: (0, i)), like(rows, n)) for rows, n in GRAD_SHAPES]


FEED_FLOPS = 13 * 2**30


def feed_first(place, after, mine, theirs, norms, cot_own, cot_other, pieces):
    square = once(1024, 1024)
    return call(
        feed_first_kernel,
        [(pl.BlockSpec((4, 2, 256, 512), lambda i: (0, i, 0, 0)), like(4, 4, 256, 512))]
        + [
            (HBM, like(1024, 1024, dtype=F32)),
            (HBM, like(1024, 1024)),
            (HBM, like(1024, 1024)),
            (square, like(1024, 1024, dtype=F32)),
            (square, like(1024, 1024)),
        ],
        [SMEM, ANY, ANY, ANY, once(16, 1024), once(4, 128, 1024), once(4, 128, 1024)]
        + [ANY] * 6,
        (place, after, mine, theirs, norms, cot_own, cot_other, *pieces),
        [pltpu.VMEM((1024, 1024), F32)]
        + [pltpu.VMEM((1024, 1024), BF)] * 2
        + [pltpu.VMEM((1024, 1024), F32)]
        + [pltpu.VMEM((1024, 1024), BF)] * 2
        + [pltpu.VMEM((1024, 1024), F32), pltpu.VMEM((1024, 2048), BF)]
        + [pltpu.VMEM((1024, 1024), F32), pltpu.VMEM((1024, 1024), BF), pltpu.VMEM((1024, 1024), BF)]
        + [pltpu.SemaphoreType.DMA((3,)), pltpu.SemaphoreType.DMA((16,)), pltpu.SemaphoreType.DMA((3, 4))],
        limit=60,
        grid=(2,),
        flops=FEED_FLOPS,
        moved=30 * MIB,
    )


def feed_second(place, normed, cot, out_in, back_in, weights):
    square = once(1024, 1024)
    return call(
        feed_second_kernel,
        grad_outs(1024)
        + [
            (once(4, 128, 1024), like(4, 128, 1024, dtype=F32)),
            (once(4, 128, 1024), like(4, 128, 1024)),
            (square, like(1024, 1024)),
        ],
        [SMEM, square, square, square, square, pl.BlockSpec((4, 2, 256, 512), lambda i: (0, i, 0, 0))],
        (place, normed, cot, out_in, back_in, weights),
        [pltpu.VMEM((1024, 1024), F32)] * 2
        + [pltpu.VMEM((1024, 1024), BF)] * 2
        + [pltpu.VMEM((1024, 1024), F32)],
        limit=60,
        grid=(2,),
        flops=FEED_FLOPS,
        moved=26 * MIB,
    )


def norm_backward(values, gain, grad):
    center = values - jnp.mean(values, -1, keepdims=True)
    inverse = lax.rsqrt(jnp.mean(center * center, -1, keepdims=True) + EPS)
    hat = center * inverse
    scaled = grad * gain
    back = inverse * (
        scaled - jnp.mean(scaled, -1, keepdims=True) - hat * jnp.mean(scaled * hat, -1, keepdims=True)
    )
    return back, grad * hat


def norm_block(values_of, mine, theirs, base_of, gain, norms, keep):
    gain = norm_row(*gain)
    gain_sum, bias_sum = jnp.zeros((8, 1024), F32), jnp.zeros((8, 1024), F32)
    for low in range(0, 1024, 128):
        rows = slice(low, low + 128)
        grad = mine.need(low)[rows, :].astype(F32) + theirs.need(low)[rows, :].astype(F32)
        back, term = norm_backward(values_of(rows), gain, grad)
        keep(rows, base_of(rows) + back)
        gain_sum = gain_sum + jnp.sum(term.reshape(16, 8, 1024), 0)
        bias_sum = bias_sum + jnp.sum(grad.reshape(16, 8, 1024), 0)
    norms[0:1, :] = jnp.sum(gain_sum, 0, keepdims=True)
    norms[1:2, :] = jnp.sum(bias_sum, 0, keepdims=True)


def pair_row(lse, pair, low, high):
    return jnp.concatenate([lse[pair, 0:1, low:high], lse[pair, 1:2, low:high]], 1)


def pair_delta(grad, mix):
    product = (grad.astype(F32) * mix.astype(F32)).T
    return jnp.concatenate([jnp.sum(product[:HD], 0, keepdims=True), jnp.sum(product[HD:], 0, keepdims=True)], 1)


def head_grads(keys, values, one, one_grad, lse, delta, mask):
    weights = jnp.exp2(dot(keys, one, NT) * (LOG2E * HD**-0.5) - lse)
    if mask is not None:
        weights = jnp.where(mask, weights, 0.0)
    slope = dot(values, one_grad, NT)
    return weights.astype(BF), (weights * (slope - delta)).astype(BF)


def cross_bwd_kernel(
    place, after, mine, theirs, cot, gain, weights, normed, text, queries, keys, mix, lse, ids, caption,
    grad_out, part_out, norms, text_part, g_own, g_side, g_over, g_low, g_high, low_grad, mix_grad, dq, dkv, grads,
):
    grad_cross, part = grad_out.ref, part_out.ref

    def keep(rows, value):
        grad_cross[rows, :] = value
        low_grad[rows, :] = value.astype(BF)

    norm_block(lambda rows: after.need(rows.start)[rows, :], mine, theirs, lambda rows: cot.need(rows.start)[rows, :].astype(F32), (gain, 4), norms, keep)
    grad_out.send()
    weights, queries, keys, mix = weights.ready(), queries.ready(), keys.ready(), mix.ready()
    project_into(mix_grad, low_grad[...], columns_of(weights, 3))

    def pair_step(pair, carry):
        lanes, v_lanes = at(pair * 128, 128), at(512 + pair * 128, 128)
        query, grad = both_heads(queries[:, lanes]), both_heads(mix_grad[:, lanes])
        prob, score_grad = head_grads(
            keys[:, lanes],
            keys[:, v_lanes],
            query,
            grad,
            pair_row(lse, pair, 0, 1024),
            pair_delta(mix_grad[:, lanes], mix[:, lanes]),
            twice(ids[...] == caption[...]),
        )
        dv_sum, dk_sum = dot(prob, grad), dot(score_grad, query)
        dq[:, lanes] = (pick_heads(dot(keys[:, lanes], score_grad, TN)) * HD**-0.5).astype(BF)
        dkv[:, lanes] = (dk_sum * HD**-0.5).astype(BF)
        dkv[:, v_lanes] = dv_sum.astype(BF)
        return carry

    lax.fori_loop(0, 4, pair_step, 0)
    project_into(part, dq[...], columns_of(weights, 0), NT)
    part_out.send()
    normed = normed.ready()
    w_text = jnp.concatenate([columns_of(weights, 1), columns_of(weights, 2)], 1)
    text_part[...] = dot(dkv[...], w_text, NT).astype(BF)
    for one, (left, right) in enumerate(
        ((normed, dq[...]), (text, dkv[:, :512]), (text, dkv[:, 512:]), (low_grad, mix[...]))
    ):
        grads[...] = dot(left[...], right, TN)
        for s in range(4):
            columns = slice(s * 512 + one * 128, s * 512 + (one + 1) * 128)
            cut_grads(
                place, grads.at[:, s * 128 : (s + 1) * 128], columns, g_own, g_side, g_over, g_low, g_high
            )


def fused_cross_backward(place, after, mine, theirs, cot, gain, weights, normed, text, queries, keys, mix, lse, ids, caption):
    return call_overlapped(
        cross_bwd_kernel,
        [
            (LATE, like(1024, 1024, dtype=F32)),
            (LATE, like(1024, 1024)),
            (VMEM, like(8, 1024, dtype=F32)),
            (VMEM, like(128, 1024)),
        ]
        + [(VMEM, like(*shape)) for shape in GRAD_SHAPES],
        [SMEM] + [ROWS] * 4 + [VMEM] + [LATE, LATE, VMEM, LATE, LATE, LATE, VMEM, VMEM, VMEM],
        (place, after, mine, theirs, cot, gain, weights, normed, text, queries, keys, mix, lse, ids, caption),
        [
            pltpu.VMEM((1024, 1024), BF),
            pltpu.VMEM((1024, 512), BF),
            pltpu.VMEM((1024, 512), BF),
            pltpu.VMEM((128, 1024), BF),
            pltpu.VMEM((1024, 512), F32),
        ],
    )


def self_bwd_kernel(
    place, after, mine, theirs, base, gain, weights, qkv, mix, lse,
    grad_out, low_out, norms, dqkv, mix_grad, dk_sum, dv_sum,
):
    core = place[1]
    grad_own, low_grad = grad_out.ref, low_out.ref

    def keep(rows, value):
        low_grad[rows, :] = value.astype(BF)

        @pl.when(core == (rows.start // 128) % 2)
        def _():
            grad_own[rows.start // 256] = value

    norm_block(lambda rows: after.need(rows.start)[rows, :], mine, theirs, lambda rows: base.need(rows.start)[rows, :], (gain, 2), norms, keep)
    grad_out.send()
    low_out.send()
    weights, qkv, mix = weights.ready(), qkv.ready(), mix.ready()
    project_into(mix_grad, low_grad[...], columns_of(weights, 3))
    causal = causal_pair(512)

    def pair_step(pair, carry):
        lanes = at(pair * 128, 128)
        k_lanes, v_lanes = at(512 + pair * 128, 128), at(1024 + pair * 128, 128)
        for low in range(0, 1024, 512):
            high = low + 512
            query, grad = both_heads(qkv[low:high, lanes]), both_heads(mix_grad[low:high, lanes])
            delta = pair_delta(mix_grad[low:high, lanes], mix[low:high, lanes])
            logsum = pair_row(lse, pair, low, high)
            total = 0.0
            for start in range(0, high, 512):
                rows = slice(start, start + 512)
                keys = qkv[rows, k_lanes]
                prob, score_grad = head_grads(
                    keys, qkv[rows, v_lanes], query, grad, logsum, delta, causal if start == low else None
                )
                dv, dk = dot(prob, grad), dot(score_grad, query)
                if start == low:
                    dv_sum[rows, :], dk_sum[rows, :] = dv, dk
                else:
                    dv_sum[rows, :] += dv
                    dk_sum[rows, :] += dk
                total = total + dot(keys, score_grad, TN)
            dqkv[low:high, lanes] = (pick_heads(total) * HD**-0.5).astype(BF)
        dqkv[:, k_lanes] = (dk_sum[...] * HD**-0.5).astype(BF)
        dqkv[:, v_lanes] = dv_sum[...].astype(BF)
        return carry

    lax.fori_loop(0, 4, pair_step, 0)


def fused_self_backward(place, after, mine, theirs, base, gain, weights, qkv, mix, lse):
    return call_overlapped(
        self_bwd_kernel,
        [
            (LATE, like(4, 128, 1024, dtype=F32)),
            (LATE, like(1024, 1024)),
            (VMEM, like(8, 1024, dtype=F32)),
            (VMEM, like(1024, 1536)),
        ],
        [SMEM] + [ROWS] * 4 + [VMEM] + [LATE] * 3 + [VMEM],
        (place, after, mine, theirs, base, gain, weights, qkv, mix, lse),
        [pltpu.VMEM((1024, 512), BF), pltpu.VMEM((1024, 128), F32), pltpu.VMEM((1024, 128), F32)],
    )


def self_grads_kernel(place, normed, low_grad, dq, dk, dv, mix, g_own, g_side, g_over, g_low, g_high, rows_t, grad_t, grads):
    @pl.when(pl.program_id(0) == 0)
    def _():
        rows_t[...] = normed[...].T
        grad_t[...] = low_grad[...].T

    grads[:, :384] = dot(rows_t[...], jnp.concatenate([dq[...], dk[...], dv[...]], 1))
    grads[:, 384:] = dot(grad_t[...], mix[...])
    cut_grads(place, grads, slice(None), g_own, g_side, g_over, g_low, g_high)


def self_grads(place, normed, low_grad, dqkv, mix):
    square = once(1024, 1024)

    def cut(offset):
        return pl.BlockSpec((1024, 128), lambda i: (0, offset + i))

    return call(
        self_grads_kernel,
        grad_outs(),
        [SMEM, square, square, cut(0), cut(4), cut(8), cut(0)],
        (place, normed, low_grad, dqkv, dqkv, dqkv, mix),
        [pltpu.VMEM((1024, 1024), BF)] * 2 + [pltpu.VMEM((1024, 512), F32)],
        limit=60,
        grid=(4,),
        flops=4 * 2**30,
        moved=12 * MIB,
    )


def self_back_kernel(place, dqkv, weights, kept, sent):
    core = place[1]
    w_in = jnp.concatenate([columns_of(weights, one) for one in range(3)], 1)
    for target, half in ((sent, 1 - core), (kept, core)):
        rows = jnp.concatenate([dqkv[at(block * 256 + half * 128, 128), :] for block in range(4)], 0)
        for low in range(0, 1024, 512):
            value = dot(rows, w_in[low : low + 512, :], NT).astype(target.dtype)
            target[:, :, low : low + 512] = value.reshape(4, 128, 512)


def self_back(place, dqkv, weights):
    return call(
        self_back_kernel,
        [(VMEM, like(4, 128, 1024, dtype=F32)), (VMEM, like(4, 128, 1024))],
        [SMEM, VMEM, VMEM],
        (place, dqkv, weights),
        limit=60,
        flops=3 * 2**30,
        moved=10 * MIB,
    )


def last_norm_kernel(place, rows, grad_own, mine, theirs, gain, text_part, sums_two, sums_three, *pieces):
    gain_sum, bias_sum = jnp.zeros((8, 1024), F32), jnp.zeros((8, 1024), F32)
    for number in range(4):
        block = (place[2] + number) % 4
        grad = mine[block] + theirs[block].astype(F32)
        back, term = norm_backward(rows[number].astype(F32), norm_row(gain, 0), grad)
        pieces[-number % 4][0:128, :] = (grad_own[block] + back).astype(BF)
        pieces[-number % 4][128:160, :] = text_part[at(block * 32, 32, 32), :]
        gain_sum = gain_sum + jnp.sum(term.reshape(16, 8, 1024), 0)
        bias_sum = bias_sum + jnp.sum(grad.reshape(16, 8, 1024), 0)
    sums = [jnp.sum(gain_sum, 0, keepdims=True), jnp.sum(bias_sum, 0, keepdims=True)]
    sums += [0.5 * sums_two[0:2, :], 0.5 * sums_three[0:2, :], jnp.zeros((10, 1024), F32)]
    sums = jnp.concatenate(sums, 0).astype(BF)
    for piece in pieces:
        piece[160:176, :] = sums


def last_norm(place, rows, grad_own, mine, theirs, gain, text_part, sums_two, sums_three):
    return call(
        last_norm_kernel,
        [(VMEM, like(176, 1024))] * 4,
        [SMEM] + [VMEM] * 8,
        (place, rows, grad_own, mine, theirs, gain, text_part, sums_two, sums_three),
    )


def finish_kernel(place, out_keep, theirs, *pieces):
    for number, piece in enumerate(pieces):
        block = (place[2] + 4 - number) % 4
        piece[...] = (out_keep[block] + theirs[block].astype(F32)).astype(BF)


def finish(place, out_keep, theirs):
    return call(
        finish_kernel,
        [(VMEM, like(128, 1024))] * 4,
        [SMEM] + [VMEM] * 2,
        (place, out_keep, theirs),
    )


def part_kernel(place, *refs):
    pieces, mine, sent = refs[:4], refs[4], refs[5]
    core, top = place[1], place[2]
    for step, piece in enumerate(pieces):
        image = (top + step) % 4

        @pl.when(image // 2 == core)
        def _():
            mine[image % 2] = piece[...]

        @pl.when(image // 2 != core)
        def _():
            sent[image % 2] = piece[...]

    if pieces[0].shape[0] > 160:
        total = 0.0
        for piece in pieces:
            total = total + piece[160:176, :].astype(F32)
        mine[0, 160:176, :] = total.astype(BF)
        sent[0, 160:176, :] = total.astype(BF)


def part_images(place, pieces):
    return call(
        part_kernel,
        [(VMEM, like(2, *pieces[0].shape))] * 2,
        [SMEM] + [VMEM] * 4,
        (place, *pieces),
    )


def land_kernel(place, mine, taken, rows, *more):
    core = place[1]
    for one in range(2):
        rows[one, at(core * 128, 128), :] = mine[one, 0:128, :].astype(rows.dtype)
        rows[one, at((1 - core) * 128, 128), :] = taken[one, 0:128, :].astype(rows.dtype)
        if more:
            more[0][one] = mine[one, 128:160, :].astype(F32) + taken[one, 128:160, :].astype(F32)
    if more:
        more[1][...] = mine[0, 160:168, :].astype(F32) + taken[0, 160:168, :].astype(F32)


def land(place, mine, taken, dtype):
    outs = [(VMEM, like(2, 256, 1024, dtype=dtype))]
    if mine.shape[1] > 128:
        outs += [(VMEM, like(2, 32, 1024, dtype=F32)), (VMEM, like(8, 1024, dtype=F32))]
    return call(land_kernel, outs, [SMEM, VMEM, VMEM], (place, mine, taken))


def relay_kernel(over, side, from_side, from_over, to_over, to_side):
    to_over[0:128, :] = (over[0:128, :].astype(F32) + from_side[...].astype(F32)).astype(BF)
    to_over[128:256, :] = over[128:256, :]
    to_side[0:128, :] = side[0:128, :]
    to_side[128:256, :] = (side[128:256, :].astype(F32) + from_over[...].astype(F32)).astype(BF)


def relay(over, side, from_side, from_over):
    return call(
        relay_kernel,
        [(VMEM, like(256, 2048))] * 2,
        [VMEM] * 4,
        (over, side, from_side, from_over),
        limit=60,
        moved=5 * MIB,
    )


def plane_sum_kernel(place, own, over, side, keep, *sent):
    for s in range(4):
        columns = at((place[2] + s) % 4 * 512, 512, 512)
        total = own[:, columns].astype(F32) + over[:, columns].astype(F32) + side[:, columns].astype(F32)
        if s:
            sent[s - 1][...] = total.astype(BF)
        else:
            keep[...] = total


def plane_sum(place, own, over, side):
    return call(
        plane_sum_kernel,
        [(VMEM, like(256, 512, dtype=F32))] + [(VMEM, like(256, 512))] * 3,
        [SMEM] + [VMEM] * 3,
        (place, own, over, side),
        limit=60,
        moved=5 * MIB,
    )


def plane_sum_whole_kernel(own, over, side, whole):
    for step in range(4):
        columns = slice(step * 512, (step + 1) * 512)
        total = own[:, columns].astype(F32) + over[:, columns].astype(F32) + side[:, columns].astype(F32)
        whole[step * 256 : (step + 1) * 256, :] = total.astype(BF)


def plane_sum_whole(own, over, side):
    return call(
        plane_sum_whole_kernel,
        [(VMEM, like(1024, 512))],
        [VMEM] * 3,
        (own, over, side),
    )[0]


def line_sum_kernel(place, keep, one, two, three, mine, other):
    core = place[1]
    for target, half in ((other, 1 - core), (mine, core)):
        rows = at(half * 128, 128)
        total = keep[rows, :]
        for part in (one, two, three):
            total = total + part[rows, :].astype(F32)
        target[...] = total.astype(target.dtype)


def line_sum(place, keep, parts):
    return call(
        line_sum_kernel,
        [(VMEM, like(128, 512, dtype=F32)), (VMEM, like(128, 512))],
        [SMEM] + [VMEM] * 4,
        (place, keep, *parts),
        limit=60,
        moved=2 * MIB,
    )


def spread_kernel(place, mine, other, *outs):
    core, columns = place[1], mine.shape[1] // len(outs)
    for one, out in enumerate(outs):
        cut = slice(one * columns, (one + 1) * columns)
        out[:, at(core * columns, columns)] = mine[:, cut].astype(F32)
        out[:, at((1 - core) * columns, columns)] = other[:, cut].astype(F32)


def spread(place, mine, other):
    return call(
        spread_kernel,
        [(VMEM, like(128, 256, dtype=F32))] * 4,
        [SMEM] + [VMEM] * 2,
        (place, mine, other),
        limit=60,
        moved=MIB,
    )


def spread_feed_kernel(place, mine_one, other_one, mine_two, other_two, *outs):
    core = place[1]
    for part, (mine, other) in enumerate(((mine_one, other_one), (mine_two, other_two))):
        for one, out in enumerate(outs):
            cut = slice(one * 256, (one + 1) * 256)
            out[:, at(core * 512 + part * 256, 256)] = mine[:, cut].astype(F32)
            out[:, at((1 - core) * 512 + part * 256, 256)] = other[:, cut].astype(F32)


def spread_feed(place, *halves):
    return call(
        spread_feed_kernel,
        [(VMEM, like(128, 1024, dtype=F32))] * 2,
        [SMEM] + [VMEM] * 4,
        (place, *halves),
        limit=60,
        moved=2 * MIB,
    )


tie = lax.optimization_barrier


def packed_layer(args):
    image_rows, text_rows, segment_ids, cotangent, *others = args
    weights, norms = others[:10], others[10:]
    chip, core, top = lax.axis_index("chip"), lax.axis_index("core"), lax.axis_index("hi")
    place = jnp.stack([chip, core, top, core * 2 + top % 2]).astype(jnp.int32)

    def swap(value):
        return lax.ppermute(value, "core", [(0, 1), (1, 0)])

    def across(value, bit):
        return lax.ppermute(value, "chip", [(i, i ^ bit) for i in range(4)])

    def shift(value, step):
        return lax.ppermute(value, "hi", [((i + step) % 4, i) for i in range(4)])

    def line(part):
        return [shift(part, step) for step in range(1, 4)]

    def exchange(pieces):
        return [pieces[0]] + [shift(piece, step) for step, piece in enumerate(pieces) if step]

    def gather_line(part):
        return lax.all_gather(part, "hi")

    def sides(value):
        return [across(value, 1), across(value, 2)]

    def corners(pair, cut):
        return [across(pair[0][:cut], 2), across(pair[1][cut:], 1)]

    def grad_corners(grads):
        return [across(grads[3], 1), across(grads[4], 2)]

    def grad_sides(grads, got, later):
        to_over, to_side, later = tie((*relay(grads[2], grads[1], *got), later))
        return [across(to_over, 2), across(to_side, 1)], later

    def halves(total):
        cut = total.reshape(2, 128, 512)
        sent = lax.dynamic_index_in_dim(cut, 1 - core, 0, False)
        return lax.dynamic_index_in_dim(cut, core, 0, False), swap(sent)

    keep, sent = prepare(place, jnp.stack(norms), weights)
    v = {"taken": swap(sent)}
    v["rows_keep"], v["rows_sent"], v["cot_keep"], v["cot_sent"], v["text_pair"] = prepare_rows(
        place, segment_ids, image_rows, text_rows, cotangent
    )
    v = tie(v)
    *v["singles"], v["near"] = join(place, keep, v.pop("taken"))
    v["rows_taken"], v["cot_taken"] = swap(v.pop("rows_sent")), swap(v.pop("cot_sent"))
    v["text_taken"] = swap(v["text_pair"])
    v = tie(v)

    v["near"] = [v["near"], *sides(v["near"])]
    lines = line(v["singles"][0])
    v["pieces"] = pick(place, v.pop("rows_keep"), v.pop("rows_taken"))
    v["cot_pieces"] = pick(place, v.pop("cot_keep"), v.pop("cot_taken"))
    v["text_pieces"] = pick(place, v.pop("text_pair"), v.pop("text_taken"))
    v = tie(v)
    v["near"] += corners(v["near"][1:], 128)
    v["line"] = lines
    v = tie(v)

    rest = stack(v.pop("line"))
    v["far_self"] = [rest, *sides(rest)]
    v["two_on"] = shift(v["pieces"][2], 2)
    line_cross = gather_line(v["singles"][1])
    v = tie(v)
    v["far_self"] += corners(v["far_self"][1:], 384)
    pieces = v.pop("pieces")
    v["pieces"] = [pieces[0], shift(pieces[1], 1), v.pop("two_on"), shift(pieces[3], 3)]
    v["line_cross"] = line_cross
    v = tie(v)
    v["rows_own"] = stack([piece[None] for piece in v.pop("pieces")])
    v["rows_other"] = swap(v["rows_own"])
    line_one = gather_line(v["singles"][2])
    v = tie(v)

    v["far_cross"] = sides(v["line_cross"])
    text_pieces, cot_pieces = v.pop("text_pieces"), v.pop("cot_pieces")
    v["text_near"] = [text_pieces[0], shift(text_pieces[1], 1), shift(text_pieces[3], 3)]
    v["text_two"], v["cot_two"] = text_pieces[2], shift(cot_pieces[2], 2)
    v["cot_near"] = [cot_pieces[0], cot_pieces[1], cot_pieces[3]]
    v["line_one"] = line_one
    v["w_self"], v["norms"], v["normed_one"], v["qkv"], v["self_mix"], v["self_lse"], v["mine"] = (
        fused_self_forward(place, v["rows_own"], v["rows_other"], v.pop("near"), v.pop("far_self"))
    )
    v = tie(v)

    v["theirs"] = swap(v["mine"])
    v["far_cross"] += corners(v["far_cross"], 2)
    line_two = gather_line(v.pop("singles")[3])
    text_near, text_two = v.pop("text_near"), shift(v.pop("text_two"), 2)
    text_pieces = [text_near[0], text_near[1], text_two, text_near[2]]
    v["text"] = arrange(place, text_pieces)
    ids = text_pieces[0][32, :128].astype(jnp.int32)
    v["caption"] = jnp.repeat(ids, 8)[None, :]
    v["ids"] = ids[:, None]
    v["one_low"], v["one_high"] = v["line_one"][:2], v["line_one"][2:]
    v = tie(v)

    low, high = v.pop("one_low"), v.pop("one_high")
    v["far_one"] = [across(low, 1), across(high, 1), across(v["line_one"], 2)]
    near, one_on, three_on = v.pop("cot_near")
    cot_pieces = [near, shift(one_on, 1), v.pop("cot_two"), shift(three_on, 3)]
    v["w_cross"], v["after_attn"], v["normed_two"], v["queries"], v["keys"], v["cross_mix"], v["cross_lse"], v["mine"] = (
        fused_cross_forward(
            place, v["rows_own"], v.pop("rows_other"), v["mine"], v["theirs"], v["norms"], v["text"], v["ids"],
            v["caption"], (v.pop("line_cross"), *v.pop("far_cross")),
        )
    )
    v["cot_own"] = join_pieces(place, cot_pieces)
    v["line_two"] = line_two
    v = tie(v)

    v["theirs"] = swap(v["mine"])
    v["far_one"] += [across(v["far_one"][0], 2), across(v["far_one"][2][2:], 1)]
    w_two = lax.all_gather(v.pop("line_two"), "chip")
    v["cot_other"] = swap(v["cot_own"])
    v = tie(v)

    v["w_two"] = w_two
    pieces = (v.pop("line_one"), *v.pop("far_one"))
    v["grads_one"], v["after_cross"], v["normed_three"], v["cot"], v["out_sum"], v["back_sum"] = feed_first(
        place, v["after_attn"], v["mine"], v["theirs"], v["norms"], v.pop("cot_own"), v.pop("cot_other"), pieces
    )
    v = tie(v)

    total_one = lax.psum_scatter(v.pop("grads_one"), "chip", scatter_dimension=0, tiled=False)
    *v["grads_two"], v["out_keep"], v["out_sent"], v["mine"] = feed_second(
        place, v.pop("normed_three"), v["cot"], v.pop("out_sum"), v.pop("back_sum"), v.pop("w_two")
    )
    v = tie(v)

    v["out_theirs"] = swap(v.pop("out_sent"))
    v = tie(v)
    v["theirs"] = swap(v["mine"])
    v["got_two"] = grad_corners(v["grads_two"])
    v["pieces"] = exchange(finish(place, v.pop("out_keep"), v.pop("out_theirs")))
    v["grad_cross"], v["part"], v["norms_three"], v["text_part"], *v["grads_three"] = fused_cross_backward(
        place, v.pop("after_cross"), v.pop("mine"), v.pop("theirs"), v.pop("cot"), v["norms"], v.pop("w_cross"),
        v.pop("normed_two"), v.pop("text"), v.pop("queries"), v.pop("keys"), v.pop("cross_mix"),
        v.pop("cross_lse"), v.pop("ids"), v.pop("caption"),
    )
    v = tie(v)

    v["theirs"] = swap(v["part"])
    v["total_one"] = total_one
    to_two = relay(v["grads_two"][2], v["grads_two"][1], *v.pop("got_two"))

    v["sides_two"] = [across(to_two[0], 2), across(to_two[1], 1)]
    v["got_three"] = grad_corners(v["grads_three"])
    v["line_one"] = lax.psum_scatter(v.pop("total_one"), "hi", scatter_dimension=0, tiled=False)
    v["grad_own"], v["low_grad"], v["norms_two"], v["dqkv"] = fused_self_backward(
        place, v.pop("after_attn"), v.pop("part"), v.pop("theirs"), v.pop("grad_cross"), v["norms"], v["w_self"],
        v.pop("qkv"), v["self_mix"], v.pop("self_lse"),
    )
    v = tie(v)

    v["sides_three"], sides_two = grad_sides(v["grads_three"], v.pop("got_three"), v.pop("sides_two"))
    total_two = plane_sum_whole(v.pop("grads_two")[0], *sides_two)
    line_two = lax.psum_scatter(total_two, "hi", scatter_dimension=0, tiled=True)
    v["grads_four"] = self_grads(place, v.pop("normed_one"), v.pop("low_grad"), v["dqkv"], v.pop("self_mix"))
    mine, sent = part_images(place, v.pop("pieces"))
    (v["result"],) = land(place, mine, swap(sent), BF)
    v["feed_one"] = halves(v.pop("line_one"))
    v = tie(v)

    v["got_four"] = grad_corners(v["grads_four"])
    total_three, dqkv = tie((plane_sum_whole(v.pop("grads_three")[0], *v.pop("sides_three")), v.pop("dqkv")))
    line_three = lax.psum_scatter(total_three, "hi", scatter_dimension=0, tiled=True)
    v["line_two"] = line_two
    v["kept"], v["sent"] = self_back(place, dqkv, v.pop("w_self"))
    v = tie(v)

    v["sides_four"], _ = grad_sides(v["grads_four"], v.pop("got_four"), place)
    pieces = last_norm(
        place, v.pop("rows_own"), v.pop("grad_own"), v.pop("kept"), swap(v.pop("sent")), v.pop("norms"),
        v.pop("text_part"), v.pop("norms_two"), v.pop("norms_three"),
    )
    input_pieces = exchange(pieces)
    v = tie(v)

    v["kept"], *sums_four = plane_sum(place, v.pop("grads_four")[0], *v.pop("sides_four"))
    v["line_four"] = [shift(piece, 3 - i) for i, piece in enumerate(sums_four)]
    v["feed_grads"] = spread_feed(place, *v.pop("feed_one"), *halves(v.pop("line_two")))
    later = tie((place, sums_four))[0]
    mine, sent = part_images(later, input_pieces)
    v["input_grad"], v["text_grad"], sums = land(place, mine, swap(sent), F32)
    sums = sums + across(sums, 1)
    sums = sums + across(sums, 2)
    v["sums"] = lax.dynamic_slice_in_dim(sums, (chip * 2 + core) * 128, 128, 1)
    v["cross_grads"] = spread(place, *halves(line_three))
    v = tie(v)

    kept, sent = line_sum(place, v.pop("kept"), v.pop("line_four"))
    own_grads = spread(place, kept, swap(sent))
    return (
        v["result"], v["input_grad"], v["text_grad"], *own_grads, *v["cross_grads"], *v["feed_grads"],
        *[v["sums"][i] for i in range(6)],
    )


def solution(mesh):
    fsdp, tensor = mesh.shape["fsdp"], mesh.shape["tensor"]

    def run(*args):
        images = args[0].shape[0] // fsdp
        tops = 2 * images
        shape = {"chip": fsdp // 2, "core": 2, "hi": tops, "lo": tensor // tops}
        fine = Mesh(mesh.devices.reshape(tuple(shape.values())), tuple(shape))
        first, second = ("chip", "core"), ("hi", "lo")
        wide, weight, norm = P(first, second, None), P(first, second), P(first)
        outs = (wide,) * 3 + (weight,) * 10 + (norm,) * 6
        packed = (
            (fsdp, tensor, images) == (8, 4, 2)
            and args[0].shape[1:] == (1024, 1024)
            and args[1].shape[1:] == (128, 1024)
            and args[12].shape == (1024, 4096)
        )
        return jax.shard_map(
            lambda *local: packed_layer(local) if packed else layer(shape, local),
            mesh=fine,
            in_specs=(wide, wide, P(first, None), wide) + (weight,) * 10 + (norm,) * 6,
            out_specs=outs,
            check_vma=False,
        )(*args)

    return run
```

```python
import functools
import math

import jax
import jax.numpy as jnp
from jax import lax
from jax.experimental import pallas as pl
from jax.experimental.pallas import tpu as pltpu
from jax.sharding import Mesh
from jax.sharding import PartitionSpec as P

HD = 64
EPS = 1e-05
NEG = -1e30
LOG2E = math.log2(math.e)
BF = jnp.bfloat16
F32 = jnp.float32
NT = (((1,), (1,)), ((), ()))
TN = (((0,), (0,)), ((), ()))
NN = (((1,), (0,)), ((), ()))


def dot(left, right, dims=NN):
    return lax.dot_general(left, right, dims, preferred_element_type=F32)


def lane_head(shape, axis, head):
    return lax.broadcasted_iota(jnp.int32, shape, axis) // HD == head


def self_forward_kernel(q_ref, k_ref, v_ref, mix_ref, lse_ref, *, block):
    length = q_ref.shape[0]
    scale = LOG2E * HD**-0.5
    causal = lax.broadcasted_iota(jnp.int32, (block, block), 0) <= lax.broadcasted_iota(
        jnp.int32, (block, block), 1
    )
    for at in range(length // block):
        lo, hi = at * block, (at + 1) * block
        query = q_ref[lo:hi, :]
        mixes = []
        for head in range(2):
            one = jnp.where(lane_head((1, 2 * HD), 1, head), query, jnp.zeros_like(query))
            diag = jnp.where(causal, dot(k_ref[lo:hi, :], one, NT), NEG)
            peak = jnp.max(diag, 0, keepdims=True)
            if at:
                past = dot(k_ref[:lo, :], one, NT)
                peak = jnp.maximum(peak, jnp.max(past, 0, keepdims=True))
            weights = jnp.exp2((diag - peak) * scale)
            total = jnp.sum(weights, 0, keepdims=True)
            mixed = dot(v_ref[lo:hi, :], weights.astype(BF), TN)
            if at:
                weights = jnp.exp2((past - peak) * scale)
                total = total + jnp.sum(weights, 0, keepdims=True)
                mixed = mixed + dot(v_ref[:lo, :], weights.astype(BF), TN)
            mixes.append(mixed / total)
            lse_ref[0, head : head + 1, lo:hi] = peak * scale + jnp.log2(total)
        both = jnp.where(lane_head((2 * HD, 1), 0, 0), mixes[0], mixes[1])
        mix_ref[lo:hi, :] = both.T.astype(BF)


def self_backward_kernel(
    q_ref, k_ref, v_ref, mix_ref, grad_ref, lse_ref, dq_ref, dk_ref, dv_ref, dk_sum, dv_sum, *, block
):
    length = q_ref.shape[0]
    scale = LOG2E * HD**-0.5
    causal = lax.broadcasted_iota(jnp.int32, (block, block), 0) <= lax.broadcasted_iota(
        jnp.int32, (block, block), 1
    )
    dk_sum[...] = jnp.zeros_like(dk_sum)
    dv_sum[...] = jnp.zeros_like(dv_sum)
    for at in range(length // block):
        lo, hi = at * block, (at + 1) * block
        query = q_ref[lo:hi, :]
        grad = grad_ref[lo:hi, :]
        product = (grad.astype(F32) * mix_ref[lo:hi, :].astype(F32)).T
        grads = []
        for head in range(2):
            picked = lane_head((1, 2 * HD), 1, head)
            one = jnp.where(picked, query, jnp.zeros_like(query))
            one_grad = jnp.where(picked, grad, jnp.zeros_like(grad))
            delta = jnp.sum(product[head * HD : (head + 1) * HD], 0, keepdims=True)
            lse = lse_ref[0, head : head + 1, lo:hi]
            total = jnp.zeros((2 * HD, block), F32)
            for start, stop in ((0, lo), (lo, hi)):
                if start == stop:
                    continue
                keys = k_ref[start:stop, :]
                weights = jnp.exp2(dot(keys, one, NT) * scale - lse)
                if start == lo:
                    weights = jnp.where(causal, weights, 0.0)
                slope = dot(v_ref[start:stop, :], one_grad, NT)
                score_grad = (weights * (slope - delta)).astype(BF)
                dv_sum[start:stop, :] += dot(weights.astype(BF), one_grad)
                dk_sum[start:stop, :] += dot(score_grad, one)
                total = total + dot(keys, score_grad, TN)
            grads.append(total)
        both = jnp.where(lane_head((2 * HD, 1), 0, 0), grads[0], grads[1])
        dq_ref[lo:hi, :] = (both.T * HD**-0.5).astype(BF)
    dk_ref[...] = (dk_sum[...] * HD**-0.5).astype(BF)
    dv_ref[...] = dv_sum[...].astype(BF)


def cross_forward_kernel(q_ref, k_ref, v_ref, ids_ref, caption_ref, mix_ref, lse_ref, *, block):
    length = q_ref.shape[0]
    scale = LOG2E * HD**-0.5
    for at in range(length // block):
        lo, hi = at * block, (at + 1) * block
        query = q_ref[lo:hi, :]
        seen = ids_ref[...] == caption_ref[:, lo:hi]
        mixes = []
        for head in range(2):
            one = jnp.where(lane_head((1, 2 * HD), 1, head), query, jnp.zeros_like(query))
            scores = jnp.where(seen, dot(k_ref[...], one, NT), NEG)
            peak = jnp.max(scores, 0, keepdims=True)
            weights = jnp.exp2((scores - peak) * scale)
            total = jnp.sum(weights, 0, keepdims=True)
            mixes.append(dot(v_ref[...], weights.astype(BF), TN) / total)
            lse_ref[0, head : head + 1, lo:hi] = peak * scale + jnp.log2(total)
        both = jnp.where(lane_head((2 * HD, 1), 0, 0), mixes[0], mixes[1])
        mix_ref[lo:hi, :] = both.T.astype(BF)


def cross_backward_kernel(
    q_ref, k_ref, v_ref, mix_ref, grad_ref, lse_ref, ids_ref, caption_ref, dq_ref, dk_ref, dv_ref, *, block
):
    length = q_ref.shape[0]
    scale = LOG2E * HD**-0.5
    keys, values = k_ref[...], v_ref[...]
    dk_sum = jnp.zeros(keys.shape, F32)
    dv_sum = jnp.zeros(keys.shape, F32)
    for at in range(length // block):
        lo, hi = at * block, (at + 1) * block
        query = q_ref[lo:hi, :]
        grad = grad_ref[lo:hi, :]
        product = (grad.astype(F32) * mix_ref[lo:hi, :].astype(F32)).T
        seen = ids_ref[...] == caption_ref[:, lo:hi]
        grads = []
        for head in range(2):
            picked = lane_head((1, 2 * HD), 1, head)
            one = jnp.where(picked, query, jnp.zeros_like(query))
            one_grad = jnp.where(picked, grad, jnp.zeros_like(grad))
            delta = jnp.sum(product[head * HD : (head + 1) * HD], 0, keepdims=True)
            lse = lse_ref[0, head : head + 1, lo:hi]
            weights = jnp.where(seen, jnp.exp2(dot(keys, one, NT) * scale - lse), 0.0)
            slope = dot(values, one_grad, NT)
            score_grad = (weights * (slope - delta)).astype(BF)
            dv_sum = dv_sum + dot(weights.astype(BF), one_grad)
            dk_sum = dk_sum + dot(score_grad, one)
            grads.append(dot(keys, score_grad, TN))
        both = jnp.where(lane_head((2 * HD, 1), 0, 0), grads[0], grads[1])
        dq_ref[lo:hi, :] = (both.T * HD**-0.5).astype(BF)
    dk_ref[...] = (dk_sum * HD**-0.5).astype(BF)
    dv_ref[...] = dv_sum.astype(BF)


def feed_kernel(
    rows_ref, cot_ref, win_ref, wout_ref, out_in, back_in, gin_ref, gout_ref, out_ref, back_ref, rows_t, cot_t, *, first
):
    step = pl.program_id(0)

    @pl.when(step == 0)
    def _():
        rows_t[...] = rows_ref[...].T
        cot_t[...] = cot_ref[...].T
        if first:
            out_ref[...] = jnp.zeros_like(out_ref)
            back_ref[...] = jnp.zeros_like(back_ref)
        else:
            out_ref[...] = out_in[...]
            back_ref[...] = back_in[...]

    pre = dot(rows_ref[...], win_ref[...])
    square = pre * pre
    slope = math.sqrt(2.0 / math.pi)
    bent = jnp.tanh(pre * (slope + slope * 0.044715 * square))
    half = 0.5 * (1.0 + bent)
    act = (pre * half).astype(BF)
    out_ref[...] += dot(act, wout_ref[...], NT)
    gout_ref[...] = dot(cot_t[...], act).astype(BF)
    bend = half + pre * (0.5 * (1.0 - bent * bent)) * (slope + 3.0 * slope * 0.044715 * square)
    pre_grad = (dot(cot_ref[...], wout_ref[...]) * bend).astype(BF)
    gin_ref[...] = dot(rows_t[...], pre_grad).astype(BF)
    back_ref[...] += dot(pre_grad, win_ref[...], NT)


VMEM_LIMIT = 60 * 1024 * 1024


def params():
    return pltpu.CompilerParams(vmem_limit_bytes=VMEM_LIMIT)


def column(rows, offset):
    return pl.BlockSpec((rows, 2 * HD), lambda i: (0, offset + i))


def self_forward(packed):
    length, width = packed.shape
    pairs = width // (6 * HD)
    return pl.pallas_call(
        functools.partial(self_forward_kernel, block=256),
        grid=(pairs,),
        in_specs=[column(length, 0), column(length, pairs), column(length, 2 * pairs)],
        out_specs=[column(length, 0), pl.BlockSpec((1, 2, length), lambda i: (i, 0, 0))],
        out_shape=[
            jax.ShapeDtypeStruct((length, pairs * 2 * HD), BF),
            jax.ShapeDtypeStruct((pairs, 2, length), F32),
        ],
        compiler_params=params(),
        cost_estimate=pl.CostEstimate(
            flops=8 * pairs * length * length * 2 * HD * 2,
            bytes_accessed=8 * pairs * length * 2 * HD,
            transcendentals=2 * pairs * length * length,
        ),
    )(packed, packed, packed)


def self_backward(packed, mix, grad, lse):
    length, width = packed.shape
    pairs = width // (6 * HD)
    part = jax.ShapeDtypeStruct((length, pairs * 2 * HD), BF)
    return pl.pallas_call(
        functools.partial(self_backward_kernel, block=256),
        grid=(pairs,),
        in_specs=[
            column(length, 0),
            column(length, pairs),
            column(length, 2 * pairs),
            column(length, 0),
            column(length, 0),
            pl.BlockSpec((1, 2, length), lambda i: (i, 0, 0)),
        ],
        out_specs=[column(length, 0)] * 3,
        out_shape=[part] * 3,
        scratch_shapes=[pltpu.VMEM((length, 2 * HD), F32)] * 2,
        compiler_params=params(),
        cost_estimate=pl.CostEstimate(
            flops=20 * pairs * length * length * 2 * HD * 2,
            bytes_accessed=16 * pairs * length * 2 * HD,
            transcendentals=2 * pairs * length * length,
        ),
    )(packed, packed, packed, mix, grad, lse)


def cross_forward(queries, keys, ids, captions):
    length, width = queries.shape
    texts = keys.shape[0]
    pairs = width // (2 * HD)
    return pl.pallas_call(
        functools.partial(cross_forward_kernel, block=min(512, length)),
        grid=(pairs,),
        in_specs=[
            column(length, 0),
            column(texts, 0),
            column(texts, pairs),
            pl.BlockSpec((texts, 1), lambda i: (0, 0)),
            pl.BlockSpec((1, length), lambda i: (0, 0)),
        ],
        out_specs=[column(length, 0), pl.BlockSpec((1, 2, length), lambda i: (i, 0, 0))],
        out_shape=[
            jax.ShapeDtypeStruct((length, width), BF),
            jax.ShapeDtypeStruct((pairs, 2, length), F32),
        ],
        compiler_params=params(),
    )(queries, keys, keys, ids, captions)


def cross_backward(queries, keys, mix, grad, lse, ids, captions):
    length, width = queries.shape
    texts = keys.shape[0]
    pairs = width // (2 * HD)
    return pl.pallas_call(
        functools.partial(cross_backward_kernel, block=min(512, length)),
        grid=(pairs,),
        in_specs=[
            column(length, 0),
            column(texts, 0),
            column(texts, pairs),
            column(length, 0),
            column(length, 0),
            pl.BlockSpec((1, 2, length), lambda i: (i, 0, 0)),
            pl.BlockSpec((texts, 1), lambda i: (0, 0)),
            pl.BlockSpec((1, length), lambda i: (0, 0)),
        ],
        out_specs=[column(length, 0), column(texts, 0), column(texts, 0)],
        out_shape=[
            jax.ShapeDtypeStruct((length, width), BF),
            jax.ShapeDtypeStruct((texts, width), BF),
            jax.ShapeDtypeStruct((texts, width), BF),
        ],
        compiler_params=params(),
    )(queries, keys, keys, mix, grad, lse, ids, captions)


def feed(rows, cot, w_in, w_out, sums):
    length, width = rows.shape
    units = w_in.shape[1]
    block = min(256, units)
    whole = pl.BlockSpec((length, width), lambda i: (0, 0))
    cut = pl.BlockSpec((width, block), lambda i: (0, i))
    first = sums is None
    kernel = functools.partial(feed_kernel, first=first)
    operands = [rows, cot, w_in, w_out]
    specs = [whole, whole, cut, cut]
    if first:
        body = lambda a, b, c, d, *rest: kernel(a, b, c, d, None, None, *rest)
    else:
        body = kernel
        operands += list(sums)
        specs += [whole, whole]
    total = jax.ShapeDtypeStruct((length, width), F32)
    part = jax.ShapeDtypeStruct((width, units), BF)
    return pl.pallas_call(
        body,
        grid=(units // block,),
        in_specs=specs,
        out_specs=[cut, cut, whole, whole],
        out_shape=[part, part, total, total],
        scratch_shapes=[pltpu.VMEM((width, length), BF)] * 2,
        compiler_params=params(),
        cost_estimate=pl.CostEstimate(
            flops=12 * length * width * units,
            bytes_accessed=8 * width * units + 8 * length * width,
            transcendentals=length * units,
        ),
    )(*operands)


def norm_parts(values):
    center = values - jnp.mean(values, -1, keepdims=True)
    inverse = lax.rsqrt(jnp.mean(center * center, -1, keepdims=True) + EPS)
    return center * inverse, inverse


def layer_norm(values, gain, offset):
    return (norm_parts(values)[0] * gain + offset).astype(BF)


def norm_back(values, gain, grad):
    hat, inverse = norm_parts(values)
    scaled = grad * gain
    back = inverse * (
        scaled
        - jnp.mean(scaled, -1, keepdims=True)
        - hat * jnp.mean(scaled * hat, -1, keepdims=True)
    )
    lead = tuple(range(values.ndim - 1))
    return back, jnp.sum(grad * hat, lead), jnp.sum(grad, lead)


def layer(shape, args):
    chips, tops, lows = shape["chip"], shape["hi"], shape["lo"]
    (
        image_rows,
        text_rows,
        segment_ids,
        cotangent,
        query_weight,
        key_weight,
        value_weight,
        attn_output,
        cross_query,
        cross_key,
        cross_value,
        cross_output,
        hidden_in,
        hidden_out,
        *norms,
    ) = args
    images, rows, width = image_rows.shape
    texts = text_rows.shape[1]
    half_rows = rows // 2
    length = rows * lows * tops
    shard = query_weight.shape[0]
    chip, core = lax.axis_index("chip"), lax.axis_index("core")
    top = lax.axis_index("hi")
    own_slot = core * images + top % images

    def swap(value):
        return lax.ppermute(value, "core", [(0, 1), (1, 0)])

    def across(value, bit):
        return lax.ppermute(value, "chip", [(i, i ^ bit) for i in range(chips)])

    def shift(value, step):
        return lax.ppermute(value, "hi", [((i + step) % tops, i) for i in range(tops)])

    def matching(number, back):
        pairs = []
        for source_core in range(2):
            for source_top in range(tops):
                slot = source_top ^ number
                target = (slot // images) * tops + source_core * images + slot % images
                source = source_core * tops + source_top
                pairs.append((target, source) if back else (source, target))
        return pairs

    def to_image(piece_of):
        got = [
            lax.ppermute(piece_of(top ^ number), ("core", "hi"), matching(number, False))
            for number in range(tops)
        ]
        whole = jnp.stack(got)
        return jnp.stack(
            [lax.dynamic_index_in_dim(whole, own_slot ^ place, 0, False) for place in range(tops)]
        )

    def from_image(pieces):
        return [
            lax.ppermute(
                lax.dynamic_index_in_dim(pieces, own_slot ^ number, 0, False),
                ("core", "hi"),
                matching(number, True),
            )
            for number in range(tops)
        ]

    def image_piece(value):
        def piece(slot):
            return lax.dynamic_slice(
                value,
                (slot % images, (slot // images) * half_rows, 0),
                (1, half_rows, width),
            )[0]

        return piece

    def to_rows(pieces):
        got = jnp.stack(from_image(pieces))
        ordered = jnp.stack(
            [lax.dynamic_index_in_dim(got, top ^ slot, 0, False) for slot in range(tops)]
        )
        ordered = ordered.reshape(2, images, half_rows, width)
        return jnp.swapaxes(ordered, 0, 1).reshape(images, rows, width)

    def tp_gather(mine):
        if lows == 1:
            other = swap(mine)
            first = jnp.where(core == 0, mine, other)
            second = jnp.where(core == 0, other, mine)
            return jnp.stack([first, second], 1).reshape(length, width)
        every = lax.all_gather(mine, ("lo", "core"))
        every = every.reshape(lows * 2, tops, half_rows, width)
        return jnp.swapaxes(every, 0, 1).reshape(length, width)

    def tp_reduce(partial):
        if lows == 1:
            cut = partial.reshape(tops, 2, half_rows, width)
            sent = lax.dynamic_index_in_dim(cut, 1 - core, 1, False).astype(BF)
            kept = lax.dynamic_index_in_dim(cut, core, 1, False)
            return kept + swap(sent).astype(F32)
        cut = jnp.swapaxes(partial.astype(BF).reshape(tops, lows * 2, half_rows, width), 0, 1)
        cut = lax.psum_scatter(cut, ("lo", "core"), scatter_dimension=0, tiled=False)
        return cut.astype(F32)

    def core_half(weight, which):
        columns = weight.shape[1] // 2
        return lax.dynamic_slice_in_dim(weight, which * columns, columns, 1)

    def pack(which):
        feeds = [core_half(weight, which) for weight in (hidden_in, hidden_out)]
        cuts = feeds[0].shape[1] // 2
        groups = [
            [core_half(w, which) for w in (query_weight, key_weight, value_weight, attn_output)],
            [core_half(w, which) for w in (cross_query, cross_key, cross_value, cross_output)],
            [w[:, :cuts] for w in feeds],
            [w[:, cuts:] for w in feeds],
        ]
        return jnp.concatenate([w for group in groups for w in group], 1)

    kept = pack(core)
    taken = swap(pack(1 - core))
    own = jnp.concatenate(
        [jnp.where(core == 0, kept, taken), jnp.where(core == 0, taken, kept)], 0
    )
    block_rows = 2 * shard
    group_width = own.shape[1] // 4

    def plane_gather(piece):
        if chips != 4:
            return lax.all_gather(piece, "chip", axis=0, tiled=True)
        side = across(piece, 1)
        over = across(piece, 2)
        corner_low = across(side[:shard], 2)
        corner_high = across(over[shard:], 1)
        corner = jnp.concatenate([corner_low, corner_high], 0)
        pieces = jnp.stack([piece, side, over, corner])
        ordered = [lax.dynamic_index_in_dim(pieces, chip ^ place, 0, False) for place in range(4)]
        return jnp.concatenate(ordered, 0)

    def plane_scatter(grads):
        if chips != 4:
            return lax.psum_scatter(grads, "chip", scatter_dimension=0, tiled=True).astype(F32)

        def rows_of(place, low, count):
            return lax.dynamic_slice_in_dim(grads, (chip ^ place) * block_rows + low, count, 0)

        by_side = across(rows_of(3, 0, shard), 1)
        by_over = across(rows_of(3, shard, shard), 2)
        to_over = jnp.concatenate(
            [rows_of(2, 0, shard).astype(F32) + by_side.astype(F32), rows_of(2, shard, shard).astype(F32)], 0
        ).astype(BF)
        to_side = jnp.concatenate(
            [rows_of(1, 0, shard).astype(F32), rows_of(1, shard, shard).astype(F32) + by_over.astype(F32)], 0
        ).astype(BF)
        over, side = across(to_over, 2), across(to_side, 1)
        return rows_of(0, 0, block_rows).astype(F32) + over.astype(F32) + side.astype(F32)

    def top_scatter(pieces):
        total = pieces[0].astype(F32)
        for step in range(1, tops):
            total = total + shift(pieces[step].astype(BF), tops - step).astype(F32)
        return total

    def core_split(total):
        cut = total.reshape(2, shard, total.shape[1])
        mine = lax.dynamic_index_in_dim(cut, core, 0, False)
        other = swap(lax.dynamic_index_in_dim(cut, 1 - core, 0, False).astype(BF)).astype(F32)
        return jnp.where(core == 0, mine, other), jnp.where(core == 0, other, mine)

    own_wide = plane_gather(own)

    def fetch(group, count):
        part = own[:, group * group_width : (group + 1) * group_width]
        columns = group_width // count
        got = [shift(part, step).reshape(block_rows, count, 1, columns) for step in range(1, tops)]
        rest = jnp.concatenate(got, 2).reshape(block_rows, (tops - 1) * group_width)
        rest = plane_gather(rest).reshape(width, count, (tops - 1) * columns)
        near = own_wide[:, group * group_width : (group + 1) * group_width]
        near = near.reshape(width, count, columns)
        return [
            jnp.concatenate([near[:, one], rest[:, one]], 1) for one in range(count)
        ]

    def give(grads):
        count = len(grads)
        columns = grads[0].shape[1] // tops
        summed = plane_scatter(jnp.concatenate(grads, 1)).reshape(block_rows, count, tops, columns)
        pieces = [summed[:, :, step].reshape(block_rows, count * columns) for step in range(tops)]
        low, high = core_split(top_scatter(pieces))
        low, high = low.reshape(shard, count, columns), high.reshape(shard, count, columns)
        return [(low[:, one], high[:, one]) for one in range(count)]

    packed_norms = lax.all_gather(jnp.stack(norms), ("chip", "core"), axis=1, tiled=True)
    gain_one, bias_one, gain_two, bias_two, gain_three, bias_three = packed_norms

    w_query, w_key, w_value, w_out = fetch(0, 4)
    inputs = to_image(image_piece(image_rows)).astype(F32)
    c_query, c_key, c_value, c_out = fetch(1, 4)
    in_low, out_low = fetch(2, 2)
    in_high, out_high = fetch(3, 2)

    text = to_image(lambda slot: text_rows[slot % images])
    if lows > 1:
        text = lax.all_gather(text, "lo", axis=1)
    text = text.reshape(tops * lows * texts, width)
    other_ids = swap(segment_ids)
    ids = jnp.where(core == top // images, segment_ids, other_ids)
    ids = lax.dynamic_index_in_dim(ids, top % images, 0, False)
    captions = jnp.repeat(ids, length // ids.shape[0])[None, :]
    ids = ids[:, None]
    cot = to_image(image_piece(cotangent))

    full_one = tp_gather(layer_norm(inputs, gain_one, bias_one))
    packed = dot(full_one, jnp.concatenate([w_query, w_key, w_value], 1)).astype(BF)
    self_mix, self_lse = self_forward(packed)
    after_attn = inputs + tp_reduce(dot(self_mix, w_out, NT))
    full_two = tp_gather(layer_norm(after_attn, gain_two, bias_two))
    queries = dot(full_two, c_query).astype(BF)
    w_text = jnp.concatenate([c_key, c_value], 1)
    keys = dot(text, w_text).astype(BF)
    cross_mix, cross_lse = cross_forward(queries, keys, ids, captions)
    after_cross = after_attn + tp_reduce(dot(cross_mix, c_out, NT))
    full_three = tp_gather(layer_norm(after_cross, gain_three, bias_three))
    full_cot = tp_gather(cot)
    gin_low, gout_low, *sums = feed(full_three, full_cot, in_low, out_low, None)
    gin_high, gout_high, out_sum, back_sum = feed(full_three, full_cot, in_high, out_high, sums)
    low_grads = give([gin_low, gout_low])
    high_grads = give([gin_high, gout_high])
    result = to_rows((after_cross + tp_reduce(out_sum)).astype(BF))

    back_three, dgain_three, dbias_three = norm_back(after_cross, gain_three, tp_reduce(back_sum))
    grad_cross = cot.astype(F32) + back_three
    full_grad = tp_gather(grad_cross.astype(BF))
    mix_grad = dot(full_grad, c_out).astype(BF)
    dq, dk, dv = cross_backward(queries, keys, cross_mix, mix_grad, cross_lse, ids, captions)
    back_sum = dot(dq, c_query, NT)
    dkv = jnp.concatenate([dk, dv], 1)
    cross_grads = give(
        [
            dot(full_two, dq, TN).astype(BF),
            dot(text, dk, TN).astype(BF),
            dot(text, dv, TN).astype(BF),
            dot(full_grad, cross_mix, TN).astype(BF),
        ]
    )
    text_part = dot(dkv, w_text, NT).astype(BF).reshape(tops, lows, texts, width)
    if lows > 1:
        text_part = lax.psum_scatter(text_part, "lo", scatter_dimension=1, tiled=True)
    got = [part.astype(F32) for part in from_image(text_part[:, 0])]
    got = jnp.stack(got)
    got = [lax.dynamic_index_in_dim(got, top ^ slot, 0, False) for slot in range(tops)]
    text_grad = jnp.stack([got[i] + got[images + i] for i in range(images)])

    back_two, dgain_two, dbias_two = norm_back(after_attn, gain_two, tp_reduce(back_sum))
    grad_attn = grad_cross + back_two
    full_grad = tp_gather(grad_attn.astype(BF))
    mix_grad = dot(full_grad, w_out).astype(BF)
    dq, dk, dv = self_backward(packed, self_mix, mix_grad, self_lse)
    dqkv = jnp.concatenate([dq, dk, dv], 1)
    dwqkv = dot(full_one, dqkv, TN).astype(BF)
    span = dq.shape[1]
    self_grads = give(
        [
            dwqkv[:, :span],
            dwqkv[:, span : 2 * span],
            dwqkv[:, 2 * span :],
            dot(full_grad, self_mix, TN).astype(BF),
        ]
    )
    back_sum = dot(dqkv, jnp.concatenate([w_query, w_key, w_value], 1), NT)
    back_one, dgain_one, dbias_one = norm_back(inputs, gain_one, tp_reduce(back_sum))
    input_grad = to_rows((grad_attn + back_one).astype(BF)).astype(F32)

    norm_sums = lax.psum(
        jnp.stack([dgain_one, dbias_one, dgain_two, dbias_two, dgain_three, dbias_three]),
        ("chip", "core", "hi", "lo"),
    )
    norm_sums = lax.dynamic_slice_in_dim(norm_sums, (chip * 2 + core) * shard, shard, 1)

    feeds = [
        jnp.concatenate([low_grads[i][0], high_grads[i][0], low_grads[i][1], high_grads[i][1]], 1)
        for i in range(2)
    ]
    joined = [jnp.concatenate(pair, 1) for pair in (*self_grads, *cross_grads)]
    return (result, input_grad, text_grad, *joined, *feeds, *[norm_sums[i] for i in range(6)])


BLOCK = 256
ANY = pl.BlockSpec(memory_space=pl.ANY)
HBM = pl.BlockSpec(memory_space=pltpu.HBM)
SMEM = pl.BlockSpec(memory_space=pltpu.SMEM)
VMEM = pl.BlockSpec(memory_space=pltpu.VMEM)
LATE, ROWS = object(), object()
MIB = 1024 * 1024


def like(*shape, dtype=BF):
    return jax.ShapeDtypeStruct(shape, dtype)


class Late:
    def __init__(self, source, target, sems, chunks=1):
        self.ref, self.rows, self.waited = target, target.shape[0] // chunks, [False] * chunks
        self.copies = []
        for i in range(chunks):
            part = slice(i * self.rows, (i + 1) * self.rows)
            self.copies.append(pltpu.make_async_copy(source.at[part], target.at[part], sems.at[i]))

    def start(self, chunk):
        self.copies[chunk].start()

    def need(self, row):
        chunk = row // self.rows
        if not self.waited[chunk]:
            self.copies[chunk].wait()
            self.waited[chunk] = True
        return self.ref

    def ready(self):
        for chunk in range(len(self.copies)):
            self.need(chunk * self.rows)
        return self.ref


def start_chunks(loads):
    for chunk in range(max((len(load.copies) for load in loads), default=0)):
        for load in loads:
            if chunk < len(load.copies):
                load.start(chunk)


class Early:
    def __init__(self, source, target, sem):
        self.ref, self.copy, self.sent = source, pltpu.make_async_copy(source, target, sem), False

    def send(self):
        self.copy.start()
        self.sent = True


def call_overlapped(body, outs, ins, operands, scratch=(), limit=60):
    late_ins = [i for i, spec in enumerate(ins) if spec in (LATE, ROWS)]
    late_outs = [i for i, (spec, _) in enumerate(outs) if spec is LATE]
    buffers = [pltpu.VMEM(operands[i].shape, operands[i].dtype) for i in late_ins]
    buffers += [pltpu.VMEM(outs[i][1].shape, outs[i][1].dtype) for i in late_outs]
    count = len(buffers)

    def wrapped(*refs):
        refs = list(refs)
        sems, load_sems = refs.pop(), refs.pop()
        extra = refs[len(refs) - count :]
        refs = refs[: len(refs) - count]
        loads = [
            Late(refs[i], extra[n], load_sems.at[n], 4 if ins[i] is ROWS else 1)
            for n, i in enumerate(late_ins)
        ]
        start_chunks([load for load in loads if len(load.copies) > 1])
        start_chunks([load for load in loads if len(load.copies) == 1])
        for load, i in zip(loads, late_ins):
            refs[i] = load
        stores = []
        for n, i in enumerate(late_outs):
            place = len(ins) + i
            stores.append(Early(extra[len(late_ins) + n], refs[place], sems.at[n]))
            refs[place] = stores[-1]
        body(*refs)
        for load in loads:
            load.ready()
        for store in stores:
            if not store.sent:
                store.send()
        for store in stores:
            store.copy.wait()

    return call(
        wrapped,
        [(HBM if spec is LATE else spec, shape) for spec, shape in outs],
        [ANY if spec in (LATE, ROWS) else spec for spec in ins],
        operands,
        [
            *scratch,
            *buffers,
            pltpu.SemaphoreType.DMA((max(len(late_ins), 1), 4)),
            pltpu.SemaphoreType.DMA((max(len(late_outs), 1),)),
        ],
        limit,
    )


def call(body, outs, ins, operands, scratch=(), limit=24, grid=None, flops=0, moved=0):
    single = not isinstance(outs, (list, tuple))
    extra = {} if grid is None else {"grid": grid}
    cost = pl.CostEstimate(flops=1, bytes_accessed=1, transcendentals=0)
    out_specs, out_shape = ([outs[0]], [outs[1]]) if single else ([o[0] for o in outs], [o[1] for o in outs])
    return list(pl.pallas_call(
        body,
        in_specs=ins,
        out_specs=out_specs,
        out_shape=out_shape,
        scratch_shapes=list(scratch),
        compiler_params=pltpu.CompilerParams(vmem_limit_bytes=limit * MIB),
        cost_estimate=cost,
        **extra,
    )(*operands))


def run_copies(copies, sems):
    started = [pltpu.make_async_copy(source, target, sems.at[i]) for i, (source, target) in enumerate(copies)]
    for copy in started:
        copy.start()
    for copy in started:
        copy.wait()


def at(offset, count, unit=128):
    return pl.ds(pl.multiple_of(offset, unit), count)


def prepare_kernel(place, norms, wq, wk, wv, wo, cq, ck, cv, co, win, wout, keep, sent, sems):
    core = place[1]
    copies = []
    for target, which in ((sent, 1 - core), (keep, core)):
        for group, weights in enumerate(((wq, wk, wv, wo), (cq, ck, cv, co))):
            for one, weight in enumerate(weights):
                copies.append(
                    (
                        weight.at[:, at(which * 128, 128)],
                        target.at[group * 128 : (group + 1) * 128, one * 128 : (one + 1) * 128],
                    )
                )
        for part in range(2):
            for one, weight in enumerate((win, wout)):
                copies.append(
                    (
                        weight.at[:, at(which * 512 + part * 256, 256)],
                        target.at[256 + part * 128 : 384 + part * 128, one * 256 : (one + 1) * 256],
                    )
                )
        rows = jnp.concatenate([norms[...], jnp.zeros((10, 128), F32)], 0).astype(BF)
        target[512:528, :] = jnp.concatenate([rows] * 4, 1)
    run_copies(copies, sems)


def prepare(place, norms, weights):
    return call(
        prepare_kernel,
        [(VMEM, like(528, 512))] * 2,
        [SMEM, VMEM] + [ANY] * 10,
        (place, norms, *weights),
        [pltpu.SemaphoreType.DMA((24,))],
    )


def prepare_rows_kernel(place, ids, image, text, cot, *outs):
    rows_keep, rows_sent, cot_keep, cot_sent, text_pair, sems = outs
    core = place[1]
    copies = []
    for target, cots, which in ((rows_sent, cot_sent, 1 - core), (rows_keep, cot_keep, core)):
        for one in range(2):
            copies.append((image.at[one, at(which * 128, 128), :], target.at[one]))
            copies.append((cot.at[one, at(which * 128, 128), :], cots.at[one]))
    for one in range(2):
        copies.append((text.at[one], text_pair.at[one, 0:32, :]))
        row = jnp.concatenate([ids[one : one + 1, :].astype(F32), jnp.zeros((1, 896), F32)], 1)
        text_pair[one, 32:48, :] = jnp.concatenate([row] * 16, 0).astype(BF)
    run_copies(copies, sems)


def prepare_rows(place, ids, image, text, cot):
    return call(
        prepare_rows_kernel,
        [(VMEM, like(2, 128, 1024))] * 4 + [(VMEM, like(2, 48, 1024))],
        [SMEM, VMEM] + [ANY] * 3,
        (place, ids, image, text, cot),
        [pltpu.SemaphoreType.DMA((10,))],
    )


def pick_kernel(place, keep, taken, *outs):
    core, top = place[1], place[2]
    for step, out in enumerate(outs):
        image = (top + 4 - step) % 4

        @pl.when(image // 2 == core)
        def _():
            out[...] = keep[image % 2]

        @pl.when(image // 2 != core)
        def _():
            out[...] = taken[image % 2]


def pick(place, keep, taken):
    return call(
        pick_kernel,
        [(VMEM, like(*keep.shape[1:]))] * 4,
        [SMEM, VMEM, VMEM],
        (place, keep, taken),
    )


def join_kernel(place, keep, taken, *refs):
    singles, near, sems = refs[:4], refs[4], refs[5]
    copies = []
    for half, source in enumerate((keep, taken)):
        core = place[1] ^ half
        for group in range(4):
            part = source.at[group * 128 : (group + 1) * 128, :]
            copies.append((part, singles[group].at[at(core * 128, 128), :]))
        copies.append((source.at[0:128, :], near.at[at(core * 128, 128), :]))
        copies.append((source.at[512:528, :], near.at[at(256 + core * 16, 16, 16), :]))
    run_copies(copies, sems)


def join(place, keep, taken):
    return call(
        join_kernel,
        [(VMEM, like(256, 512))] * 4 + [(VMEM, like(288, 512))],
        [SMEM] + [ANY] * 2,
        (place, keep, taken),
        [pltpu.SemaphoreType.DMA((12,))],
    )


def stack_kernel(*refs):
    *parts, whole, sems = refs
    copies, low = [], 0
    for part in parts:
        copies.append((part, whole.at[low : low + part.shape[0]]))
        low += part.shape[0]
    run_copies(copies, sems)


def stack(parts):
    rows = sum(part.shape[0] for part in parts)
    return call(
        stack_kernel,
        [(VMEM, like(rows, *parts[0].shape[1:]))],
        [ANY] * len(parts),
        parts,
        [pltpu.SemaphoreType.DMA((len(parts),))],
    )[0]


def join_pieces_kernel(place, *refs):
    pieces, whole, sems = refs[:4], refs[4], refs[5]
    run_copies([(piece, whole.at[i]) for i, piece in enumerate(pieces)], sems)


def join_pieces(place, pieces):
    return call(
        join_pieces_kernel,
        [(VMEM, like(4, *pieces[0].shape))],
        [SMEM] + [ANY] * 4,
        (place, *pieces),
        [pltpu.SemaphoreType.DMA((4,))],
    )[0]


def arrange_kernel(place, *refs):
    messages, text, sems = refs[:4], refs[4], refs[5]
    run_copies(
        [(m.at[0:32, :], text.at[at((place[2] + i) % 4 * 32, 32, 32), :]) for i, m in enumerate(messages)], sems
    )


def arrange(place, messages):
    return call(
        arrange_kernel,
        [(VMEM, like(128, 1024))],
        [SMEM] + [ANY] * 4,
        (place, *messages),
        [pltpu.SemaphoreType.DMA((4,))],
    )[0]


def started(pairs, sems):
    copies = [pltpu.make_async_copy(source, target, sems.at[i]) for i, (source, target) in enumerate(pairs)]
    for copy in copies:
        copy.start()
    return copies


def wait_all(copies):
    for copy in copies:
        copy.wait()


def first_pieces(place, near, far, buffer, norms):
    chip, top = place[0], place[2]
    weights, rows = [], []
    for source in range(4):
        for half in range(2):
            row = at((chip ^ source) * 256 + half * 128, 128)
            piece, first = (near[source], half * 128) if source < 3 else (near[3 + half], 0)
            weights.append((piece.at[first : first + 128, :], buffer.at[row, at(top * 512, 512, 512)]))
            low = 256 + half * 16 if source < 3 else 128 + half * 16
            piece = near[source] if source < 3 else near[4]
            column = at((chip ^ source) * 256 + half * 128, 128)
            rows.append((piece.at[low : low + 16, 0:128], norms.at[:, column]))
            for step in range(3):
                first = step * 256 + half * 128
                piece = far[source] if source < 3 else far[3 + first // 384]
                first = first if source < 3 else first % 384
                columns = at((top + 1 + step) % 4 * 512, 512, 512)
                weights.append((piece.at[first : first + 128, :], buffer.at[row, columns]))
    return weights, rows


def later_pieces(place, pieces, buffer):
    groups = (pieces[:1], pieces[1:-3], pieces[-3:-2], pieces[-2:])
    chip = place[0]
    weights = []
    for source, parts in enumerate(groups):
        for top in range(4):
            part, each = parts[top * len(parts) // 4], 4 // len(parts)
            rows, columns = at((chip ^ source) * 256, 256), slice(top * 512, (top + 1) * 512)
            weights.append((part.at[top % each], buffer.at[rows, columns]))
    return weights


def norm_row(norms, one):
    return norms[one : one + 1, :].astype(F32)


def normalized(values, gain, bias):
    center = values - jnp.mean(values, -1, keepdims=True)
    inverse = lax.rsqrt(jnp.mean(center * center, -1, keepdims=True) + EPS)
    return (center * inverse * gain + bias).astype(BF)


def columns_of(weights, one, count=128):
    return jnp.concatenate([weights[:, s * 512 + one * count : s * 512 + (one + 1) * count] for s in range(4)], 1)


def project_into(target, rows, weights, dims=NN, step=512):
    count = weights.shape[0] if dims == NT else weights.shape[1]
    for low in range(0, count, step):
        part = weights[low : low + step, :] if dims == NT else weights[:, low : low + step]
        target[:, low : low + step] = dot(rows, part, dims).astype(target.dtype)


def image_blocks(place, own, other):
    core, top = place[1], place[2]
    for number in range(4):
        yield (top + number) % 4 * 256 + core * 128, own, number
        yield (top + number) % 4 * 256 + (1 - core) * 128, other, number


def one_head(values, head):
    return jnp.where(lane_head((1, 2 * HD), 1, head), values, jnp.zeros_like(values))


def both_heads(values):
    return jnp.concatenate([one_head(values, 0), one_head(values, 1)], 0)


def pick_heads(values):
    count = values.shape[1] // 2
    return jnp.where(lane_head((128, 1), 0, 0), values[:, :count], values[:, count:]).T


def causal_pair(count):
    rows = lax.broadcasted_iota(jnp.int32, (count, 2 * count), 0)
    columns = lax.broadcasted_iota(jnp.int32, (count, 2 * count), 1)
    return rows <= jnp.where(columns >= count, columns - count, columns)


def twice(row):
    return jnp.concatenate([row, row], 1)


def softmax_mix(scores, values):
    scale = LOG2E * HD**-0.5
    peak = jnp.max(scores[0], 0, keepdims=True)
    for part in scores[1:]:
        peak = jnp.maximum(peak, jnp.max(part, 0, keepdims=True))
    total, mixed = 0.0, 0.0
    for part, rows in zip(scores, values):
        weights = jnp.exp2((part - peak) * scale)
        total = total + jnp.sum(weights, 0, keepdims=True)
        mixed = mixed + dot(rows, weights.astype(BF), TN)
    return mixed / total, peak * scale + jnp.log2(total)


def causal_mask():
    return lax.broadcasted_iota(jnp.int32, (BLOCK, BLOCK), 0) <= lax.broadcasted_iota(
        jnp.int32, (BLOCK, BLOCK), 1
    )


def self_fwd_kernel(place, own, other, *refs):
    near, far = refs[:5], refs[5:10]
    whole, norms, normed, qkv, mix, lse, part, weights, loads, store = refs[10:]
    pieces, rows = first_pieces(place, near, far, weights, norms)
    copies = started(rows + pieces, loads)
    wait_all(copies[: len(rows)])
    gain, bias = norm_row(norms, 0), norm_row(norms, 1)
    for row, half, number in image_blocks(place, own, other):
        normed[at(row, 128), :] = normalized(half[number].astype(F32), gain, bias)
    wait_all(copies[len(rows) :])
    (stored,) = started([(weights, whole)], store)
    for one in range(3):
        qkv[:, one * 512 : (one + 1) * 512] = dot(normed[...], columns_of(weights, one)).astype(BF)
    causal = causal_pair(512)

    def pair_step(pair, carry):
        lanes = at(pair * 128, 128)
        k_lanes, v_lanes = at(512 + pair * 128, 128), at(1024 + pair * 128, 128)
        for low in range(0, 1024, 512):
            high = low + 512
            both = both_heads(qkv[low:high, lanes])
            scores = [jnp.where(causal, dot(qkv[low:high, k_lanes], both, NT), NEG)]
            values = [qkv[low:high, v_lanes]]
            if low:
                scores.append(dot(qkv[:low, k_lanes], both, NT))
                values.append(qkv[:low, v_lanes])
            mixed, logsum = softmax_mix(scores, values)
            for head in range(2):
                lse[pair, head : head + 1, low:high] = logsum[:, head * 512 : (head + 1) * 512]
            mix[low:high, lanes] = pick_heads(mixed).astype(BF)
        return carry

    lax.fori_loop(0, 4, pair_step, 0)
    project_into(part, mix[...], columns_of(weights, 3), NT)
    stored.wait()


def fused_self_forward(place, own, other, near, far):
    return call(
        self_fwd_kernel,
        [
            (HBM, like(1024, 2048)),
            (VMEM, like(16, 1024)),
            (VMEM, like(1024, 1024)),
            (VMEM, like(1024, 1536)),
            (VMEM, like(1024, 512)),
            (VMEM, like(4, 2, 1024, dtype=F32)),
            (VMEM, like(1024, 1024)),
        ],
        [SMEM, VMEM, VMEM] + [ANY] * 10,
        (place, own, other, *near, *far),
        [pltpu.VMEM((1024, 2048), BF), pltpu.SemaphoreType.DMA((40,)), pltpu.SemaphoreType.DMA((1,))],
        limit=60,
    )


def cross_fwd_kernel(
    place, own, other, mine_in, theirs_in, norms, text, ids, caption, *refs
):
    pieces = refs[:5]
    whole, after, normed, queries, keys, mix, lse, part, weights, mine, theirs, loads, store, row_sems = refs[5:]
    late = [
        Late(source, target, row_sems.at[i], 4)
        for i, (source, target) in enumerate(((mine_in, mine), (theirs_in, theirs)))
    ]
    start_chunks(late)
    copies = started(later_pieces(place, pieces, weights), loads)
    gain, bias = norm_row(norms, 2), norm_row(norms, 3)
    core, top = place[1], place[2]
    for block in range(4):
        for load in late:
            load.need(block * 256)
        for half, which in ((own, core), (other, 1 - core)):
            rows = at(block * 256 + which * 128, 128)
            values = half[(block + 4 - top) % 4].astype(F32)
            values = values + (mine[rows, :].astype(F32) + theirs[rows, :].astype(F32))
            after[rows, :] = values
            normed[rows, :] = normalized(values, gain, bias)
    wait_all(copies)
    (stored,) = started([(weights, whole)], store)
    project_into(queries, normed[...], columns_of(weights, 0))
    w_text = jnp.concatenate([columns_of(weights, 1), columns_of(weights, 2)], 1)
    keys[...] = dot(text[...], w_text).astype(BF)

    def pair_step(pair, carry):
        lanes, v_lanes = at(pair * 128, 128), at(512 + pair * 128, 128)
        seen = twice(ids[...] == caption[...])
        scores = jnp.where(seen, dot(keys[:, lanes], both_heads(queries[:, lanes]), NT), NEG)
        mixed, logsum = softmax_mix([scores], [keys[:, v_lanes]])
        for head in range(2):
            lse[pair, head : head + 1, :] = logsum[:, head * 1024 : (head + 1) * 1024]
        mix[:, lanes] = pick_heads(mixed).astype(BF)
        return carry

    lax.fori_loop(0, 4, pair_step, 0)
    project_into(part, mix[...], columns_of(weights, 3), NT)
    stored.wait()


def fused_cross_forward(place, own, other, mine, theirs, norms, text, ids, caption, pieces):
    return call(
        cross_fwd_kernel,
        [
            (HBM, like(1024, 2048)),
            (VMEM, like(1024, 1024, dtype=F32)),
            (VMEM, like(1024, 1024)),
            (VMEM, like(1024, 512)),
            (VMEM, like(128, 1024)),
            (VMEM, like(1024, 512)),
            (VMEM, like(4, 2, 1024, dtype=F32)),
            (VMEM, like(1024, 1024)),
        ],
        [SMEM, VMEM, VMEM, ANY, ANY] + [VMEM] * 4 + [ANY] * 5,
        (place, own, other, mine, theirs, norms, text, ids, caption, *pieces),
        [pltpu.VMEM((1024, 2048), BF)]
        + [pltpu.VMEM((1024, 1024), BF)] * 2
        + [pltpu.SemaphoreType.DMA((16,)), pltpu.SemaphoreType.DMA((1,)), pltpu.SemaphoreType.DMA((2, 4))],
        limit=60,
    )


def cut_grads(place, grads, columns, own, side, over, low, high):
    chip = place[0]
    own[:, columns] = grads[at(chip * 256, 256), :].astype(BF)
    side[:, columns] = grads[at((chip ^ 1) * 256, 256), :].astype(BF)
    over[:, columns] = grads[at((chip ^ 2) * 256, 256), :].astype(BF)
    low[:, columns] = grads[at((chip ^ 3) * 256, 128), :].astype(BF)
    high[:, columns] = grads[at((chip ^ 3) * 256 + 128, 128), :].astype(BF)


GRAD_SHAPES = [(256, 2048)] * 3 + [(128, 2048)] * 2


def feed_step(rows, cot, rows_t, cot_t, weights, out_sum, back_sum, grads):
    w_in = jnp.concatenate([weights[0][:, :256], weights[1][:, :256]], 1)
    w_out = jnp.concatenate([weights[0][:, 256:], weights[1][:, 256:]], 1)
    slope = math.sqrt(2.0 / math.pi)
    pre = dot(rows[...], w_in)
    square = pre * pre
    bent = jnp.tanh(pre * (slope + slope * 0.044715 * square))
    half = 0.5 * (1.0 + bent)
    act = (pre * half).astype(BF)
    bend = half + pre * (0.5 * (1.0 - bent * bent)) * (slope + 3.0 * slope * 0.044715 * square)
    pre_grad = (dot(cot[...], w_out) * bend).astype(BF)
    for low in range(0, 1024, 512):
        part = slice(low, low + 512)
        out_sum[:, part] += dot(act, w_out[part, :], NT)
        back_sum[:, part] += dot(pre_grad, w_in[part, :], NT)
    for block in range(2):
        part = slice(block * 256, (block + 1) * 256)
        grads[:, block * 512 : block * 512 + 256] = dot(rows_t[...], pre_grad[:, part])
        grads[:, block * 512 + 256 : (block + 1) * 512] = dot(cot_t[...], act[:, part])


def feed_first_kernel(
    place, after_in, mine_in, theirs_in, norms, cot_own, cot_other, *refs
):
    pieces = refs[:6]
    g_whole, after_out, normed_out, cot_out, out_sum, back = refs[6:12]
    after_cross, normed, cot, back_sum, rows_t, cot_t, grads, weights, after, mine, theirs, sems, loads, row_sems = refs[12:]
    step = pl.program_id(0)
    pairs = ((after_cross, after_out), (normed, normed_out), (cot, cot_out))
    stores = [pltpu.make_async_copy(a, b, sems.at[i]) for i, (a, b) in enumerate(pairs)]

    @pl.when(step == 0)
    def _():
        arrays = ((after_in, after), (mine_in, mine), (theirs_in, theirs))
        late = [Late(source, target, row_sems.at[i], 4) for i, (source, target) in enumerate(arrays)]
        start_chunks(late)
        copies = started(later_pieces(place, pieces, weights), loads)
        gain, bias = norm_row(norms, 4), norm_row(norms, 5)
        for low in range(0, 1024, 128):
            for load in late:
                load.need(low)
            rows = slice(low, low + 128)
            values = after[rows, :] + (mine[rows, :].astype(F32) + theirs[rows, :].astype(F32))
            after_cross[rows, :] = values
            normed[rows, :] = normalized(values, gain, bias)
        for row, half, number in image_blocks(place, cot_own, cot_other):
            cot[at(row, 128), :] = half[number]
        for store in stores:
            store.start()
        rows_t[...] = normed[...].T
        cot_t[...] = cot[...].T
        out_sum[...] = jnp.zeros_like(out_sum)
        for block in range(4):
            rows = at(block * 256 + place[1] * 128, 128)
            out_sum[rows, :] = after_cross[rows, :]
        back_sum[...] = jnp.zeros_like(back_sum)
        wait_all(copies)

    blocks = [weights[:, at(step * 1024 + block * 512, 512, 512)] for block in range(2)]
    feed_step(normed, cot, rows_t, cot_t, blocks, out_sum, back_sum, grads)
    for chip in range(4):
        for block in range(2):
            part = grads[chip * 256 : (chip + 1) * 256, block * 512 : (block + 1) * 512]
            g_whole[chip, block] = part.astype(BF)

    @pl.when(step == 1)
    def _():
        back[...] = back_sum[...].astype(BF)
        for store in stores:
            store.wait()


def feed_second_kernel(
    place, normed, cot, out_in, back_in, weights,
    g_own, g_side, g_over, g_low, g_high, out_keep, out_sent, back, out_sum, back_sum, rows_t, cot_t, grads,
):
    step, core = pl.program_id(0), place[1]

    @pl.when(step == 0)
    def _():
        rows_t[...] = normed[...].T
        cot_t[...] = cot[...].T
        out_sum[...] = out_in[...]
        back_sum[...] = back_in[...].astype(F32)

    blocks = [weights[:, block].reshape(1024, 512) for block in range(2)]
    feed_step(normed, cot, rows_t, cot_t, blocks, out_sum, back_sum, grads)
    cut_grads(place, grads, slice(None), g_own, g_side, g_over, g_low, g_high)

    @pl.when(step == 1)
    def _():
        back[...] = back_sum[...].astype(BF)
        for block in range(4):
            out_keep[block] = out_sum[at(block * 256 + core * 128, 128), :]
            out_sent[block] = out_sum[at(block * 256 + (1 - core) * 128, 128), :].astype(BF)


def once(*shape):
    zeros = (0,) * len(shape)
    return pl.BlockSpec(shape, lambda i: zeros, pipeline_mode=pl.Buffered(1))


def grad_outs(width=512):
    return [(pl.BlockSpec((rows, width), lambda i: (0, i)), like(rows, n)) for rows, n in GRAD_SHAPES]


FEED_FLOPS = 13 * 2**30


def feed_first(place, after, mine, theirs, norms, cot_own, cot_other, pieces):
    square = once(1024, 1024)
    return call(
        feed_first_kernel,
        [(pl.BlockSpec((4, 2, 256, 512), lambda i: (0, i, 0, 0)), like(4, 4, 256, 512))]
        + [
            (HBM, like(1024, 1024, dtype=F32)),
            (HBM, like(1024, 1024)),
            (HBM, like(1024, 1024)),
            (square, like(1024, 1024, dtype=F32)),
            (square, like(1024, 1024)),
        ],
        [SMEM, ANY, ANY, ANY, once(16, 1024), once(4, 128, 1024), once(4, 128, 1024)]
        + [ANY] * 6,
        (place, after, mine, theirs, norms, cot_own, cot_other, *pieces),
        [pltpu.VMEM((1024, 1024), F32)]
        + [pltpu.VMEM((1024, 1024), BF)] * 2
        + [pltpu.VMEM((1024, 1024), F32)]
        + [pltpu.VMEM((1024, 1024), BF)] * 2
        + [pltpu.VMEM((1024, 1024), F32), pltpu.VMEM((1024, 2048), BF)]
        + [pltpu.VMEM((1024, 1024), F32), pltpu.VMEM((1024, 1024), BF), pltpu.VMEM((1024, 1024), BF)]
        + [pltpu.SemaphoreType.DMA((3,)), pltpu.SemaphoreType.DMA((16,)), pltpu.SemaphoreType.DMA((3, 4))],
        grid=(2,),
        flops=FEED_FLOPS,
        moved=30 * MIB,
        limit=60,
    )


def feed_second(place, normed, cot, out_in, back_in, weights):
    square = once(1024, 1024)
    return call(
        feed_second_kernel,
        grad_outs(1024)
        + [
            (once(4, 128, 1024), like(4, 128, 1024, dtype=F32)),
            (once(4, 128, 1024), like(4, 128, 1024)),
            (square, like(1024, 1024)),
        ],
        [SMEM, square, square, square, square, pl.BlockSpec((4, 2, 256, 512), lambda i: (0, i, 0, 0))],
        (place, normed, cot, out_in, back_in, weights),
        [pltpu.VMEM((1024, 1024), F32)] * 2
        + [pltpu.VMEM((1024, 1024), BF)] * 2
        + [pltpu.VMEM((1024, 1024), F32)],
        grid=(2,),
        flops=FEED_FLOPS,
        moved=26 * MIB,
        limit=60,
    )


def norm_backward(values, gain, grad):
    center = values - jnp.mean(values, -1, keepdims=True)
    inverse = lax.rsqrt(jnp.mean(center * center, -1, keepdims=True) + EPS)
    hat = center * inverse
    scaled = grad * gain
    back = inverse * (
        scaled - jnp.mean(scaled, -1, keepdims=True) - hat * jnp.mean(scaled * hat, -1, keepdims=True)
    )
    return back, grad * hat


def norm_block(values_of, mine, theirs, base_of, gain, norms, keep):
    gain = norm_row(*gain)
    gain_sum, bias_sum = jnp.zeros((8, 1024), F32), jnp.zeros((8, 1024), F32)
    for low in range(0, 1024, 128):
        rows = slice(low, low + 128)
        grad = mine.need(low)[rows, :].astype(F32) + theirs.need(low)[rows, :].astype(F32)
        back, term = norm_backward(values_of(rows), gain, grad)
        keep(rows, base_of(rows) + back)
        gain_sum = gain_sum + jnp.sum(term.reshape(16, 8, 1024), 0)
        bias_sum = bias_sum + jnp.sum(grad.reshape(16, 8, 1024), 0)
    norms[0:1, :] = jnp.sum(gain_sum, 0, keepdims=True)
    norms[1:2, :] = jnp.sum(bias_sum, 0, keepdims=True)


def pair_row(lse, pair, low, high):
    return jnp.concatenate([lse[pair, 0:1, low:high], lse[pair, 1:2, low:high]], 1)


def pair_delta(grad, mix):
    product = (grad.astype(F32) * mix.astype(F32)).T
    return jnp.concatenate([jnp.sum(product[:HD], 0, keepdims=True), jnp.sum(product[HD:], 0, keepdims=True)], 1)


def head_grads(keys, values, one, one_grad, lse, delta, mask):
    weights = jnp.exp2(dot(keys, one, NT) * (LOG2E * HD**-0.5) - lse)
    if mask is not None:
        weights = jnp.where(mask, weights, 0.0)
    slope = dot(values, one_grad, NT)
    return weights.astype(BF), (weights * (slope - delta)).astype(BF)


def cross_bwd_kernel(
    place, after, mine, theirs, cot, gain, weights, normed, text, queries, keys, mix, lse, ids, caption,
    grad_out, part_out, norms, text_part, g_own, g_side, g_over, g_low, g_high, low_grad, mix_grad, dq, dkv, grads,
):
    grad_cross, part = grad_out.ref, part_out.ref

    def keep(rows, value):
        grad_cross[rows, :] = value
        low_grad[rows, :] = value.astype(BF)

    norm_block(lambda rows: after.need(rows.start)[rows, :], mine, theirs, lambda rows: cot.need(rows.start)[rows, :].astype(F32), (gain, 4), norms, keep)
    grad_out.send()
    weights, queries, keys, mix = weights.ready(), queries.ready(), keys.ready(), mix.ready()
    project_into(mix_grad, low_grad[...], columns_of(weights, 3))

    def pair_step(pair, carry):
        lanes, v_lanes = at(pair * 128, 128), at(512 + pair * 128, 128)
        query, grad = both_heads(queries[:, lanes]), both_heads(mix_grad[:, lanes])
        prob, score_grad = head_grads(
            keys[:, lanes],
            keys[:, v_lanes],
            query,
            grad,
            pair_row(lse, pair, 0, 1024),
            pair_delta(mix_grad[:, lanes], mix[:, lanes]),
            twice(ids[...] == caption[...]),
        )
        dv_sum, dk_sum = dot(prob, grad), dot(score_grad, query)
        dq[:, lanes] = (pick_heads(dot(keys[:, lanes], score_grad, TN)) * HD**-0.5).astype(BF)
        dkv[:, lanes] = (dk_sum * HD**-0.5).astype(BF)
        dkv[:, v_lanes] = dv_sum.astype(BF)
        return carry

    lax.fori_loop(0, 4, pair_step, 0)
    project_into(part, dq[...], columns_of(weights, 0), NT)
    part_out.send()
    normed = normed.ready()
    w_text = jnp.concatenate([columns_of(weights, 1), columns_of(weights, 2)], 1)
    text_part[...] = dot(dkv[...], w_text, NT).astype(BF)
    for one, (left, right) in enumerate(
        ((normed, dq[...]), (text, dkv[:, :512]), (text, dkv[:, 512:]), (low_grad, mix[...]))
    ):
        grads[...] = dot(left[...], right, TN)
        for s in range(4):
            columns = slice(s * 512 + one * 128, s * 512 + (one + 1) * 128)
            cut_grads(
                place, grads.at[:, s * 128 : (s + 1) * 128], columns, g_own, g_side, g_over, g_low, g_high
            )


def fused_cross_backward(place, after, mine, theirs, cot, gain, weights, normed, text, queries, keys, mix, lse, ids, caption):
    return call_overlapped(
        cross_bwd_kernel,
        [
            (LATE, like(1024, 1024, dtype=F32)),
            (LATE, like(1024, 1024)),
            (VMEM, like(8, 1024, dtype=F32)),
            (VMEM, like(128, 1024)),
        ]
        + [(VMEM, like(*shape)) for shape in GRAD_SHAPES],
        [SMEM] + [ROWS] * 4 + [VMEM] + [LATE, LATE, VMEM, LATE, LATE, LATE, VMEM, VMEM, VMEM],
        (place, after, mine, theirs, cot, gain, weights, normed, text, queries, keys, mix, lse, ids, caption),
        [
            pltpu.VMEM((1024, 1024), BF),
            pltpu.VMEM((1024, 512), BF),
            pltpu.VMEM((1024, 512), BF),
            pltpu.VMEM((128, 1024), BF),
            pltpu.VMEM((1024, 512), F32),
        ],
    )


def self_bwd_kernel(
    place, after, mine, theirs, base, gain, weights, qkv, mix, lse,
    grad_out, low_out, norms, dqkv, mix_grad, dk_sum, dv_sum,
):
    core = place[1]
    grad_own, low_grad = grad_out.ref, low_out.ref

    def keep(rows, value):
        low_grad[rows, :] = value.astype(BF)

        @pl.when(core == (rows.start // 128) % 2)
        def _():
            grad_own[rows.start // 256] = value

    norm_block(lambda rows: after.need(rows.start)[rows, :], mine, theirs, lambda rows: base.need(rows.start)[rows, :], (gain, 2), norms, keep)
    grad_out.send()
    low_out.send()
    weights, qkv, mix = weights.ready(), qkv.ready(), mix.ready()
    project_into(mix_grad, low_grad[...], columns_of(weights, 3))
    causal = causal_pair(512)

    def pair_step(pair, carry):
        lanes = at(pair * 128, 128)
        k_lanes, v_lanes = at(512 + pair * 128, 128), at(1024 + pair * 128, 128)
        for low in range(0, 1024, 512):
            high = low + 512
            query, grad = both_heads(qkv[low:high, lanes]), both_heads(mix_grad[low:high, lanes])
            delta = pair_delta(mix_grad[low:high, lanes], mix[low:high, lanes])
            logsum = pair_row(lse, pair, low, high)
            total = 0.0
            for start in range(0, high, 512):
                rows = slice(start, start + 512)
                keys = qkv[rows, k_lanes]
                prob, score_grad = head_grads(
                    keys, qkv[rows, v_lanes], query, grad, logsum, delta, causal if start == low else None
                )
                dv, dk = dot(prob, grad), dot(score_grad, query)
                if start == low:
                    dv_sum[rows, :], dk_sum[rows, :] = dv, dk
                else:
                    dv_sum[rows, :] += dv
                    dk_sum[rows, :] += dk
                total = total + dot(keys, score_grad, TN)
            dqkv[low:high, lanes] = (pick_heads(total) * HD**-0.5).astype(BF)
        dqkv[:, k_lanes] = (dk_sum[...] * HD**-0.5).astype(BF)
        dqkv[:, v_lanes] = dv_sum[...].astype(BF)
        return carry

    lax.fori_loop(0, 4, pair_step, 0)


def fused_self_backward(place, after, mine, theirs, base, gain, weights, qkv, mix, lse):
    return call_overlapped(
        self_bwd_kernel,
        [
            (LATE, like(4, 128, 1024, dtype=F32)),
            (LATE, like(1024, 1024)),
            (VMEM, like(8, 1024, dtype=F32)),
            (VMEM, like(1024, 1536)),
        ],
        [SMEM] + [ROWS] * 4 + [VMEM] + [LATE] * 3 + [VMEM],
        (place, after, mine, theirs, base, gain, weights, qkv, mix, lse),
        [pltpu.VMEM((1024, 512), BF), pltpu.VMEM((1024, 128), F32), pltpu.VMEM((1024, 128), F32)],
    )


def self_grads_kernel(place, normed, low_grad, dq, dk, dv, mix, g_own, g_side, g_over, g_low, g_high, rows_t, grad_t, grads):
    @pl.when(pl.program_id(0) == 0)
    def _():
        rows_t[...] = normed[...].T
        grad_t[...] = low_grad[...].T

    grads[:, :384] = dot(rows_t[...], jnp.concatenate([dq[...], dk[...], dv[...]], 1))
    grads[:, 384:] = dot(grad_t[...], mix[...])
    cut_grads(place, grads, slice(None), g_own, g_side, g_over, g_low, g_high)


def self_grads(place, normed, low_grad, dqkv, mix):
    square = once(1024, 1024)

    def cut(offset):
        return pl.BlockSpec((1024, 128), lambda i: (0, offset + i))

    return call(
        self_grads_kernel,
        grad_outs(),
        [SMEM, square, square, cut(0), cut(4), cut(8), cut(0)],
        (place, normed, low_grad, dqkv, dqkv, dqkv, mix),
        [pltpu.VMEM((1024, 1024), BF)] * 2 + [pltpu.VMEM((1024, 512), F32)],
        grid=(4,),
        flops=4 * 2**30,
        moved=12 * MIB,
        limit=60,
    )


def self_back_kernel(place, dqkv, weights, kept, sent):
    core = place[1]
    w_in = jnp.concatenate([columns_of(weights, one) for one in range(3)], 1)
    for target, half in ((sent, 1 - core), (kept, core)):
        rows = jnp.concatenate([dqkv[at(block * 256 + half * 128, 128), :] for block in range(4)], 0)
        for low in range(0, 1024, 512):
            value = dot(rows, w_in[low : low + 512, :], NT).astype(target.dtype)
            target[:, :, low : low + 512] = value.reshape(4, 128, 512)


def self_back(place, dqkv, weights):
    return call(
        self_back_kernel,
        [(VMEM, like(4, 128, 1024, dtype=F32)), (VMEM, like(4, 128, 1024))],
        [SMEM, VMEM, VMEM],
        (place, dqkv, weights),
        flops=3 * 2**30,
        moved=10 * MIB,
        limit=60,
    )


def last_norm_kernel(place, rows, grad_own, mine, theirs, gain, text_part, sums_two, sums_three, *pieces):
    gain_sum, bias_sum = jnp.zeros((8, 1024), F32), jnp.zeros((8, 1024), F32)
    for number in range(4):
        block = (place[2] + number) % 4
        grad = mine[block] + theirs[block].astype(F32)
        back, term = norm_backward(rows[number].astype(F32), norm_row(gain, 0), grad)
        pieces[-number % 4][0:128, :] = (grad_own[block] + back).astype(BF)
        pieces[-number % 4][128:160, :] = text_part[at(block * 32, 32, 32), :]
        gain_sum = gain_sum + jnp.sum(term.reshape(16, 8, 1024), 0)
        bias_sum = bias_sum + jnp.sum(grad.reshape(16, 8, 1024), 0)
    sums = [jnp.sum(gain_sum, 0, keepdims=True), jnp.sum(bias_sum, 0, keepdims=True)]
    sums += [0.5 * sums_two[0:2, :], 0.5 * sums_three[0:2, :], jnp.zeros((10, 1024), F32)]
    sums = jnp.concatenate(sums, 0).astype(BF)
    for piece in pieces:
        piece[160:176, :] = sums


def last_norm(place, rows, grad_own, mine, theirs, gain, text_part, sums_two, sums_three):
    return call(
        last_norm_kernel,
        [(VMEM, like(176, 1024))] * 4,
        [SMEM] + [VMEM] * 8,
        (place, rows, grad_own, mine, theirs, gain, text_part, sums_two, sums_three),
    )


def finish_kernel(place, out_keep, theirs, *pieces):
    for number, piece in enumerate(pieces):
        block = (place[2] + 4 - number) % 4
        piece[...] = (out_keep[block] + theirs[block].astype(F32)).astype(BF)


def finish(place, out_keep, theirs):
    return call(
        finish_kernel,
        [(VMEM, like(128, 1024))] * 4,
        [SMEM] + [VMEM] * 2,
        (place, out_keep, theirs),
    )


def part_kernel(place, *refs):
    pieces, mine, sent = refs[:4], refs[4], refs[5]
    core, top = place[1], place[2]
    for step, piece in enumerate(pieces):
        image = (top + step) % 4

        @pl.when(image // 2 == core)
        def _():
            mine[image % 2] = piece[...]

        @pl.when(image // 2 != core)
        def _():
            sent[image % 2] = piece[...]

    if pieces[0].shape[0] > 160:
        total = 0.0
        for piece in pieces:
            total = total + piece[160:176, :].astype(F32)
        mine[0, 160:176, :] = total.astype(BF)
        sent[0, 160:176, :] = total.astype(BF)


def part_images(place, pieces):
    return call(
        part_kernel,
        [(VMEM, like(2, *pieces[0].shape))] * 2,
        [SMEM] + [VMEM] * 4,
        (place, *pieces),
    )


def land_kernel(place, mine, taken, rows, *more):
    core = place[1]
    for one in range(2):
        rows[one, at(core * 128, 128), :] = mine[one, 0:128, :].astype(rows.dtype)
        rows[one, at((1 - core) * 128, 128), :] = taken[one, 0:128, :].astype(rows.dtype)
        if more:
            more[0][one] = mine[one, 128:160, :].astype(F32) + taken[one, 128:160, :].astype(F32)
    if more:
        more[1][...] = mine[0, 160:168, :].astype(F32) + taken[0, 160:168, :].astype(F32)


def land(place, mine, taken, dtype):
    outs = [(VMEM, like(2, 256, 1024, dtype=dtype))]
    if mine.shape[1] > 128:
        outs += [(VMEM, like(2, 32, 1024, dtype=F32)), (VMEM, like(8, 1024, dtype=F32))]
    return call(land_kernel, outs, [SMEM, VMEM, VMEM], (place, mine, taken))


def relay_kernel(over, side, from_side, from_over, to_over, to_side):
    to_over[0:128, :] = (over[0:128, :].astype(F32) + from_side[...].astype(F32)).astype(BF)
    to_over[128:256, :] = over[128:256, :]
    to_side[0:128, :] = side[0:128, :]
    to_side[128:256, :] = (side[128:256, :].astype(F32) + from_over[...].astype(F32)).astype(BF)


def relay(over, side, from_side, from_over):
    return call(
        relay_kernel,
        [(VMEM, like(256, 2048))] * 2,
        [VMEM] * 4,
        (over, side, from_side, from_over),
        moved=5 * MIB,
    )


def plane_sum_kernel(place, own, over, side, keep, *sent):
    for s in range(4):
        columns = at((place[2] + s) % 4 * 512, 512, 512)
        total = own[:, columns].astype(F32) + over[:, columns].astype(F32) + side[:, columns].astype(F32)
        if s:
            sent[s - 1][...] = total.astype(BF)
        else:
            keep[...] = total


def plane_sum(place, own, over, side):
    return call(
        plane_sum_kernel,
        [(VMEM, like(256, 512, dtype=F32))] + [(VMEM, like(256, 512))] * 3,
        [SMEM] + [VMEM] * 3,
        (place, own, over, side),
        moved=5 * MIB,
    )


def plane_sum_whole_kernel(own, over, side, whole):
    for step in range(4):
        columns = slice(step * 512, (step + 1) * 512)
        total = own[:, columns].astype(F32) + over[:, columns].astype(F32) + side[:, columns].astype(F32)
        whole[step * 256 : (step + 1) * 256, :] = total.astype(BF)


def plane_sum_whole(own, over, side):
    return call(
        plane_sum_whole_kernel,
        [(VMEM, like(1024, 512))],
        [VMEM] * 3,
        (own, over, side),
    )[0]


def line_sum_kernel(place, keep, one, two, three, mine, other):
    core = place[1]
    for target, half in ((other, 1 - core), (mine, core)):
        rows = at(half * 128, 128)
        total = keep[rows, :]
        for part in (one, two, three):
            total = total + part[rows, :].astype(F32)
        target[...] = total.astype(target.dtype)


def line_sum(place, keep, parts):
    return call(
        line_sum_kernel,
        [(VMEM, like(128, 512, dtype=F32)), (VMEM, like(128, 512))],
        [SMEM] + [VMEM] * 4,
        (place, keep, *parts),
        moved=2 * MIB,
    )


def spread_kernel(place, mine, other, *outs):
    core, columns = place[1], mine.shape[1] // len(outs)
    for one, out in enumerate(outs):
        cut = slice(one * columns, (one + 1) * columns)
        out[:, at(core * columns, columns)] = mine[:, cut].astype(F32)
        out[:, at((1 - core) * columns, columns)] = other[:, cut].astype(F32)


def spread(place, mine, other):
    return call(
        spread_kernel,
        [(VMEM, like(128, 256, dtype=F32))] * 4,
        [SMEM] + [VMEM] * 2,
        (place, mine, other),
        moved=MIB,
    )


def spread_feed_kernel(place, mine_one, other_one, mine_two, other_two, *outs):
    core = place[1]
    for part, (mine, other) in enumerate(((mine_one, other_one), (mine_two, other_two))):
        for one, out in enumerate(outs):
            cut = slice(one * 256, (one + 1) * 256)
            out[:, at(core * 512 + part * 256, 256)] = mine[:, cut].astype(F32)
            out[:, at((1 - core) * 512 + part * 256, 256)] = other[:, cut].astype(F32)


def spread_feed(place, *halves):
    return call(
        spread_feed_kernel,
        [(VMEM, like(128, 1024, dtype=F32))] * 2,
        [SMEM] + [VMEM] * 4,
        (place, *halves),
        moved=2 * MIB,
    )


tie = lax.optimization_barrier


def packed_layer(args):
    image_rows, text_rows, segment_ids, cotangent, *others = args
    weights, norms = others[:10], others[10:]
    chip, core, top = lax.axis_index("chip"), lax.axis_index("core"), lax.axis_index("hi")
    place = jnp.stack([chip, core, top, core * 2 + top % 2]).astype(jnp.int32)

    def swap(value):
        return lax.ppermute(value, "core", [(0, 1), (1, 0)])

    def across(value, bit):
        return lax.ppermute(value, "chip", [(i, i ^ bit) for i in range(4)])

    def shift(value, step):
        return lax.ppermute(value, "hi", [((i + step) % 4, i) for i in range(4)])

    def line(part):
        return [shift(part, step) for step in range(1, 4)]

    def exchange(pieces):
        return [pieces[0]] + [shift(piece, step) for step, piece in enumerate(pieces) if step]

    def gather_line(part):
        return lax.all_gather(part, "hi")

    def sides(value):
        return [across(value, 1), across(value, 2)]

    def corners(pair, cut):
        return [across(pair[0][:cut], 2), across(pair[1][cut:], 1)]

    def grad_corners(grads):
        return [across(grads[3], 1), across(grads[4], 2)]

    def grad_sides(grads, got, later):
        to_over, to_side, later = tie((*relay(grads[2], grads[1], *got), later))
        return [across(to_over, 2), across(to_side, 1)], later

    def halves(total):
        cut = total.reshape(2, 128, 512)
        sent = lax.dynamic_index_in_dim(cut, 1 - core, 0, False)
        return lax.dynamic_index_in_dim(cut, core, 0, False), swap(sent)

    keep, sent = prepare(place, jnp.stack(norms), weights)
    v = {"taken": swap(sent)}
    v["rows_keep"], v["rows_sent"], v["cot_keep"], v["cot_sent"], v["text_pair"] = prepare_rows(
        place, segment_ids, image_rows, text_rows, cotangent
    )
    v = tie(v)
    *v["singles"], v["near"] = join(place, keep, v.pop("taken"))
    v["rows_taken"], v["cot_taken"] = swap(v.pop("rows_sent")), swap(v.pop("cot_sent"))
    v["text_taken"] = swap(v["text_pair"])
    v = tie(v)

    v["near"] = [v["near"], *sides(v["near"])]
    lines = line(v["singles"][0])
    v["pieces"] = pick(place, v.pop("rows_keep"), v.pop("rows_taken"))
    v["cot_pieces"] = pick(place, v.pop("cot_keep"), v.pop("cot_taken"))
    v["text_pieces"] = pick(place, v.pop("text_pair"), v.pop("text_taken"))
    v = tie(v)
    v["near"] += corners(v["near"][1:], 128)
    v["line"] = lines
    v = tie(v)

    rest = stack(v.pop("line"))
    v["far_self"] = [rest, *sides(rest)]
    v["two_on"] = shift(v["pieces"][2], 2)
    line_cross = gather_line(v["singles"][1])
    v = tie(v)
    v["far_self"] += corners(v["far_self"][1:], 384)
    pieces = v.pop("pieces")
    v["pieces"] = [pieces[0], shift(pieces[1], 1), v.pop("two_on"), shift(pieces[3], 3)]
    v["line_cross"] = line_cross
    v = tie(v)
    v["rows_own"] = stack([piece[None] for piece in v.pop("pieces")])
    v["rows_other"] = swap(v["rows_own"])
    line_one = gather_line(v["singles"][2])
    v = tie(v)

    v["far_cross"] = sides(v["line_cross"])
    text_pieces, cot_pieces = v.pop("text_pieces"), v.pop("cot_pieces")
    v["text_near"] = [text_pieces[0], shift(text_pieces[1], 1), shift(text_pieces[3], 3)]
    v["text_two"], v["cot_two"] = text_pieces[2], shift(cot_pieces[2], 2)
    v["cot_near"] = [cot_pieces[0], cot_pieces[1], cot_pieces[3]]
    v["line_one"] = line_one
    v["w_self"], v["norms"], v["normed_one"], v["qkv"], v["self_mix"], v["self_lse"], v["mine"] = (
        fused_self_forward(place, v["rows_own"], v["rows_other"], v.pop("near"), v.pop("far_self"))
    )
    v = tie(v)

    v["theirs"] = swap(v["mine"])
    v["far_cross"] += corners(v["far_cross"], 2)
    line_two = gather_line(v.pop("singles")[3])
    text_near, text_two = v.pop("text_near"), shift(v.pop("text_two"), 2)
    text_pieces = [text_near[0], text_near[1], text_two, text_near[2]]
    v["text"] = arrange(place, text_pieces)
    ids = text_pieces[0][32, :128].astype(jnp.int32)
    v["caption"] = jnp.repeat(ids, 8)[None, :]
    v["ids"] = ids[:, None]
    v["one_low"], v["one_high"] = v["line_one"][:2], v["line_one"][2:]
    v = tie(v)

    low, high = v.pop("one_low"), v.pop("one_high")
    v["far_one"] = [across(low, 1), across(high, 1), across(v["line_one"], 2)]
    near, one_on, three_on = v.pop("cot_near")
    cot_pieces = [near, shift(one_on, 1), v.pop("cot_two"), shift(three_on, 3)]
    v["w_cross"], v["after_attn"], v["normed_two"], v["queries"], v["keys"], v["cross_mix"], v["cross_lse"], v["mine"] = (
        fused_cross_forward(
            place, v["rows_own"], v.pop("rows_other"), v["mine"], v["theirs"], v["norms"], v["text"], v["ids"],
            v["caption"], (v.pop("line_cross"), *v.pop("far_cross")),
        )
    )
    v["cot_own"] = join_pieces(place, cot_pieces)
    v["line_two"] = line_two
    v = tie(v)

    v["theirs"] = swap(v["mine"])
    v["far_one"] += [across(v["far_one"][0], 2), across(v["far_one"][2][2:], 1)]
    w_two = lax.all_gather(v.pop("line_two"), "chip")
    v["cot_other"] = swap(v["cot_own"])
    v = tie(v)

    v["w_two"] = w_two
    pieces = (v.pop("line_one"), *v.pop("far_one"))
    v["grads_one"], v["after_cross"], v["normed_three"], v["cot"], v["out_sum"], v["back_sum"] = feed_first(
        place, v["after_attn"], v["mine"], v["theirs"], v["norms"], v.pop("cot_own"), v.pop("cot_other"), pieces
    )
    v = tie(v)

    total_one = lax.psum_scatter(v.pop("grads_one"), "chip", scatter_dimension=0, tiled=False)
    *v["grads_two"], v["out_keep"], v["out_sent"], v["mine"] = feed_second(
        place, v.pop("normed_three"), v["cot"], v.pop("out_sum"), v.pop("back_sum"), v.pop("w_two")
    )
    v = tie(v)

    v["out_theirs"] = swap(v.pop("out_sent"))
    v = tie(v)
    v["theirs"] = swap(v["mine"])
    v["got_two"] = grad_corners(v["grads_two"])
    v["pieces"] = exchange(finish(place, v.pop("out_keep"), v.pop("out_theirs")))
    v["grad_cross"], v["part"], v["norms_three"], v["text_part"], *v["grads_three"] = fused_cross_backward(
        place, v.pop("after_cross"), v.pop("mine"), v.pop("theirs"), v.pop("cot"), v["norms"], v.pop("w_cross"),
        v.pop("normed_two"), v.pop("text"), v.pop("queries"), v.pop("keys"), v.pop("cross_mix"),
        v.pop("cross_lse"), v.pop("ids"), v.pop("caption"),
    )
    v = tie(v)

    v["theirs"] = swap(v["part"])
    v["total_one"] = total_one
    to_two = relay(v["grads_two"][2], v["grads_two"][1], *v.pop("got_two"))

    v["sides_two"] = [across(to_two[0], 2), across(to_two[1], 1)]
    v["got_three"] = grad_corners(v["grads_three"])
    v["line_one"] = lax.psum_scatter(v.pop("total_one"), "hi", scatter_dimension=0, tiled=False)
    v["grad_own"], v["low_grad"], v["norms_two"], v["dqkv"] = fused_self_backward(
        place, v.pop("after_attn"), v.pop("part"), v.pop("theirs"), v.pop("grad_cross"), v["norms"], v["w_self"],
        v.pop("qkv"), v["self_mix"], v.pop("self_lse"),
    )
    v = tie(v)

    v["sides_three"], sides_two = grad_sides(v["grads_three"], v.pop("got_three"), v.pop("sides_two"))
    total_two = plane_sum_whole(v.pop("grads_two")[0], *sides_two)
    line_two = lax.psum_scatter(total_two, "hi", scatter_dimension=0, tiled=True)
    v["grads_four"] = self_grads(place, v.pop("normed_one"), v.pop("low_grad"), v["dqkv"], v.pop("self_mix"))
    mine, sent = part_images(place, v.pop("pieces"))
    (v["result"],) = land(place, mine, swap(sent), BF)
    v["feed_one"] = halves(v.pop("line_one"))
    v = tie(v)

    v["got_four"] = grad_corners(v["grads_four"])
    total_three, dqkv = tie((plane_sum_whole(v.pop("grads_three")[0], *v.pop("sides_three")), v.pop("dqkv")))
    line_three = lax.psum_scatter(total_three, "hi", scatter_dimension=0, tiled=True)
    v["line_two"] = line_two
    v["kept"], v["sent"] = self_back(place, dqkv, v.pop("w_self"))
    v = tie(v)

    v["sides_four"], _ = grad_sides(v["grads_four"], v.pop("got_four"), place)
    pieces = last_norm(
        place, v.pop("rows_own"), v.pop("grad_own"), v.pop("kept"), swap(v.pop("sent")), v.pop("norms"),
        v.pop("text_part"), v.pop("norms_two"), v.pop("norms_three"),
    )
    input_pieces = exchange(pieces)
    v = tie(v)

    v["kept"], *sums_four = plane_sum(place, v.pop("grads_four")[0], *v.pop("sides_four"))
    v["line_four"] = [shift(piece, 3 - i) for i, piece in enumerate(sums_four)]
    v["feed_grads"] = spread_feed(place, *v.pop("feed_one"), *halves(v.pop("line_two")))
    later = tie((place, sums_four))[0]
    mine, sent = part_images(later, input_pieces)
    v["input_grad"], v["text_grad"], sums = land(place, mine, swap(sent), F32)
    sums = sums + across(sums, 1)
    sums = sums + across(sums, 2)
    v["sums"] = lax.dynamic_slice_in_dim(sums, (chip * 2 + core) * 128, 128, 1)
    v["cross_grads"] = spread(place, *halves(line_three))
    v = tie(v)

    kept, sent = line_sum(place, v.pop("kept"), v.pop("line_four"))
    own_grads = spread(place, kept, swap(sent))
    return (
        v["result"], v["input_grad"], v["text_grad"], *own_grads, *v["cross_grads"], *v["feed_grads"],
        *[v["sums"][i] for i in range(6)],
    )


def solution(mesh):
    fsdp, tensor = mesh.shape["fsdp"], mesh.shape["tensor"]

    def run(*args):
        images = args[0].shape[0] // fsdp
        tops = 2 * images
        shape = {"chip": fsdp // 2, "core": 2, "hi": tops, "lo": tensor // tops}
        fine = Mesh(mesh.devices.reshape(tuple(shape.values())), tuple(shape))
        first, second = ("chip", "core"), ("hi", "lo")
        wide, weight, norm = P(first, second, None), P(first, second), P(first)
        outs = (wide,) * 3 + (weight,) * 10 + (norm,) * 6
        packed = (
            (fsdp, tensor, images) == (8, 4, 2)
            and args[0].shape[1:] == (1024, 1024)
            and args[1].shape[1:] == (128, 1024)
            and args[12].shape == (1024, 4096)
        )
        return jax.shard_map(
            lambda *local: packed_layer(local) if packed else layer(shape, local),
            mesh=fine,
            in_specs=(wide, wide, P(first, None), wide) + (weight,) * 10 + (norm,) * 6,
            out_specs=outs,
            check_vma=False,
        )(*args)

    return run
```

```python
import functools
import math

import jax
import jax.numpy as jnp
from jax import lax
from jax.experimental import pallas as pl
from jax.experimental.pallas import tpu as pltpu
from jax.sharding import Mesh
from jax.sharding import PartitionSpec as P

HD = 64
EPS = 1e-05
NEG = -1e30
LOG2E = math.log2(math.e)
BF = jnp.bfloat16
F32 = jnp.float32
NT = (((1,), (1,)), ((), ()))
TN = (((0,), (0,)), ((), ()))
NN = (((1,), (0,)), ((), ()))


def dot(left, right, dims=NN):
    return lax.dot_general(left, right, dims, preferred_element_type=F32)


def lane_head(shape, axis, head):
    return lax.broadcasted_iota(jnp.int32, shape, axis) // HD == head


def self_forward_kernel(q_ref, k_ref, v_ref, mix_ref, lse_ref, *, block):
    length = q_ref.shape[0]
    scale = LOG2E * HD**-0.5
    causal = lax.broadcasted_iota(jnp.int32, (block, block), 0) <= lax.broadcasted_iota(
        jnp.int32, (block, block), 1
    )
    for at in range(length // block):
        lo, hi = at * block, (at + 1) * block
        query = q_ref[lo:hi, :]
        mixes = []
        for head in range(2):
            one = jnp.where(lane_head((1, 2 * HD), 1, head), query, jnp.zeros_like(query))
            diag = jnp.where(causal, dot(k_ref[lo:hi, :], one, NT), NEG)
            peak = jnp.max(diag, 0, keepdims=True)
            if at:
                past = dot(k_ref[:lo, :], one, NT)
                peak = jnp.maximum(peak, jnp.max(past, 0, keepdims=True))
            weights = jnp.exp2((diag - peak) * scale)
            total = jnp.sum(weights, 0, keepdims=True)
            mixed = dot(v_ref[lo:hi, :], weights.astype(BF), TN)
            if at:
                weights = jnp.exp2((past - peak) * scale)
                total = total + jnp.sum(weights, 0, keepdims=True)
                mixed = mixed + dot(v_ref[:lo, :], weights.astype(BF), TN)
            mixes.append(mixed / total)
            lse_ref[0, head : head + 1, lo:hi] = peak * scale + jnp.log2(total)
        both = jnp.where(lane_head((2 * HD, 1), 0, 0), mixes[0], mixes[1])
        mix_ref[lo:hi, :] = both.T.astype(BF)


def self_backward_kernel(
    q_ref, k_ref, v_ref, mix_ref, grad_ref, lse_ref, dq_ref, dk_ref, dv_ref, dk_sum, dv_sum, *, block
):
    length = q_ref.shape[0]
    scale = LOG2E * HD**-0.5
    causal = lax.broadcasted_iota(jnp.int32, (block, block), 0) <= lax.broadcasted_iota(
        jnp.int32, (block, block), 1
    )
    dk_sum[...] = jnp.zeros_like(dk_sum)
    dv_sum[...] = jnp.zeros_like(dv_sum)
    for at in range(length // block):
        lo, hi = at * block, (at + 1) * block
        query = q_ref[lo:hi, :]
        grad = grad_ref[lo:hi, :]
        product = (grad.astype(F32) * mix_ref[lo:hi, :].astype(F32)).T
        grads = []
        for head in range(2):
            picked = lane_head((1, 2 * HD), 1, head)
            one = jnp.where(picked, query, jnp.zeros_like(query))
            one_grad = jnp.where(picked, grad, jnp.zeros_like(grad))
            delta = jnp.sum(product[head * HD : (head + 1) * HD], 0, keepdims=True)
            lse = lse_ref[0, head : head + 1, lo:hi]
            total = jnp.zeros((2 * HD, block), F32)
            for start, stop in ((0, lo), (lo, hi)):
                if start == stop:
                    continue
                keys = k_ref[start:stop, :]
                weights = jnp.exp2(dot(keys, one, NT) * scale - lse)
                if start == lo:
                    weights = jnp.where(causal, weights, 0.0)
                slope = dot(v_ref[start:stop, :], one_grad, NT)
                score_grad = (weights * (slope - delta)).astype(BF)
                dv_sum[start:stop, :] += dot(weights.astype(BF), one_grad)
                dk_sum[start:stop, :] += dot(score_grad, one)
                total = total + dot(keys, score_grad, TN)
            grads.append(total)
        both = jnp.where(lane_head((2 * HD, 1), 0, 0), grads[0], grads[1])
        dq_ref[lo:hi, :] = (both.T * HD**-0.5).astype(BF)
    dk_ref[...] = (dk_sum[...] * HD**-0.5).astype(BF)
    dv_ref[...] = dv_sum[...].astype(BF)


def cross_forward_kernel(q_ref, k_ref, v_ref, ids_ref, caption_ref, mix_ref, lse_ref, *, block):
    length = q_ref.shape[0]
    scale = LOG2E * HD**-0.5
    for at in range(length // block):
        lo, hi = at * block, (at + 1) * block
        query = q_ref[lo:hi, :]
        seen = ids_ref[...] == caption_ref[:, lo:hi]
        mixes = []
        for head in range(2):
            one = jnp.where(lane_head((1, 2 * HD), 1, head), query, jnp.zeros_like(query))
            scores = jnp.where(seen, dot(k_ref[...], one, NT), NEG)
            peak = jnp.max(scores, 0, keepdims=True)
            weights = jnp.exp2((scores - peak) * scale)
            total = jnp.sum(weights, 0, keepdims=True)
            mixes.append(dot(v_ref[...], weights.astype(BF), TN) / total)
            lse_ref[0, head : head + 1, lo:hi] = peak * scale + jnp.log2(total)
        both = jnp.where(lane_head((2 * HD, 1), 0, 0), mixes[0], mixes[1])
        mix_ref[lo:hi, :] = both.T.astype(BF)


def cross_backward_kernel(
    q_ref, k_ref, v_ref, mix_ref, grad_ref, lse_ref, ids_ref, caption_ref, dq_ref, dk_ref, dv_ref, *, block
):
    length = q_ref.shape[0]
    scale = LOG2E * HD**-0.5
    keys, values = k_ref[...], v_ref[...]
    dk_sum = jnp.zeros(keys.shape, F32)
    dv_sum = jnp.zeros(keys.shape, F32)
    for at in range(length // block):
        lo, hi = at * block, (at + 1) * block
        query = q_ref[lo:hi, :]
        grad = grad_ref[lo:hi, :]
        product = (grad.astype(F32) * mix_ref[lo:hi, :].astype(F32)).T
        seen = ids_ref[...] == caption_ref[:, lo:hi]
        grads = []
        for head in range(2):
            picked = lane_head((1, 2 * HD), 1, head)
            one = jnp.where(picked, query, jnp.zeros_like(query))
            one_grad = jnp.where(picked, grad, jnp.zeros_like(grad))
            delta = jnp.sum(product[head * HD : (head + 1) * HD], 0, keepdims=True)
            lse = lse_ref[0, head : head + 1, lo:hi]
            weights = jnp.where(seen, jnp.exp2(dot(keys, one, NT) * scale - lse), 0.0)
            slope = dot(values, one_grad, NT)
            score_grad = (weights * (slope - delta)).astype(BF)
            dv_sum = dv_sum + dot(weights.astype(BF), one_grad)
            dk_sum = dk_sum + dot(score_grad, one)
            grads.append(dot(keys, score_grad, TN))
        both = jnp.where(lane_head((2 * HD, 1), 0, 0), grads[0], grads[1])
        dq_ref[lo:hi, :] = (both.T * HD**-0.5).astype(BF)
    dk_ref[...] = (dk_sum * HD**-0.5).astype(BF)
    dv_ref[...] = dv_sum.astype(BF)


def feed_kernel(
    rows_ref, cot_ref, win_ref, wout_ref, out_in, back_in, gin_ref, gout_ref, out_ref, back_ref, rows_t, cot_t, *, first
):
    step = pl.program_id(0)

    @pl.when(step == 0)
    def _():
        rows_t[...] = rows_ref[...].T
        cot_t[...] = cot_ref[...].T
        if first:
            out_ref[...] = jnp.zeros_like(out_ref)
            back_ref[...] = jnp.zeros_like(back_ref)
        else:
            out_ref[...] = out_in[...]
            back_ref[...] = back_in[...]

    pre = dot(rows_ref[...], win_ref[...])
    square = pre * pre
    slope = math.sqrt(2.0 / math.pi)
    bent = jnp.tanh(pre * (slope + slope * 0.044715 * square))
    half = 0.5 * (1.0 + bent)
    act = (pre * half).astype(BF)
    out_ref[...] += dot(act, wout_ref[...], NT)
    gout_ref[...] = dot(cot_t[...], act).astype(BF)
    bend = half + pre * (0.5 * (1.0 - bent * bent)) * (slope + 3.0 * slope * 0.044715 * square)
    pre_grad = (dot(cot_ref[...], wout_ref[...]) * bend).astype(BF)
    gin_ref[...] = dot(rows_t[...], pre_grad).astype(BF)
    back_ref[...] += dot(pre_grad, win_ref[...], NT)


VMEM_LIMIT = 60 * 1024 * 1024


def params():
    return pltpu.CompilerParams(vmem_limit_bytes=VMEM_LIMIT)


def column(rows, offset):
    return pl.BlockSpec((rows, 2 * HD), lambda i: (0, offset + i))


def self_forward(packed):
    length, width = packed.shape
    pairs = width // (6 * HD)
    return pl.pallas_call(
        functools.partial(self_forward_kernel, block=256),
        grid=(pairs,),
        in_specs=[column(length, 0), column(length, pairs), column(length, 2 * pairs)],
        out_specs=[column(length, 0), pl.BlockSpec((1, 2, length), lambda i: (i, 0, 0))],
        out_shape=[
            jax.ShapeDtypeStruct((length, pairs * 2 * HD), BF),
            jax.ShapeDtypeStruct((pairs, 2, length), F32),
        ],
        compiler_params=params(),
        cost_estimate=pl.CostEstimate(
            flops=8 * pairs * length * length * 2 * HD * 2,
            bytes_accessed=8 * pairs * length * 2 * HD,
            transcendentals=2 * pairs * length * length,
        ),
    )(packed, packed, packed)


def self_backward(packed, mix, grad, lse):
    length, width = packed.shape
    pairs = width // (6 * HD)
    part = jax.ShapeDtypeStruct((length, pairs * 2 * HD), BF)
    return pl.pallas_call(
        functools.partial(self_backward_kernel, block=256),
        grid=(pairs,),
        in_specs=[
            column(length, 0),
            column(length, pairs),
            column(length, 2 * pairs),
            column(length, 0),
            column(length, 0),
            pl.BlockSpec((1, 2, length), lambda i: (i, 0, 0)),
        ],
        out_specs=[column(length, 0)] * 3,
        out_shape=[part] * 3,
        scratch_shapes=[pltpu.VMEM((length, 2 * HD), F32)] * 2,
        compiler_params=params(),
        cost_estimate=pl.CostEstimate(
            flops=20 * pairs * length * length * 2 * HD * 2,
            bytes_accessed=16 * pairs * length * 2 * HD,
            transcendentals=2 * pairs * length * length,
        ),
    )(packed, packed, packed, mix, grad, lse)


def cross_forward(queries, keys, ids, captions):
    length, width = queries.shape
    texts = keys.shape[0]
    pairs = width // (2 * HD)
    return pl.pallas_call(
        functools.partial(cross_forward_kernel, block=min(512, length)),
        grid=(pairs,),
        in_specs=[
            column(length, 0),
            column(texts, 0),
            column(texts, pairs),
            pl.BlockSpec((texts, 1), lambda i: (0, 0)),
            pl.BlockSpec((1, length), lambda i: (0, 0)),
        ],
        out_specs=[column(length, 0), pl.BlockSpec((1, 2, length), lambda i: (i, 0, 0))],
        out_shape=[
            jax.ShapeDtypeStruct((length, width), BF),
            jax.ShapeDtypeStruct((pairs, 2, length), F32),
        ],
        compiler_params=params(),
    )(queries, keys, keys, ids, captions)


def cross_backward(queries, keys, mix, grad, lse, ids, captions):
    length, width = queries.shape
    texts = keys.shape[0]
    pairs = width // (2 * HD)
    return pl.pallas_call(
        functools.partial(cross_backward_kernel, block=min(512, length)),
        grid=(pairs,),
        in_specs=[
            column(length, 0),
            column(texts, 0),
            column(texts, pairs),
            column(length, 0),
            column(length, 0),
            pl.BlockSpec((1, 2, length), lambda i: (i, 0, 0)),
            pl.BlockSpec((texts, 1), lambda i: (0, 0)),
            pl.BlockSpec((1, length), lambda i: (0, 0)),
        ],
        out_specs=[column(length, 0), column(texts, 0), column(texts, 0)],
        out_shape=[
            jax.ShapeDtypeStruct((length, width), BF),
            jax.ShapeDtypeStruct((texts, width), BF),
            jax.ShapeDtypeStruct((texts, width), BF),
        ],
        compiler_params=params(),
    )(queries, keys, keys, mix, grad, lse, ids, captions)


def feed(rows, cot, w_in, w_out, sums):
    length, width = rows.shape
    units = w_in.shape[1]
    block = min(256, units)
    whole = pl.BlockSpec((length, width), lambda i: (0, 0))
    cut = pl.BlockSpec((width, block), lambda i: (0, i))
    first = sums is None
    kernel = functools.partial(feed_kernel, first=first)
    operands = [rows, cot, w_in, w_out]
    specs = [whole, whole, cut, cut]
    if first:
        body = lambda a, b, c, d, *rest: kernel(a, b, c, d, None, None, *rest)
    else:
        body = kernel
        operands += list(sums)
        specs += [whole, whole]
    total = jax.ShapeDtypeStruct((length, width), F32)
    part = jax.ShapeDtypeStruct((width, units), BF)
    return pl.pallas_call(
        body,
        grid=(units // block,),
        in_specs=specs,
        out_specs=[cut, cut, whole, whole],
        out_shape=[part, part, total, total],
        scratch_shapes=[pltpu.VMEM((width, length), BF)] * 2,
        compiler_params=params(),
        cost_estimate=pl.CostEstimate(
            flops=12 * length * width * units,
            bytes_accessed=8 * width * units + 8 * length * width,
            transcendentals=length * units,
        ),
    )(*operands)


def norm_parts(values):
    center = values - jnp.mean(values, -1, keepdims=True)
    inverse = lax.rsqrt(jnp.mean(center * center, -1, keepdims=True) + EPS)
    return center * inverse, inverse


def layer_norm(values, gain, offset):
    return (norm_parts(values)[0] * gain + offset).astype(BF)


def norm_back(values, gain, grad):
    hat, inverse = norm_parts(values)
    scaled = grad * gain
    back = inverse * (
        scaled
        - jnp.mean(scaled, -1, keepdims=True)
        - hat * jnp.mean(scaled * hat, -1, keepdims=True)
    )
    lead = tuple(range(values.ndim - 1))
    return back, jnp.sum(grad * hat, lead), jnp.sum(grad, lead)


def layer(shape, args):
    chips, tops, lows = shape["chip"], shape["hi"], shape["lo"]
    (
        image_rows,
        text_rows,
        segment_ids,
        cotangent,
        query_weight,
        key_weight,
        value_weight,
        attn_output,
        cross_query,
        cross_key,
        cross_value,
        cross_output,
        hidden_in,
        hidden_out,
        *norms,
    ) = args
    images, rows, width = image_rows.shape
    texts = text_rows.shape[1]
    half_rows = rows // 2
    length = rows * lows * tops
    shard = query_weight.shape[0]
    chip, core = lax.axis_index("chip"), lax.axis_index("core")
    top = lax.axis_index("hi")
    own_slot = core * images + top % images

    def swap(value):
        return lax.ppermute(value, "core", [(0, 1), (1, 0)])

    def across(value, bit):
        return lax.ppermute(value, "chip", [(i, i ^ bit) for i in range(chips)])

    def shift(value, step):
        return lax.ppermute(value, "hi", [((i + step) % tops, i) for i in range(tops)])

    def matching(number, back):
        pairs = []
        for source_core in range(2):
            for source_top in range(tops):
                slot = source_top ^ number
                target = (slot // images) * tops + source_core * images + slot % images
                source = source_core * tops + source_top
                pairs.append((target, source) if back else (source, target))
        return pairs

    def to_image(piece_of):
        got = [
            lax.ppermute(piece_of(top ^ number), ("core", "hi"), matching(number, False))
            for number in range(tops)
        ]
        whole = jnp.stack(got)
        return jnp.stack(
            [lax.dynamic_index_in_dim(whole, own_slot ^ place, 0, False) for place in range(tops)]
        )

    def from_image(pieces):
        return [
            lax.ppermute(
                lax.dynamic_index_in_dim(pieces, own_slot ^ number, 0, False),
                ("core", "hi"),
                matching(number, True),
            )
            for number in range(tops)
        ]

    def image_piece(value):
        def piece(slot):
            return lax.dynamic_slice(
                value,
                (slot % images, (slot // images) * half_rows, 0),
                (1, half_rows, width),
            )[0]

        return piece

    def to_rows(pieces):
        got = jnp.stack(from_image(pieces))
        ordered = jnp.stack(
            [lax.dynamic_index_in_dim(got, top ^ slot, 0, False) for slot in range(tops)]
        )
        ordered = ordered.reshape(2, images, half_rows, width)
        return jnp.swapaxes(ordered, 0, 1).reshape(images, rows, width)

    def tp_gather(mine):
        if lows == 1:
            other = swap(mine)
            first = jnp.where(core == 0, mine, other)
            second = jnp.where(core == 0, other, mine)
            return jnp.stack([first, second], 1).reshape(length, width)
        every = lax.all_gather(mine, ("lo", "core"))
        every = every.reshape(lows * 2, tops, half_rows, width)
        return jnp.swapaxes(every, 0, 1).reshape(length, width)

    def tp_reduce(partial):
        if lows == 1:
            cut = partial.reshape(tops, 2, half_rows, width)
            sent = lax.dynamic_index_in_dim(cut, 1 - core, 1, False).astype(BF)
            kept = lax.dynamic_index_in_dim(cut, core, 1, False)
            return kept + swap(sent).astype(F32)
        cut = jnp.swapaxes(partial.astype(BF).reshape(tops, lows * 2, half_rows, width), 0, 1)
        cut = lax.psum_scatter(cut, ("lo", "core"), scatter_dimension=0, tiled=False)
        return cut.astype(F32)

    def core_half(weight, which):
        columns = weight.shape[1] // 2
        return lax.dynamic_slice_in_dim(weight, which * columns, columns, 1)

    def pack(which):
        feeds = [core_half(weight, which) for weight in (hidden_in, hidden_out)]
        cuts = feeds[0].shape[1] // 2
        groups = [
            [core_half(w, which) for w in (query_weight, key_weight, value_weight, attn_output)],
            [core_half(w, which) for w in (cross_query, cross_key, cross_value, cross_output)],
            [w[:, :cuts] for w in feeds],
            [w[:, cuts:] for w in feeds],
        ]
        return jnp.concatenate([w for group in groups for w in group], 1)

    kept = pack(core)
    taken = swap(pack(1 - core))
    own = jnp.concatenate(
        [jnp.where(core == 0, kept, taken), jnp.where(core == 0, taken, kept)], 0
    )
    block_rows = 2 * shard
    group_width = own.shape[1] // 4

    def plane_gather(piece):
        if chips != 4:
            return lax.all_gather(piece, "chip", axis=0, tiled=True)
        side = across(piece, 1)
        over = across(piece, 2)
        corner_low = across(side[:shard], 2)
        corner_high = across(over[shard:], 1)
        corner = jnp.concatenate([corner_low, corner_high], 0)
        pieces = jnp.stack([piece, side, over, corner])
        ordered = [lax.dynamic_index_in_dim(pieces, chip ^ place, 0, False) for place in range(4)]
        return jnp.concatenate(ordered, 0)

    def plane_scatter(grads):
        if chips != 4:
            return lax.psum_scatter(grads, "chip", scatter_dimension=0, tiled=True).astype(F32)

        def rows_of(place, low, count):
            return lax.dynamic_slice_in_dim(grads, (chip ^ place) * block_rows + low, count, 0)

        by_side = across(rows_of(3, 0, shard), 1)
        by_over = across(rows_of(3, shard, shard), 2)
        to_over = jnp.concatenate(
            [rows_of(2, 0, shard).astype(F32) + by_side.astype(F32), rows_of(2, shard, shard).astype(F32)], 0
        ).astype(BF)
        to_side = jnp.concatenate(
            [rows_of(1, 0, shard).astype(F32), rows_of(1, shard, shard).astype(F32) + by_over.astype(F32)], 0
        ).astype(BF)
        over, side = across(to_over, 2), across(to_side, 1)
        return rows_of(0, 0, block_rows).astype(F32) + over.astype(F32) + side.astype(F32)

    def top_scatter(pieces):
        total = pieces[0].astype(F32)
        for step in range(1, tops):
            total = total + shift(pieces[step].astype(BF), tops - step).astype(F32)
        return total

    def core_split(total):
        cut = total.reshape(2, shard, total.shape[1])
        mine = lax.dynamic_index_in_dim(cut, core, 0, False)
        other = swap(lax.dynamic_index_in_dim(cut, 1 - core, 0, False).astype(BF)).astype(F32)
        return jnp.where(core == 0, mine, other), jnp.where(core == 0, other, mine)

    own_wide = plane_gather(own)

    def fetch(group, count):
        part = own[:, group * group_width : (group + 1) * group_width]
        columns = group_width // count
        got = [shift(part, step).reshape(block_rows, count, 1, columns) for step in range(1, tops)]
        rest = jnp.concatenate(got, 2).reshape(block_rows, (tops - 1) * group_width)
        rest = plane_gather(rest).reshape(width, count, (tops - 1) * columns)
        near = own_wide[:, group * group_width : (group + 1) * group_width]
        near = near.reshape(width, count, columns)
        return [
            jnp.concatenate([near[:, one], rest[:, one]], 1) for one in range(count)
        ]

    def give(grads):
        count = len(grads)
        columns = grads[0].shape[1] // tops
        summed = plane_scatter(jnp.concatenate(grads, 1)).reshape(block_rows, count, tops, columns)
        pieces = [summed[:, :, step].reshape(block_rows, count * columns) for step in range(tops)]
        low, high = core_split(top_scatter(pieces))
        low, high = low.reshape(shard, count, columns), high.reshape(shard, count, columns)
        return [(low[:, one], high[:, one]) for one in range(count)]

    packed_norms = lax.all_gather(jnp.stack(norms), ("chip", "core"), axis=1, tiled=True)
    gain_one, bias_one, gain_two, bias_two, gain_three, bias_three = packed_norms

    w_query, w_key, w_value, w_out = fetch(0, 4)
    inputs = to_image(image_piece(image_rows)).astype(F32)
    c_query, c_key, c_value, c_out = fetch(1, 4)
    in_low, out_low = fetch(2, 2)
    in_high, out_high = fetch(3, 2)

    text = to_image(lambda slot: text_rows[slot % images])
    if lows > 1:
        text = lax.all_gather(text, "lo", axis=1)
    text = text.reshape(tops * lows * texts, width)
    other_ids = swap(segment_ids)
    ids = jnp.where(core == top // images, segment_ids, other_ids)
    ids = lax.dynamic_index_in_dim(ids, top % images, 0, False)
    captions = jnp.repeat(ids, length // ids.shape[0])[None, :]
    ids = ids[:, None]
    cot = to_image(image_piece(cotangent))

    full_one = tp_gather(layer_norm(inputs, gain_one, bias_one))
    packed = dot(full_one, jnp.concatenate([w_query, w_key, w_value], 1)).astype(BF)
    self_mix, self_lse = self_forward(packed)
    after_attn = inputs + tp_reduce(dot(self_mix, w_out, NT))
    full_two = tp_gather(layer_norm(after_attn, gain_two, bias_two))
    queries = dot(full_two, c_query).astype(BF)
    w_text = jnp.concatenate([c_key, c_value], 1)
    keys = dot(text, w_text).astype(BF)
    cross_mix, cross_lse = cross_forward(queries, keys, ids, captions)
    after_cross = after_attn + tp_reduce(dot(cross_mix, c_out, NT))
    full_three = tp_gather(layer_norm(after_cross, gain_three, bias_three))
    full_cot = tp_gather(cot)
    gin_low, gout_low, *sums = feed(full_three, full_cot, in_low, out_low, None)
    gin_high, gout_high, out_sum, back_sum = feed(full_three, full_cot, in_high, out_high, sums)
    low_grads = give([gin_low, gout_low])
    high_grads = give([gin_high, gout_high])
    result = to_rows((after_cross + tp_reduce(out_sum)).astype(BF))

    back_three, dgain_three, dbias_three = norm_back(after_cross, gain_three, tp_reduce(back_sum))
    grad_cross = cot.astype(F32) + back_three
    full_grad = tp_gather(grad_cross.astype(BF))
    mix_grad = dot(full_grad, c_out).astype(BF)
    dq, dk, dv = cross_backward(queries, keys, cross_mix, mix_grad, cross_lse, ids, captions)
    back_sum = dot(dq, c_query, NT)
    dkv = jnp.concatenate([dk, dv], 1)
    cross_grads = give(
        [
            dot(full_two, dq, TN).astype(BF),
            dot(text, dk, TN).astype(BF),
            dot(text, dv, TN).astype(BF),
            dot(full_grad, cross_mix, TN).astype(BF),
        ]
    )
    text_part = dot(dkv, w_text, NT).astype(BF).reshape(tops, lows, texts, width)
    if lows > 1:
        text_part = lax.psum_scatter(text_part, "lo", scatter_dimension=1, tiled=True)
    got = [part.astype(F32) for part in from_image(text_part[:, 0])]
    got = jnp.stack(got)
    got = [lax.dynamic_index_in_dim(got, top ^ slot, 0, False) for slot in range(tops)]
    text_grad = jnp.stack([got[i] + got[images + i] for i in range(images)])

    back_two, dgain_two, dbias_two = norm_back(after_attn, gain_two, tp_reduce(back_sum))
    grad_attn = grad_cross + back_two
    full_grad = tp_gather(grad_attn.astype(BF))
    mix_grad = dot(full_grad, w_out).astype(BF)
    dq, dk, dv = self_backward(packed, self_mix, mix_grad, self_lse)
    dqkv = jnp.concatenate([dq, dk, dv], 1)
    dwqkv = dot(full_one, dqkv, TN).astype(BF)
    span = dq.shape[1]
    self_grads = give(
        [
            dwqkv[:, :span],
            dwqkv[:, span : 2 * span],
            dwqkv[:, 2 * span :],
            dot(full_grad, self_mix, TN).astype(BF),
        ]
    )
    back_sum = dot(dqkv, jnp.concatenate([w_query, w_key, w_value], 1), NT)
    back_one, dgain_one, dbias_one = norm_back(inputs, gain_one, tp_reduce(back_sum))
    input_grad = to_rows((grad_attn + back_one).astype(BF)).astype(F32)

    norm_sums = lax.psum(
        jnp.stack([dgain_one, dbias_one, dgain_two, dbias_two, dgain_three, dbias_three]),
        ("chip", "core", "hi", "lo"),
    )
    norm_sums = lax.dynamic_slice_in_dim(norm_sums, (chip * 2 + core) * shard, shard, 1)

    feeds = [
        jnp.concatenate([low_grads[i][0], high_grads[i][0], low_grads[i][1], high_grads[i][1]], 1)
        for i in range(2)
    ]
    joined = [jnp.concatenate(pair, 1) for pair in (*self_grads, *cross_grads)]
    return (result, input_grad, text_grad, *joined, *feeds, *[norm_sums[i] for i in range(6)])


BLOCK = 256
ANY = pl.BlockSpec(memory_space=pl.ANY)
HBM = pl.BlockSpec(memory_space=pltpu.HBM)
SMEM = pl.BlockSpec(memory_space=pltpu.SMEM)
VMEM = pl.BlockSpec(memory_space=pltpu.VMEM)
LATE, ROWS = object(), object()
MIB = 1024 * 1024


def like(*shape, dtype=BF):
    return jax.ShapeDtypeStruct(shape, dtype)


class Late:
    def __init__(self, source, target, sems, chunks=1):
        self.ref, self.rows, self.waited = target, target.shape[0] // chunks, [False] * chunks
        self.copies = []
        for i in range(chunks):
            part = slice(i * self.rows, (i + 1) * self.rows)
            self.copies.append(pltpu.make_async_copy(source.at[part], target.at[part], sems.at[i]))

    def start(self, chunk):
        self.copies[chunk].start()

    def need(self, row):
        chunk = row // self.rows
        if not self.waited[chunk]:
            self.copies[chunk].wait()
            self.waited[chunk] = True
        return self.ref

    def ready(self):
        for chunk in range(len(self.copies)):
            self.need(chunk * self.rows)
        return self.ref


def start_chunks(loads):
    for chunk in range(max((len(load.copies) for load in loads), default=0)):
        for load in loads:
            if chunk < len(load.copies):
                load.start(chunk)


class Early:
    def __init__(self, source, target, sem):
        self.ref, self.copy, self.sent = source, pltpu.make_async_copy(source, target, sem), False

    def send(self):
        self.copy.start()
        self.sent = True


def call_overlapped(body, outs, ins, operands, scratch=(), limit=60):
    late_ins = [i for i, spec in enumerate(ins) if spec in (LATE, ROWS)]
    late_outs = [i for i, (spec, _) in enumerate(outs) if spec is LATE]
    buffers = [pltpu.VMEM(operands[i].shape, operands[i].dtype) for i in late_ins]
    buffers += [pltpu.VMEM(outs[i][1].shape, outs[i][1].dtype) for i in late_outs]
    count = len(buffers)

    def wrapped(*refs):
        refs = list(refs)
        sems, load_sems = refs.pop(), refs.pop()
        extra = refs[len(refs) - count :]
        refs = refs[: len(refs) - count]
        loads = [
            Late(refs[i], extra[n], load_sems.at[n], 4 if ins[i] is ROWS else 1)
            for n, i in enumerate(late_ins)
        ]
        start_chunks([load for load in loads if len(load.copies) > 1])
        start_chunks([load for load in loads if len(load.copies) == 1])
        for load, i in zip(loads, late_ins):
            refs[i] = load
        stores = []
        for n, i in enumerate(late_outs):
            place = len(ins) + i
            stores.append(Early(extra[len(late_ins) + n], refs[place], sems.at[n]))
            refs[place] = stores[-1]
        body(*refs)
        for load in loads:
            load.ready()
        for store in stores:
            if not store.sent:
                store.send()
        for store in stores:
            store.copy.wait()

    return call(
        wrapped,
        [(HBM if spec is LATE else spec, shape) for spec, shape in outs],
        [ANY if spec in (LATE, ROWS) else spec for spec in ins],
        operands,
        [
            *scratch,
            *buffers,
            pltpu.SemaphoreType.DMA((max(len(late_ins), 1), 4)),
            pltpu.SemaphoreType.DMA((max(len(late_outs), 1),)),
        ],
        limit,
    )


def call(body, outs, ins, operands, scratch=(), limit=24, grid=None, flops=0, moved=0):
    single = not isinstance(outs, (list, tuple))
    extra = {} if grid is None else {"grid": grid}
    cost = pl.CostEstimate(flops=1, bytes_accessed=1, transcendentals=0)
    out_specs, out_shape = ([outs[0]], [outs[1]]) if single else ([o[0] for o in outs], [o[1] for o in outs])
    return list(pl.pallas_call(
        body,
        in_specs=ins,
        out_specs=out_specs,
        out_shape=out_shape,
        scratch_shapes=list(scratch),
        compiler_params=pltpu.CompilerParams(vmem_limit_bytes=limit * MIB),
        cost_estimate=cost,
        **extra,
    )(*operands))


def run_copies(copies, sems):
    started = [pltpu.make_async_copy(source, target, sems.at[i]) for i, (source, target) in enumerate(copies)]
    for copy in started:
        copy.start()
    for copy in started:
        copy.wait()


def at(offset, count, unit=128):
    return pl.ds(pl.multiple_of(offset, unit), count)


def prepare_kernel(place, norms, wq, wk, wv, wo, cq, ck, cv, co, win, wout, keep, sent, sems):
    core = place[1]
    copies = []
    for target, which in ((sent, 1 - core), (keep, core)):
        for group, weights in enumerate(((wq, wk, wv, wo), (cq, ck, cv, co))):
            for one, weight in enumerate(weights):
                copies.append(
                    (
                        weight.at[:, at(which * 128, 128)],
                        target.at[group * 128 : (group + 1) * 128, one * 128 : (one + 1) * 128],
                    )
                )
        for part in range(2):
            for one, weight in enumerate((win, wout)):
                copies.append(
                    (
                        weight.at[:, at(which * 512 + part * 256, 256)],
                        target.at[256 + part * 128 : 384 + part * 128, one * 256 : (one + 1) * 256],
                    )
                )
        rows = jnp.concatenate([norms[...], jnp.zeros((10, 128), F32)], 0).astype(BF)
        target[512:528, :] = jnp.concatenate([rows] * 4, 1)
    run_copies(copies, sems)


def prepare(place, norms, weights):
    return call(
        prepare_kernel,
        [(VMEM, like(528, 512))] * 2,
        [SMEM, VMEM] + [ANY] * 10,
        (place, norms, *weights),
        [pltpu.SemaphoreType.DMA((24,))],
    )


def prepare_rows_kernel(place, ids, image, text, cot, *outs):
    rows_keep, rows_sent, cot_keep, cot_sent, text_pair, sems = outs
    core = place[1]
    copies = []
    for target, cots, which in ((rows_sent, cot_sent, 1 - core), (rows_keep, cot_keep, core)):
        for one in range(2):
            copies.append((image.at[one, at(which * 128, 128), :], target.at[one]))
            copies.append((cot.at[one, at(which * 128, 128), :], cots.at[one]))
    for one in range(2):
        copies.append((text.at[one], text_pair.at[one, 0:32, :]))
        row = jnp.concatenate([ids[one : one + 1, :].astype(F32), jnp.zeros((1, 896), F32)], 1)
        text_pair[one, 32:48, :] = jnp.concatenate([row] * 16, 0).astype(BF)
    run_copies(copies, sems)


def prepare_rows(place, ids, image, text, cot):
    return call(
        prepare_rows_kernel,
        [(VMEM, like(2, 128, 1024))] * 4 + [(VMEM, like(2, 48, 1024))],
        [SMEM, VMEM] + [ANY] * 3,
        (place, ids, image, text, cot),
        [pltpu.SemaphoreType.DMA((10,))],
    )


def pick_kernel(place, keep, taken, *outs):
    core, top = place[1], place[2]
    for step, out in enumerate(outs):
        image = (top + 4 - step) % 4

        @pl.when(image // 2 == core)
        def _():
            out[...] = keep[image % 2]

        @pl.when(image // 2 != core)
        def _():
            out[...] = taken[image % 2]


def pick(place, keep, taken):
    return call(
        pick_kernel,
        [(VMEM, like(*keep.shape[1:]))] * 4,
        [SMEM, VMEM, VMEM],
        (place, keep, taken),
    )


def join_kernel(place, keep, taken, *refs):
    singles, near, sems = refs[:4], refs[4], refs[5]
    copies = []
    for half, source in enumerate((keep, taken)):
        core = place[1] ^ half
        for group in range(4):
            part = source.at[group * 128 : (group + 1) * 128, :]
            copies.append((part, singles[group].at[at(core * 128, 128), :]))
        copies.append((source.at[0:128, :], near.at[at(core * 128, 128), :]))
        copies.append((source.at[512:528, :], near.at[at(256 + core * 16, 16, 16), :]))
    run_copies(copies, sems)


def join(place, keep, taken):
    return call(
        join_kernel,
        [(VMEM, like(256, 512))] * 4 + [(VMEM, like(288, 512))],
        [SMEM] + [ANY] * 2,
        (place, keep, taken),
        [pltpu.SemaphoreType.DMA((12,))],
    )


def stack_kernel(*refs):
    *parts, whole, sems = refs
    copies, low = [], 0
    for part in parts:
        copies.append((part, whole.at[low : low + part.shape[0]]))
        low += part.shape[0]
    run_copies(copies, sems)


def stack(parts):
    rows = sum(part.shape[0] for part in parts)
    return call(
        stack_kernel,
        [(VMEM, like(rows, *parts[0].shape[1:]))],
        [ANY] * len(parts),
        parts,
        [pltpu.SemaphoreType.DMA((len(parts),))],
    )[0]


def join_pieces_kernel(place, *refs):
    pieces, whole, sems = refs[:4], refs[4], refs[5]
    run_copies([(piece, whole.at[i]) for i, piece in enumerate(pieces)], sems)


def join_pieces(place, pieces):
    return call(
        join_pieces_kernel,
        [(VMEM, like(4, *pieces[0].shape))],
        [SMEM] + [ANY] * 4,
        (place, *pieces),
        [pltpu.SemaphoreType.DMA((4,))],
    )[0]


def arrange_kernel(place, *refs):
    messages, text, sems = refs[:4], refs[4], refs[5]
    run_copies(
        [(m.at[0:32, :], text.at[at((place[2] + i) % 4 * 32, 32, 32), :]) for i, m in enumerate(messages)], sems
    )


def arrange(place, messages):
    return call(
        arrange_kernel,
        [(VMEM, like(128, 1024))],
        [SMEM] + [ANY] * 4,
        (place, *messages),
        [pltpu.SemaphoreType.DMA((4,))],
    )[0]


def started(pairs, sems):
    copies = [pltpu.make_async_copy(source, target, sems.at[i]) for i, (source, target) in enumerate(pairs)]
    for copy in copies:
        copy.start()
    return copies


def wait_all(copies):
    for copy in copies:
        copy.wait()


def first_pieces(place, near, far, buffer, norms):
    chip, top = place[0], place[2]
    weights, rows = [], []
    for source in range(4):
        for half in range(2):
            row = at((chip ^ source) * 256 + half * 128, 128)
            piece, first = (near[source], half * 128) if source < 3 else (near[3 + half], 0)
            weights.append((piece.at[first : first + 128, :], buffer.at[row, at(top * 512, 512, 512)]))
            low = 256 + half * 16 if source < 3 else 128 + half * 16
            piece = near[source] if source < 3 else near[4]
            column = at((chip ^ source) * 256 + half * 128, 128)
            rows.append((piece.at[low : low + 16, 0:128], norms.at[:, column]))
            for step in range(3):
                first = step * 256 + half * 128
                piece = far[source] if source < 3 else far[3 + first // 384]
                first = first if source < 3 else first % 384
                columns = at((top + 1 + step) % 4 * 512, 512, 512)
                weights.append((piece.at[first : first + 128, :], buffer.at[row, columns]))
    return weights, rows


def later_pieces(place, pieces, buffer):
    groups = (pieces[:1], pieces[1:-3], pieces[-3:-2], pieces[-2:])
    chip = place[0]
    weights = []
    for source, parts in enumerate(groups):
        for top in range(4):
            part, each = parts[top * len(parts) // 4], 4 // len(parts)
            rows, columns = at((chip ^ source) * 256, 256), slice(top * 512, (top + 1) * 512)
            weights.append((part.at[top % each], buffer.at[rows, columns]))
    return weights


def norm_row(norms, one):
    return norms[one : one + 1, :].astype(F32)


def normalized(values, gain, bias):
    center = values - jnp.mean(values, -1, keepdims=True)
    inverse = lax.rsqrt(jnp.mean(center * center, -1, keepdims=True) + EPS)
    return (center * inverse * gain + bias).astype(BF)


def columns_of(weights, one, count=128):
    return jnp.concatenate([weights[:, s * 512 + one * count : s * 512 + (one + 1) * count] for s in range(4)], 1)


def project_into(target, rows, weights, dims=NN, step=512):
    count = weights.shape[0] if dims == NT else weights.shape[1]
    for low in range(0, count, step):
        part = weights[low : low + step, :] if dims == NT else weights[:, low : low + step]
        target[:, low : low + step] = dot(rows, part, dims).astype(target.dtype)


def image_blocks(place, own, other):
    core, top = place[1], place[2]
    for number in range(4):
        yield (top + number) % 4 * 256 + core * 128, own, number
        yield (top + number) % 4 * 256 + (1 - core) * 128, other, number


def one_head(values, head):
    return jnp.where(lane_head((1, 2 * HD), 1, head), values, jnp.zeros_like(values))


def both_heads(values):
    return jnp.concatenate([one_head(values, 0), one_head(values, 1)], 0)


def pick_heads(values):
    count = values.shape[1] // 2
    return jnp.where(lane_head((128, 1), 0, 0), values[:, :count], values[:, count:]).T


def causal_pair(count):
    rows = lax.broadcasted_iota(jnp.int32, (count, 2 * count), 0)
    columns = lax.broadcasted_iota(jnp.int32, (count, 2 * count), 1)
    return rows <= jnp.where(columns >= count, columns - count, columns)


def twice(row):
    return jnp.concatenate([row, row], 1)


def softmax_mix(scores, values):
    scale = LOG2E * HD**-0.5
    peak = jnp.max(scores[0], 0, keepdims=True)
    for part in scores[1:]:
        peak = jnp.maximum(peak, jnp.max(part, 0, keepdims=True))
    total, mixed = 0.0, 0.0
    for part, rows in zip(scores, values):
        weights = jnp.exp2((part - peak) * scale)
        total = total + jnp.sum(weights, 0, keepdims=True)
        mixed = mixed + dot(rows, weights.astype(BF), TN)
    return mixed / total, peak * scale + jnp.log2(total)


def causal_mask():
    return lax.broadcasted_iota(jnp.int32, (BLOCK, BLOCK), 0) <= lax.broadcasted_iota(
        jnp.int32, (BLOCK, BLOCK), 1
    )


def self_fwd_kernel(place, own, other, *refs):
    near, far = refs[:5], refs[5:10]
    whole, norms, normed, qkv, mix, lse, part, weights, loads, store = refs[10:]
    pieces, rows = first_pieces(place, near, far, weights, norms)
    copies = started(rows + pieces, loads)
    wait_all(copies[: len(rows)])
    gain, bias = norm_row(norms, 0), norm_row(norms, 1)
    for row, half, number in image_blocks(place, own, other):
        normed[at(row, 128), :] = normalized(half[number].astype(F32), gain, bias)
    wait_all(copies[len(rows) :])
    (stored,) = started([(weights, whole)], store)
    for one in range(3):
        qkv[:, one * 512 : (one + 1) * 512] = dot(normed[...], columns_of(weights, one)).astype(BF)
    causal = causal_pair(512)

    def pair_step(pair, carry):
        lanes = at(pair * 128, 128)
        k_lanes, v_lanes = at(512 + pair * 128, 128), at(1024 + pair * 128, 128)
        for low in range(0, 1024, 512):
            high = low + 512
            both = both_heads(qkv[low:high, lanes])
            scores = [jnp.where(causal, dot(qkv[low:high, k_lanes], both, NT), NEG)]
            values = [qkv[low:high, v_lanes]]
            if low:
                scores.append(dot(qkv[:low, k_lanes], both, NT))
                values.append(qkv[:low, v_lanes])
            mixed, logsum = softmax_mix(scores, values)
            for head in range(2):
                lse[pair, head : head + 1, low:high] = logsum[:, head * 512 : (head + 1) * 512]
            mix[low:high, lanes] = pick_heads(mixed).astype(BF)
        return carry

    lax.fori_loop(0, 4, pair_step, 0)
    project_into(part, mix[...], columns_of(weights, 3), NT)
    stored.wait()


def fused_self_forward(place, own, other, near, far):
    return call(
        self_fwd_kernel,
        [
            (HBM, like(1024, 2048)),
            (VMEM, like(16, 1024)),
            (VMEM, like(1024, 1024)),
            (VMEM, like(1024, 1536)),
            (VMEM, like(1024, 512)),
            (VMEM, like(4, 2, 1024, dtype=F32)),
            (VMEM, like(1024, 1024)),
        ],
        [SMEM, VMEM, VMEM] + [ANY] * 10,
        (place, own, other, *near, *far),
        [pltpu.VMEM((1024, 2048), BF), pltpu.SemaphoreType.DMA((40,)), pltpu.SemaphoreType.DMA((1,))],
        limit=60,
    )


def cross_fwd_kernel(
    place, own, other, mine_in, theirs_in, norms, text, ids, caption, *refs
):
    pieces = refs[:5]
    whole, after, normed, queries, keys, mix, lse, part, weights, mine, theirs, loads, store, row_sems = refs[5:]
    late = [
        Late(source, target, row_sems.at[i], 4)
        for i, (source, target) in enumerate(((mine_in, mine), (theirs_in, theirs)))
    ]
    start_chunks(late)
    copies = started(later_pieces(place, pieces, weights), loads)
    gain, bias = norm_row(norms, 2), norm_row(norms, 3)
    core, top = place[1], place[2]
    for block in range(4):
        for load in late:
            load.need(block * 256)
        for half, which in ((own, core), (other, 1 - core)):
            rows = at(block * 256 + which * 128, 128)
            values = half[(block + 4 - top) % 4].astype(F32)
            values = values + (mine[rows, :].astype(F32) + theirs[rows, :].astype(F32))
            after[rows, :] = values
            normed[rows, :] = normalized(values, gain, bias)
    wait_all(copies)
    (stored,) = started([(weights, whole)], store)
    project_into(queries, normed[...], columns_of(weights, 0))
    w_text = jnp.concatenate([columns_of(weights, 1), columns_of(weights, 2)], 1)
    keys[...] = dot(text[...], w_text).astype(BF)

    def pair_step(pair, carry):
        lanes, v_lanes = at(pair * 128, 128), at(512 + pair * 128, 128)
        seen = twice(ids[...] == caption[...])
        scores = jnp.where(seen, dot(keys[:, lanes], both_heads(queries[:, lanes]), NT), NEG)
        mixed, logsum = softmax_mix([scores], [keys[:, v_lanes]])
        for head in range(2):
            lse[pair, head : head + 1, :] = logsum[:, head * 1024 : (head + 1) * 1024]
        mix[:, lanes] = pick_heads(mixed).astype(BF)
        return carry

    lax.fori_loop(0, 4, pair_step, 0)
    project_into(part, mix[...], columns_of(weights, 3), NT)
    stored.wait()


def fused_cross_forward(place, own, other, mine, theirs, norms, text, ids, caption, pieces):
    return call(
        cross_fwd_kernel,
        [
            (HBM, like(1024, 2048)),
            (VMEM, like(1024, 1024, dtype=F32)),
            (VMEM, like(1024, 1024)),
            (VMEM, like(1024, 512)),
            (VMEM, like(128, 1024)),
            (VMEM, like(1024, 512)),
            (VMEM, like(4, 2, 1024, dtype=F32)),
            (VMEM, like(1024, 1024)),
        ],
        [SMEM, VMEM, VMEM, ANY, ANY] + [VMEM] * 4 + [ANY] * 5,
        (place, own, other, mine, theirs, norms, text, ids, caption, *pieces),
        [pltpu.VMEM((1024, 2048), BF)]
        + [pltpu.VMEM((1024, 1024), BF)] * 2
        + [pltpu.SemaphoreType.DMA((16,)), pltpu.SemaphoreType.DMA((1,)), pltpu.SemaphoreType.DMA((2, 4))],
        limit=60,
    )


def cut_grads(place, grads, columns, own, side, over, low, high):
    chip = place[0]
    own[:, columns] = grads[at(chip * 256, 256), :].astype(BF)
    side[:, columns] = grads[at((chip ^ 1) * 256, 256), :].astype(BF)
    over[:, columns] = grads[at((chip ^ 2) * 256, 256), :].astype(BF)
    low[:, columns] = grads[at((chip ^ 3) * 256, 128), :].astype(BF)
    high[:, columns] = grads[at((chip ^ 3) * 256 + 128, 128), :].astype(BF)


GRAD_SHAPES = [(256, 2048)] * 3 + [(128, 2048)] * 2


def feed_step(rows, cot, rows_t, cot_t, weights, out_sum, back_sum, grads):
    w_in = jnp.concatenate([weights[0][:, :256], weights[1][:, :256]], 1)
    w_out = jnp.concatenate([weights[0][:, 256:], weights[1][:, 256:]], 1)
    slope = math.sqrt(2.0 / math.pi)
    pre = dot(rows[...], w_in)
    square = pre * pre
    bent = jnp.tanh(pre * (slope + slope * 0.044715 * square))
    half = 0.5 * (1.0 + bent)
    act = (pre * half).astype(BF)
    bend = half + pre * (0.5 * (1.0 - bent * bent)) * (slope + 3.0 * slope * 0.044715 * square)
    pre_grad = (dot(cot[...], w_out) * bend).astype(BF)
    for low in range(0, 1024, 512):
        part = slice(low, low + 512)
        out_sum[:, part] += dot(act, w_out[part, :], NT)
        back_sum[:, part] += dot(pre_grad, w_in[part, :], NT)
    for block in range(2):
        part = slice(block * 256, (block + 1) * 256)
        grads[:, block * 512 : block * 512 + 256] = dot(rows_t[...], pre_grad[:, part])
        grads[:, block * 512 + 256 : (block + 1) * 512] = dot(cot_t[...], act[:, part])


def feed_first_kernel(
    place, after_in, mine_in, theirs_in, norms, cot_own, cot_other, *refs
):
    pieces = refs[:6]
    g_whole, after_out, normed_out, cot_out, out_sum, back = refs[6:12]
    after_cross, normed, cot, back_sum, rows_t, cot_t, grads, weights, after, mine, theirs, sems, loads, row_sems = refs[12:]
    step = pl.program_id(0)
    pairs = ((after_cross, after_out), (normed, normed_out), (cot, cot_out))
    stores = [pltpu.make_async_copy(a, b, sems.at[i]) for i, (a, b) in enumerate(pairs)]

    @pl.when(step == 0)
    def _():
        arrays = ((after_in, after), (mine_in, mine), (theirs_in, theirs))
        late = [Late(source, target, row_sems.at[i], 4) for i, (source, target) in enumerate(arrays)]
        start_chunks(late)
        copies = started(later_pieces(place, pieces, weights), loads)
        gain, bias = norm_row(norms, 4), norm_row(norms, 5)
        for low in range(0, 1024, 128):
            for load in late:
                load.need(low)
            rows = slice(low, low + 128)
            values = after[rows, :] + (mine[rows, :].astype(F32) + theirs[rows, :].astype(F32))
            after_cross[rows, :] = values
            normed[rows, :] = normalized(values, gain, bias)
        for row, half, number in image_blocks(place, cot_own, cot_other):
            cot[at(row, 128), :] = half[number]
        for store in stores:
            store.start()
        rows_t[...] = normed[...].T
        cot_t[...] = cot[...].T
        out_sum[...] = jnp.zeros_like(out_sum)
        for block in range(4):
            rows = at(block * 256 + place[1] * 128, 128)
            out_sum[rows, :] = after_cross[rows, :]
        back_sum[...] = jnp.zeros_like(back_sum)
        wait_all(copies)

    blocks = [weights[:, at(step * 1024 + block * 512, 512, 512)] for block in range(2)]
    feed_step(normed, cot, rows_t, cot_t, blocks, out_sum, back_sum, grads)
    for chip in range(4):
        for block in range(2):
            part = grads[chip * 256 : (chip + 1) * 256, block * 512 : (block + 1) * 512]
            g_whole[chip, block] = part.astype(BF)

    @pl.when(step == 1)
    def _():
        back[...] = back_sum[...].astype(BF)
        for store in stores:
            store.wait()


def feed_second_kernel(
    place, normed, cot, out_in, back_in, weights,
    g_own, g_side, g_over, g_low, g_high, out_keep, out_sent, back, out_sum, back_sum, rows_t, cot_t, grads,
):
    step, core = pl.program_id(0), place[1]

    @pl.when(step == 0)
    def _():
        rows_t[...] = normed[...].T
        cot_t[...] = cot[...].T
        out_sum[...] = out_in[...]
        back_sum[...] = back_in[...].astype(F32)

    blocks = [weights[:, block].reshape(1024, 512) for block in range(2)]
    feed_step(normed, cot, rows_t, cot_t, blocks, out_sum, back_sum, grads)
    cut_grads(place, grads, slice(None), g_own, g_side, g_over, g_low, g_high)

    @pl.when(step == 1)
    def _():
        back[...] = back_sum[...].astype(BF)
        for block in range(4):
            out_keep[block] = out_sum[at(block * 256 + core * 128, 128), :]
            out_sent[block] = out_sum[at(block * 256 + (1 - core) * 128, 128), :].astype(BF)


def once(*shape):
    zeros = (0,) * len(shape)
    return pl.BlockSpec(shape, lambda i: zeros, pipeline_mode=pl.Buffered(1))


def grad_outs(width=512):
    return [(pl.BlockSpec((rows, width), lambda i: (0, i)), like(rows, n)) for rows, n in GRAD_SHAPES]


FEED_FLOPS = 13 * 2**30


def feed_first(place, after, mine, theirs, norms, cot_own, cot_other, pieces):
    square = once(1024, 1024)
    return call(
        feed_first_kernel,
        [(pl.BlockSpec((4, 2, 256, 512), lambda i: (0, i, 0, 0)), like(4, 4, 256, 512))]
        + [
            (HBM, like(1024, 1024, dtype=F32)),
            (HBM, like(1024, 1024)),
            (HBM, like(1024, 1024)),
            (square, like(1024, 1024, dtype=F32)),
            (square, like(1024, 1024)),
        ],
        [SMEM, ANY, ANY, ANY, once(16, 1024), once(4, 128, 1024), once(4, 128, 1024)]
        + [ANY] * 6,
        (place, after, mine, theirs, norms, cot_own, cot_other, *pieces),
        [pltpu.VMEM((1024, 1024), F32)]
        + [pltpu.VMEM((1024, 1024), BF)] * 2
        + [pltpu.VMEM((1024, 1024), F32)]
        + [pltpu.VMEM((1024, 1024), BF)] * 2
        + [pltpu.VMEM((1024, 1024), F32), pltpu.VMEM((1024, 2048), BF)]
        + [pltpu.VMEM((1024, 1024), F32), pltpu.VMEM((1024, 1024), BF), pltpu.VMEM((1024, 1024), BF)]
        + [pltpu.SemaphoreType.DMA((3,)), pltpu.SemaphoreType.DMA((16,)), pltpu.SemaphoreType.DMA((3, 4))],
        grid=(2,),
        flops=FEED_FLOPS,
        moved=30 * MIB,
        limit=60,
    )


def feed_second(place, normed, cot, out_in, back_in, weights):
    square = once(1024, 1024)
    return call(
        feed_second_kernel,
        grad_outs(1024)
        + [
            (once(4, 128, 1024), like(4, 128, 1024, dtype=F32)),
            (once(4, 128, 1024), like(4, 128, 1024)),
            (square, like(1024, 1024)),
        ],
        [SMEM, square, square, square, square, pl.BlockSpec((4, 2, 256, 512), lambda i: (0, i, 0, 0))],
        (place, normed, cot, out_in, back_in, weights),
        [pltpu.VMEM((1024, 1024), F32)] * 2
        + [pltpu.VMEM((1024, 1024), BF)] * 2
        + [pltpu.VMEM((1024, 1024), F32)],
        grid=(2,),
        flops=FEED_FLOPS,
        moved=26 * MIB,
        limit=60,
    )


def norm_backward(values, gain, grad):
    center = values - jnp.mean(values, -1, keepdims=True)
    inverse = lax.rsqrt(jnp.mean(center * center, -1, keepdims=True) + EPS)
    hat = center * inverse
    scaled = grad * gain
    back = inverse * (
        scaled - jnp.mean(scaled, -1, keepdims=True) - hat * jnp.mean(scaled * hat, -1, keepdims=True)
    )
    return back, grad * hat


def norm_block(values_of, mine, theirs, base_of, gain, norms, keep):
    gain = norm_row(*gain)
    gain_sum, bias_sum = jnp.zeros((8, 1024), F32), jnp.zeros((8, 1024), F32)
    for low in range(0, 1024, 128):
        rows = slice(low, low + 128)
        grad = mine.need(low)[rows, :].astype(F32) + theirs.need(low)[rows, :].astype(F32)
        back, term = norm_backward(values_of(rows), gain, grad)
        keep(rows, base_of(rows) + back)
        gain_sum = gain_sum + jnp.sum(term.reshape(16, 8, 1024), 0)
        bias_sum = bias_sum + jnp.sum(grad.reshape(16, 8, 1024), 0)
    norms[0:1, :] = jnp.sum(gain_sum, 0, keepdims=True)
    norms[1:2, :] = jnp.sum(bias_sum, 0, keepdims=True)


def pair_row(lse, pair, low, high):
    return jnp.concatenate([lse[pair, 0:1, low:high], lse[pair, 1:2, low:high]], 1)


def pair_delta(grad, mix):
    product = (grad.astype(F32) * mix.astype(F32)).T
    return jnp.concatenate([jnp.sum(product[:HD], 0, keepdims=True), jnp.sum(product[HD:], 0, keepdims=True)], 1)


def head_grads(keys, values, one, one_grad, lse, delta, mask):
    weights = jnp.exp2(dot(keys, one, NT) * (LOG2E * HD**-0.5) - lse)
    if mask is not None:
        weights = jnp.where(mask, weights, 0.0)
    slope = dot(values, one_grad, NT)
    return weights.astype(BF), (weights * (slope - delta)).astype(BF)


def cross_bwd_kernel(
    place, after, mine, theirs, cot, gain, weights, normed, text, queries, keys, mix, lse, ids, caption,
    grad_out, part_out, norms, text_part, g_own, g_side, g_over, g_low, g_high, low_grad, mix_grad, dq, dkv, grads,
):
    grad_cross, part = grad_out.ref, part_out.ref

    def keep(rows, value):
        grad_cross[rows, :] = value
        low_grad[rows, :] = value.astype(BF)

    norm_block(lambda rows: after.need(rows.start)[rows, :], mine, theirs, lambda rows: cot.need(rows.start)[rows, :].astype(F32), (gain, 4), norms, keep)
    grad_out.send()
    weights, queries, keys, mix = weights.ready(), queries.ready(), keys.ready(), mix.ready()
    project_into(mix_grad, low_grad[...], columns_of(weights, 3))

    def pair_step(pair, carry):
        lanes, v_lanes = at(pair * 128, 128), at(512 + pair * 128, 128)
        query, grad = both_heads(queries[:, lanes]), both_heads(mix_grad[:, lanes])
        prob, score_grad = head_grads(
            keys[:, lanes],
            keys[:, v_lanes],
            query,
            grad,
            pair_row(lse, pair, 0, 1024),
            pair_delta(mix_grad[:, lanes], mix[:, lanes]),
            twice(ids[...] == caption[...]),
        )
        dv_sum, dk_sum = dot(prob, grad), dot(score_grad, query)
        dq[:, lanes] = (pick_heads(dot(keys[:, lanes], score_grad, TN)) * HD**-0.5).astype(BF)
        dkv[:, lanes] = (dk_sum * HD**-0.5).astype(BF)
        dkv[:, v_lanes] = dv_sum.astype(BF)
        return carry

    lax.fori_loop(0, 4, pair_step, 0)
    project_into(part, dq[...], columns_of(weights, 0), NT)
    part_out.send()
    normed = normed.ready()
    w_text = jnp.concatenate([columns_of(weights, 1), columns_of(weights, 2)], 1)
    text_part[...] = dot(dkv[...], w_text, NT).astype(BF)
    for one, (left, right) in enumerate(
        ((normed, dq[...]), (text, dkv[:, :512]), (text, dkv[:, 512:]), (low_grad, mix[...]))
    ):
        grads[...] = dot(left[...], right, TN)
        for s in range(4):
            columns = slice(s * 512 + one * 128, s * 512 + (one + 1) * 128)
            cut_grads(
                place, grads.at[:, s * 128 : (s + 1) * 128], columns, g_own, g_side, g_over, g_low, g_high
            )


def fused_cross_backward(place, after, mine, theirs, cot, gain, weights, normed, text, queries, keys, mix, lse, ids, caption):
    return call_overlapped(
        cross_bwd_kernel,
        [
            (LATE, like(1024, 1024, dtype=F32)),
            (LATE, like(1024, 1024)),
            (VMEM, like(8, 1024, dtype=F32)),
            (VMEM, like(128, 1024)),
        ]
        + [(VMEM, like(*shape)) for shape in GRAD_SHAPES],
        [SMEM] + [ROWS] * 4 + [VMEM] + [LATE, LATE, VMEM, LATE, LATE, LATE, VMEM, VMEM, VMEM],
        (place, after, mine, theirs, cot, gain, weights, normed, text, queries, keys, mix, lse, ids, caption),
        [
            pltpu.VMEM((1024, 1024), BF),
            pltpu.VMEM((1024, 512), BF),
            pltpu.VMEM((1024, 512), BF),
            pltpu.VMEM((128, 1024), BF),
            pltpu.VMEM((1024, 512), F32),
        ],
    )


def self_bwd_kernel(
    place, after, mine, theirs, base, gain, weights, qkv, mix, lse,
    grad_out, low_out, norms, dqkv, mix_grad, dk_sum, dv_sum,
):
    core = place[1]
    grad_own, low_grad = grad_out.ref, low_out.ref

    def keep(rows, value):
        low_grad[rows, :] = value.astype(BF)

        @pl.when(core == (rows.start // 128) % 2)
        def _():
            grad_own[rows.start // 256] = value

    norm_block(lambda rows: after.need(rows.start)[rows, :], mine, theirs, lambda rows: base.need(rows.start)[rows, :], (gain, 2), norms, keep)
    grad_out.send()
    low_out.send()
    weights, qkv, mix = weights.ready(), qkv.ready(), mix.ready()
    project_into(mix_grad, low_grad[...], columns_of(weights, 3))
    causal = causal_pair(512)

    def pair_step(pair, carry):
        lanes = at(pair * 128, 128)
        k_lanes, v_lanes = at(512 + pair * 128, 128), at(1024 + pair * 128, 128)
        for low in range(0, 1024, 512):
            high = low + 512
            query, grad = both_heads(qkv[low:high, lanes]), both_heads(mix_grad[low:high, lanes])
            delta = pair_delta(mix_grad[low:high, lanes], mix[low:high, lanes])
            logsum = pair_row(lse, pair, low, high)
            total = 0.0
            for start in range(0, high, 512):
                rows = slice(start, start + 512)
                keys = qkv[rows, k_lanes]
                prob, score_grad = head_grads(
                    keys, qkv[rows, v_lanes], query, grad, logsum, delta, causal if start == low else None
                )
                dv, dk = dot(prob, grad), dot(score_grad, query)
                if start == low:
                    dv_sum[rows, :], dk_sum[rows, :] = dv, dk
                else:
                    dv_sum[rows, :] += dv
                    dk_sum[rows, :] += dk
                total = total + dot(keys, score_grad, TN)
            dqkv[low:high, lanes] = (pick_heads(total) * HD**-0.5).astype(BF)
        dqkv[:, k_lanes] = (dk_sum[...] * HD**-0.5).astype(BF)
        dqkv[:, v_lanes] = dv_sum[...].astype(BF)
        return carry

    lax.fori_loop(0, 4, pair_step, 0)


def fused_self_backward(place, after, mine, theirs, base, gain, weights, qkv, mix, lse):
    return call_overlapped(
        self_bwd_kernel,
        [
            (LATE, like(4, 128, 1024, dtype=F32)),
            (LATE, like(1024, 1024)),
            (VMEM, like(8, 1024, dtype=F32)),
            (VMEM, like(1024, 1536)),
        ],
        [SMEM] + [ROWS] * 4 + [VMEM] + [LATE] * 3 + [VMEM],
        (place, after, mine, theirs, base, gain, weights, qkv, mix, lse),
        [pltpu.VMEM((1024, 512), BF), pltpu.VMEM((1024, 128), F32), pltpu.VMEM((1024, 128), F32)],
    )


def self_grads_kernel(place, normed, low_grad, dq, dk, dv, mix, g_own, g_side, g_over, g_low, g_high, rows_t, grad_t, grads):
    @pl.when(pl.program_id(0) == 0)
    def _():
        rows_t[...] = normed[...].T
        grad_t[...] = low_grad[...].T

    grads[:, :384] = dot(rows_t[...], jnp.concatenate([dq[...], dk[...], dv[...]], 1))
    grads[:, 384:] = dot(grad_t[...], mix[...])
    cut_grads(place, grads, slice(None), g_own, g_side, g_over, g_low, g_high)


def self_grads(place, normed, low_grad, dqkv, mix):
    square = once(1024, 1024)

    def cut(offset):
        return pl.BlockSpec((1024, 128), lambda i: (0, offset + i))

    return call(
        self_grads_kernel,
        grad_outs(),
        [SMEM, square, square, cut(0), cut(4), cut(8), cut(0)],
        (place, normed, low_grad, dqkv, dqkv, dqkv, mix),
        [pltpu.VMEM((1024, 1024), BF)] * 2 + [pltpu.VMEM((1024, 512), F32)],
        grid=(4,),
        flops=4 * 2**30,
        moved=12 * MIB,
        limit=36,
    )


def self_back_kernel(place, dqkv, weights, kept, sent):
    core = place[1]
    w_in = jnp.concatenate([columns_of(weights, one) for one in range(3)], 1)
    for target, half in ((sent, 1 - core), (kept, core)):
        rows = jnp.concatenate([dqkv[at(block * 256 + half * 128, 128), :] for block in range(4)], 0)
        for low in range(0, 1024, 512):
            value = dot(rows, w_in[low : low + 512, :], NT).astype(target.dtype)
            target[:, :, low : low + 512] = value.reshape(4, 128, 512)


def self_back(place, dqkv, weights):
    return call(
        self_back_kernel,
        [(VMEM, like(4, 128, 1024, dtype=F32)), (VMEM, like(4, 128, 1024))],
        [SMEM, VMEM, VMEM],
        (place, dqkv, weights),
        flops=3 * 2**30,
        moved=10 * MIB,
        limit=36,
    )


def last_norm_kernel(place, rows, grad_own, mine, theirs, gain, text_part, sums_two, sums_three, *pieces):
    gain_sum, bias_sum = jnp.zeros((8, 1024), F32), jnp.zeros((8, 1024), F32)
    for number in range(4):
        block = (place[2] + number) % 4
        grad = mine[block] + theirs[block].astype(F32)
        back, term = norm_backward(rows[number].astype(F32), norm_row(gain, 0), grad)
        pieces[-number % 4][0:128, :] = (grad_own[block] + back).astype(BF)
        pieces[-number % 4][128:160, :] = text_part[at(block * 32, 32, 32), :]
        gain_sum = gain_sum + jnp.sum(term.reshape(16, 8, 1024), 0)
        bias_sum = bias_sum + jnp.sum(grad.reshape(16, 8, 1024), 0)
    sums = [jnp.sum(gain_sum, 0, keepdims=True), jnp.sum(bias_sum, 0, keepdims=True)]
    sums += [0.5 * sums_two[0:2, :], 0.5 * sums_three[0:2, :], jnp.zeros((10, 1024), F32)]
    sums = jnp.concatenate(sums, 0).astype(BF)
    for piece in pieces:
        piece[160:176, :] = sums


def last_norm(place, rows, grad_own, mine, theirs, gain, text_part, sums_two, sums_three):
    return call(
        last_norm_kernel,
        [(VMEM, like(176, 1024))] * 4,
        [SMEM] + [VMEM] * 8,
        (place, rows, grad_own, mine, theirs, gain, text_part, sums_two, sums_three),
    )


def finish_kernel(place, out_keep, theirs, *pieces):
    for number, piece in enumerate(pieces):
        block = (place[2] + 4 - number) % 4
        piece[...] = (out_keep[block] + theirs[block].astype(F32)).astype(BF)


def finish(place, out_keep, theirs):
    return call(
        finish_kernel,
        [(VMEM, like(128, 1024))] * 4,
        [SMEM] + [VMEM] * 2,
        (place, out_keep, theirs),
    )


def part_kernel(place, *refs):
    pieces, mine, sent = refs[:4], refs[4], refs[5]
    core, top = place[1], place[2]
    for step, piece in enumerate(pieces):
        image = (top + step) % 4

        @pl.when(image // 2 == core)
        def _():
            mine[image % 2] = piece[...]

        @pl.when(image // 2 != core)
        def _():
            sent[image % 2] = piece[...]

    if pieces[0].shape[0] > 160:
        total = 0.0
        for piece in pieces:
            total = total + piece[160:176, :].astype(F32)
        mine[0, 160:176, :] = total.astype(BF)
        sent[0, 160:176, :] = total.astype(BF)


def part_images(place, pieces):
    return call(
        part_kernel,
        [(VMEM, like(2, *pieces[0].shape))] * 2,
        [SMEM] + [VMEM] * 4,
        (place, *pieces),
    )


def land_kernel(place, mine, taken, rows, *more):
    core = place[1]
    for one in range(2):
        rows[one, at(core * 128, 128), :] = mine[one, 0:128, :].astype(rows.dtype)
        rows[one, at((1 - core) * 128, 128), :] = taken[one, 0:128, :].astype(rows.dtype)
        if more:
            more[0][one] = mine[one, 128:160, :].astype(F32) + taken[one, 128:160, :].astype(F32)
    if more:
        more[1][...] = mine[0, 160:168, :].astype(F32) + taken[0, 160:168, :].astype(F32)


def land(place, mine, taken, dtype):
    outs = [(VMEM, like(2, 256, 1024, dtype=dtype))]
    if mine.shape[1] > 128:
        outs += [(VMEM, like(2, 32, 1024, dtype=F32)), (VMEM, like(8, 1024, dtype=F32))]
    return call(land_kernel, outs, [SMEM, VMEM, VMEM], (place, mine, taken))


def relay_kernel(over, side, from_side, from_over, to_over, to_side):
    to_over[0:128, :] = (over[0:128, :].astype(F32) + from_side[...].astype(F32)).astype(BF)
    to_over[128:256, :] = over[128:256, :]
    to_side[0:128, :] = side[0:128, :]
    to_side[128:256, :] = (side[128:256, :].astype(F32) + from_over[...].astype(F32)).astype(BF)


def relay(over, side, from_side, from_over):
    return call(
        relay_kernel,
        [(VMEM, like(256, 2048))] * 2,
        [VMEM] * 4,
        (over, side, from_side, from_over),
        moved=5 * MIB,
    )


def plane_sum_kernel(place, own, over, side, keep, *sent):
    for s in range(4):
        columns = at((place[2] + s) % 4 * 512, 512, 512)
        total = own[:, columns].astype(F32) + over[:, columns].astype(F32) + side[:, columns].astype(F32)
        if s:
            sent[s - 1][...] = total.astype(BF)
        else:
            keep[...] = total


def plane_sum(place, own, over, side):
    return call(
        plane_sum_kernel,
        [(VMEM, like(256, 512, dtype=F32))] + [(VMEM, like(256, 512))] * 3,
        [SMEM] + [VMEM] * 3,
        (place, own, over, side),
        moved=5 * MIB,
    )


def plane_sum_whole_kernel(own, over, side, whole):
    for step in range(4):
        columns = slice(step * 512, (step + 1) * 512)
        total = own[:, columns].astype(F32) + over[:, columns].astype(F32) + side[:, columns].astype(F32)
        whole[step * 256 : (step + 1) * 256, :] = total.astype(BF)


def plane_sum_whole(own, over, side):
    return call(
        plane_sum_whole_kernel,
        [(VMEM, like(1024, 512))],
        [VMEM] * 3,
        (own, over, side),
    )[0]


def line_sum_kernel(place, keep, one, two, three, mine, other):
    core = place[1]
    for target, half in ((other, 1 - core), (mine, core)):
        rows = at(half * 128, 128)
        total = keep[rows, :]
        for part in (one, two, three):
            total = total + part[rows, :].astype(F32)
        target[...] = total.astype(target.dtype)


def line_sum(place, keep, parts):
    return call(
        line_sum_kernel,
        [(VMEM, like(128, 512, dtype=F32)), (VMEM, like(128, 512))],
        [SMEM] + [VMEM] * 4,
        (place, keep, *parts),
        moved=2 * MIB,
    )


def spread_kernel(place, mine, other, *outs):
    core, columns = place[1], mine.shape[1] // len(outs)
    for one, out in enumerate(outs):
        cut = slice(one * columns, (one + 1) * columns)
        out[:, at(core * columns, columns)] = mine[:, cut].astype(F32)
        out[:, at((1 - core) * columns, columns)] = other[:, cut].astype(F32)


def spread(place, mine, other):
    return call(
        spread_kernel,
        [(VMEM, like(128, 256, dtype=F32))] * 4,
        [SMEM] + [VMEM] * 2,
        (place, mine, other),
        moved=MIB,
    )


def spread_feed_kernel(place, mine_one, other_one, mine_two, other_two, *outs):
    core = place[1]
    for part, (mine, other) in enumerate(((mine_one, other_one), (mine_two, other_two))):
        for one, out in enumerate(outs):
            cut = slice(one * 256, (one + 1) * 256)
            out[:, at(core * 512 + part * 256, 256)] = mine[:, cut].astype(F32)
            out[:, at((1 - core) * 512 + part * 256, 256)] = other[:, cut].astype(F32)


def spread_feed(place, *halves):
    return call(
        spread_feed_kernel,
        [(VMEM, like(128, 1024, dtype=F32))] * 2,
        [SMEM] + [VMEM] * 4,
        (place, *halves),
        moved=2 * MIB,
    )


tie = lax.optimization_barrier


def packed_layer(args):
    image_rows, text_rows, segment_ids, cotangent, *others = args
    weights, norms = others[:10], others[10:]
    chip, core, top = lax.axis_index("chip"), lax.axis_index("core"), lax.axis_index("hi")
    place = jnp.stack([chip, core, top, core * 2 + top % 2]).astype(jnp.int32)

    def swap(value):
        return lax.ppermute(value, "core", [(0, 1), (1, 0)])

    def across(value, bit):
        return lax.ppermute(value, "chip", [(i, i ^ bit) for i in range(4)])

    def shift(value, step):
        return lax.ppermute(value, "hi", [((i + step) % 4, i) for i in range(4)])

    def line(part):
        return [shift(part, step) for step in range(1, 4)]

    def exchange(pieces):
        return [pieces[0]] + [shift(piece, step) for step, piece in enumerate(pieces) if step]

    def gather_line(part):
        return lax.all_gather(part, "hi")

    def sides(value):
        return [across(value, 1), across(value, 2)]

    def corners(pair, cut):
        return [across(pair[0][:cut], 2), across(pair[1][cut:], 1)]

    def grad_corners(grads):
        return [across(grads[3], 1), across(grads[4], 2)]

    def grad_sides(grads, got, later):
        to_over, to_side, later = tie((*relay(grads[2], grads[1], *got), later))
        return [across(to_over, 2), across(to_side, 1)], later

    def halves(total):
        cut = total.reshape(2, 128, 512)
        sent = lax.dynamic_index_in_dim(cut, 1 - core, 0, False)
        return lax.dynamic_index_in_dim(cut, core, 0, False), swap(sent)

    keep, sent = prepare(place, jnp.stack(norms), weights)
    v = {"taken": swap(sent)}
    v["rows_keep"], v["rows_sent"], v["cot_keep"], v["cot_sent"], v["text_pair"] = prepare_rows(
        place, segment_ids, image_rows, text_rows, cotangent
    )
    v = tie(v)
    *v["singles"], v["near"] = join(place, keep, v.pop("taken"))
    v["rows_taken"], v["cot_taken"] = swap(v.pop("rows_sent")), swap(v.pop("cot_sent"))
    v["text_taken"] = swap(v["text_pair"])
    v = tie(v)

    v["near"] = [v["near"], *sides(v["near"])]
    lines = line(v["singles"][0])
    v["pieces"] = pick(place, v.pop("rows_keep"), v.pop("rows_taken"))
    v["cot_pieces"] = pick(place, v.pop("cot_keep"), v.pop("cot_taken"))
    v["text_pieces"] = pick(place, v.pop("text_pair"), v.pop("text_taken"))
    v = tie(v)
    v["near"] += corners(v["near"][1:], 128)
    v["line"] = lines
    v = tie(v)

    rest = stack(v.pop("line"))
    v["far_self"] = [rest, *sides(rest)]
    v["two_on"] = shift(v["pieces"][2], 2)
    line_cross = gather_line(v["singles"][1])
    v = tie(v)
    v["far_self"] += corners(v["far_self"][1:], 384)
    pieces = v.pop("pieces")
    v["pieces"] = [pieces[0], shift(pieces[1], 1), v.pop("two_on"), shift(pieces[3], 3)]
    v["line_cross"] = line_cross
    v = tie(v)
    v["rows_own"] = stack([piece[None] for piece in v.pop("pieces")])
    v["rows_other"] = swap(v["rows_own"])
    line_one = gather_line(v["singles"][2])
    v = tie(v)

    v["far_cross"] = sides(v["line_cross"])
    text_pieces, cot_pieces = v.pop("text_pieces"), v.pop("cot_pieces")
    v["text_near"] = [text_pieces[0], shift(text_pieces[1], 1), shift(text_pieces[3], 3)]
    v["text_two"], v["cot_two"] = text_pieces[2], shift(cot_pieces[2], 2)
    v["cot_near"] = [cot_pieces[0], cot_pieces[1], cot_pieces[3]]
    v["line_one"] = line_one
    v["w_self"], v["norms"], v["normed_one"], v["qkv"], v["self_mix"], v["self_lse"], v["mine"] = (
        fused_self_forward(place, v["rows_own"], v["rows_other"], v.pop("near"), v.pop("far_self"))
    )
    v = tie(v)

    v["theirs"] = swap(v["mine"])
    v["far_cross"] += corners(v["far_cross"], 2)
    line_two = gather_line(v.pop("singles")[3])
    text_near, text_two = v.pop("text_near"), shift(v.pop("text_two"), 2)
    text_pieces = [text_near[0], text_near[1], text_two, text_near[2]]
    v["text"] = arrange(place, text_pieces)
    ids = text_pieces[0][32, :128].astype(jnp.int32)
    v["caption"] = jnp.repeat(ids, 8)[None, :]
    v["ids"] = ids[:, None]
    v["one_low"], v["one_high"] = v["line_one"][:2], v["line_one"][2:]
    v = tie(v)

    low, high = v.pop("one_low"), v.pop("one_high")
    v["far_one"] = [across(low, 1), across(high, 1), across(v["line_one"], 2)]
    near, one_on, three_on = v.pop("cot_near")
    cot_pieces = [near, shift(one_on, 1), v.pop("cot_two"), shift(three_on, 3)]
    v["w_cross"], v["after_attn"], v["normed_two"], v["queries"], v["keys"], v["cross_mix"], v["cross_lse"], v["mine"] = (
        fused_cross_forward(
            place, v["rows_own"], v.pop("rows_other"), v["mine"], v["theirs"], v["norms"], v["text"], v["ids"],
            v["caption"], (v.pop("line_cross"), *v.pop("far_cross")),
        )
    )
    v["cot_own"] = join_pieces(place, cot_pieces)
    v["line_two"] = line_two
    v = tie(v)

    v["theirs"] = swap(v["mine"])
    v["far_one"] += [across(v["far_one"][0], 2), across(v["far_one"][2][2:], 1)]
    w_two = lax.all_gather(v.pop("line_two"), "chip")
    v["cot_other"] = swap(v["cot_own"])
    v = tie(v)

    v["w_two"] = w_two
    pieces = (v.pop("line_one"), *v.pop("far_one"))
    v["grads_one"], v["after_cross"], v["normed_three"], v["cot"], v["out_sum"], v["back_sum"] = feed_first(
        place, v["after_attn"], v["mine"], v["theirs"], v["norms"], v.pop("cot_own"), v.pop("cot_other"), pieces
    )
    v = tie(v)

    total_one = lax.psum_scatter(v.pop("grads_one"), "chip", scatter_dimension=0, tiled=False)
    *v["grads_two"], v["out_keep"], v["out_sent"], v["mine"] = feed_second(
        place, v.pop("normed_three"), v["cot"], v.pop("out_sum"), v.pop("back_sum"), v.pop("w_two")
    )
    v = tie(v)

    v["out_theirs"] = swap(v.pop("out_sent"))
    v = tie(v)
    v["theirs"] = swap(v["mine"])
    v["got_two"] = grad_corners(v["grads_two"])
    v["pieces"] = exchange(finish(place, v.pop("out_keep"), v.pop("out_theirs")))
    v["grad_cross"], v["part"], v["norms_three"], v["text_part"], *v["grads_three"] = fused_cross_backward(
        place, v.pop("after_cross"), v.pop("mine"), v.pop("theirs"), v.pop("cot"), v["norms"], v.pop("w_cross"),
        v.pop("normed_two"), v.pop("text"), v.pop("queries"), v.pop("keys"), v.pop("cross_mix"),
        v.pop("cross_lse"), v.pop("ids"), v.pop("caption"),
    )
    v = tie(v)

    v["theirs"] = swap(v["part"])
    v["total_one"] = total_one
    to_two = relay(v["grads_two"][2], v["grads_two"][1], *v.pop("got_two"))

    v["sides_two"] = [across(to_two[0], 2), across(to_two[1], 1)]
    v["got_three"] = grad_corners(v["grads_three"])
    v["line_one"] = lax.psum_scatter(v.pop("total_one"), "hi", scatter_dimension=0, tiled=False)
    v["grad_own"], v["low_grad"], v["norms_two"], v["dqkv"] = fused_self_backward(
        place, v.pop("after_attn"), v.pop("part"), v.pop("theirs"), v.pop("grad_cross"), v["norms"], v["w_self"],
        v.pop("qkv"), v["self_mix"], v.pop("self_lse"),
    )
    v = tie(v)

    v["sides_three"], sides_two = grad_sides(v["grads_three"], v.pop("got_three"), v.pop("sides_two"))
    total_two = plane_sum_whole(v.pop("grads_two")[0], *sides_two)
    line_two = lax.psum_scatter(total_two, "hi", scatter_dimension=0, tiled=True)
    v["grads_four"] = self_grads(place, v.pop("normed_one"), v.pop("low_grad"), v["dqkv"], v.pop("self_mix"))
    mine, sent = part_images(place, v.pop("pieces"))
    (v["result"],) = land(place, mine, swap(sent), BF)
    v["feed_one"] = halves(v.pop("line_one"))
    v = tie(v)

    v["got_four"] = grad_corners(v["grads_four"])
    total_three, dqkv = tie((plane_sum_whole(v.pop("grads_three")[0], *v.pop("sides_three")), v.pop("dqkv")))
    line_three = lax.psum_scatter(total_three, "hi", scatter_dimension=0, tiled=True)
    v["line_two"] = line_two
    v["kept"], v["sent"] = self_back(place, dqkv, v.pop("w_self"))
    v = tie(v)

    v["sides_four"], _ = grad_sides(v["grads_four"], v.pop("got_four"), place)
    pieces = last_norm(
        place, v.pop("rows_own"), v.pop("grad_own"), v.pop("kept"), swap(v.pop("sent")), v.pop("norms"),
        v.pop("text_part"), v.pop("norms_two"), v.pop("norms_three"),
    )
    input_pieces = exchange(pieces)
    v = tie(v)

    v["kept"], *sums_four = plane_sum(place, v.pop("grads_four")[0], *v.pop("sides_four"))
    v["line_four"] = [shift(piece, 3 - i) for i, piece in enumerate(sums_four)]
    v["feed_grads"] = spread_feed(place, *v.pop("feed_one"), *halves(v.pop("line_two")))
    later = tie((place, sums_four))[0]
    mine, sent = part_images(later, input_pieces)
    v["input_grad"], v["text_grad"], sums = land(place, mine, swap(sent), F32)
    sums = sums + across(sums, 1)
    sums = sums + across(sums, 2)
    v["sums"] = lax.dynamic_slice_in_dim(sums, (chip * 2 + core) * 128, 128, 1)
    v["cross_grads"] = spread(place, *halves(line_three))
    v = tie(v)

    kept, sent = line_sum(place, v.pop("kept"), v.pop("line_four"))
    own_grads = spread(place, kept, swap(sent))
    return (
        v["result"], v["input_grad"], v["text_grad"], *own_grads, *v["cross_grads"], *v["feed_grads"],
        *[v["sums"][i] for i in range(6)],
    )


def solution(mesh):
    fsdp, tensor = mesh.shape["fsdp"], mesh.shape["tensor"]

    def run(*args):
        images = args[0].shape[0] // fsdp
        tops = 2 * images
        shape = {"chip": fsdp // 2, "core": 2, "hi": tops, "lo": tensor // tops}
        fine = Mesh(mesh.devices.reshape(tuple(shape.values())), tuple(shape))
        first, second = ("chip", "core"), ("hi", "lo")
        wide, weight, norm = P(first, second, None), P(first, second), P(first)
        outs = (wide,) * 3 + (weight,) * 10 + (norm,) * 6
        packed = (
            (fsdp, tensor, images) == (8, 4, 2)
            and args[0].shape[1:] == (1024, 1024)
            and args[1].shape[1:] == (128, 1024)
            and args[12].shape == (1024, 4096)
        )
        return jax.shard_map(
            lambda *local: packed_layer(local) if packed else layer(shape, local),
            mesh=fine,
            in_specs=(wide, wide, P(first, None), wide) + (weight,) * 10 + (norm,) * 6,
            out_specs=outs,
            check_vma=False,
        )(*args)

    return run
```
